32 devices in a mesh: rows: 16 (over z, x, core), batch: 2 (over y).
Axes of the slice: x: 2, y: 2, z: 4, core: 2. Of those that a mesh axis runs over, the one named last changes fastest.
Arguments:
- features: bfloat16 [3, 8, 32, 64, 384], P(None, 'batch', 'rows'), may hold values from -6 to 6
- drop_mask: int32 [3, 8], P(None, 'batch'), may hold values 0 or 1
- labels: int32 [3, 8], P(None, 'batch'), may hold values from 0 to 999
- params: float32 [3153920], P('rows'), may hold values from -4 to 4, as said below
- moment1: float32 [3153920], P('rows'), may hold values from -1 to 1, as said below
- moment2: float32 [3153920], P('rows'), may hold values from 0 to 1, as said below
Outputs:
- new_params: float32 [3153920], P('rows')
- new_moment1: float32 [3153920], P('rows')
- new_moment2: float32 [3153920], P('rows')
- loss_sum: float32 [], replicated
- grad_norm: float32 [], replicated
- feature_grad: float32 [3, 8, 32, 64, 384], P(None, 'batch', 'rows')
The draws below stay inside these ranges and needn't reach their ends.
Inputs may be any that keep to these rules, and one draw needn't show every extreme that they name: `params`: master parameters laid out as the steps say; gains near one, weights scaled by fan-in. `moment1`: first moments of both signs. `moment2`: positive second moments.
All inputs are finite; a program needn't handle non-finite values. No bound on the sum of `drop_mask` on one device may be relied on, other than what follows from the above.
Results may differ from the reference program's by a relative error of at most 0.0073.
Values may be sent and summed in bfloat16 or wider, within the bound.
A program may use at most 256 MiB of HBM per device.

```python
import jax
import jax.numpy as jnp
from jax import lax

C = 384
HID = 1536
DOUT = 768
CLS = 1000
COLS = 64
MICRO = 3
STEP = 10
IMAGES = 8
HEIGHT = 32
RAW = 3153640
P_SIZE = 3153920


def segment_table():
    return [(49 * C, 1.0 / 7.0, 0.0), (C * HID, C ** (-0.5), 0.0), (HID, 0.2, 0.0), (HID * C, HID ** (-0.5), 0.0), (C, 0.2, 0.0), (C, 0.1, 1.0), (C, 0.2, 0.0), (C, 0.2, 0.0), (C, 0.3, 1.0), (C, 0.1, 1.0), (C, 0.2, 0.0), (4 * C * DOUT, (4 * C) ** (-0.5), 0.0), (DOUT, 0.2, 0.0), (DOUT, 0.1, 1.0), (DOUT, 0.2, 0.0), (DOUT * CLS, 2.0 * DOUT ** (-0.5), 0.0), (CLS, 0.5, 0.0), (P_SIZE - RAW, 0.02, 0.0)]


def shape_noise(noise):
    table = segment_table()
    scales = jnp.concatenate([jnp.full((entry[0],), entry[1], jnp.float32) for entry in table])
    offsets = jnp.concatenate([jnp.full((entry[0],), entry[2], jnp.float32) for entry in table])
    return noise * scales + offsets


def draw_params(key, part):
    key = jax.random.fold_in(key, 11)
    noise = jax.random.normal(key, (P_SIZE,), jnp.float32)
    return shape_noise(noise)


def draw_moment1(key, part):
    key = jax.random.fold_in(key, 12)
    typical = 0.01 * P_SIZE ** (-0.5)
    return jax.random.normal(key, (P_SIZE,), jnp.float32) * (0.11 * typical)


def draw_moment2(key, part):
    key = jax.random.fold_in(key, 13)
    typical = 0.01 * P_SIZE ** (-0.5)
    lowest = jnp.log(0.0005 * typical * typical)
    highest = jnp.log(0.008 * typical * typical)
    return jnp.exp(jax.random.uniform(key, (P_SIZE,), jnp.float32, lowest, highest))


def set_ends(array, own_key, low, largest):
    longest = array.shape.index(max(array.shape))
    spots = []
    for shift in (0, 1):
        where = [jax.random.randint(jax.random.fold_in(own_key, axis), (), 0, length) for axis, length in enumerate(array.shape)]
        where[longest] = (where[longest] + shift) % array.shape[longest]
        spots.append(tuple(where))
    return array.at[spots[0]].set(low).at[spots[1]].set(largest)


def levels(key, extent, split, least, largest):
    level = 1.0
    for dim, parts in split:
        steps = jax.random.uniform(jax.random.fold_in(jax.random.fold_in(key, 6), dim), (parts,), jnp.float32, least / len(split), largest / len(split))
        level = level * jnp.repeat(jnp.exp(steps), extent[dim] // parts).reshape((-1,) + (1,) * (len(extent) - 1 - dim))
    return level


def normal_values(rng, extent, scale, bound, cuts=(), kind=jnp.bfloat16):
    drawn = scale * jax.random.normal(rng, extent, jnp.float32)
    if cuts:
        drawn = drawn * levels(rng, extent, cuts, -0.22, 0.18)
    return jnp.clip(drawn, -bound, bound).astype(kind)


def setup_inputs(seed: int = 0) -> dict:
    seeds = jax.random.split(jax.random.key(seed), 7)
    features = normal_values(seeds[0], (MICRO, IMAGES, HEIGHT, COLS, C), 1.0, 6.0, ((1, 2), (2, 16)))
    drop_mask = set_ends((jax.random.randint(seeds[1], (MICRO, IMAGES), 0, 5) < 4).astype(jnp.int32), jax.random.fold_in(seeds[1], 1), 0, 1)
    labels = set_ends(jax.random.randint(seeds[2], (MICRO, IMAGES), 0, CLS), jax.random.fold_in(seeds[2], 1), 0, CLS - 1).astype(jnp.int32)
    params = draw_params(jax.random.fold_in(seeds[6], 71), 0)
    moment1 = draw_moment1(jax.random.fold_in(seeds[6], 71), 0)
    moment2 = draw_moment2(jax.random.fold_in(seeds[6], 71), 0)
    return {"features": features, "drop_mask": drop_mask, "labels": labels, "params": params, "moment1": moment1, "moment2": moment2}


KEEP = 0.8
CLIP = 0.01
RATE = 0.05
BETA_ONE = 0.9
BETA_TWO = 0.999
DECAY = 0.05
EPS_ADAM = 1e-08
EPS_NORM = 1e-06
HIGH = lax.Precision.HIGHEST

@jax.custom_vjp
def low(v):
    return lax.optimization_barrier(v.astype(jnp.bfloat16)).astype(jnp.float32)

@jax.custom_vjp
def low_back(v):
    return v

def low_keep(v):
    return (low(v), None)

def low_pass(kept, grad):
    return (grad,)

def back_keep(v):
    return (v, None)

def back_low(kept, grad):
    return (low(grad),)
low.defvjp(low_keep, low_pass)
low_back.defvjp(back_keep, back_low)

def unpack(flat):
    lengths = [49 * C, C * HID, HID, HID * C, 7 * C, 4 * C * DOUT, 3 * DOUT, DOUT * CLS, CLS]
    pieces = []
    offset = 0
    for length in lengths:
        pieces.append(flat[offset:offset + length])
        offset += length
    return (pieces[0].reshape(7, 7, C), pieces[1].reshape(C, HID), pieces[2], pieces[3].reshape(HID, C), pieces[4].reshape(7, C), pieces[5].reshape(4 * C, DOUT), pieces[6].reshape(3, DOUT), pieces[7].reshape(DOUT, CLS), pieces[8])

def layer_norm(values, gain, shift):
    centred = values - lax.optimization_barrier(jnp.mean(values, -1, keepdims=True))
    spread = lax.optimization_barrier(jnp.mean(centred * centred, -1, keepdims=True))
    return centred * lax.rsqrt(spread + EPS_NORM) * gain + shift

def depthwise(padded, kernel, bias_vec):
    row_count = padded.shape[1] - 6
    col_count = padded.shape[2] - 6
    result = jnp.zeros(padded.shape[:1] + (row_count, col_count, padded.shape[3]), jnp.float32) + bias_vec
    for offset_r in range(7):
        for offset_c in range(7):
            result = result + padded[:, offset_r:offset_r + row_count, offset_c:offset_c + col_count, :] * kernel[offset_r, offset_c]
    return result

def forward(flat, feats, mask, labs):
    kernel, w_up, c_up, w_down, vec_c, w_ds, vec_o, w_head, b_head = unpack(flat)
    images, height, width, chans = feats.shape
    padded = jnp.pad(feats, ((0, 0), (3, 3), (3, 3), (0, 0)))
    conv_out = depthwise(padded, kernel, vec_c[0])
    normed = low(layer_norm(conv_out, vec_c[1], vec_c[2]))
    hidden = low_back(jnp.dot(normed.reshape(-1, C), low(w_up), precision=HIGH) + c_up)
    active = low(jax.nn.gelu(hidden, approximate=True))
    branch = low_back(jnp.dot(active, low(w_down), precision=HIGH) + vec_c[3]).reshape(feats.shape)
    scaled = (mask.astype(jnp.float32) / KEEP)[:, None, None, None]
    resid = feats + scaled * vec_c[4] * branch
    normed2 = low(layer_norm(resid, vec_c[5], vec_c[6]))
    patches = normed2.reshape(images, height // 2, 2, width // 2, 2, C).transpose(0, 1, 3, 2, 4, 5).reshape(-1, 4 * C)
    down = low_back(jnp.dot(patches, low(w_ds), precision=HIGH) + vec_o[0]).reshape(images, -1, DOUT)
    pooled = lax.optimization_barrier(jnp.mean(down, 1))
    query = low(layer_norm(pooled, vec_o[1], vec_o[2]))
    logits = low_back(jnp.dot(query, low(w_head), precision=HIGH) + b_head)
    top = lax.optimization_barrier(jnp.max(logits, 1, keepdims=True))
    lse = top[:, 0] + jnp.log(lax.optimization_barrier(jnp.sum(jnp.exp(logits - top), 1)))
    onehot = (jnp.arange(CLS)[None, :] == labs[:, None]).astype(jnp.float32)
    return jnp.sum(lse - lax.optimization_barrier(jnp.sum(logits * onehot, 1)))

def reference(features, drop_mask, labels, params, moment1, moment2):
    weight = 1.0 / (MICRO * IMAGES)

    def one_batch(carry, item):
        feats, mask, labs = item
        loss, back = jax.vjp(lambda flat, maps: forward(flat, maps, mask, labs), params, feats.astype(jnp.float32))
        g_params, g_feats = back(jnp.ones((), jnp.float32) * weight)
        return ((carry[0] + g_params, carry[1] + loss), g_feats)
    init = (jnp.zeros((P_SIZE,), jnp.float32), jnp.zeros((), jnp.float32))
    (grads, loss_sum), feature_grad = lax.scan(one_batch, init, (features, drop_mask, labels))
    grad_norm = jnp.sqrt(jnp.sum(grads * grads))
    clipped = grads * jnp.minimum(1.0, CLIP / (grad_norm + 1e-06))
    first = BETA_ONE * moment1 + (1.0 - BETA_ONE) * clipped
    second = BETA_TWO * moment2 + (1.0 - BETA_TWO) * clipped * clipped
    ratio = first / (1.0 - BETA_ONE ** STEP) / (jnp.sqrt(second / (1.0 - BETA_TWO ** STEP)) + EPS_ADAM)
    new_params = params - RATE * (ratio + DECAY * params)
    return (new_params, first, second, loss_sum, grad_norm, feature_grad)
```

```python
import functools

import jax
import jax.numpy as jnp
from jax import lax
from jax.experimental import pallas as pl
from jax.experimental.pallas import tpu as pltpu
from jax.sharding import PartitionSpec as P

C = 384
HID = 1536
DOUT = 768
CLS = 1000
MICRO = 3
STEP = 10
P_SIZE = 3153920
KEEP = 0.8
CLIP = 0.01
RATE = 0.05
BETA_ONE = 0.9
BETA_TWO = 0.999
DECAY = 0.05
EPS_ADAM = 1e-08
EPS_NORM = 1e-06

MESH = pl.DeviceIdType.MESH
F32 = jnp.float32
BF16 = jnp.bfloat16
MB = 1 << 20

LANES = 128
J = C // LANES
GROUP = 4
OWN = 8
COLS = 64
PADC = COLS + 6
SUB = 16
POS = COLS * OWN
NPOS = MICRO * POS
FLAT = P_SIZE // LANES
ROW_K = 0
ROW_UP = 49 * J
ROW_CUP = ROW_UP + C * HID // LANES
ROW_DOWN = ROW_CUP + HID // LANES
ROW_VEC = ROW_DOWN + C * HID // LANES
ROW_DS = ROW_VEC + 7 * J
ROW_OUT = ROW_DS + 4 * C * DOUT // LANES
ROW_HEAD = ROW_OUT + 3 * DOUT // LANES
ROW_BH = ROW_HEAD + DOUT * CLS // LANES
TABLES = (
    (ROW_K, 49 * J, 0),
    (ROW_CUP, HID // LANES, 152),
    (ROW_VEC, 7 * J, 168),
    (ROW_OUT, 3 * DOUT // LANES, 192),
    (ROW_BH, FLAT - ROW_BH, 216),
)
TAB_ROWS = 232
TAB_SPAN = (152, 16, 24, 24, 16)
T_CUP, T_VEC, T_OUT, T_BH = 152, 168, 192, 216
SG_ROWS = 256
SG_CUP, SG_VEC = 152, 168
CLSP = 1024


class Env:
    pass


def xrow(j, m):
    return (j * MICRO + m) * PADC * SUB


def rows_of(refs, row, count):
    return refs[row : row + count, :]


def lane_row(ref, row, count):
    return jnp.concatenate([ref[row + k : row + k + 1, :] for k in range(count)], axis=1)


def ln_parts(blocks, width):
    total = blocks[0]
    for block in blocks[1:]:
        total = total + block
    mean = jnp.sum(total, -1, keepdims=True) * (1.0 / width)
    centred = [block - mean for block in blocks]
    square = centred[0] * centred[0]
    for block in centred[1:]:
        square = square + block * block
    spread = jnp.sum(square, -1, keepdims=True) * (1.0 / width)
    scale = lax.rsqrt(spread + EPS_NORM)
    return [block * scale for block in centred], scale


def here(e):
    e.r = lax.axis_index("rows")
    e.b = lax.axis_index("batch")
    e.g = e.r // GROUP
    e.i = e.r % GROUP


def dev(e, r=None, b=None):
    return {"rows": e.r if r is None else r, "batch": e.b if b is None else b}


def remote(e, src, dst, send, recv, r=None, b=None):
    return pltpu.make_async_remote_copy(
        src, dst, send, recv, device_id=(e.r if r is None else r, e.b if b is None else b), device_id_type=MESH
    )


def ph_barrier_signal(e, B):
    barrier = pltpu.get_barrier_semaphore()
    for d in range(1, e.n):
        pl.semaphore_signal(barrier, inc=1, device_id=(lax.rem(e.r + d, e.n), e.b), device_id_type=MESH)
    for d in range(1, e.nb):
        pl.semaphore_signal(barrier, inc=1, device_id=(e.r, lax.rem(e.b + d, e.nb)), device_id_type=MESH)


def ph_barrier_wait(e, B):
    pl.semaphore_wait(pltpu.get_barrier_semaphore(), e.n - 1 + e.nb - 1)


def ph_feat_start(e, B):
    e.feat = []
    own = pltpu.make_async_copy(
        B.features.at[:, e.i], B.xg.at[:, pl.ds(3 + 2 * e.i, 2)], B.s_own.at[0]
    )
    own.start()
    e.feat_own = own
    for d in range(1, GROUP):
        j = lax.rem(e.i + d, GROUP)
        cp = remote(
            e,
            B.features.at[:, j],
            B.xg.at[:, pl.ds(3 + 2 * e.i, 2)],
            B.s_feat.at[d],
            B.r_feat.at[d],
            r=e.g * GROUP + j,
        )
        cp.start()
        e.feat.append(cp)


def ph_feat_zero(e, B):
    zero = jnp.zeros((MICRO, 3, COLS, C), BF16)

    @pl.when(e.g == 0)
    def _():
        B.xg[:, 0:3] = zero

    @pl.when(e.g == e.G - 1)
    def _():
        B.xg[:, 11:14] = zero


def ph_feat_halo(e, B):
    e.feat_own.wait()
    for cp in e.feat:
        cp.wait_recv()
    down = remote(e, B.xg.at[:, 3:6], B.xg.at[:, 11:14], B.s_halo.at[0], B.r_halo.at[0], r=e.r - GROUP)
    up = remote(e, B.xg.at[:, 8:11], B.xg.at[:, 0:3], B.s_halo.at[1], B.r_halo.at[1], r=e.r + GROUP)

    @pl.when(e.g > 0)
    def _():
        down.start()

    @pl.when(e.g < e.G - 1)
    def _():
        up.start()

    @pl.when(e.g < e.G - 1)
    def _():
        down.wait_recv()

    @pl.when(e.g > 0)
    def _():
        up.wait_recv()

    for cp in e.feat:
        cp.wait_send()

    @pl.when(e.g > 0)
    def _():
        down.wait_send()

    @pl.when(e.g < e.G - 1)
    def _():
        up.wait_send()


def ph_cast(e, B):
    whole = e.slab // 16 * 16
    slot = B.gw.at[e.r]
    slot[0:whole, :] = B.params[0:whole, :].astype(BF16)
    rest = e.slab - whole
    if rest:
        tail = jnp.concatenate([B.params[whole : e.slab, :], jnp.zeros((16 - rest, LANES), F32)], axis=0)
        slot[whole : whole + 16, :] = tail.astype(BF16)
    for k, (first, count, place) in enumerate(TABLES):
        off = first % e.slab
        B.stage[place : place + count, :] = B.params[off : off + count, :]


def table_copies(e, B, k):
    first, count, place = TABLES[k]
    owner = first // e.slab
    span = TAB_SPAN[k]
    return owner, [
        remote(
            e,
            B.stage.at[place : place + span],
            B.tab.at[place : place + span],
            B.s_tab.at[k, d],
            B.r_tab.at[k],
            r=lax.rem(owner + d, e.n),
        )
        for d in range(1, e.n)
    ]


def ph_tables_start(e, B):
    for k in range(len(TABLES)):
        first, count, place = TABLES[k]
        owner, copies = table_copies(e, B, k)

        @pl.when(e.r == owner)
        def _(copies=copies, place=place, k=k):
            for cp in copies:
                cp.start()
            B.tab[place : place + TAB_SPAN[k], :] = B.stage[place : place + TAB_SPAN[k], :]


def ph_tables_wait(e, B):
    for k in range(len(TABLES)):
        owner, copies = table_copies(e, B, k)

        @pl.when(e.r == owner)
        def _(copies=copies):
            for cp in copies:
                cp.wait_send()

        @pl.when(e.r != owner)
        def _(copies=copies):
            copies[0].wait_recv()


def line_copy(e, B, level, up, d):
    slot = level * GROUP + e.i
    return remote(
        e,
        B.gw.at[slot],
        B.gw.at[slot],
        B.s_line.at[0 if up else 1, d],
        B.r_line.at[0 if up else 1, d],
        r=e.r + GROUP if up else e.r - GROUP,
    )


def pair_copy(e, B, level):
    slot = level * GROUP + e.i
    return remote(
        e,
        B.gw.at[slot],
        B.gw.at[slot],
        B.s_pair.at[level],
        B.r_pair.at[level],
        r=e.g * GROUP + lax.rem(e.i + 2, GROUP),
    )


def core_copy(e, B, level, other):
    i = lax.rem(e.i + 2, GROUP) if other else e.i
    slot = level * GROUP + i
    sib = e.g * GROUP + e.i + 1 - 2 * (e.i % 2)
    return remote(e, B.gw.at[slot], B.gw.at[slot], B.s_core.at[int(other), level], B.r_core.at[int(other), level], r=sib)


def ph_gather(e, B):
    G = e.G
    pair_copy(e, B, e.g).start()
    core_copy(e, B, e.g, False).start()
    for d in range(G - 1):
        lo = e.g - d
        hi = e.g + d

        @pl.when(jnp.logical_and(lo >= 0, e.g + 1 < G))
        def _():
            line_copy(e, B, lo, True, d).start()

        @pl.when(jnp.logical_and(hi < G, e.g >= 1))
        def _():
            line_copy(e, B, hi, False, d).start()

        @pl.when(lo - 1 >= 0)
        def _():
            line_copy(e, B, lo - 1, True, d).wait_recv()
            pair_copy(e, B, lo - 1).start()
            core_copy(e, B, lo - 1, False).start()

        @pl.when(hi + 1 < G)
        def _():
            line_copy(e, B, hi + 1, False, d).wait_recv()
            pair_copy(e, B, hi + 1).start()
            core_copy(e, B, hi + 1, False).start()

    for level in range(G):
        pair_copy(e, B, level).wait_recv()
        core_copy(e, B, level, True).start()
    for level in range(G):
        core_copy(e, B, level, False).wait_recv()
        core_copy(e, B, level, True).wait_recv()
    for level in range(G):
        core_copy(e, B, level, False).wait_send()
        core_copy(e, B, level, True).wait_send()
        pair_copy(e, B, level).wait_send()
    for d in range(G - 1):
        lo = e.g - d
        hi = e.g + d

        @pl.when(jnp.logical_and(lo >= 0, e.g + 1 < G))
        def _():
            line_copy(e, B, lo, True, d).wait_send()

        @pl.when(jnp.logical_and(hi < G, e.g >= 1))
        def _():
            line_copy(e, B, hi, False, d).wait_send()


def flatten(e, B, first, last):
    step = 128
    whole = e.slab // step
    left = e.slab - whole * step
    s0 = first // e.slab
    for s in range(s0, (last - 1) // e.slab + 1):
        base = e.slab * (s - s0)

        def body(t, _, s=s, base=base):
            B.big[pl.ds(base + t * step, step), :] = B.gw[s, pl.ds(pl.multiple_of(t * step, step), step), :].astype(F32)
            return 0

        lax.fori_loop(0, whole, body, 0)
        if left:
            size = (left + 15) // 16 * 16
            B.big[pl.ds(base + whole * step, size), :] = B.gw[s, whole * step : whole * step + size, :].astype(F32)
    return e.slab * s0


def ph_weights_mlp(e, B):
    base = flatten(e, B, ROW_UP, ROW_VEC)
    for j in range(HID // LANES):
        B.wup[:, LANES * j : LANES * (j + 1)] = B.big[pl.ds(ROW_UP - base + j, C, stride=HID // LANES), :].astype(BF16)
    for j in range(J):
        B.wdn[:, LANES * j : LANES * (j + 1)] = B.big[pl.ds(ROW_DOWN - base + j, HID, stride=J), :].astype(BF16)


def ph_weights_head(e, B):
    base = flatten(e, B, ROW_DS, ROW_OUT)
    per = DOUT // LANES
    for j in range(per):
        B.wds[:, LANES * j : LANES * (j + 1)] = B.big[pl.ds(ROW_DS - base + j, 4 * C, stride=per), :].astype(BF16)
    base = flatten(e, B, ROW_HEAD, ROW_BH)
    lane = lax.broadcasted_iota(jnp.int32, (DOUT // 16, LANES), 1)
    for kk in range(16):
        first, off = divmod(CLS * kk, LANES)
        parts = [B.big[pl.ds(ROW_HEAD - base + first + t, DOUT // 16, stride=125), :] for t in range(9 if off else 8)]
        if off:
            parts = [pltpu.roll(part, LANES - off, 1) for part in parts]
        for t in range(8):
            tile = parts[t]
            if off:
                tile = jnp.where(lane < LANES - off, parts[t], parts[t + 1])
            if t == 7:
                tile = jnp.where(lane < CLS - 7 * LANES, tile, 0.0)
            B.dx[pl.ds(DOUT * t + kk, DOUT // 16, stride=16), :] = tile
    for t in range(8):
        B.wh[:, LANES * t : LANES * (t + 1)] = B.dx[DOUT * t : DOUT * (t + 1), :].astype(BF16)


def ph_transpose(e, B):
    pad = jnp.zeros((3 * SUB, LANES), F32)

    def body(m, _):
        for j in range(J):
            B.big[pl.ds(xrow(j, m), 3 * SUB), :] = pad
            B.big[pl.ds(xrow(j, m) + (COLS + 3) * SUB, 3 * SUB), :] = pad
            for row in range(14):
                v = B.xg[m, row, :, LANES * j : LANES * (j + 1)].astype(F32)
                B.big[pl.ds(xrow(j, m) + 3 * SUB + row, COLS, stride=SUB), :] = v
                if 3 <= row < 11:
                    B.xc[j, pl.ds(m * POS + row - 3, COLS, stride=OWN), :] = v
        return 0

    lax.fori_loop(0, MICRO, body, 0)


def ph_taps(e, B):
    def body(t, _):
        B.kb[t] = jnp.broadcast_to(B.tab[pl.ds(t, 1), :], (8, LANES))
        return 0

    lax.fori_loop(0, 49 * J, body, 0)


def vec_row(B, v, j):
    row = T_VEC + v * J + j
    return B.tab[row : row + 1, :]


def ph_conv_fwd(e, B):
    tile = 8
    per = COLS // tile

    def body(it, _):
        m = it // per
        c0 = (it % per) * tile
        sums = []
        for j in range(J):
            acc = jnp.broadcast_to(vec_row(B, 0, j).reshape(1, 1, LANES), (tile, OWN, LANES))
            for a in range(7):
                cols = [B.big[pl.ds(xrow(j, m) + (c0 + c) * SUB + a, OWN), :] for c in range(tile + 6)]
                for b in range(7):
                    acc = acc + jnp.stack(cols[b : b + tile]) * B.kb[(a * 7 + b) * J + j]
            sums.append(acc.reshape(tile * OWN, LANES))
        hat, scale = ln_parts(sums, C)
        at = pl.multiple_of(m * POS + c0 * OWN, tile * OWN)
        B.rs1[pl.ds(at, tile * OWN), :] = jnp.broadcast_to(scale, (tile * OWN, LANES))
        for j in range(J):
            B.v1[pl.ds(at, tile * OWN), LANES * j : LANES * (j + 1)] = hat[j]
            B.n[pl.ds(at, tile * OWN), LANES * j : LANES * (j + 1)] = (
                hat[j] * vec_row(B, 1, j) + vec_row(B, 2, j)
            ).astype(BF16)
        return 0

    lax.fori_loop(0, MICRO * per, body, 0)


def ph_mlp_fwd(e, B):
    chunk = 256
    width = 256
    c0 = 0.7978845608028654
    c1 = 0.044715 * c0
    B.ps[...] = jnp.zeros_like(B.ps)

    def body(it, _):
        at = pl.multiple_of(it * chunk, chunk)
        m = it // (POS // chunk)
        keep = B.mask[m, e.i].astype(F32) * (1.0 / KEEP)
        rows = B.n[pl.ds(at, chunk), :]
        for k in range(HID // width):
            lanes = slice(width * k, width * (k + 1))
            bias = lane_row(B.tab, T_CUP + k * width // LANES, width // LANES)
            h = jnp.dot(rows, B.wup[:, lanes], preferred_element_type=F32) + bias
            sq = h * h
            half = 0.5 * jnp.tanh(h * (c0 + c1 * sq)) + 0.5
            u = h * half
            B.u[pl.ds(at, chunk), lanes] = u.astype(BF16)
            slope = half + u * (1.0 - half) * (2.0 * c0 + 6.0 * c1 * sq)
            B.gp[pl.ds(at, chunk), lanes] = slope.astype(BF16)
        z = jnp.dot(B.u[pl.ds(at, chunk), :], B.wdn[...], preferred_element_type=F32)
        resid = []
        for j in range(J):
            zj = z[:, LANES * j : LANES * (j + 1)] + vec_row(B, 3, j)
            B.z[pl.ds(at, chunk), LANES * j : LANES * (j + 1)] = zj
            resid.append(B.xc[j, pl.ds(at, chunk), :] + (vec_row(B, 4, j) * keep) * zj)
        hat, scale = ln_parts(resid, C)
        B.rs2[pl.ds(at, chunk), :] = jnp.broadcast_to(scale, (chunk, LANES))
        for j in range(J):
            B.v2[pl.ds(at, chunk), LANES * j : LANES * (j + 1)] = hat[j]
            low = (hat[j] * vec_row(B, 5, j) + vec_row(B, 6, j)).astype(BF16).astype(F32)
            low = jnp.sum(low.reshape(chunk // 16, 2, OWN, LANES), 0)
            B.ps[m, :, :, LANES * j : LANES * (j + 1)] += low
        return 0

    lax.fori_loop(0, NPOS // chunk, body, 0)


def ph_patch_local(e, B):
    even = lax.broadcasted_iota(jnp.int32, (OWN, C), 0) % 2 == 0
    pick = lax.broadcasted_iota(jnp.int32, (8, C), 0)
    for parity in range(2):
        for side in range(2):
            tile = jnp.zeros((8, C), F32)
            for m in range(MICRO):
                v = B.ps[m, side]
                part = jnp.sum(jnp.where(even if parity == 0 else jnp.logical_not(even), v, 0.0), 0, keepdims=True)
                tile = jnp.where(pick == m, part, tile)
            q = 2 * parity + side
            B.sl[8 * q : 8 * q + 8, :] = tile


def patch_copy(e, B, d):
    to = lax.rem(e.g + d, e.G)
    return remote(e, B.sl, B.sr.at[d], B.s_patch.at[d], B.r_patch.at[d], r=to * GROUP + e.i)


def ph_patch_exchange(e, B):
    for d in range(1, e.G):
        patch_copy(e, B, d).start()
    B.sr[0] = B.sl[...]
    for d in range(1, e.G):
        patch_copy(e, B, d).wait_recv()
    for d in range(1, e.G):
        patch_copy(e, B, d).wait_send()


def split3(v):
    hi = v.astype(BF16).astype(F32)
    mid = (v - hi).astype(BF16).astype(F32)
    return hi, mid, v - hi - mid


def ph_head(e, B):
    total = None
    for level in range(e.G):
        part = B.sr[lax.rem(e.g - level + e.G, e.G)]
        total = part if total is None else total + part
    per = DOUT // LANES
    gain = lane_row(B.tab, T_OUT + per, per)
    shift = lane_row(B.tab, T_OUT + 2 * per, per)
    mean = total * (1.0 / e.positions)
    pooled = lane_row(B.tab, T_OUT, per)
    for q in range(4):
        parts = jnp.concatenate(split3(mean[8 * q : 8 * q + 8, :]), axis=0).astype(BF16)
        prod = jnp.dot(parts, B.wds[C * q : C * (q + 1), :], preferred_element_type=F32)
        pooled = pooled + (prod[0:8] + (prod[8:16] + prod[16:24]))
    rows = lax.broadcasted_iota(jnp.int32, (8, 1), 0)
    live = rows < MICRO
    (hat,), scale = ln_parts([pooled], DOUT)
    query = (hat * gain + shift).astype(BF16)
    lane = lax.broadcasted_iota(jnp.int32, (8, CLSP), 1)
    logits = jnp.dot(query, B.wh[...], preferred_element_type=F32) + lane_row(B.tab, T_BH, CLSP // LANES)
    logits = jnp.where(lane < CLS, logits, -1e30)
    top = jnp.max(logits, 1, keepdims=True)
    powers = jnp.exp(logits - top)
    expsum = jnp.sum(powers, 1, keepdims=True)
    label = jnp.zeros((8, 1), jnp.int32)
    for m in range(MICRO):
        label = jnp.where(rows == m, B.labels[m, e.i], label)
    onehot = (lane == label).astype(F32)
    own = jnp.sum(jnp.where(lane == label, logits, 0.0), 1, keepdims=True)
    loss = jnp.sum(jnp.where(live, top + jnp.log(expsum) - own, 0.0), 0, keepdims=True)
    grad = jnp.where(live, (powers / expsum - onehot) * e.inv_count, 0.0).astype(BF16)
    grad_query = lax.dot_general(grad, B.wh[...], (((1,), (1,)), ((), ())), preferred_element_type=F32)
    dn = grad_query * gain
    m1 = jnp.sum(dn, 1, keepdims=True) * (1.0 / DOUT)
    m2 = jnp.sum(dn * hat, 1, keepdims=True) * (1.0 / DOUT)
    grad_pool = scale * (dn - m1 - hat * m2)
    down = jnp.where(live, grad_pool * (1.0 / e.positions), 0.0).astype(BF16)
    for q in range(4):
        B.dn2[8 * q : 8 * q + 8, :] = lax.dot_general(
            down, B.wds[C * q : C * (q + 1), :], (((1,), (1,)), ((), ())), preferred_element_type=F32
        )
    low = grad.astype(F32)
    d32 = down.astype(F32)
    q32 = jnp.where(live, query.astype(F32), 0.0)
    zero3 = jnp.zeros((3, C), F32)
    g3 = jnp.sum(jnp.where(live, grad_query * hat, 0.0), 0, keepdims=True)
    s3 = jnp.sum(jnp.where(live, grad_query, 0.0), 0, keepdims=True)
    vec = jnp.concatenate([g3, s3], axis=1)
    vec_parts = split3(vec)
    loss_parts = split3(loss)
    for q in range(4):
        at = slice(C * q, C * (q + 1))
        s_hi, s_mid, _ = split3(total[8 * q : 8 * q + 8, :])
        B.pb[0:8, at] = jnp.zeros((8, C), F32)
        B.pb[8:16, at] = jnp.zeros((8, C), F32)
        B.pb[0:3, at] = s_hi[0:3]
        B.pb[3:6, at] = s_mid[0:3]
    B.pb[6:9, 0:DOUT] = d32[0:3]
    B.pb[6:9, DOUT : 2 * DOUT] = q32[0:3]
    B.pb[9:12, 0:CLSP] = low[0:3]
    for k in range(3):
        B.pb[12 + k : 13 + k, :] = vec_parts[k]
        B.pb[15:16, LANES * k : LANES * (k + 1)] = jnp.broadcast_to(loss_parts[k], (1, LANES))
    B.pall[e.i * e.nb + e.b] = B.pb[...].astype(BF16)
    even = lax.broadcasted_iota(jnp.int32, (OWN, C), 0) % 2 == 0
    for m in range(MICRO):
        for side in range(2):
            first = B.dn2[8 * side + m : 8 * side + m + 1, :]
            second = B.dn2[8 * (2 + side) + m : 8 * (2 + side) + m + 1, :]
            B.dnt[m, side] = jnp.where(even, first, second)


def batch_copy(e, B, d):
    slot = e.i * e.nb + e.b
    return remote(e, B.pall.at[slot], B.pall.at[slot], B.s_pb.at[d], B.r_pb.at[d], b=lax.rem(e.b + d, e.nb))


def group_copy(e, B, d):
    at = pl.ds(e.i * e.nb, e.nb)
    to = e.g * GROUP + lax.rem(e.i + d, GROUP)
    return remote(e, B.pall.at[at], B.pall.at[at], B.s_pg.at[d], B.r_pg.at[d], r=to)


def ph_payload_batch(e, B):
    for d in range(1, e.nb):
        batch_copy(e, B, d).start()


def ph_payload_group(e, B):
    for d in range(1, e.nb):
        batch_copy(e, B, d).wait_recv()
    for d in range(1, GROUP):
        group_copy(e, B, d).start()


def ph_payload_wait(e, B):
    for d in range(1, GROUP):
        group_copy(e, B, d).wait_recv()
    for d in range(1, e.nb):
        batch_copy(e, B, d).wait_send()
    for d in range(1, GROUP):
        group_copy(e, B, d).wait_send()


def lane_sum(blocks):
    total = blocks[0]
    for block in blocks[1:]:
        total = total + block
    return jnp.sum(total, -1, keepdims=True) * (1.0 / C)


def fold8(v):
    return jnp.sum(v.reshape(v.shape[0] // 8, 8, v.shape[1]), 0)


def ph_mlp_bwd(e, B):
    chunk = 256
    width = 256
    half = chunk // 16
    B.acc[...] = jnp.zeros_like(B.acc)
    B.acup[...] = jnp.zeros_like(B.acup)
    B.vs[...] = jnp.zeros_like(B.vs)

    def body(it, _):
        at = pl.multiple_of(it * chunk, chunk)
        m = it // (POS // chunk)
        c0 = (it % (POS // chunk)) * (chunk // OWN)
        keep = B.mask[m, e.i].astype(F32) * (1.0 / KEEP)
        span = pl.ds(at, chunk)
        lanes = [slice(LANES * j, LANES * (j + 1)) for j in range(J)]
        dg = [B.dnt[m, :, :, lanes[j]] * vec_row(B, 5, j) for j in range(J)]
        m1 = lane_sum(dg)
        hat = [B.v2[span, lanes[j]].reshape(half, 2, OWN, LANES) for j in range(J)]
        m2 = lane_sum([dg[j] * hat[j] for j in range(J)])
        scale = B.rs2[span, :].reshape(half, 2, OWN, LANES)
        for j in range(J):
            dr = (scale * (dg[j] - m1 - hat[j] * m2)).reshape(chunk, LANES)
            B.vs[m, :, :, lanes[j]] += jnp.sum(hat[j], 0)
            dz = (dr * (vec_row(B, 4, j) * keep)).astype(BF16)
            B.dz[span, lanes[j]] = dz
            B.acc[3, :, lanes[j]] += fold8(dz.astype(F32))
            B.acc[4, :, lanes[j]] += fold8(dr * B.z[span, lanes[j]]) * keep
            B.z[span, lanes[j]] = dr
        dz = B.dz[span, :]
        for k in range(HID // width):
            hid = slice(width * k, width * (k + 1))
            du = lax.dot_general(dz, B.wdn[hid, :], (((1,), (1,)), ((), ())), preferred_element_type=F32)
            dh = (du * B.gp[span, hid].astype(F32)).astype(BF16)
            B.gp[span, hid] = dh
            B.acup[:, hid] += fold8(dh.astype(F32))
        dn = lax.dot_general(B.gp[span, :], B.wup[...], (((1,), (1,)), ((), ())), preferred_element_type=F32)
        dns = [dn[:, lanes[j]] for j in range(J)]
        dg = [dns[j] * vec_row(B, 1, j) for j in range(J)]
        hat = [B.v1[span, lanes[j]] for j in range(J)]
        m1 = lane_sum(dg)
        m2 = lane_sum([dg[j] * hat[j] for j in range(J)])
        scale = B.rs1[span, :]
        for j in range(J):
            dy = scale * (dg[j] - m1 - hat[j] * m2)
            B.acc[0, :, lanes[j]] += fold8(dy)
            B.acc[1, :, lanes[j]] += fold8(dns[j] * hat[j])
            B.acc[2, :, lanes[j]] += fold8(dns[j])
            for c in range(chunk // OWN):
                B.big[pl.ds(xrow(j, m) + (3 + c0 + c) * SUB + 3, OWN), :] = dy[OWN * c : OWN * (c + 1), :]
        return 0

    lax.fori_loop(0, NPOS // chunk, body, 0)
    for m in range(MICRO):
        B.acc[5] += B.dnt[m, 0] * B.vs[m, 0] + B.dnt[m, 1] * B.vs[m, 1]
        B.acc[6] += (B.dnt[m, 0] + B.dnt[m, 1]) * float(COLS // 2)


def ph_wgrad(e, B):
    per = 96 // e.n
    width = 256
    for k in range(HID // width):
        w = lax.dot_general(
            B.n[...], B.gp[:, width * k : width * (k + 1)], (((0,), (0,)), ((), ())), preferred_element_type=F32
        )
        w = w.reshape(48, 8, width)
        w = jnp.concatenate([w[:, :, :LANES], w[:, :, LANES:]], axis=1).astype(BF16)
        B.gb[0 : e.G // 2, :, :, :, k] = w.reshape(e.G // 2, 2, 2, per, 16, LANES)
    for k in range(4):
        w = lax.dot_general(
            B.u[:, C * k : C * (k + 1)], B.dz[...], (((0,), (0,)), ((), ())), preferred_element_type=F32
        )
        w = w.reshape(24, 16, C)
        a, b = w[:, 0:8], w[:, 8:16]
        units = [v[:, :, LANES * j : LANES * (j + 1)] for v in (a, b) for j in range(J)]
        tiles = [jnp.concatenate(units[2 * t : 2 * t + 2], axis=1).astype(BF16) for t in range(3)]
        for q in range(24):
            block = 48 + 12 * k + q // 2
            piece, inner = divmod(block, per)
            for t in range(3):
                B.gb[piece // 4, piece // 2 % 2, piece % 2, inner, 3 * (q % 2) + t] = tiles[t][q]


def ph_dy_pack(e, B):
    zero = jnp.zeros((3 * SUB, LANES), F32)
    for m in range(MICRO):
        for j in range(J):
            B.big[pl.ds(xrow(j, m), 3 * SUB), :] = zero
            B.big[pl.ds(xrow(j, m) + (COLS + 3) * SUB, 3 * SUB), :] = zero
            for side in range(2):
                for k in range(3):
                    row = 3 + k if side == 0 else 8 + k
                    v = B.big[pl.ds(xrow(j, m) + 3 * SUB + row, COLS, stride=SUB), :]
                    B.hs[side, m, k, :, LANES * j : LANES * (j + 1)] = v.astype(BF16)


def ph_dy_halo(e, B):
    down = remote(e, B.hs.at[0], B.hr.at[1], B.s_dy.at[0], B.r_dy.at[0], r=e.r - GROUP)
    up = remote(e, B.hs.at[1], B.hr.at[0], B.s_dy.at[1], B.r_dy.at[1], r=e.r + GROUP)

    @pl.when(e.g > 0)
    def _():
        down.start()

    @pl.when(e.g == 0)
    def _():
        B.hr[0] = jnp.zeros_like(B.hr[0])

    @pl.when(e.g < e.G - 1)
    def _():
        up.start()

    @pl.when(e.g == e.G - 1)
    def _():
        B.hr[1] = jnp.zeros_like(B.hr[1])


def ph_dy_unpack(e, B):
    down = remote(e, B.hs.at[0], B.hr.at[1], B.s_dy.at[0], B.r_dy.at[0], r=e.r - GROUP)
    up = remote(e, B.hs.at[1], B.hr.at[0], B.s_dy.at[1], B.r_dy.at[1], r=e.r + GROUP)

    @pl.when(e.g < e.G - 1)
    def _():
        down.wait_recv()
        up.wait_send()

    @pl.when(e.g > 0)
    def _():
        up.wait_recv()
        down.wait_send()

    for m in range(MICRO):
        for j in range(J):
            for side in range(2):
                for k in range(3):
                    row = k if side == 0 else 11 + k
                    v = B.hr[side, m, k, :, LANES * j : LANES * (j + 1)].astype(F32)
                    B.big[pl.ds(xrow(j, m) + 3 * SUB + row, COLS, stride=SUB), :] = v


def ph_conv_bwd(e, B):
    tile = 8
    per = COLS // tile
    for j in range(J):
        lanes = slice(LANES * j, LANES * (j + 1))

        def first(it, _):
            span = pl.ds(pl.multiple_of(it * 256, 256), 256)
            B.dx[pl.ds(pl.multiple_of(j * NPOS + it * 256, 256), 256), :] = B.z[span, lanes]
            return 0

        lax.fori_loop(0, NPOS // 256, first, 0)

        def taps(a, _, j=j):
            def body(it, dk):
                m = it // per
                c0 = (it % per) * tile
                at = pl.multiple_of(m * POS + c0 * OWN, tile * OWN)
                cols = [B.big[pl.ds(xrow(j, m) + (c0 + c) * SUB + a, OWN), :] for c in range(tile + 6)]
                x = B.xc[j, pl.ds(at, tile * OWN), :].reshape(tile, OWN, LANES)
                acc = B.dx[pl.ds(j * NPOS + at, tile * OWN), :].reshape(tile, OWN, LANES)
                out = []
                for b in range(7):
                    d = jnp.stack(cols[b : b + tile])
                    tap = (6 - a) * 7 + 6 - b
                    acc = acc + d * B.kb[tap * J + j]
                    out.append(dk[b] + jnp.sum(d * x, 0))
                B.dx[pl.ds(j * NPOS + at, tile * OWN), :] = acc.reshape(tile * OWN, LANES)
                return tuple(out)

            zero = jnp.zeros((OWN, LANES), F32)
            dk = lax.fori_loop(0, MICRO * per, body, (zero,) * 7)
            for b in range(7):
                tap = (6 - a) * 7 + 6 - b
                B.sg[pl.ds(tap * J + j, 1), :] = jnp.sum(dk[b], 0, keepdims=True)
            return 0

        lax.fori_loop(0, 7, taps, 0)


def ph_small_fill(e, B):
    for k in range(HID // LANES):
        B.sg[SG_CUP + k : SG_CUP + k + 1, :] = jnp.sum(B.acup[:, LANES * k : LANES * (k + 1)], 0, keepdims=True)
    for v in range(7):
        for j in range(J):
            row = SG_VEC + v * J + j
            B.sg[row : row + 1, :] = jnp.sum(B.acc[v, :, LANES * j : LANES * (j + 1)], 0, keepdims=True)


def ph_out_pack(e, B):
    def body(m, _):
        for row in range(OWN):
            for j in range(J):
                v = B.dx[pl.ds(j * NPOS + m * POS + row, COLS, stride=OWN), :]
                B.xg[m, 3 + row, :, LANES * j : LANES * (j + 1)] = v.astype(BF16)
        return 0

    lax.fori_loop(0, MICRO, body, 0)


def out_copy(e, B, d):
    j = lax.rem(e.i + d, GROUP)
    return remote(
        e,
        B.xg.at[:, pl.ds(3 + 2 * j, 2)],
        B.fo.at[:, e.i],
        B.s_out.at[d],
        B.r_out.at[d],
        r=e.g * GROUP + j,
    )


def own_out_copy(e, B):
    return pltpu.make_async_copy(B.xg.at[:, pl.ds(3 + 2 * e.i, 2)], B.fo.at[:, e.i], B.s_own.at[1])


def ph_out_start(e, B):
    own_out_copy(e, B).start()
    for d in range(1, GROUP):
        out_copy(e, B, d).start()


def ph_out_wait(e, B):
    own_out_copy(e, B).wait()
    for d in range(1, GROUP):
        out_copy(e, B, d).wait()


def rs_first(e, B):
    c = e.i % 2
    return remote(e, B.gb.at[:, :, 1 - c], B.ra1, B.s_rs.at[0], B.r_rs.at[0], r=e.r + 1 - 2 * c)


def rs_second(e, B):
    return remote(
        e, B.sa2, B.ra2, B.s_rs.at[1], B.r_rs.at[1], r=e.g * GROUP + lax.rem(e.i + 2, GROUP)
    )


def rs_third(e, B, d):
    to = lax.rem(e.g + d, e.G)
    return remote(e, B.sc.at[to], B.rc.at[d], B.s_rc.at[d], B.r_rc.at[d], r=to * GROUP + e.i)


def rs_fourth(e, B, d):
    return remote(e, B.rb.at[0], B.rb.at[d], B.s_rb.at[d], B.r_rb.at[d], b=lax.rem(e.b + d, e.nb))


def ph_rs_first(e, B):
    rs_first(e, B).start()


def ph_rs_second(e, B):
    x, c = e.i // 2, e.i % 2
    rs_first(e, B).wait_recv()
    for g in range(e.G):
        B.sa2[g] = (B.gb[g, 1 - x, c].astype(F32) + B.ra1[g, 1 - x].astype(F32)).astype(BF16)
    rs_second(e, B).start()
    for g in range(e.G):
        B.h1[g] = B.gb[g, x, c].astype(F32) + B.ra1[g, x].astype(F32)


def ph_rs_third(e, B):
    rs_second(e, B).wait_recv()
    for g in range(e.G):
        B.h1[g] = B.h1[g] + B.ra2[g].astype(F32)
        B.sc[g] = B.h1[g].astype(BF16)
    for d in range(1, e.G):
        rs_third(e, B, d).start()


def ph_rs_fourth(e, B):
    total = B.h1[e.g]
    for d in range(1, e.G):
        rs_third(e, B, d).wait_recv()
        total = total + B.rc[d].astype(F32)
    B.rb[0] = total.astype(BF16)
    for d in range(1, e.nb):
        rs_fourth(e, B, d).start()


def piece_start(e, r):
    rows = FLAT_PIECES // e.n
    return jnp.where(r < e.n // 2, ROW_UP + rows * r, ROW_DOWN + rows * (r - e.n // 2))


FLAT_PIECES = 2 * C * HID // LANES


def own_copy(e, B, owner):
    return remote(
        e, B.fp, B.ro.at[lax.rem(e.r, 4)], B.s_ro.at[0], B.r_ro.at[lax.rem(e.r, 4)], r=owner
    )


def own_copy2(e, B, owner):
    return remote(
        e, B.fp, B.ro.at[lax.rem(e.r, 4)], B.s_ro.at[1], B.r_ro.at[lax.rem(e.r, 4)], r=owner
    )


def ph_rs_fifth(e, B):
    per = 96 // e.n
    for d in range(1, e.nb):
        rs_fourth(e, B, d).wait_recv()

    def summed(k):
        total = None
        for b in range(e.nb):
            part = B.rb[lax.rem(e.b - b + e.nb, e.nb), k].astype(F32)
            total = part if total is None else total + part
        return total

    @pl.when(e.r < e.n // 2)
    def _():
        for k in range(per):
            v = summed(k)
            for t in range(6):
                for h in range(2):
                    B.fp[pl.ds(96 * k + 2 * t + h, 8, stride=12), :] = v[t, 8 * h : 8 * h + 8, :]

    @pl.when(e.r >= e.n // 2)
    def _():
        for k in range(per):
            v = summed(k)
            for t in range(6):
                for h in range(2):
                    unit = 2 * t + h
                    B.fp[pl.ds(96 * k + 24 * (unit // 3) + unit % 3, 8, stride=3), :] = v[t, 8 * h : 8 * h + 8, :]

    rows = FLAT_PIECES // e.n
    start = piece_start(e, e.r)
    lo = start // e.slab
    hi = (start + rows - 1) // e.slab

    @pl.when(lo != e.r)
    def _():
        own_copy(e, B, lo).start()

    @pl.when(jnp.logical_and(hi != lo, hi != e.r))
    def _():
        own_copy2(e, B, hi).start()


def ph_rs_place(e, B):
    rows = FLAT_PIECES // e.n
    for k in range(e.n):
        start = piece_start(e, k)
        off = start - e.slab * e.r
        overlap = jnp.logical_and(off < e.slab, off + rows > 0)

        @pl.when(jnp.logical_and(overlap, e.r != k))
        def _(k=k, off=off):
            pltpu.make_async_remote_copy(
                B.fp, B.ro.at[k % 4], B.s_ro.at[0], B.r_ro.at[k % 4], device_id=(k, e.b), device_id_type=MESH
            ).wait_recv()
            B.gf[pl.ds(MARGIN + off, rows), :] = B.ro[k % 4]

        @pl.when(jnp.logical_and(overlap, e.r == k))
        def _(off=off):
            B.gf[pl.ds(MARGIN + off, rows), :] = B.fp[...]


def ph_rs_done(e, B):
    rs_first(e, B).wait_send()
    rs_second(e, B).wait_send()
    for d in range(1, e.G):
        rs_third(e, B, d).wait_send()
    for d in range(1, e.nb):
        rs_fourth(e, B, d).wait_send()
    rows = FLAT_PIECES // e.n
    start = piece_start(e, e.r)
    lo = start // e.slab
    hi = (start + rows - 1) // e.slab

    @pl.when(lo != e.r)
    def _():
        own_copy(e, B, lo).wait_send()

    @pl.when(jnp.logical_and(hi != lo, hi != e.r))
    def _():
        own_copy2(e, B, hi).wait_send()


MARGIN = 1792


def ph_small_first(e, B):
    for d in range(1, e.n):
        small_copy(e, B, d).start()


def small_copy(e, B, d):
    per = SG_ROWS // e.n
    to = lax.rem(e.r + d, e.n)
    return remote(
        e, B.sg.at[pl.ds(pl.multiple_of(to * per, per), per)], B.rsg.at[d], B.s_sg.at[0, d], B.r_sg.at[0, d], r=to
    )


def small_batch(e, B, d):
    return remote(e, B.sgb.at[0], B.sgb.at[d], B.s_sgb.at[d], B.r_sgb.at[d], b=lax.rem(e.b + d, e.nb))


def small_back(e, B, d):
    return remote(e, B.sga.at[e.r], B.sga.at[e.r], B.s_sg.at[1, d], B.r_sg.at[1, d], r=lax.rem(e.r + d, e.n))


def ph_small_second(e, B):
    per = SG_ROWS // e.n
    total = B.sg[pl.ds(pl.multiple_of(e.r * per, per), per), :]
    for d in range(1, e.n):
        small_copy(e, B, d).wait_recv()
        total = total + B.rsg[d]
    B.sgb[0] = total
    for d in range(1, e.nb):
        small_batch(e, B, d).start()


def ph_small_third(e, B):
    for d in range(1, e.nb):
        small_batch(e, B, d).wait_recv()
    total = None
    for b in range(e.nb):
        part = B.sgb[lax.rem(e.b - b + e.nb, e.nb)]
        total = part if total is None else total + part
    B.sga[e.r] = total
    for d in range(1, e.n):
        small_back(e, B, d).start()


def ph_small_place(e, B):
    for d in range(1, e.n):
        small_back(e, B, d).wait_recv()
    per = SG_ROWS // e.n
    for k in range(e.n):
        B.sg2[per * k : per * (k + 1), :] = B.sga[k]
    for k, (first, at, count) in enumerate(((ROW_K, 0, 49 * J), (ROW_CUP, SG_CUP, HID // LANES), (ROW_VEC, SG_VEC, 7 * J))):
        off = MARGIN + first % e.slab

        @pl.when(e.r == first // e.slab)
        def _(off=off, at=at, count=count):
            B.gf[off : off + count, :] = B.sg2[at : at + count, :]


def ph_small_done(e, B):
    for d in range(1, e.n):
        small_copy(e, B, d).wait_send()
        small_back(e, B, d).wait_send()
    for d in range(1, e.nb):
        small_batch(e, B, d).wait_send()


def ph_head_grads(e, B):
    parts = GROUP * e.nb
    rows = 16 * parts
    sums = None
    for p in range(parts):
        x = B.pall[p].astype(F32)
        sums = x if sums is None else sums + x
        dd = x[6:9, 0:DOUT]
        B.gp[16 * p : 16 * p + 16, 0:DOUT] = jnp.concatenate([dd, dd, jnp.zeros((10, DOUT), F32)], axis=0).astype(BF16)
        dl = x[9:12, 0:CLSP]
        B.gp[rows + 16 * p : rows + 16 * p + 16, 0:CLSP] = jnp.concatenate(
            [jnp.zeros((6, CLSP), F32), dl, jnp.zeros((7, CLSP), F32)], axis=0
        ).astype(BF16)
    B.psum[...] = sums
    for q in range(4):
        for p in range(parts):
            B.v2[16 * p : 16 * p + 16, :] = B.pall[p, :, C * q : C * (q + 1)].astype(F32)
        for j in range(J):
            t = J * q + j
            B.u[LANES * t : LANES * (t + 1), 0:rows] = B.v2[0:rows, LANES * j : LANES * (j + 1)].T.astype(BF16)
    per = DOUT // LANES
    base = MARGIN - e.slab * e.r

    kc = 288
    low = e.slab * e.r - ROW_DS

    @pl.when(jnp.logical_and(low < 4 * C * per, low + e.slab > 0))
    def _():
        k0 = jnp.clip(low // (16 * per) * 16, 0, 4 * C - kc)
        k0 = pl.multiple_of(k0, 16)
        w = jnp.dot(B.u[pl.ds(k0, kc), 0:rows], B.gp[0:rows, 0:DOUT], preferred_element_type=F32)
        for j in range(per):
            B.gf[pl.ds(base + ROW_DS + per * k0 + j, kc, stride=per), :] = w[:, LANES * j : LANES * (j + 1)]

    low2 = e.slab * e.r - ROW_HEAD

    @pl.when(jnp.logical_and(low2 < DOUT * CLS // LANES, low2 + e.slab > 0))
    def _():
        g0 = jnp.clip(low2 // 125, 0, DOUT // 16 - 16)
        k0 = pl.multiple_of(DOUT + 16 * g0, 16)
        for t in range(8):
            B.big[256 * t : 256 * (t + 1), :] = jnp.dot(
                B.u[pl.ds(k0, 256), 0:rows],
                B.gp[rows : 2 * rows, LANES * t : LANES * (t + 1)],
                preferred_element_type=F32,
            )
        lane = lax.broadcasted_iota(jnp.int32, (16, LANES), 1)
        held = None
        for kk in range(16):
            o = (-CLS * kk) % LANES
            tiles = [B.big[pl.ds(256 * t + kk, 16, stride=16), :] for t in range(8)]
            if o:
                tiles = [pltpu.roll(tile, LANES - o, 1) for tile in tiles]
            for s in range(CLS * kk // LANES, (CLS * kk + CLS - 1) // LANES + 1):
                t0 = (LANES * s - CLS * kk) // LANES
                if o == 0:
                    value = tiles[t0]
                elif t0 < 0:
                    value = tiles[0]
                elif t0 + 1 > 7:
                    value = tiles[t0]
                else:
                    value = jnp.where(lane < LANES - o, tiles[t0], tiles[t0 + 1])
                border = CLS * kk - LANES * s
                if border > 0:
                    value = jnp.where(lane < border, held, value)
                if LANES * (s + 1) > CLS * (kk + 1):
                    held = value
                else:
                    B.gf[pl.ds(base + ROW_HEAD + 125 * g0 + s, 16, stride=125), :] = value

    @pl.when(e.r == ROW_OUT // e.slab)
    def _():
        off = MARGIN + ROW_OUT % e.slab
        for j in range(per):
            at = slice(LANES * j, LANES * (j + 1))
            B.gf[off + j : off + j + 1, :] = B.psum[6:7, at] * e.positions + (
                B.psum[7:8, at] * e.positions + B.psum[8:9, at] * e.positions
            )
            gain = B.psum[12:13, at] + B.psum[13:14, at] + B.psum[14:15, at]
            B.gf[off + per + j : off + per + j + 1, :] = gain
            at = slice(DOUT + LANES * j, DOUT + LANES * (j + 1))
            shift = B.psum[12:13, at] + B.psum[13:14, at] + B.psum[14:15, at]
            B.gf[off + 2 * per + j : off + 2 * per + j + 1, :] = shift

    @pl.when(e.r == ROW_BH // e.slab)
    def _():
        off = MARGIN + ROW_BH % e.slab
        for j in range(CLSP // LANES):
            at = slice(LANES * j, LANES * (j + 1))
            B.gf[off + j : off + j + 1, :] = B.psum[9:10, at] + B.psum[10:11, at] + B.psum[11:12, at]
        rest = FLAT - ROW_BH - CLSP // LANES
        B.gf[off + CLSP // LANES : off + CLSP // LANES + rest, :] = jnp.zeros((rest, LANES), F32)


def norm_copy(e, B, d):
    return remote(e, B.nrm.at[0], B.nrm.at[d], B.s_nrm.at[d], B.r_nrm.at[d], r=lax.rem(e.r + d, e.n))


def ph_norm(e, B):
    def body(k, acc):
        v = B.gf[pl.ds(MARGIN + 44 * k, 44), :]
        return acc + jnp.sum(v * v, 0, keepdims=True)

    if e.slab % 44 == 0:
        part = lax.fori_loop(0, e.slab // 44, body, jnp.zeros((1, LANES), F32))
    else:
        v = B.gf[MARGIN : MARGIN + e.slab, :]
        part = jnp.sum(v * v, 0, keepdims=True)
    B.nrm[0] = jnp.broadcast_to(part, (8, LANES))
    for d in range(1, e.n):
        norm_copy(e, B, d).start()


def ph_norm_wait(e, B):
    for d in range(1, e.n):
        norm_copy(e, B, d).wait_recv()
    total = None
    for k in range(e.n):
        part = B.nrm[lax.rem(e.r - k + e.n, e.n)]
        total = part if total is None else total + part
    square = jnp.sum(total, 1, keepdims=True)
    B.o_norm[...] = jnp.broadcast_to(jnp.sqrt(square), (8, LANES))
    loss = B.psum[15:16, :]
    loss = loss[:, 0:LANES] + loss[:, LANES : 2 * LANES] + loss[:, 2 * LANES : 3 * LANES]
    B.o_loss[...] = jnp.broadcast_to(loss, (8, LANES))
    for d in range(1, e.n):
        norm_copy(e, B, d).wait_send()


def buffers(e):
    n, G, nb, slab = e.n, e.G, e.nb, e.slab
    per = 96 // n
    slot = (slab + 15) // 16 * 16
    parts = GROUP * nb
    V = pltpu.VMEM
    D = pltpu.SemaphoreType.DMA
    return dict(
        gw=V((n, slot, LANES), BF16),
        stage=V((TAB_ROWS, LANES), F32),
        tab=V((TAB_ROWS, LANES), F32),
        big=V((10816, LANES), F32),
        dx=V((8 * DOUT, LANES), F32),
        wup=V((C, HID), BF16),
        wdn=V((HID, C), BF16),
        wds=V((4 * C, DOUT), BF16),
        wh=V((DOUT, CLSP), BF16),
        xg=V((MICRO, 14, COLS, C), BF16),
        xc=V((J, NPOS, LANES), F32),
        kb=V((49 * J, 8, LANES), F32),
        v1=V((NPOS, C), F32),
        rs1=V((NPOS, LANES), F32),
        v2=V((NPOS, C), F32),
        rs2=V((NPOS, LANES), F32),
        n=V((NPOS, C), BF16),
        u=V((NPOS, HID), BF16),
        gp=V((NPOS, HID), BF16),
        z=V((NPOS, C), F32),
        dz=V((NPOS, C), BF16),
        ps=V((MICRO, 2, OWN, C), F32),
        vs=V((MICRO, 2, OWN, C), F32),
        sl=V((32, C), F32),
        sr=V((G, 32, C), F32),
        dn2=V((32, C), F32),
        dnt=V((MICRO, 2, OWN, C), F32),
        pb=V((16, 4 * C), F32),
        pall=V((parts, 16, 4 * C), BF16),
        psum=V((16, 4 * C), F32),
        acc=V((7, 8, C), F32),
        acup=V((8, HID), F32),
        hs=V((2, MICRO, 3, COLS, C), BF16),
        hr=V((2, MICRO, 3, COLS, C), BF16),
        gb=V((G, 2, 2, per, 6, 16, LANES), BF16),
        ra1=V((G, 2, per, 6, 16, LANES), BF16),
        sa2=V((G, per, 6, 16, LANES), BF16),
        ra2=V((G, per, 6, 16, LANES), BF16),
        h1=V((G, per, 6, 16, LANES), F32),
        sc=V((G, per, 6, 16, LANES), BF16),
        rc=V((G, per, 6, 16, LANES), BF16),
        rb=V((nb, per, 6, 16, LANES), BF16),
        fp=V((FLAT_PIECES // n, LANES), F32),
        ro=V((4, FLAT_PIECES // n, LANES), F32),
        gf=V((MARGIN + slab + MARGIN, LANES), F32),
        sg=V((SG_ROWS, LANES), F32),
        sg2=V((SG_ROWS, LANES), F32),
        rsg=V((n, SG_ROWS // n, LANES), F32),
        sgb=V((nb, SG_ROWS // n, LANES), F32),
        sga=V((n, SG_ROWS // n, LANES), F32),
        nrm=V((n, 8, LANES), F32),
        s_own=D((2,)),
        s_feat=D((GROUP,)),
        r_feat=D((GROUP,)),
        s_halo=D((2,)),
        r_halo=D((2,)),
        s_tab=D((len(TABLES), n)),
        r_tab=D((len(TABLES),)),
        s_line=D((2, G)),
        r_line=D((2, G)),
        s_pair=D((G,)),
        r_pair=D((G,)),
        s_core=D((2, G)),
        r_core=D((2, G)),
        s_patch=D((G,)),
        r_patch=D((G,)),
        s_pb=D((nb,)),
        r_pb=D((nb,)),
        s_pg=D((GROUP,)),
        r_pg=D((GROUP,)),
        s_dy=D((2,)),
        r_dy=D((2,)),
        s_out=D((GROUP,)),
        r_out=D((GROUP,)),
        s_rs=D((2,)),
        r_rs=D((2,)),
        s_rc=D((G,)),
        r_rc=D((G,)),
        s_rb=D((nb,)),
        r_rb=D((nb,)),
        s_ro=D((2,)),
        r_ro=D((4,)),
        s_sg=D((2, n)),
        r_sg=D((2, n)),
        s_sgb=D((nb,)),
        r_sgb=D((nb,)),
        s_nrm=D((n,)),
        r_nrm=D((n,)),
    )


def ph_clear(e, B):
    B.sg[...] = jnp.zeros_like(B.sg)


def ph_result(e, B):
    B.o_grad[...] = B.gf[MARGIN : MARGIN + e.slab, :]


PHASES = (
    ph_barrier_signal,
    ph_cast,
    ph_feat_zero,
    ph_clear,
    ph_barrier_wait,
    ph_feat_start,
    ph_tables_start,
    ph_feat_halo,
    ph_gather,
    ph_tables_wait,
    ph_transpose,
    ph_taps,
    ph_conv_fwd,
    ph_weights_mlp,
    ph_mlp_fwd,
    ph_weights_head,
    ph_patch_local,
    ph_patch_exchange,
    ph_head,
    ph_payload_batch,
    ph_mlp_bwd,
    ph_payload_group,
    ph_dy_pack,
    ph_dy_halo,
    ph_wgrad,
    ph_rs_first,
    ph_dy_unpack,
    ph_conv_bwd,
    ph_small_fill,
    ph_small_first,
    ph_rs_second,
    ph_out_pack,
    ph_out_start,
    ph_small_second,
    ph_rs_third,
    ph_small_third,
    ph_rs_fourth,
    ph_payload_wait,
    ph_head_grads,
    ph_rs_fifth,
    ph_small_place,
    ph_rs_place,
    ph_norm,
    ph_out_wait,
    ph_rs_done,
    ph_small_done,
    ph_norm_wait,
    ph_result,
)


def step_kernel(e, names, phases, *refs):
    B = Env()
    for name, ref in zip(names, refs):
        setattr(B, name, ref)
    here(e)
    for phase in phases:
        phase(e, B)


def train_step(e, features, mask, labels, params):
    bufs = buffers(e)
    names = ["mask", "labels", "features", "params", "o_grad", "o_norm", "o_loss", "fo"] + list(bufs)
    return pl.pallas_call(
        functools.partial(step_kernel, e, names, PHASES),
        out_shape=(
            jax.ShapeDtypeStruct((e.slab, LANES), F32),
            jax.ShapeDtypeStruct((8, LANES), F32),
            jax.ShapeDtypeStruct((8, LANES), F32),
            jax.ShapeDtypeStruct((MICRO, GROUP, 2, COLS, C), BF16),
        ),
        in_specs=[
            pl.BlockSpec(memory_space=pltpu.SMEM),
            pl.BlockSpec(memory_space=pltpu.SMEM),
            pl.BlockSpec(memory_space=pl.ANY),
            pl.BlockSpec(memory_space=pltpu.VMEM),
        ],
        out_specs=(
            pl.BlockSpec(memory_space=pltpu.VMEM),
            pl.BlockSpec(memory_space=pltpu.VMEM),
            pl.BlockSpec(memory_space=pltpu.VMEM),
            pl.BlockSpec(memory_space=pl.ANY),
        ),
        scratch_shapes=list(bufs.values()),
        compiler_params=pltpu.CompilerParams(collective_id=0, has_side_effects=True, vmem_limit_bytes=64 * MB - 65536),
        name="train_step",
    )(mask, labels, features, params)


def update_kernel(grad, norm, params, m1, m2, out, new_params, first, second, feats):
    scale = jnp.minimum(1.0, CLIP / (norm[0:1, 0:1] + 1e-06))
    clipped = grad[...] * scale
    one = BETA_ONE * m1[...] + (1.0 - BETA_ONE) * clipped
    two = BETA_TWO * m2[...] + (1.0 - BETA_TWO) * clipped * clipped
    first[...] = one
    second[...] = two
    ratio = one / (1.0 - BETA_ONE**STEP) / (jnp.sqrt(two / (1.0 - BETA_TWO**STEP)) + EPS_ADAM)
    new_params[...] = params[...] - RATE * (ratio + DECAY * params[...])
    for k in range(MICRO):
        feats[k] = out[k].astype(F32)


def update(e, grad, norm, params, m1, m2, out):
    flat = jax.ShapeDtypeStruct((e.slab, LANES), F32)
    return pl.pallas_call(
        update_kernel,
        out_shape=(flat, flat, flat, jax.ShapeDtypeStruct((MICRO, GROUP, 2, COLS, C), F32)),
        compiler_params=pltpu.CompilerParams(vmem_limit_bytes=48 * MB),
        name="update",
    )(grad, norm, params, m1, m2, out)


def local(e, features, drop_mask, labels, params, moment1, moment2):
    flat = [v.reshape(e.slab, LANES) for v in (params, moment1, moment2)]
    grad, norm, loss, out = train_step(e, features, drop_mask, labels, flat[0])
    new_params, first, second, feats = update(e, grad, norm, *flat, out)
    size = e.slab * LANES
    return (
        new_params.reshape(size),
        first.reshape(size),
        second.reshape(size),
        loss[0, 0],
        norm[0, 0],
        feats,
    )


def solution(mesh):
    e = Env()
    e.n = mesh.shape["rows"]
    e.nb = mesh.shape["batch"]
    e.G = e.n // GROUP
    e.slab = FLAT // e.n
    e.positions = float(e.n * COLS // 2)
    e.inv_count = 1.0 / (MICRO * GROUP * e.nb)
    return jax.shard_map(
        functools.partial(local, e),
        mesh=mesh,
        in_specs=(
            P(None, "batch", "rows", None, None),
            P(None, "batch"),
            P(None, "batch"),
            P("rows"),
            P("rows"),
            P("rows"),
        ),
        out_specs=(P("rows"), P("rows"), P("rows"), P(), P(), P(None, "batch", "rows", None, None)),
        check_vma=False,
    )
```

```python
import functools

import jax
import jax.numpy as jnp
from jax import lax
from jax.experimental import pallas as pl
from jax.experimental.pallas import tpu as pltpu
from jax.sharding import PartitionSpec as P

C = 384
HID = 1536
DOUT = 768
CLS = 1000
MICRO = 3
STEP = 10
P_SIZE = 3153920
KEEP = 0.8
CLIP = 0.01
RATE = 0.05
BETA_ONE = 0.9
BETA_TWO = 0.999
DECAY = 0.05
EPS_ADAM = 1e-08
EPS_NORM = 1e-06

MESH = pl.DeviceIdType.MESH
F32 = jnp.float32
BF16 = jnp.bfloat16
MB = 1 << 20

LANES = 128
J = C // LANES
GROUP = 4
OWN = 8
COLS = 64
PADC = COLS + 6
SUB = 16
POS = COLS * OWN
NPOS = MICRO * POS
FLAT = P_SIZE // LANES
ROW_K = 0
ROW_UP = 49 * J
ROW_CUP = ROW_UP + C * HID // LANES
ROW_DOWN = ROW_CUP + HID // LANES
ROW_VEC = ROW_DOWN + C * HID // LANES
ROW_DS = ROW_VEC + 7 * J
ROW_OUT = ROW_DS + 4 * C * DOUT // LANES
ROW_HEAD = ROW_OUT + 3 * DOUT // LANES
ROW_BH = ROW_HEAD + DOUT * CLS // LANES
TABLES = (
    (ROW_K, 49 * J, 0),
    (ROW_CUP, HID // LANES, 152),
    (ROW_VEC, 7 * J, 168),
    (ROW_OUT, 3 * DOUT // LANES, 192),
    (ROW_BH, FLAT - ROW_BH, 216),
)
TAB_ROWS = 232
TAB_SPAN = (152, 16, 24, 24, 16)
T_CUP, T_VEC, T_OUT, T_BH = 152, 168, 192, 216
SG_ROWS = 256
SG_CUP, SG_VEC = 152, 168
CLSP = 1024


class Env:
    pass


def xrow(j, m):
    return (j * MICRO + m) * PADC * SUB


def rows_of(refs, row, count):
    return refs[row : row + count, :]


def lane_row(ref, row, count):
    return jnp.concatenate([ref[row + k : row + k + 1, :] for k in range(count)], axis=1)


def ln_parts(blocks, width):
    total = blocks[0]
    for block in blocks[1:]:
        total = total + block
    mean = jnp.sum(total, -1, keepdims=True) * (1.0 / width)
    centred = [block - mean for block in blocks]
    square = centred[0] * centred[0]
    for block in centred[1:]:
        square = square + block * block
    spread = jnp.sum(square, -1, keepdims=True) * (1.0 / width)
    scale = lax.rsqrt(spread + EPS_NORM)
    return [block * scale for block in centred], scale


def here(e):
    e.r = lax.axis_index("rows")
    e.b = lax.axis_index("batch")
    e.g = e.r // GROUP
    e.i = e.r % GROUP
    e.h = e.b % 2


def dev(e, r=None, b=None):
    return {"rows": e.r if r is None else r, "batch": e.b if b is None else b}


def remote(e, src, dst, send, recv, r=None, b=None):
    return pltpu.make_async_remote_copy(
        src, dst, send, recv, device_id=(e.r if r is None else r, e.b if b is None else b), device_id_type=MESH
    )


def ph_barrier_signal(e, B):
    barrier = pltpu.get_barrier_semaphore()
    for d in range(1, e.n):
        pl.semaphore_signal(barrier, inc=1, device_id=(lax.rem(e.r + d, e.n), e.b), device_id_type=MESH)
    for d in range(1, e.nb):
        pl.semaphore_signal(barrier, inc=1, device_id=(e.r, lax.rem(e.b + d, e.nb)), device_id_type=MESH)


def ph_barrier_wait(e, B):
    pl.semaphore_wait(pltpu.get_barrier_semaphore(), e.n - 1 + e.nb - 1)


def feat_copy(e, B, m, d):
    j = lax.rem(e.i + d, GROUP)
    return remote(
        e,
        B.features.at[m, j],
        B.xg.at[m, pl.ds(3 + 2 * e.i, 2)],
        B.s_feat.at[m, d],
        B.r_feat.at[m, d],
        r=e.g * GROUP + j,
    )


def feat_own(e, B):
    return pltpu.make_async_copy(B.features.at[:, e.i], B.xg.at[:, pl.ds(3 + 2 * e.i, 2)], B.s_own.at[0])


def ph_feat_start(e, B):
    feat_own(e, B).start()
    for m in range(MICRO):
        for d in (2, 1, 3):
            feat_copy(e, B, m, d).start()


def ph_feat_zero(e, B):
    zero = jnp.zeros((MICRO, 3, COLS, C), BF16)

    @pl.when(e.g == 0)
    def _():
        B.xg[:, 0:3] = zero

    @pl.when(e.g == e.G - 1)
    def _():
        B.xg[:, 11:14] = zero


def halo_copy(e, B, m, up):
    if up:
        return remote(e, B.xg.at[m, 8:11], B.xg.at[m, 0:3], B.s_halo.at[1, m], B.r_halo.at[1, m], r=e.r + GROUP)
    return remote(e, B.xg.at[m, 3:6], B.xg.at[m, 11:14], B.s_halo.at[0, m], B.r_halo.at[0, m], r=e.r - GROUP)


def halo_start(e, B, m):
    if m == 0:
        feat_own(e, B).wait()
    for d in range(1, GROUP):
        feat_copy(e, B, m, d).wait_recv()

    @pl.when(e.g > 0)
    def _():
        halo_copy(e, B, m, False).start()

    @pl.when(e.g < e.G - 1)
    def _():
        halo_copy(e, B, m, True).start()


def halo_wait(e, B, m):
    @pl.when(e.g < e.G - 1)
    def _():
        halo_copy(e, B, m, False).wait_recv()

    @pl.when(e.g > 0)
    def _():
        halo_copy(e, B, m, True).wait_recv()


def ph_feat_done(e, B):
    for m in range(MICRO):
        for d in range(1, GROUP):
            feat_copy(e, B, m, d).wait_send()

        @pl.when(e.g > 0)
        def _(m=m):
            halo_copy(e, B, m, False).wait_send()

        @pl.when(e.g < e.G - 1)
        def _(m=m):
            halo_copy(e, B, m, True).wait_send()


def ph_cast(e, B):
    for h in range(2):
        count = e.half if h == 0 else e.slab - e.half
        whole = count // 16 * 16
        B.gw[e.r, h, 0:whole, :] = B.params[h * e.half : h * e.half + whole, :].astype(BF16)
        rest = count - whole
        if whole < e.half:
            parts = [jnp.zeros((e.half - whole - rest, LANES), F32)]
            if rest:
                parts = [B.params[e.slab - rest : e.slab, :]] + parts
            B.gw[e.r, h, whole : e.half, :] = jnp.concatenate(parts, axis=0).astype(BF16)
    for k, (first, count, place) in enumerate(TABLES):
        off = first % e.slab
        B.stage[place : place + count, :] = B.params[off : off + count, :]


def table_line(e, B, k, d):
    first, count, place = TABLES[k]
    owner = first // e.slab
    part = pl.ds(place, TAB_SPAN[k])
    return remote(e, B.stage.at[part], B.tab.at[part], B.s_tab.at[k, d], B.r_tab.at[k], r=lax.rem(owner + GROUP * d, e.n))


def table_group(e, B, k, d):
    first, count, place = TABLES[k]
    part = pl.ds(place, TAB_SPAN[k])
    to = e.g * GROUP + lax.rem(e.i + d, GROUP)
    return remote(e, B.tab.at[part], B.tab.at[part], B.s_tabg.at[k, d], B.r_tab.at[k], r=to)


def ph_tables_start(e, B):
    for k, (first, count, place) in enumerate(TABLES):
        owner = first // e.slab

        @pl.when(e.r == owner)
        def _(k=k, place=place):
            for d in range(1, e.G):
                table_line(e, B, k, d).start()
            B.tab[place : place + TAB_SPAN[k], :] = B.stage[place : place + TAB_SPAN[k], :]
            for d in range(1, GROUP):
                table_group(e, B, k, d).start()


def tables_forward(e, B, some):
    for k in some:
        owner = TABLES[k][0] // e.slab

        @pl.when(jnp.logical_and(e.i == owner % GROUP, e.r != owner))
        def _(k=k):
            table_line(e, B, k, 1).wait_recv()
            for d in range(1, GROUP):
                table_group(e, B, k, d).start()


def tables_wait(e, B, some):
    for k in some:
        owner = TABLES[k][0] // e.slab

        @pl.when(e.i != owner % GROUP)
        def _(k=k):
            table_group(e, B, k, 1).wait_recv()


def ph_tables_done(e, B):
    for k, (first, count, place) in enumerate(TABLES):
        owner = first // e.slab

        @pl.when(e.r == owner)
        def _(k=k):
            for d in range(1, e.G):
                table_line(e, B, k, d).wait_send()

        @pl.when(e.i == owner % GROUP)
        def _(k=k):
            for d in range(1, GROUP):
                table_group(e, B, k, d).wait_send()


def half_ref(B, slot, h):
    return B.gw.at[slot, h]


def line_copy(e, B, level, up, d):
    ref = half_ref(B, level * GROUP + e.i, e.h)
    k = 0 if up else 1
    return remote(e, ref, ref, B.s_line.at[k, d], B.r_line.at[k, d], r=e.r + GROUP if up else e.r - GROUP)


def pair_copy(e, B, level):
    ref = half_ref(B, level * GROUP + e.i, e.h)
    return remote(e, ref, ref, B.s_pair.at[level], B.r_pair.at[level], r=e.g * GROUP + lax.rem(e.i + 2, GROUP))


def row_copy(e, B, level, other):
    i = lax.rem(e.i + 2, GROUP) if other else e.i
    ref = half_ref(B, level * GROUP + i, e.h)
    k = int(other)
    return remote(e, ref, ref, B.s_row.at[k, level], B.r_row.at[k, level], b=e.b + 1 - 2 * e.h)


def core_copy(e, B, level, other, mine):
    i = lax.rem(e.i + 2, GROUP) if other else e.i
    ref = half_ref(B, level * GROUP + i, e.h if mine else 1 - e.h)
    k = 2 * int(other) + int(mine)
    sib = e.g * GROUP + e.i + 1 - 2 * (e.i % 2)
    return remote(e, ref, ref, B.s_core.at[k, level], B.r_core.at[k, level], r=sib)


def line_start(e, B):
    @pl.when(e.g + 1 < e.G)
    def _():
        line_copy(e, B, e.g, True, 0).start()

    @pl.when(e.g >= 1)
    def _():
        line_copy(e, B, e.g, False, 0).start()


def line_step(e, B, d):
    lo = e.g - d - 1
    hi = e.g + d + 1
    more = d + 1 < e.G - 1

    @pl.when(lo >= 0)
    def _():
        line_copy(e, B, lo, True, d).wait_recv()
        if more:

            @pl.when(e.g + 1 < e.G)
            def _():
                line_copy(e, B, lo, True, d + 1).start()

        row_copy(e, B, lo, False).start()

    @pl.when(hi < e.G)
    def _():
        line_copy(e, B, hi, False, d).wait_recv()
        if more:

            @pl.when(e.g >= 1)
            def _():
                line_copy(e, B, hi, False, d + 1).start()

        row_copy(e, B, hi, False).start()


def pair_step(e, B, levels):
    for level in levels:
        pair_copy(e, B, level).start()
        core_copy(e, B, level, False, True).start()

        @pl.when(e.g == level)
        def _(level=level):
            core_copy(e, B, level, False, False).start()


def row_step(e, B, levels):
    for level in levels:
        pair_copy(e, B, level).wait_recv()
        row_copy(e, B, level, True).start()
        core_copy(e, B, level, True, True).start()


def core_step(e, B, levels):
    for level in levels:

        @pl.when(e.g != level)
        def _(level=level):
            row_copy(e, B, level, False).wait_recv()
            core_copy(e, B, level, False, False).start()

    for level in levels:
        row_copy(e, B, level, True).wait_recv()
        core_copy(e, B, level, True, False).start()


def gather_ready(e, B, levels):
    for level in levels:
        for other in (False, True):
            for mine in (False, True):
                core_copy(e, B, level, other, mine).wait_recv()


def ph_gather_done(e, B):
    G = e.G
    for level in range(G):
        pair_copy(e, B, level).wait_send()
        row_copy(e, B, level, True).wait_send()

        @pl.when(e.g != level)
        def _(level=level):
            row_copy(e, B, level, False).wait_send()

        for other in (False, True):
            for mine in (False, True):
                core_copy(e, B, level, other, mine).wait_send()
    for d in range(G - 1):

        @pl.when(jnp.logical_and(e.g - d >= 0, e.g + 1 < G))
        def _(d=d):
            line_copy(e, B, e.g - d, True, d).wait_send()

        @pl.when(jnp.logical_and(e.g + d < G, e.g >= 1))
        def _(d=d):
            line_copy(e, B, e.g + d, False, d).wait_send()


def flatten(e, B, first, last):
    step = 112
    s0 = first // e.slab

    def slab(k, _):
        for h in range(2):
            count = e.half if h == 0 else e.slab - e.half
            whole = count // step
            left = (count - whole * step + 15) // 16 * 16
            base = e.slab * k + h * e.half

            def body(t, _, h=h, base=base):
                at = pl.multiple_of(t * step, 16)
                B.big[pl.ds(base + t * step, step), :] = B.gw[s0 + k, h, pl.ds(at, step), :].astype(F32)
                return 0

            lax.fori_loop(0, whole, body, 0)
            if left:
                last = B.gw[s0 + k, h, whole * step : whole * step + left, :]
                B.big[pl.ds(base + whole * step, left), :] = last.astype(F32)
        return 0

    lax.fori_loop(0, (last - 1) // e.slab - s0 + 1, slab, 0)
    return e.slab * s0


def ph_weights_mlp(e, B):
    base = flatten(e, B, ROW_UP, ROW_VEC)
    for j in range(HID // LANES):
        B.wup[:, LANES * j : LANES * (j + 1)] = B.big[pl.ds(ROW_UP - base + j, C, stride=HID // LANES), :].astype(BF16)
    for j in range(J):
        B.wdn[:, LANES * j : LANES * (j + 1)] = B.big[pl.ds(ROW_DOWN - base + j, HID, stride=J), :].astype(BF16)


def ph_weights_head(e, B):
    base = flatten(e, B, ROW_DS, ROW_OUT)
    per = DOUT // LANES
    for j in range(per):
        B.wds[:, LANES * j : LANES * (j + 1)] = B.big[pl.ds(ROW_DS - base + j, 4 * C, stride=per), :].astype(BF16)
    base = flatten(e, B, ROW_HEAD, ROW_BH)
    lane = lax.broadcasted_iota(jnp.int32, (DOUT // 16, LANES), 1)
    for kk in range(16):
        first, off = divmod(CLS * kk, LANES)
        parts = [B.big[pl.ds(ROW_HEAD - base + first + t, DOUT // 16, stride=125), :] for t in range(9 if off else 8)]
        if off:
            parts = [pltpu.roll(part, LANES - off, 1) for part in parts]
        for t in range(8):
            tile = parts[t]
            if off:
                tile = jnp.where(lane < LANES - off, parts[t], parts[t + 1])
            if t == 7:
                tile = jnp.where(lane < CLS - 7 * LANES, tile, 0.0)
            B.dx[pl.ds(DOUT * t + kk, DOUT // 16, stride=16), :] = tile
    for t in range(8):
        B.wh[:, LANES * t : LANES * (t + 1)] = B.dx[DOUT * t : DOUT * (t + 1), :].astype(BF16)


def hooks(it, steps):
    for k, some in steps.items():

        @pl.when(it == k)
        def _(some=some):
            for step in some:
                step()


def transpose(e, B, m):
    pad = jnp.zeros((3 * SUB, LANES), F32)
    for j in range(J):
        B.big[pl.ds(xrow(j, m), 3 * SUB), :] = pad
        B.big[pl.ds(xrow(j, m) + (COLS + 3) * SUB, 3 * SUB), :] = pad
        for row in range(14):
            v = B.xg[m, row, :, LANES * j : LANES * (j + 1)].astype(F32)
            B.big[pl.ds(xrow(j, m) + 3 * SUB + row, COLS, stride=SUB), :] = v
            if 3 <= row < 11:
                B.xc[pl.ds(j * NPOS + m * POS + row - 3, COLS, stride=OWN), :] = v


def ph_taps(e, B):
    def body(t, _):
        B.kb[t] = jnp.broadcast_to(B.tab[pl.ds(t, 1), :], (8, LANES))
        return 0

    lax.fori_loop(0, 49 * J, body, 0)


def vec_row(B, v, j):
    row = T_VEC + v * J + j
    return B.tab[row : row + 1, :]


def conv_tile(B, m, j, c0, tile, acc, flip):
    for a in range(7):
        taps = [B.kb[((6 - a) * 7 + 6 - b if flip else a * 7 + b) * J + j] for b in range(7)]
        for c in range(tile + 6):
            d = B.big[pl.ds(xrow(j, m) + (c0 + c) * SUB + a, OWN), :]
            for b in range(7):
                if 0 <= c - b < tile:
                    acc[c - b] = acc[c - b] + d * taps[b]
    return acc


TILE = 32


def ph_conv_fwd(e, B, steps):
    halves = COLS // TILE

    def body(it, _):
        hooks(it, steps)
        m = it // (J * halves)
        j = it // halves % J
        c0 = it % halves * TILE
        bias = jnp.broadcast_to(B.tab[pl.ds(T_VEC + j, 1), :], (OWN, LANES))
        acc = conv_tile(B, m, j, c0, TILE, [bias] * TILE, False)
        at = j * NPOS + m * POS + c0 * OWN
        for c in range(TILE):
            B.dx[pl.ds(pl.multiple_of(at + OWN * c, OWN), OWN), :] = acc[c]
        return 0

    lax.fori_loop(0, MICRO * J * halves, body, 0)


def ph_norm_one(e, B):
    size = 128

    def body(it, _):
        at = pl.multiple_of(it * size, size)
        hat, scale = ln_parts([B.dx[pl.ds(j * NPOS + at, size), :] for j in range(J)], C)
        B.rs1[pl.ds(at, size), :] = jnp.broadcast_to(scale, (size, LANES))
        for j in range(J):
            B.v1[pl.ds(at, size), LANES * j : LANES * (j + 1)] = hat[j]
            B.n[pl.ds(at, size), LANES * j : LANES * (j + 1)] = (
                hat[j] * vec_row(B, 1, j) + vec_row(B, 2, j)
            ).astype(BF16)
        return 0

    lax.fori_loop(0, NPOS // size, body, 0)


def ph_mlp_fwd(e, B, steps):
    chunk = 256
    width = 256
    c0 = 0.7978845608028654
    c1 = 0.044715 * c0
    B.ps[...] = jnp.zeros_like(B.ps)

    def body(it, _):
        hooks(it, steps)
        at = pl.multiple_of(it * chunk, chunk)
        m = it // (POS // chunk)
        keep = B.mask[m, e.i].astype(F32) * (1.0 / KEEP)
        rows = B.n[pl.ds(at, chunk), :]
        for k in range(HID // width):
            lanes = slice(width * k, width * (k + 1))
            bias = lane_row(B.tab, T_CUP + k * width // LANES, width // LANES)
            h = jnp.dot(rows, B.wup[:, lanes], preferred_element_type=F32) + bias
            sq = h * h
            half = 0.5 * jnp.tanh(h * (c0 + c1 * sq)) + 0.5
            u = h * half
            B.u[pl.ds(at, chunk), lanes] = u.astype(BF16)
            slope = half + u * (1.0 - half) * (2.0 * c0 + 6.0 * c1 * sq)
            B.gp[pl.ds(at, chunk), lanes] = slope.astype(BF16)
        z = jnp.dot(B.u[pl.ds(at, chunk), :], B.wdn[...], preferred_element_type=F32)
        resid = []
        for j in range(J):
            zj = z[:, LANES * j : LANES * (j + 1)] + vec_row(B, 3, j)
            B.z[pl.ds(j * NPOS + at, chunk), :] = zj
            resid.append(B.xc[pl.ds(j * NPOS + at, chunk), :] + (vec_row(B, 4, j) * keep) * zj)
        hat, scale = ln_parts(resid, C)
        B.rs2[pl.ds(at, chunk), :] = jnp.broadcast_to(scale, (chunk, LANES))
        for j in range(J):
            B.v2[pl.ds(at, chunk), LANES * j : LANES * (j + 1)] = hat[j]
            low = (hat[j] * vec_row(B, 5, j) + vec_row(B, 6, j)).astype(BF16).astype(F32)
            low = jnp.sum(low.reshape(chunk // 16, 2, OWN, LANES), 0)
            B.ps[m, :, :, LANES * j : LANES * (j + 1)] += low
        return 0

    lax.fori_loop(0, NPOS // chunk, body, 0)


def ph_patch_local(e, B):
    even = lax.broadcasted_iota(jnp.int32, (OWN, C), 0) % 2 == 0
    pick = lax.broadcasted_iota(jnp.int32, (8, C), 0)
    for parity in range(2):
        for side in range(2):
            tile = jnp.zeros((8, C), F32)
            for m in range(MICRO):
                v = B.ps[m, side]
                part = jnp.sum(jnp.where(even if parity == 0 else jnp.logical_not(even), v, 0.0), 0, keepdims=True)
                tile = jnp.where(pick == m, part, tile)
            q = 2 * parity + side
            B.sl[8 * q : 8 * q + 8, :] = tile


def patch_copy(e, B, d):
    to = lax.rem(e.g + d, e.G)
    return remote(e, B.sl, B.sr.at[d], B.s_patch.at[d], B.r_patch.at[d], r=to * GROUP + e.i)


def patch_start(e, B):
    for d in range(1, e.G):
        patch_copy(e, B, d).start()
    B.sr[0] = B.sl[...]


def patch_wait(e, B):
    for d in range(1, e.G):
        patch_copy(e, B, d).wait_recv()
    for d in range(1, e.G):
        patch_copy(e, B, d).wait_send()


def split3(v):
    hi = v.astype(BF16).astype(F32)
    mid = (v - hi).astype(BF16).astype(F32)
    return hi, mid, v - hi - mid


def ph_head(e, B):
    total = None
    for level in range(e.G):
        part = B.sr[lax.rem(e.g - level + e.G, e.G)]
        total = part if total is None else total + part
    per = DOUT // LANES
    gain = lane_row(B.tab, T_OUT + per, per)
    shift = lane_row(B.tab, T_OUT + 2 * per, per)
    mean = total * (1.0 / e.positions)
    pooled = lane_row(B.tab, T_OUT, per)
    for q in range(4):
        parts = jnp.concatenate(split3(mean[8 * q : 8 * q + 8, :]), axis=0).astype(BF16)
        prod = jnp.dot(parts, B.wds[C * q : C * (q + 1), :], preferred_element_type=F32)
        pooled = pooled + (prod[0:8] + (prod[8:16] + prod[16:24]))
    rows = lax.broadcasted_iota(jnp.int32, (8, 1), 0)
    live = rows < MICRO
    (hat,), scale = ln_parts([pooled], DOUT)
    query = (hat * gain + shift).astype(BF16)
    lane = lax.broadcasted_iota(jnp.int32, (8, CLSP), 1)
    logits = jnp.dot(query, B.wh[...], preferred_element_type=F32) + lane_row(B.tab, T_BH, CLSP // LANES)
    logits = jnp.where(lane < CLS, logits, -1e30)
    top = jnp.max(logits, 1, keepdims=True)
    powers = jnp.exp(logits - top)
    expsum = jnp.sum(powers, 1, keepdims=True)
    label = jnp.zeros((8, 1), jnp.int32)
    for m in range(MICRO):
        label = jnp.where(rows == m, B.labels[m, e.i], label)
    onehot = (lane == label).astype(F32)
    own = jnp.sum(jnp.where(lane == label, logits, 0.0), 1, keepdims=True)
    loss = jnp.sum(jnp.where(live, top + jnp.log(expsum) - own, 0.0), 0, keepdims=True)
    grad = jnp.where(live, (powers / expsum - onehot) * e.inv_count, 0.0).astype(BF16)
    grad_query = lax.dot_general(grad, B.wh[...], (((1,), (1,)), ((), ())), preferred_element_type=F32)
    dn = grad_query * gain
    m1 = jnp.sum(dn, 1, keepdims=True) * (1.0 / DOUT)
    m2 = jnp.sum(dn * hat, 1, keepdims=True) * (1.0 / DOUT)
    grad_pool = scale * (dn - m1 - hat * m2)
    down = jnp.where(live, grad_pool * (1.0 / e.positions), 0.0).astype(BF16)
    for q in range(4):
        B.dn2[8 * q : 8 * q + 8, :] = lax.dot_general(
            down, B.wds[C * q : C * (q + 1), :], (((1,), (1,)), ((), ())), preferred_element_type=F32
        )
    low = grad.astype(F32)
    d32 = down.astype(F32)
    q32 = jnp.where(live, query.astype(F32), 0.0)
    zero3 = jnp.zeros((3, C), F32)
    g3 = jnp.sum(jnp.where(live, grad_query * hat, 0.0), 0, keepdims=True)
    s3 = jnp.sum(jnp.where(live, grad_query, 0.0), 0, keepdims=True)
    vec = jnp.concatenate([g3, s3], axis=1)
    vec_parts = split3(vec)
    loss_parts = split3(loss)
    for q in range(4):
        at = slice(C * q, C * (q + 1))
        s_hi, s_mid, _ = split3(total[8 * q : 8 * q + 8, :])
        B.pb[0:8, at] = jnp.zeros((8, C), F32)
        B.pb[8:16, at] = jnp.zeros((8, C), F32)
        B.pb[0:3, at] = s_hi[0:3]
        B.pb[3:6, at] = s_mid[0:3]
    B.pb[6:9, 0:DOUT] = d32[0:3]
    B.pb[6:9, DOUT : 2 * DOUT] = q32[0:3]
    B.pb[9:12, 0:CLSP] = low[0:3]
    for k in range(3):
        B.pb[12 + k : 13 + k, :] = vec_parts[k]
        B.pb[15:16, LANES * k : LANES * (k + 1)] = jnp.broadcast_to(loss_parts[k], (1, LANES))
    B.pall[e.i * e.nb + e.b] = B.pb[...].astype(BF16)
    even = lax.broadcasted_iota(jnp.int32, (OWN, C), 0) % 2 == 0
    for m in range(MICRO):
        for side in range(2):
            first = B.dn2[8 * side + m : 8 * side + m + 1, :]
            second = B.dn2[8 * (2 + side) + m : 8 * (2 + side) + m + 1, :]
            B.dnt[m, side] = jnp.where(even, first, second)


def batch_copy(e, B, d):
    slot = e.i * e.nb + e.b
    return remote(e, B.pall.at[slot], B.pall.at[slot], B.s_pb.at[d], B.r_pb.at[d], b=lax.rem(e.b + d, e.nb))


def group_copy(e, B, d):
    at = pl.ds(e.i * e.nb, e.nb)
    to = e.g * GROUP + lax.rem(e.i + d, GROUP)
    return remote(e, B.pall.at[at], B.pall.at[at], B.s_pg.at[d], B.r_pg.at[d], r=to)


def ph_payload_batch(e, B):
    for d in range(1, e.nb):
        batch_copy(e, B, d).start()


def ph_payload_group(e, B):
    for d in range(1, e.nb):
        batch_copy(e, B, d).wait_recv()
    for d in range(1, GROUP):
        group_copy(e, B, d).start()


def ph_payload_wait(e, B):
    for d in range(1, GROUP):
        group_copy(e, B, d).wait_recv()
    for d in range(1, e.nb):
        batch_copy(e, B, d).wait_send()
    for d in range(1, GROUP):
        group_copy(e, B, d).wait_send()


def lane_sum(blocks):
    total = blocks[0]
    for block in blocks[1:]:
        total = total + block
    return jnp.sum(total, -1, keepdims=True) * (1.0 / C)


def fold8(v):
    return jnp.sum(v.reshape(v.shape[0] // 8, 8, v.shape[1]), 0)


def ph_bwd_one(e, B):
    chunk = 256
    half = chunk // 16
    B.acc[...] = jnp.zeros_like(B.acc)
    B.acup[...] = jnp.zeros_like(B.acup)
    B.vs[...] = jnp.zeros_like(B.vs)

    def body(it, _):
        at = pl.multiple_of(it * chunk, chunk)
        m = it // (POS // chunk)
        keep = B.mask[m, e.i].astype(F32) * (1.0 / KEEP)
        span = pl.ds(at, chunk)
        lanes = [slice(LANES * j, LANES * (j + 1)) for j in range(J)]
        dg = [B.dnt[m, :, :, lanes[j]] * vec_row(B, 5, j) for j in range(J)]
        m1 = lane_sum(dg)
        hat = [B.v2[span, lanes[j]].reshape(half, 2, OWN, LANES) for j in range(J)]
        m2 = lane_sum([dg[j] * hat[j] for j in range(J)])
        scale = B.rs2[span, :].reshape(half, 2, OWN, LANES)
        for j in range(J):
            zspan = pl.ds(j * NPOS + at, chunk)
            dr = (scale * (dg[j] - m1 - hat[j] * m2)).reshape(chunk, LANES)
            B.vs[m, :, :, lanes[j]] += jnp.sum(hat[j], 0)
            dz = (dr * (vec_row(B, 4, j) * keep)).astype(BF16)
            B.dz[span, lanes[j]] = dz
            B.acc[3, :, lanes[j]] += fold8(dz.astype(F32))
            B.acc[4, :, lanes[j]] += fold8(dr * B.z[zspan, :]) * keep
            B.z[zspan, :] = dr
        return 0

    lax.fori_loop(0, NPOS // chunk, body, 0)
    for m in range(MICRO):
        B.acc[5] += B.dnt[m, 0] * B.vs[m, 0] + B.dnt[m, 1] * B.vs[m, 1]
        B.acc[6] += (B.dnt[m, 0] + B.dnt[m, 1]) * float(COLS // 2)


def ph_bwd_two(e, B, steps):
    chunk = 256
    width = 256

    def body(it, _):
        hooks(it, steps)
        at = pl.multiple_of(it * chunk, chunk)
        m = it // (POS // chunk)
        c0 = (it % (POS // chunk)) * (chunk // OWN)
        span = pl.ds(at, chunk)
        lanes = [slice(LANES * j, LANES * (j + 1)) for j in range(J)]
        dz = B.dz[span, :]
        for k in range(HID // width):
            hid = slice(width * k, width * (k + 1))
            du = lax.dot_general(dz, B.wdn[hid, :], (((1,), (1,)), ((), ())), preferred_element_type=F32)
            dh = (du * B.gp[span, hid].astype(F32)).astype(BF16)
            B.gp[span, hid] = dh
            B.acup[:, hid] += fold8(dh.astype(F32))
        dn = lax.dot_general(B.gp[span, :], B.wup[...], (((1,), (1,)), ((), ())), preferred_element_type=F32)
        dns = [dn[:, lanes[j]] for j in range(J)]
        dg = [dns[j] * vec_row(B, 1, j) for j in range(J)]
        hat = [B.v1[span, lanes[j]] for j in range(J)]
        m1 = lane_sum(dg)
        m2 = lane_sum([dg[j] * hat[j] for j in range(J)])
        scale = B.rs1[span, :]
        for j in range(J):
            dy = scale * (dg[j] - m1 - hat[j] * m2)
            B.acc[0, :, lanes[j]] += fold8(dy)
            B.acc[1, :, lanes[j]] += fold8(dns[j] * hat[j])
            B.acc[2, :, lanes[j]] += fold8(dns[j])
            for c in range(chunk // OWN):
                B.big[pl.ds(xrow(j, m) + (3 + c0 + c) * SUB + 3, OWN), :] = dy[OWN * c : OWN * (c + 1), :]
        return 0

    lax.fori_loop(0, NPOS // chunk, body, 0)


def ph_wgrad_down(e, B):
    for k in range(4):
        w = lax.dot_general(
            B.u[:, C * k : C * (k + 1)], B.dz[...], (((0,), (0,)), ((), ())), preferred_element_type=F32
        )
        w = w.reshape(24, 16, C)
        a, b = w[:, 0:8], w[:, 8:16]
        units = [v[:, :, LANES * j : LANES * (j + 1)] for v in (a, b) for j in range(J)]
        tiles = [jnp.concatenate(units[2 * t : 2 * t + 2], axis=1).astype(BF16) for t in range(3)]
        for q in range(24):
            piece, inner = divmod(12 * k + q // 2, 3)
            for t in range(3):
                B.gb[0, piece // 4, piece // 2 % 2, piece % 2, inner, 3 * (q % 2) + t] = tiles[t][q]


def ph_wgrad_up(e, B):
    width = 256
    for k in range(HID // width):
        w = lax.dot_general(
            B.n[...], B.gp[:, width * k : width * (k + 1)], (((0,), (0,)), ((), ())), preferred_element_type=F32
        )
        w = w.reshape(48, 8, width)
        w = jnp.concatenate([w[:, :, :LANES], w[:, :, LANES:]], axis=1).astype(BF16)
        B.gb[1, :, :, :, :, k] = w.reshape(4, 2, 2, 3, 16, LANES)


def dy_copy(e, B, m, up):
    if up:
        return remote(e, B.hs.at[m, 1], B.hr.at[m, 0], B.s_dy.at[1, m], B.r_dy.at[1, m], r=e.r + GROUP)
    return remote(e, B.hs.at[m, 0], B.hr.at[m, 1], B.s_dy.at[0, m], B.r_dy.at[0, m], r=e.r - GROUP)


def dy_send(e, B, m):
    zero = jnp.zeros((3 * SUB, LANES), F32)
    for j in range(J):
        B.big[pl.ds(xrow(j, m), 3 * SUB), :] = zero
        B.big[pl.ds(xrow(j, m) + (COLS + 3) * SUB, 3 * SUB), :] = zero
        for side in range(2):
            for k in range(3):
                row = 3 + k if side == 0 else 8 + k
                v = B.big[pl.ds(xrow(j, m) + 3 * SUB + row, COLS, stride=SUB), :]
                B.hs[m, side, k, :, LANES * j : LANES * (j + 1)] = v.astype(BF16)

    @pl.when(e.g > 0)
    def _():
        dy_copy(e, B, m, False).start()

    @pl.when(e.g < e.G - 1)
    def _():
        dy_copy(e, B, m, True).start()


def ph_dy_edges(e, B):
    zero = jnp.zeros((MICRO, 3, COLS, C), BF16)

    @pl.when(e.g == 0)
    def _():
        B.hr[:, 0] = zero

    @pl.when(e.g == e.G - 1)
    def _():
        B.hr[:, 1] = zero


def dy_take(e, B, m):
    @pl.when(e.g < e.G - 1)
    def _():
        dy_copy(e, B, m, False).wait_recv()

    @pl.when(e.g > 0)
    def _():
        dy_copy(e, B, m, True).wait_recv()

    for j in range(J):
        for side in range(2):
            for k in range(3):
                row = k if side == 0 else 11 + k
                v = B.hr[m, side, k, :, LANES * j : LANES * (j + 1)].astype(F32)
                B.big[pl.ds(xrow(j, m) + 3 * SUB + row, COLS, stride=SUB), :] = v


def ph_dy_done(e, B):
    for m in range(MICRO):

        @pl.when(e.g > 0)
        def _(m=m):
            dy_copy(e, B, m, False).wait_send()

        @pl.when(e.g < e.G - 1)
        def _(m=m):
            dy_copy(e, B, m, True).wait_send()


def ph_conv_kernel(e, B, steps):
    halves = COLS // TILE

    def taps(it, _):
        hooks(it, steps)
        j = it // 7
        a = it % 7

        def body(k, dk):
            m = k // halves
            c0 = k % halves * TILE
            dk = list(dk)
            at = j * NPOS + m * POS + c0 * OWN
            xs = [B.xc[pl.ds(pl.multiple_of(at + OWN * c, OWN), OWN), :] for c in range(TILE)]
            for c in range(TILE + 6):
                d = B.big[pl.ds(xrow(j, m) + (c0 + c) * SUB + a, OWN), :]
                for b in range(7):
                    if 0 <= c - b < TILE:
                        dk[b] = dk[b] + d * xs[c - b]
            return tuple(dk)

        zero = jnp.zeros((OWN, LANES), F32)
        dk = lax.fori_loop(0, MICRO * halves, body, (zero,) * 7)
        for b in range(7):
            tap = (6 - a) * 7 + 6 - b
            B.sg[pl.ds(tap * J + j, 1), :] = jnp.sum(dk[b], 0, keepdims=True)
        return 0

    lax.fori_loop(0, 7 * J, taps, 0)


def ph_conv_input(e, B, steps):
    halves = COLS // TILE

    def body(it, _):
        hooks(it, steps)
        m = it // (J * halves)
        j = it // halves % J
        c0 = it % halves * TILE
        at = j * NPOS + m * POS + c0 * OWN
        acc = [B.z[pl.ds(pl.multiple_of(at + OWN * c, OWN), OWN), :] for c in range(TILE)]
        acc = conv_tile(B, m, j, c0, TILE, acc, True)
        for c in range(TILE):
            B.dx[pl.ds(pl.multiple_of(at + OWN * c, OWN), OWN), :] = acc[c]
        return 0

    lax.fori_loop(0, MICRO * J * halves, body, 0)


def ph_small_fill(e, B):
    for k in range(HID // LANES):
        B.sg[SG_CUP + k : SG_CUP + k + 1, :] = jnp.sum(B.acup[:, LANES * k : LANES * (k + 1)], 0, keepdims=True)
    for v in range(7):
        for j in range(J):
            row = SG_VEC + v * J + j
            B.sg[row : row + 1, :] = jnp.sum(B.acc[v, :, LANES * j : LANES * (j + 1)], 0, keepdims=True)


def out_copy(e, B, m, d):
    j = lax.rem(e.i + d, GROUP)
    return remote(
        e,
        B.xg.at[m, pl.ds(3 + 2 * j, 2)],
        B.fo.at[m, e.i],
        B.s_out.at[m, d],
        B.r_out.at[m, d],
        r=e.g * GROUP + j,
    )


def own_out_copy(e, B, m):
    return pltpu.make_async_copy(B.xg.at[m, pl.ds(3 + 2 * e.i, 2)], B.fo.at[m, e.i], B.s_outown.at[m])


def out_send(e, B, m):
    for row in range(OWN):
        for j in range(J):
            v = B.dx[pl.ds(j * NPOS + m * POS + row, COLS, stride=OWN), :]
            B.xg[m, 3 + row, :, LANES * j : LANES * (j + 1)] = v.astype(BF16)
    own_out_copy(e, B, m).start()
    for d in (2, 1, 3):
        out_copy(e, B, m, d).start()


def ph_out_wait(e, B):
    for m in range(MICRO):
        own_out_copy(e, B, m).wait()
        for d in range(1, GROUP):
            out_copy(e, B, m, d).wait()


PIECE = C * HID // LANES // 16
START = (ROW_DOWN, ROW_UP)


def rs_first(e, B, f):
    c = e.i % 2
    return remote(e, B.gb.at[f, :, :, 1 - c], B.ra1.at[f], B.s_rs.at[f, 0], B.r_rs.at[f, 0], r=e.r + 1 - 2 * c)


def rs_second(e, B, f):
    to = e.g * GROUP + lax.rem(e.i + 2, GROUP)
    return remote(e, B.sa2.at[f], B.ra2.at[f], B.s_rs.at[f, 1], B.r_rs.at[f, 1], r=to)


def group_of(e, q):
    return q * (e.G // 4)


def rs_third(e, B, f, q):
    to = group_of(e, q)
    d = lax.rem(to - e.g + e.G, e.G)
    return remote(e, B.sc.at[f, q], B.rc.at[f, d], B.s_rc.at[f, q], B.r_rc.at[f, d], r=to * GROUP + e.i)


def rs_third_wait(e, B, f, d):
    return remote(e, B.sc.at[f, 0], B.rc.at[f, d], B.s_rc.at[f, 0], B.r_rc.at[f, d], r=lax.rem(e.r + GROUP, e.n))


def rs_fourth(e, B, f, d):
    return remote(e, B.rb.at[f, 0], B.rb.at[f, d], B.s_rb.at[f, d], B.r_rb.at[f, d], b=lax.rem(e.b + d, e.nb))


def ends_here(e, body):
    if e.G == 4:
        body()
    else:
        pl.when(e.g % (e.G // 4) == 0)(body)


def rs_step1(e, B, f):
    rs_first(e, B, f).start()


def rs_step2(e, B, f):
    x, c = e.i // 2, e.i % 2
    rs_first(e, B, f).wait_recv()
    for q in range(4):
        B.sa2[f, q] = (B.gb[f, q, 1 - x, c].astype(F32) + B.ra1[f, q, 1 - x].astype(F32)).astype(BF16)
    rs_second(e, B, f).start()
    for q in range(4):
        B.h1[f, q] = B.gb[f, q, x, c].astype(F32) + B.ra1[f, q, x].astype(F32)


def rs_step3(e, B, f):
    rs_second(e, B, f).wait_recv()
    for q in range(4):
        B.h1[f, q] = B.h1[f, q] + B.ra2[f, q].astype(F32)
        B.sc[f, q] = B.h1[f, q].astype(BF16)
    for q in range(4):

        @pl.when(e.g != group_of(e, q))
        def _(q=q):
            rs_third(e, B, f, q).start()


def rs_step4(e, B, f):
    def body():
        total = B.h1[f, e.g // (e.G // 4)]
        for d in range(1, e.G):
            rs_third_wait(e, B, f, d).wait_recv()
            total = total + B.rc[f, d].astype(F32)
        B.rb[f, 0] = total.astype(BF16)
        for d in range(1, e.nb):
            rs_fourth(e, B, f, d).start()

    ends_here(e, body)


def piece_owners(e, f):
    start = START[f] + PIECE * (e.g // (e.G // 4) * 4 + e.i)
    return start // e.slab, (start + PIECE - 1) // e.slab


def own_copy(e, B, f, k, owner):
    slot = lax.rem(e.g // (e.G // 4) * 4 + e.i, 8)
    return remote(e, B.fp.at[f], B.ro.at[f, slot], B.s_ro.at[f, k], B.r_ro.at[f, slot], r=owner)


def rs_step5(e, B, f):
    def body():
        for d in range(1, e.nb):
            rs_fourth(e, B, f, d).wait_recv()
        for k in range(3):
            total = None
            for b in range(e.nb):
                part = B.rb[f, lax.rem(e.b - b + e.nb, e.nb), k].astype(F32)
                total = part if total is None else total + part
            for t in range(6):
                for h in range(2):
                    unit = 2 * t + h
                    tile = total[t, 8 * h : 8 * h + 8, :]
                    if f == 1:
                        B.ft[pl.ds(96 * k + unit, 8, stride=12), :] = tile
                    else:
                        B.ft[pl.ds(96 * k + 24 * (unit // 3) + unit % 3, 8, stride=3), :] = tile
        B.fp[f] = B.ft[...].astype(BF16)
        lo, hi = piece_owners(e, f)

        @pl.when(lo != e.r)
        def _():
            own_copy(e, B, f, 0, lo).start()

        @pl.when(jnp.logical_and(hi != lo, hi != e.r))
        def _():
            own_copy(e, B, f, 1, hi).start()

    ends_here(e, body)


def rs_place(e, B, f):
    for p in range(16):
        off = START[f] + PIECE * p - e.slab * e.r
        home = group_of(e, p // 4) * GROUP + p % 4
        overlap = jnp.logical_and(off < e.slab, off + PIECE > 0)

        @pl.when(jnp.logical_and(overlap, e.r != home))
        def _(p=p, off=off, home=home):
            slot = p % 8
            remote(e, B.fp.at[f], B.ro.at[f, slot], B.s_ro.at[f, 0], B.r_ro.at[f, slot], r=home).wait_recv()
            B.gf[pl.ds(MARGIN + off, PIECE), :] = B.ro[f, slot].astype(F32)

        @pl.when(jnp.logical_and(overlap, e.r == home))
        def _(off=off):
            B.gf[pl.ds(MARGIN + off, PIECE), :] = B.fp[f].astype(F32)


def ph_rs_done(e, B):
    for f in range(2):
        rs_first(e, B, f).wait_send()
        rs_second(e, B, f).wait_send()
        for q in range(4):

            @pl.when(e.g != group_of(e, q))
            def _(f=f, q=q):
                rs_third(e, B, f, q).wait_send()

        def body(f=f):
            for d in range(1, e.nb):
                rs_fourth(e, B, f, d).wait_send()
            lo, hi = piece_owners(e, f)

            @pl.when(lo != e.r)
            def _():
                own_copy(e, B, f, 0, lo).wait_send()

            @pl.when(jnp.logical_and(hi != lo, hi != e.r))
            def _():
                own_copy(e, B, f, 1, hi).wait_send()

        ends_here(e, body)


MARGIN = 1792


def ph_small_first(e, B):
    for d in range(1, e.n):
        small_copy(e, B, d).start()


def small_copy(e, B, d):
    per = SG_ROWS // e.n
    to = lax.rem(e.r + d, e.n)
    return remote(
        e, B.sg.at[pl.ds(pl.multiple_of(to * per, per), per)], B.rsg.at[d], B.s_sg.at[0, d], B.r_sg.at[0, d], r=to
    )


def small_batch(e, B, d):
    return remote(e, B.sgb.at[0], B.sgb.at[d], B.s_sgb.at[d], B.r_sgb.at[d], b=lax.rem(e.b + d, e.nb))


def small_back(e, B, d):
    return remote(e, B.sga.at[e.r], B.sga.at[e.r], B.s_sg.at[1, d], B.r_sg.at[1, d], r=lax.rem(e.r + d, e.n))


def ph_small_second(e, B):
    per = SG_ROWS // e.n
    total = B.sg[pl.ds(pl.multiple_of(e.r * per, per), per), :]
    for d in range(1, e.n):
        small_copy(e, B, d).wait_recv()
        total = total + B.rsg[d]
    B.sgb[0] = total
    for d in range(1, e.nb):
        small_batch(e, B, d).start()


def ph_small_third(e, B):
    for d in range(1, e.nb):
        small_batch(e, B, d).wait_recv()
    total = None
    for b in range(e.nb):
        part = B.sgb[lax.rem(e.b - b + e.nb, e.nb)]
        total = part if total is None else total + part
    B.sga[e.r] = total
    for d in range(1, e.n):
        small_back(e, B, d).start()


def ph_small_place(e, B):
    for d in range(1, e.n):
        small_back(e, B, d).wait_recv()
    per = SG_ROWS // e.n
    for k in range(e.n):
        B.sg2[per * k : per * (k + 1), :] = B.sga[k]
    for k, (first, at, count) in enumerate(((ROW_K, 0, 49 * J), (ROW_CUP, SG_CUP, HID // LANES), (ROW_VEC, SG_VEC, 7 * J))):
        off = MARGIN + first % e.slab

        @pl.when(e.r == first // e.slab)
        def _(off=off, at=at, count=count):
            B.gf[off : off + count, :] = B.sg2[at : at + count, :]


def ph_small_done(e, B):
    for d in range(1, e.n):
        small_copy(e, B, d).wait_send()
        small_back(e, B, d).wait_send()
    for d in range(1, e.nb):
        small_batch(e, B, d).wait_send()


def ph_head_grads(e, B):
    parts = GROUP * e.nb
    rows = 16 * parts
    sums = None
    for p in range(parts):
        x = B.pall[p].astype(F32)
        sums = x if sums is None else sums + x
        dd = x[6:9, 0:DOUT]
        B.gp[16 * p : 16 * p + 16, 0:DOUT] = jnp.concatenate([dd, dd, jnp.zeros((10, DOUT), F32)], axis=0).astype(BF16)
        dl = x[9:12, 0:CLSP]
        B.gp[rows + 16 * p : rows + 16 * p + 16, 0:CLSP] = jnp.concatenate(
            [jnp.zeros((6, CLSP), F32), dl, jnp.zeros((7, CLSP), F32)], axis=0
        ).astype(BF16)
    B.psum[...] = sums
    for q in range(4):
        for p in range(parts):
            B.v2[16 * p : 16 * p + 16, :] = B.pall[p, :, C * q : C * (q + 1)].astype(F32)
        for j in range(J):
            t = J * q + j
            B.u[LANES * t : LANES * (t + 1), 0:rows] = B.v2[0:rows, LANES * j : LANES * (j + 1)].T.astype(BF16)
    per = DOUT // LANES
    base = MARGIN - e.slab * e.r

    kc = 288
    low = e.slab * e.r - ROW_DS

    @pl.when(jnp.logical_and(low < 4 * C * per, low + e.slab > 0))
    def _():
        k0 = jnp.clip(low // (16 * per) * 16, 0, 4 * C - kc)
        k0 = pl.multiple_of(k0, 16)
        w = jnp.dot(B.u[pl.ds(k0, kc), 0:rows], B.gp[0:rows, 0:DOUT], preferred_element_type=F32)
        for j in range(per):
            B.gf[pl.ds(base + ROW_DS + per * k0 + j, kc, stride=per), :] = w[:, LANES * j : LANES * (j + 1)]

    low2 = e.slab * e.r - ROW_HEAD

    @pl.when(jnp.logical_and(low2 < DOUT * CLS // LANES, low2 + e.slab > 0))
    def _():
        g0 = jnp.clip(low2 // 125, 0, DOUT // 16 - 16)
        k0 = pl.multiple_of(DOUT + 16 * g0, 16)
        for t in range(8):
            B.big[256 * t : 256 * (t + 1), :] = jnp.dot(
                B.u[pl.ds(k0, 256), 0:rows],
                B.gp[rows : 2 * rows, LANES * t : LANES * (t + 1)],
                preferred_element_type=F32,
            )
        lane = lax.broadcasted_iota(jnp.int32, (16, LANES), 1)
        held = None
        for kk in range(16):
            o = (-CLS * kk) % LANES
            tiles = [B.big[pl.ds(256 * t + kk, 16, stride=16), :] for t in range(8)]
            if o:
                tiles = [pltpu.roll(tile, LANES - o, 1) for tile in tiles]
            for s in range(CLS * kk // LANES, (CLS * kk + CLS - 1) // LANES + 1):
                t0 = (LANES * s - CLS * kk) // LANES
                if o == 0:
                    value = tiles[t0]
                elif t0 < 0:
                    value = tiles[0]
                elif t0 + 1 > 7:
                    value = tiles[t0]
                else:
                    value = jnp.where(lane < LANES - o, tiles[t0], tiles[t0 + 1])
                border = CLS * kk - LANES * s
                if border > 0:
                    value = jnp.where(lane < border, held, value)
                if LANES * (s + 1) > CLS * (kk + 1):
                    held = value
                else:
                    B.gf[pl.ds(base + ROW_HEAD + 125 * g0 + s, 16, stride=125), :] = value

    @pl.when(e.r == ROW_OUT // e.slab)
    def _():
        off = MARGIN + ROW_OUT % e.slab
        for j in range(per):
            at = slice(LANES * j, LANES * (j + 1))
            B.gf[off + j : off + j + 1, :] = B.psum[6:7, at] * e.positions + (
                B.psum[7:8, at] * e.positions + B.psum[8:9, at] * e.positions
            )
            gain = B.psum[12:13, at] + B.psum[13:14, at] + B.psum[14:15, at]
            B.gf[off + per + j : off + per + j + 1, :] = gain
            at = slice(DOUT + LANES * j, DOUT + LANES * (j + 1))
            shift = B.psum[12:13, at] + B.psum[13:14, at] + B.psum[14:15, at]
            B.gf[off + 2 * per + j : off + 2 * per + j + 1, :] = shift

    @pl.when(e.r == ROW_BH // e.slab)
    def _():
        off = MARGIN + ROW_BH % e.slab
        for j in range(CLSP // LANES):
            at = slice(LANES * j, LANES * (j + 1))
            B.gf[off + j : off + j + 1, :] = B.psum[9:10, at] + B.psum[10:11, at] + B.psum[11:12, at]
        rest = FLAT - ROW_BH - CLSP // LANES
        B.gf[off + CLSP // LANES : off + CLSP // LANES + rest, :] = jnp.zeros((rest, LANES), F32)


def norm_copy(e, B, d):
    return remote(e, B.nrm.at[0], B.nrm.at[d], B.s_nrm.at[d], B.r_nrm.at[d], r=lax.rem(e.r + d, e.n))


def ph_norm(e, B):
    size = 64
    whole = e.slab // size

    def body(k, acc):
        v = B.gf[pl.ds(pl.multiple_of(MARGIN + size * k, 8), size), :]
        return acc + jnp.sum((v * v).reshape(size // 8, 8, LANES), 0)

    part = lax.fori_loop(0, whole, body, jnp.zeros((8, LANES), F32))
    v = B.gf[MARGIN + whole * size : MARGIN + e.slab, :]
    B.nrm[0] = part + jnp.broadcast_to(jnp.sum(v * v, 0, keepdims=True) * 0.125, (8, LANES))
    for d in range(1, e.n):
        norm_copy(e, B, d).start()


def ph_norm_wait(e, B):
    for d in range(1, e.n):
        norm_copy(e, B, d).wait_recv()
    total = None
    for k in range(e.n):
        part = B.nrm[lax.rem(e.r - k + e.n, e.n)]
        total = part if total is None else total + part
    square = jnp.sum(jnp.sum(total, 0, keepdims=True), 1, keepdims=True)
    B.o_norm[...] = jnp.broadcast_to(jnp.sqrt(square), (8, LANES))
    loss = B.psum[15:16, :]
    loss = loss[:, 0:LANES] + loss[:, LANES : 2 * LANES] + loss[:, 2 * LANES : 3 * LANES]
    B.o_loss[...] = jnp.broadcast_to(loss, (8, LANES))
    for d in range(1, e.n):
        norm_copy(e, B, d).wait_send()


def buffers(e):
    n, G, nb, slab = e.n, e.G, e.nb, e.slab
    tiles = (3, 6, 16, LANES)
    parts = GROUP * nb
    V = pltpu.VMEM
    D = pltpu.SemaphoreType.DMA
    return dict(
        gw=V((n, 2, e.half, LANES), BF16),
        stage=V((TAB_ROWS, LANES), F32),
        tab=V((TAB_ROWS, LANES), F32),
        big=V((10816, LANES), F32),
        dx=V((8 * DOUT, LANES), F32),
        wup=V((C, HID), BF16),
        wdn=V((HID, C), BF16),
        wds=V((4 * C, DOUT), BF16),
        wh=V((DOUT, CLSP), BF16),
        xg=V((MICRO, 14, COLS, C), BF16),
        xc=V((J * NPOS, LANES), F32),
        kb=V((49 * J, 8, LANES), F32),
        v1=V((NPOS, C), F32),
        rs1=V((NPOS, LANES), F32),
        v2=V((NPOS, C), F32),
        rs2=V((NPOS, LANES), F32),
        n=V((NPOS, C), BF16),
        u=V((NPOS, HID), BF16),
        gp=V((NPOS, HID), BF16),
        z=V((J * NPOS, LANES), F32),
        dz=V((NPOS, C), BF16),
        ps=V((MICRO, 2, OWN, C), F32),
        vs=V((MICRO, 2, OWN, C), F32),
        sl=V((32, C), F32),
        sr=V((G, 32, C), F32),
        dn2=V((32, C), F32),
        dnt=V((MICRO, 2, OWN, C), F32),
        pb=V((16, 4 * C), F32),
        pall=V((parts, 16, 4 * C), BF16),
        psum=V((16, 4 * C), F32),
        acc=V((7, 8, C), F32),
        acup=V((8, HID), F32),
        hs=V((MICRO, 2, 3, COLS, C), BF16),
        hr=V((MICRO, 2, 3, COLS, C), BF16),
        gb=V((2, 4, 2, 2) + tiles, BF16),
        ra1=V((2, 4, 2) + tiles, BF16),
        sa2=V((2, 4) + tiles, BF16),
        ra2=V((2, 4) + tiles, BF16),
        h1=V((2, 4) + tiles, F32),
        sc=V((2, 4) + tiles, BF16),
        rc=V((2, G) + tiles, BF16),
        rb=V((2, nb) + tiles, BF16),
        ft=V((PIECE, LANES), F32),
        fp=V((2, PIECE, LANES), BF16),
        ro=V((2, 8, PIECE, LANES), BF16),
        gf=V((MARGIN + slab + MARGIN, LANES), F32),
        sg=V((SG_ROWS, LANES), F32),
        sg2=V((SG_ROWS, LANES), F32),
        rsg=V((n, SG_ROWS // n, LANES), F32),
        sgb=V((nb, SG_ROWS // n, LANES), F32),
        sga=V((n, SG_ROWS // n, LANES), F32),
        nrm=V((n, 8, LANES), F32),
        s_own=D((1,)),
        s_feat=D((MICRO, GROUP)),
        r_feat=D((MICRO, GROUP)),
        s_halo=D((2, MICRO)),
        r_halo=D((2, MICRO)),
        s_tab=D((len(TABLES), G)),
        s_tabg=D((len(TABLES), GROUP)),
        r_tab=D((len(TABLES),)),
        s_line=D((2, G)),
        r_line=D((2, G)),
        s_pair=D((G,)),
        r_pair=D((G,)),
        s_row=D((2, G)),
        r_row=D((2, G)),
        s_core=D((4, G)),
        r_core=D((4, G)),
        s_patch=D((G,)),
        r_patch=D((G,)),
        s_pb=D((nb,)),
        r_pb=D((nb,)),
        s_pg=D((GROUP,)),
        r_pg=D((GROUP,)),
        s_dy=D((2, MICRO)),
        r_dy=D((2, MICRO)),
        s_out=D((MICRO, GROUP)),
        r_out=D((MICRO, GROUP)),
        s_outown=D((MICRO,)),
        s_rs=D((2, 2)),
        r_rs=D((2, 2)),
        s_rc=D((2, 4)),
        r_rc=D((2, G)),
        s_rb=D((2, nb)),
        r_rb=D((2, nb)),
        s_ro=D((2, 2)),
        r_ro=D((2, 8)),
        s_sg=D((2, n)),
        r_sg=D((2, n)),
        s_sgb=D((nb,)),
        r_sgb=D((nb,)),
        s_nrm=D((n,)),
        r_nrm=D((n,)),
    )


def ph_clear(e, B):
    B.sg[...] = jnp.zeros_like(B.sg)


def ph_result(e, B):
    B.o_grad[...] = B.gf[MARGIN : MARGIN + e.slab, :]


def schedule(e, B):
    def do(step, *args):
        return lambda: step(e, B, *args)

    first = range((ROW_VEC - 1) // e.slab // GROUP + 1)
    rest = range(len(first), e.G)
    ph_barrier_signal(e, B)
    ph_cast(e, B)
    ph_feat_zero(e, B)
    ph_clear(e, B)
    ph_barrier_wait(e, B)
    ph_feat_start(e, B)
    ph_tables_start(e, B)
    line_start(e, B)
    halo_start(e, B, 0)
    tables_forward(e, B, (0,))
    line_step(e, B, 0)
    halo_start(e, B, 1)
    for d in range(1, e.G - 2):
        line_step(e, B, d)
    tables_forward(e, B, (1, 2, 3, 4))
    halo_start(e, B, 2)
    line_step(e, B, e.G - 2)
    pair_step(e, B, first)
    pair_step(e, B, rest)
    tables_wait(e, B, (0, 2))
    ph_taps(e, B)
    ph_conv_fwd(
        e,
        B,
        {
            0: [do(halo_wait, 0), do(transpose, 0)],
            6: [do(halo_wait, 1), do(transpose, 1)],
            9: [do(row_step, first)],
            12: [do(halo_wait, 2), do(transpose, 2)],
            16: [do(core_step, first)],
        },
    )
    ph_norm_one(e, B)
    tables_wait(e, B, (1, 3, 4))
    gather_ready(e, B, first)
    ph_weights_mlp(e, B)
    ph_mlp_fwd(e, B, {0: [do(row_step, rest)], 4: [do(core_step, rest)]})
    ph_patch_local(e, B)
    patch_start(e, B)
    gather_ready(e, B, rest)
    ph_weights_head(e, B)
    patch_wait(e, B)
    ph_head(e, B)
    ph_payload_batch(e, B)
    ph_dy_edges(e, B)
    ph_bwd_one(e, B)
    ph_wgrad_down(e, B)
    rs_step1(e, B, 0)
    ph_bwd_two(
        e,
        B,
        {
            1: [do(ph_payload_group)],
            2: [do(dy_send, 0), do(rs_step2, 0)],
            4: [do(dy_send, 1)],
        },
    )
    dy_send(e, B, 2)
    ph_wgrad_up(e, B)
    rs_step1(e, B, 1)
    for m in range(MICRO):
        dy_take(e, B, m)
    ph_conv_kernel(
        e,
        B,
        {
            1: [do(rs_step3, 0)],
            5: [do(rs_step2, 1)],
            14: [do(rs_step4, 0)],
            18: [do(rs_step3, 1)],
        },
    )
    ph_small_fill(e, B)
    ph_small_first(e, B)
    ph_feat_done(e, B)
    ph_conv_input(
        e,
        B,
        {
            2: [do(rs_step5, 0)],
            5: [do(ph_small_second)],
            6: [do(out_send, 0)],
            9: [do(ph_small_third)],
            11: [do(rs_step4, 1)],
            12: [do(out_send, 1)],
            14: [do(ph_payload_wait), do(ph_head_grads)],
            16: [do(rs_step5, 1)],
        },
    )
    out_send(e, B, 2)
    ph_small_place(e, B)
    rs_place(e, B, 0)
    rs_place(e, B, 1)
    ph_norm(e, B)
    ph_tables_done(e, B)
    ph_gather_done(e, B)
    ph_dy_done(e, B)
    ph_rs_done(e, B)
    ph_small_done(e, B)
    ph_out_wait(e, B)
    ph_norm_wait(e, B)
    ph_result(e, B)


def step_kernel(e, names, *refs):
    B = Env()
    for name, ref in zip(names, refs):
        setattr(B, name, ref)
    here(e)
    schedule(e, B)


def train_step(e, features, mask, labels, params):
    bufs = buffers(e)
    names = ["mask", "labels", "features", "params", "o_grad", "o_norm", "o_loss", "fo"] + list(bufs)
    return pl.pallas_call(
        functools.partial(step_kernel, e, names),
        out_shape=(
            jax.ShapeDtypeStruct((e.slab, LANES), F32),
            jax.ShapeDtypeStruct((8, LANES), F32),
            jax.ShapeDtypeStruct((8, LANES), F32),
            jax.ShapeDtypeStruct((MICRO, GROUP, 2, COLS, C), BF16),
        ),
        in_specs=[
            pl.BlockSpec(memory_space=pltpu.SMEM),
            pl.BlockSpec(memory_space=pltpu.SMEM),
            pl.BlockSpec(memory_space=pl.ANY),
            pl.BlockSpec(memory_space=pltpu.VMEM),
        ],
        out_specs=(
            pl.BlockSpec(memory_space=pltpu.VMEM),
            pl.BlockSpec(memory_space=pltpu.VMEM),
            pl.BlockSpec(memory_space=pltpu.VMEM),
            pl.BlockSpec(memory_space=pl.ANY),
        ),
        scratch_shapes=list(bufs.values()),
        compiler_params=pltpu.CompilerParams(collective_id=0, has_side_effects=True, vmem_limit_bytes=64 * MB - 65536),
        name="train_step",
    )(mask, labels, features, params)


def update_kernel(norm, loss, grad, params, m1, m2, out, o_norm, o_loss, new_params, first, second, feats):
    scale = jnp.minimum(1.0, CLIP / (norm[0:1, 0:1] + 1e-06))
    clipped = grad[...] * scale
    one = BETA_ONE * m1[...] + (1.0 - BETA_ONE) * clipped
    two = BETA_TWO * m2[...] + (1.0 - BETA_TWO) * clipped * clipped
    first[...] = one
    second[...] = two
    ratio = one / (1.0 - BETA_ONE**STEP) / (jnp.sqrt(two / (1.0 - BETA_TWO**STEP)) + EPS_ADAM)
    new_params[...] = params[...] - RATE * (ratio + DECAY * params[...])
    feats[...] = out[...].astype(F32)

    @pl.when(pl.program_id(0) == 0)
    def _():
        o_norm[0, 0] = jnp.max(norm[...])
        o_loss[0, 0] = jnp.max(loss[...])


def update(e, grad, norm, loss, params, m1, m2, out):
    flat = jax.ShapeDtypeStruct((e.slab, LANES), F32)
    steps = MICRO * GROUP
    rows = (e.slab // steps + 8) // 8 * 8
    line = pl.BlockSpec((rows, LANES), lambda k: (k, 0))
    whole = pl.BlockSpec((8, LANES), lambda k: (0, 0))
    part = pl.BlockSpec((1, 1, 2, COLS, C), lambda k: (k // GROUP, k % GROUP, 0, 0, 0))
    one = pl.BlockSpec(memory_space=pltpu.SMEM)
    scalar = jax.ShapeDtypeStruct((1, 1), F32)
    return pl.pallas_call(
        update_kernel,
        grid=(steps,),
        in_specs=[whole, whole, line, line, line, line, part],
        out_specs=(one, one, line, line, line, part),
        out_shape=(scalar, scalar, flat, flat, flat, jax.ShapeDtypeStruct((MICRO, GROUP, 2, COLS, C), F32)),
        compiler_params=pltpu.CompilerParams(vmem_limit_bytes=48 * MB),
        name="update",
    )(norm, loss, grad, params, m1, m2, out)


def local(e, features, drop_mask, labels, params, moment1, moment2):
    flat = [v.reshape(e.slab, LANES) for v in (params, moment1, moment2)]
    grad, norm, loss, out = train_step(e, features, drop_mask, labels, flat[0])
    norm, loss, new_params, first, second, feats = update(e, grad, norm, loss, *flat, out)
    size = e.slab * LANES
    return (
        new_params.reshape(size),
        first.reshape(size),
        second.reshape(size),
        loss.reshape(()),
        norm.reshape(()),
        feats,
    )


def solution(mesh):
    e = Env()
    e.n = mesh.shape["rows"]
    e.nb = mesh.shape["batch"]
    e.G = e.n // GROUP
    e.slab = FLAT // e.n
    e.half = (e.slab + 31) // 32 * 16
    e.positions = float(e.n * COLS // 2)
    e.inv_count = 1.0 / (MICRO * GROUP * e.nb)
    return jax.shard_map(
        functools.partial(local, e),
        mesh=mesh,
        in_specs=(
            P(None, "batch", "rows", None, None),
            P(None, "batch"),
            P(None, "batch"),
            P("rows"),
            P("rows"),
            P("rows"),
        ),
        out_specs=(P("rows"), P("rows"), P("rows"), P(), P(), P(None, "batch", "rows", None, None)),
        check_vma=False,
    )
```

```python
import functools

import jax
import jax.numpy as jnp
from jax import lax
from jax.experimental import pallas as pl
from jax.experimental.pallas import tpu as pltpu
from jax.sharding import PartitionSpec as P

C = 384
HID = 1536
DOUT = 768
CLS = 1000
MICRO = 3
STEP = 10
P_SIZE = 3153920
KEEP = 0.8
CLIP = 0.01
RATE = 0.05
BETA_ONE = 0.9
BETA_TWO = 0.999
DECAY = 0.05
EPS_ADAM = 1e-08
EPS_NORM = 1e-06

MESH = pl.DeviceIdType.MESH
F32 = jnp.float32
BF16 = jnp.bfloat16
MB = 1 << 20

LANES = 128
J = C // LANES
GROUP = 4
OWN = 8
COLS = 64
PADC = COLS + 6
SUB = 16
POS = COLS * OWN
NPOS = MICRO * POS
FLAT = P_SIZE // LANES
ROW_K = 0
ROW_UP = 49 * J
ROW_CUP = ROW_UP + C * HID // LANES
ROW_DOWN = ROW_CUP + HID // LANES
ROW_VEC = ROW_DOWN + C * HID // LANES
ROW_DS = ROW_VEC + 7 * J
ROW_OUT = ROW_DS + 4 * C * DOUT // LANES
ROW_HEAD = ROW_OUT + 3 * DOUT // LANES
ROW_BH = ROW_HEAD + DOUT * CLS // LANES
TABLES = (
    (ROW_K, 49 * J, 0),
    (ROW_CUP, HID // LANES, 152),
    (ROW_VEC, 7 * J, 168),
    (ROW_OUT, 3 * DOUT // LANES, 192),
    (ROW_BH, FLAT - ROW_BH, 216),
)
TAB_ROWS = 232
TAB_SPAN = (152, 16, 24, 24, 16)
T_CUP, T_VEC, T_OUT, T_BH = 152, 168, 192, 216
SG_ROWS = 256
SG_CUP, SG_VEC = 152, 168
CLSP = 1024


class Env:
    pass


def xrow(j, m):
    return (j * MICRO + m) * PADC * SUB


def rows_of(refs, row, count):
    return refs[row : row + count, :]


def lane_row(ref, row, count):
    return jnp.concatenate([ref[row + k : row + k + 1, :] for k in range(count)], axis=1)


def ln_parts(blocks, width):
    total = blocks[0]
    for block in blocks[1:]:
        total = total + block
    mean = jnp.sum(total, -1, keepdims=True) * (1.0 / width)
    centred = [block - mean for block in blocks]
    square = centred[0] * centred[0]
    for block in centred[1:]:
        square = square + block * block
    spread = jnp.sum(square, -1, keepdims=True) * (1.0 / width)
    scale = lax.rsqrt(spread + EPS_NORM)
    return [block * scale for block in centred], scale


def here(e):
    e.r = lax.axis_index("rows")
    e.b = lax.axis_index("batch")
    e.g = e.r // GROUP
    e.i = e.r % GROUP
    e.h = e.b % 2


def dev(e, r=None, b=None):
    return {"rows": e.r if r is None else r, "batch": e.b if b is None else b}


def remote(e, src, dst, send, recv, r=None, b=None):
    return pltpu.make_async_remote_copy(
        src, dst, send, recv, device_id=(e.r if r is None else r, e.b if b is None else b), device_id_type=MESH
    )


def ph_barrier_signal(e, B):
    barrier = pltpu.get_barrier_semaphore()
    for d in range(1, e.n):
        pl.semaphore_signal(barrier, inc=1, device_id=(lax.rem(e.r + d, e.n), e.b), device_id_type=MESH)
    for d in range(1, e.nb):
        pl.semaphore_signal(barrier, inc=1, device_id=(e.r, lax.rem(e.b + d, e.nb)), device_id_type=MESH)


def ph_barrier_wait(e, B):
    pl.semaphore_wait(pltpu.get_barrier_semaphore(), e.n - 1 + e.nb - 1)


def feat_copy(e, B, m, d):
    j = lax.rem(e.i + d, GROUP)
    return remote(
        e,
        B.features.at[m, j],
        B.xg.at[m, pl.ds(3 + 2 * e.i, 2)],
        B.s_feat.at[m, d],
        B.r_feat.at[m, d],
        r=e.g * GROUP + j,
    )


def feat_own(e, B):
    return pltpu.make_async_copy(B.features.at[:, e.i], B.xg.at[:, pl.ds(3 + 2 * e.i, 2)], B.s_own.at[0])


def ph_feat_start(e, B):
    feat_own(e, B).start()
    for m in range(MICRO):
        for d in (2, 1, 3):
            feat_copy(e, B, m, d).start()


def ph_feat_zero(e, B):
    zero = jnp.zeros((MICRO, 3, COLS, C), BF16)

    @pl.when(e.g == 0)
    def _():
        B.xg[:, 0:3] = zero

    @pl.when(e.g == e.G - 1)
    def _():
        B.xg[:, 11:14] = zero


def halo_copy(e, B, m, up):
    if up:
        return remote(e, B.xg.at[m, 8:11], B.xg.at[m, 0:3], B.s_halo.at[1, m], B.r_halo.at[1, m], r=e.r + GROUP)
    return remote(e, B.xg.at[m, 3:6], B.xg.at[m, 11:14], B.s_halo.at[0, m], B.r_halo.at[0, m], r=e.r - GROUP)


def halo_start(e, B, m):
    if m == 0:
        feat_own(e, B).wait()
    for d in range(1, GROUP):
        feat_copy(e, B, m, d).wait_recv()

    @pl.when(e.g > 0)
    def _():
        halo_copy(e, B, m, False).start()

    @pl.when(e.g < e.G - 1)
    def _():
        halo_copy(e, B, m, True).start()


def halo_wait(e, B, m):
    @pl.when(e.g < e.G - 1)
    def _():
        halo_copy(e, B, m, False).wait_recv()

    @pl.when(e.g > 0)
    def _():
        halo_copy(e, B, m, True).wait_recv()


def ph_feat_done(e, B):
    for m in range(MICRO):
        for d in range(1, GROUP):
            feat_copy(e, B, m, d).wait_send()

        @pl.when(e.g > 0)
        def _(m=m):
            halo_copy(e, B, m, False).wait_send()

        @pl.when(e.g < e.G - 1)
        def _(m=m):
            halo_copy(e, B, m, True).wait_send()


def ph_cast(e, B):
    for h in range(2):
        count = e.half if h == 0 else e.slab - e.half
        whole = count // 16 * 16
        B.gw[e.r, h, 0:whole, :] = B.params[h * e.half : h * e.half + whole, :].astype(BF16)
        rest = count - whole
        if whole < e.half:
            parts = [jnp.zeros((e.half - whole - rest, LANES), F32)]
            if rest:
                parts = [B.params[e.slab - rest : e.slab, :]] + parts
            B.gw[e.r, h, whole : e.half, :] = jnp.concatenate(parts, axis=0).astype(BF16)
    for k, (first, count, place) in enumerate(TABLES):
        off = first % e.slab
        B.stage[place : place + count, :] = B.params[off : off + count, :]


def table_line(e, B, k, d):
    first, count, place = TABLES[k]
    owner = first // e.slab
    part = pl.ds(place, TAB_SPAN[k])
    return remote(e, B.stage.at[part], B.tab.at[part], B.s_tab.at[k, d], B.r_tab.at[k], r=lax.rem(owner + GROUP * d, e.n))


def table_group(e, B, k, d):
    first, count, place = TABLES[k]
    part = pl.ds(place, TAB_SPAN[k])
    to = e.g * GROUP + lax.rem(e.i + d, GROUP)
    return remote(e, B.tab.at[part], B.tab.at[part], B.s_tabg.at[k, d], B.r_tab.at[k], r=to)


def ph_tables_start(e, B):
    for k, (first, count, place) in enumerate(TABLES):
        owner = first // e.slab

        @pl.when(e.r == owner)
        def _(k=k, place=place):
            for d in range(1, e.G):
                table_line(e, B, k, d).start()
            B.tab[place : place + TAB_SPAN[k], :] = B.stage[place : place + TAB_SPAN[k], :]
            for d in range(1, GROUP):
                table_group(e, B, k, d).start()


def tables_forward(e, B, some):
    for k in some:
        owner = TABLES[k][0] // e.slab

        @pl.when(jnp.logical_and(e.i == owner % GROUP, e.r != owner))
        def _(k=k):
            table_line(e, B, k, 1).wait_recv()
            for d in range(1, GROUP):
                table_group(e, B, k, d).start()


def tables_wait(e, B, some):
    for k in some:
        owner = TABLES[k][0] // e.slab

        @pl.when(e.i != owner % GROUP)
        def _(k=k):
            table_group(e, B, k, 1).wait_recv()


def ph_tables_done(e, B):
    for k, (first, count, place) in enumerate(TABLES):
        owner = first // e.slab

        @pl.when(e.r == owner)
        def _(k=k):
            for d in range(1, e.G):
                table_line(e, B, k, d).wait_send()

        @pl.when(e.i == owner % GROUP)
        def _(k=k):
            for d in range(1, GROUP):
                table_group(e, B, k, d).wait_send()


def half_ref(B, slot, h):
    return B.gw.at[slot, h]


def line_copy(e, B, d):
    ref = half_ref(B, e.r, e.h)
    to = lax.rem(e.g + d, e.G)
    return remote(e, ref, ref, B.s_line.at[d], B.r_line.at[e.g], r=to * GROUP + e.i)


def line_wait(e, B, level):
    ref = half_ref(B, level * GROUP + e.i, e.h)
    return remote(e, ref, ref, B.s_line.at[0], B.r_line.at[level], r=lax.rem(e.r + GROUP, e.n))


def pair_copy(e, B, level):
    ref = half_ref(B, level * GROUP + e.i, e.h)
    return remote(e, ref, ref, B.s_pair.at[level], B.r_pair.at[level], r=e.g * GROUP + lax.rem(e.i + 2, GROUP))


def row_copy(e, B, level, other):
    i = lax.rem(e.i + 2, GROUP) if other else e.i
    ref = half_ref(B, level * GROUP + i, e.h)
    k = int(other)
    return remote(e, ref, ref, B.s_row.at[k, level], B.r_row.at[k, level], b=e.b + 1 - 2 * e.h)


def core_copy(e, B, level, other, mine):
    i = lax.rem(e.i + 2, GROUP) if other else e.i
    ref = half_ref(B, level * GROUP + i, e.h if mine else 1 - e.h)
    k = 2 * int(other) + int(mine)
    sib = e.g * GROUP + e.i + 1 - 2 * (e.i % 2)
    return remote(e, ref, ref, B.s_core.at[k, level], B.r_core.at[k, level], r=sib)


def line_send(e, B, levels):
    @pl.when(jnp.logical_and(e.g >= levels.start, e.g < levels.stop))
    def _():
        for d in range(1, e.G):
            line_copy(e, B, d).start()


def line_step(e, B, levels):
    for level in levels:

        @pl.when(e.g != level)
        def _(level=level):
            line_wait(e, B, level).wait_recv()
            row_copy(e, B, level, False).start()

        pair_copy(e, B, level).start()
        core_copy(e, B, level, False, True).start()

        @pl.when(e.g == level)
        def _(level=level):
            core_copy(e, B, level, False, False).start()


def row_step(e, B, levels):
    for level in levels:
        pair_copy(e, B, level).wait_recv()
        row_copy(e, B, level, True).start()
        core_copy(e, B, level, True, True).start()


def core_step(e, B, levels):
    for level in levels:

        @pl.when(e.g != level)
        def _(level=level):
            row_copy(e, B, level, False).wait_recv()
            core_copy(e, B, level, False, False).start()

    for level in levels:
        row_copy(e, B, level, True).wait_recv()
        core_copy(e, B, level, True, False).start()


def gather_ready(e, B, levels):
    for level in levels:
        for other in (False, True):
            for mine in (False, True):
                core_copy(e, B, level, other, mine).wait_recv()


def ph_gather_done(e, B):
    G = e.G
    for level in range(G):
        pair_copy(e, B, level).wait_send()
        row_copy(e, B, level, True).wait_send()

        @pl.when(e.g != level)
        def _(level=level):
            row_copy(e, B, level, False).wait_send()

        for other in (False, True):
            for mine in (False, True):
                core_copy(e, B, level, other, mine).wait_send()
    for d in range(1, G):
        line_copy(e, B, d).wait_send()


def flatten(e, B, first, last):
    step = 112
    s0 = first // e.slab

    def slab(k, _):
        for h in range(2):
            count = e.half if h == 0 else e.slab - e.half
            whole = count // step
            left = (count - whole * step + 15) // 16 * 16
            base = e.slab * k + h * e.half

            def body(t, _, h=h, base=base):
                at = pl.multiple_of(t * step, 16)
                B.big[pl.ds(base + t * step, step), :] = B.gw[s0 + k, h, pl.ds(at, step), :].astype(F32)
                return 0

            lax.fori_loop(0, whole, body, 0)
            if left:
                last = B.gw[s0 + k, h, whole * step : whole * step + left, :]
                B.big[pl.ds(base + whole * step, left), :] = last.astype(F32)
        return 0

    lax.fori_loop(0, (last - 1) // e.slab - s0 + 1, slab, 0)
    return e.slab * s0


def ph_weights_up(e, B):
    base = flatten(e, B, ROW_UP, ROW_CUP)
    for j in range(HID // LANES):
        B.wup[:, LANES * j : LANES * (j + 1)] = B.big[pl.ds(ROW_UP - base + j, C, stride=HID // LANES), :].astype(BF16)


def ph_weights_down(e, B):
    base = flatten(e, B, ROW_DOWN, ROW_VEC)
    for j in range(J):
        B.wdn[:, LANES * j : LANES * (j + 1)] = B.big[pl.ds(ROW_DOWN - base + j, HID, stride=J), :].astype(BF16)


def ph_weights_head(e, B):
    base = flatten(e, B, ROW_DS, ROW_OUT)
    per = DOUT // LANES
    for j in range(per):
        B.wds[:, LANES * j : LANES * (j + 1)] = B.big[pl.ds(ROW_DS - base + j, 4 * C, stride=per), :].astype(BF16)
    base = flatten(e, B, ROW_HEAD, ROW_BH)
    lane = lax.broadcasted_iota(jnp.int32, (DOUT // 16, LANES), 1)
    for kk in range(16):
        first, off = divmod(CLS * kk, LANES)
        parts = [B.big[pl.ds(ROW_HEAD - base + first + t, DOUT // 16, stride=125), :] for t in range(9 if off else 8)]
        if off:
            parts = [pltpu.roll(part, LANES - off, 1) for part in parts]
        for t in range(8):
            tile = parts[t]
            if off:
                tile = jnp.where(lane < LANES - off, parts[t], parts[t + 1])
            if t == 7:
                tile = jnp.where(lane < CLS - 7 * LANES, tile, 0.0)
            B.dx[pl.ds(DOUT * t + kk, DOUT // 16, stride=16), :] = tile
    for t in range(8):
        B.wh[:, LANES * t : LANES * (t + 1)] = B.dx[DOUT * t : DOUT * (t + 1), :].astype(BF16)


def hooks(it, steps):
    for k, some in steps.items():

        @pl.when(it == k)
        def _(some=some):
            for step in some:
                step()


def transpose(e, B, m):
    pad = jnp.zeros((3 * SUB, LANES), F32)
    for j in range(J):
        B.big[pl.ds(xrow(j, m), 3 * SUB), :] = pad
        B.big[pl.ds(xrow(j, m) + (COLS + 3) * SUB, 3 * SUB), :] = pad
        for row in range(14):
            v = B.xg[m, row, :, LANES * j : LANES * (j + 1)].astype(F32)
            B.big[pl.ds(xrow(j, m) + 3 * SUB + row, COLS, stride=SUB), :] = v
            if 3 <= row < 11:
                B.xc[pl.ds(j * NPOS + m * POS + row - 3, COLS, stride=OWN), :] = v


def ph_taps(e, B):
    def body(t, _):
        B.kb[t] = jnp.broadcast_to(B.tab[pl.ds(t, 1), :], (8, LANES))
        return 0

    lax.fori_loop(0, 49 * J, body, 0)


def vec_row(B, v, j):
    row = T_VEC + v * J + j
    return B.tab[row : row + 1, :]


def conv_tile(B, m, j, c0, tile, acc, flip):
    for a in range(7):
        taps = [B.kb[((6 - a) * 7 + 6 - b if flip else a * 7 + b) * J + j] for b in range(7)]
        for c in range(tile + 6):
            d = B.big[pl.ds(xrow(j, m) + (c0 + c) * SUB + a, OWN), :]
            for b in range(7):
                if 0 <= c - b < tile:
                    acc[c - b] = acc[c - b] + d * taps[b]
    return acc


TILE = 32


def ph_conv_fwd(e, B, steps):
    halves = COLS // TILE

    def body(it, _):
        hooks(it, steps)
        m = it // (J * halves)
        j = it // halves % J
        c0 = it % halves * TILE
        bias = jnp.broadcast_to(B.tab[pl.ds(T_VEC + j, 1), :], (OWN, LANES))
        acc = conv_tile(B, m, j, c0, TILE, [bias] * TILE, False)
        at = j * NPOS + m * POS + c0 * OWN
        for c in range(TILE):
            B.dx[pl.ds(pl.multiple_of(at + OWN * c, OWN), OWN), :] = acc[c]
        return 0

    lax.fori_loop(0, MICRO * J * halves, body, 0)


def ph_norm_one(e, B):
    size = 128

    def body(it, _):
        at = pl.multiple_of(it * size, size)
        hat, scale = ln_parts([B.dx[pl.ds(j * NPOS + at, size), :] for j in range(J)], C)
        B.rs1[pl.ds(at, size), :] = jnp.broadcast_to(scale, (size, LANES))
        for j in range(J):
            B.v1[pl.ds(at, size), LANES * j : LANES * (j + 1)] = hat[j]
            B.n[pl.ds(at, size), LANES * j : LANES * (j + 1)] = (
                hat[j] * vec_row(B, 1, j) + vec_row(B, 2, j)
            ).astype(BF16)
        return 0

    lax.fori_loop(0, NPOS // size, body, 0)


def ph_mlp_up(e, B, steps):
    chunk = 256
    width = 256
    c0 = 0.7978845608028654
    c1 = 0.044715 * c0

    def body(it, _):
        hooks(it, steps)
        at = pl.multiple_of(it * chunk, chunk)
        rows = B.n[pl.ds(at, chunk), :]
        for k in range(HID // width):
            lanes = slice(width * k, width * (k + 1))
            bias = lane_row(B.tab, T_CUP + k * width // LANES, width // LANES)
            h = jnp.dot(rows, B.wup[:, lanes], preferred_element_type=F32) + bias
            sq = h * h
            half = 0.5 * jnp.tanh(h * (c0 + c1 * sq)) + 0.5
            u = h * half
            B.u[pl.ds(at, chunk), lanes] = u.astype(BF16)
            slope = half + u * (1.0 - half) * (2.0 * c0 + 6.0 * c1 * sq)
            B.gp[pl.ds(at, chunk), lanes] = slope.astype(BF16)
        return 0

    lax.fori_loop(0, NPOS // chunk, body, 0)


def ph_mlp_down(e, B, steps):
    chunk = 256
    B.ps[...] = jnp.zeros_like(B.ps)

    def body(it, _):
        hooks(it, steps)
        at = pl.multiple_of(it * chunk, chunk)
        m = it // (POS // chunk)
        keep = B.mask[m, e.i].astype(F32) * (1.0 / KEEP)
        z = jnp.dot(B.u[pl.ds(at, chunk), :], B.wdn[...], preferred_element_type=F32)
        resid = []
        for j in range(J):
            zj = z[:, LANES * j : LANES * (j + 1)] + vec_row(B, 3, j)
            B.z[pl.ds(j * NPOS + at, chunk), :] = zj
            resid.append(B.xc[pl.ds(j * NPOS + at, chunk), :] + (vec_row(B, 4, j) * keep) * zj)
        hat, scale = ln_parts(resid, C)
        B.rs2[pl.ds(at, chunk), :] = jnp.broadcast_to(scale, (chunk, LANES))
        for j in range(J):
            B.v2[pl.ds(at, chunk), LANES * j : LANES * (j + 1)] = hat[j]
            low = (hat[j] * vec_row(B, 5, j) + vec_row(B, 6, j)).astype(BF16).astype(F32)
            low = jnp.sum(low.reshape(chunk // 16, 2, OWN, LANES), 0)
            B.ps[m, :, :, LANES * j : LANES * (j + 1)] += low
        return 0

    lax.fori_loop(0, NPOS // chunk, body, 0)


def ph_patch_local(e, B):
    even = lax.broadcasted_iota(jnp.int32, (OWN, C), 0) % 2 == 0
    pick = lax.broadcasted_iota(jnp.int32, (8, C), 0)
    for parity in range(2):
        for side in range(2):
            tile = jnp.zeros((8, C), F32)
            for m in range(MICRO):
                v = B.ps[m, side]
                part = jnp.sum(jnp.where(even if parity == 0 else jnp.logical_not(even), v, 0.0), 0, keepdims=True)
                tile = jnp.where(pick == m, part, tile)
            q = 2 * parity + side
            B.sl[8 * q : 8 * q + 8, :] = tile


def patch_copy(e, B, d):
    to = lax.rem(e.g + d, e.G)
    return remote(e, B.sl, B.sr.at[d], B.s_patch.at[d], B.r_patch.at[d], r=to * GROUP + e.i)


def patch_start(e, B):
    for d in range(1, e.G):
        patch_copy(e, B, d).start()
    B.sr[0] = B.sl[...]


def patch_wait(e, B):
    for d in range(1, e.G):
        patch_copy(e, B, d).wait_recv()
    for d in range(1, e.G):
        patch_copy(e, B, d).wait_send()


def split3(v):
    hi = v.astype(BF16).astype(F32)
    mid = (v - hi).astype(BF16).astype(F32)
    return hi, mid, v - hi - mid


def ph_head(e, B):
    total = None
    for level in range(e.G):
        part = B.sr[lax.rem(e.g - level + e.G, e.G)]
        total = part if total is None else total + part
    per = DOUT // LANES
    gain = lane_row(B.tab, T_OUT + per, per)
    shift = lane_row(B.tab, T_OUT + 2 * per, per)
    mean = total * (1.0 / e.positions)
    pooled = lane_row(B.tab, T_OUT, per)
    for q in range(4):
        parts = jnp.concatenate(split3(mean[8 * q : 8 * q + 8, :]), axis=0).astype(BF16)
        prod = jnp.dot(parts, B.wds[C * q : C * (q + 1), :], preferred_element_type=F32)
        pooled = pooled + (prod[0:8] + (prod[8:16] + prod[16:24]))
    rows = lax.broadcasted_iota(jnp.int32, (8, 1), 0)
    live = rows < MICRO
    (hat,), scale = ln_parts([pooled], DOUT)
    query = (hat * gain + shift).astype(BF16)
    lane = lax.broadcasted_iota(jnp.int32, (8, CLSP), 1)
    logits = jnp.dot(query, B.wh[...], preferred_element_type=F32) + lane_row(B.tab, T_BH, CLSP // LANES)
    logits = jnp.where(lane < CLS, logits, -1e30)
    top = jnp.max(logits, 1, keepdims=True)
    powers = jnp.exp(logits - top)
    expsum = jnp.sum(powers, 1, keepdims=True)
    label = jnp.zeros((8, 1), jnp.int32)
    for m in range(MICRO):
        label = jnp.where(rows == m, B.labels[m, e.i], label)
    onehot = (lane == label).astype(F32)
    own = jnp.sum(jnp.where(lane == label, logits, 0.0), 1, keepdims=True)
    loss = jnp.sum(jnp.where(live, top + jnp.log(expsum) - own, 0.0), 0, keepdims=True)
    grad = jnp.where(live, (powers / expsum - onehot) * e.inv_count, 0.0).astype(BF16)
    grad_query = lax.dot_general(grad, B.wh[...], (((1,), (1,)), ((), ())), preferred_element_type=F32)
    dn = grad_query * gain
    m1 = jnp.sum(dn, 1, keepdims=True) * (1.0 / DOUT)
    m2 = jnp.sum(dn * hat, 1, keepdims=True) * (1.0 / DOUT)
    grad_pool = scale * (dn - m1 - hat * m2)
    down = jnp.where(live, grad_pool * (1.0 / e.positions), 0.0).astype(BF16)
    for q in range(4):
        B.dn2[8 * q : 8 * q + 8, :] = lax.dot_general(
            down, B.wds[C * q : C * (q + 1), :], (((1,), (1,)), ((), ())), preferred_element_type=F32
        )
    low = grad.astype(F32)
    d32 = down.astype(F32)
    q32 = jnp.where(live, query.astype(F32), 0.0)
    zero3 = jnp.zeros((3, C), F32)
    g3 = jnp.sum(jnp.where(live, grad_query * hat, 0.0), 0, keepdims=True)
    s3 = jnp.sum(jnp.where(live, grad_query, 0.0), 0, keepdims=True)
    vec = jnp.concatenate([g3, s3], axis=1)
    vec_parts = split3(vec)
    loss_parts = split3(loss)
    for q in range(4):
        at = slice(C * q, C * (q + 1))
        s_hi, s_mid, _ = split3(total[8 * q : 8 * q + 8, :])
        B.pb[0:8, at] = jnp.zeros((8, C), F32)
        B.pb[8:16, at] = jnp.zeros((8, C), F32)
        B.pb[0:3, at] = s_hi[0:3]
        B.pb[3:6, at] = s_mid[0:3]
    B.pb[6:9, 0:DOUT] = d32[0:3]
    B.pb[6:9, DOUT : 2 * DOUT] = q32[0:3]
    B.pb[9:12, 0:CLSP] = low[0:3]
    for k in range(3):
        B.pb[12 + k : 13 + k, :] = vec_parts[k]
        B.pb[15:16, LANES * k : LANES * (k + 1)] = jnp.broadcast_to(loss_parts[k], (1, LANES))
    B.pall[e.i * e.nb + e.b] = B.pb[...].astype(BF16)
    even = lax.broadcasted_iota(jnp.int32, (OWN, C), 0) % 2 == 0
    for m in range(MICRO):
        for side in range(2):
            first = B.dn2[8 * side + m : 8 * side + m + 1, :]
            second = B.dn2[8 * (2 + side) + m : 8 * (2 + side) + m + 1, :]
            B.dnt[m, side] = jnp.where(even, first, second)


def batch_copy(e, B, d):
    slot = e.i * e.nb + e.b
    return remote(e, B.pall.at[slot], B.pall.at[slot], B.s_pb.at[d], B.r_pb.at[d], b=lax.rem(e.b + d, e.nb))


def group_copy(e, B, d):
    at = pl.ds(e.i * e.nb, e.nb)
    to = e.g * GROUP + lax.rem(e.i + d, GROUP)
    return remote(e, B.pall.at[at], B.pall.at[at], B.s_pg.at[d], B.r_pg.at[d], r=to)


def ph_payload_batch(e, B):
    for d in range(1, e.nb):
        batch_copy(e, B, d).start()


def ph_payload_group(e, B):
    for d in range(1, e.nb):
        batch_copy(e, B, d).wait_recv()
    for d in range(1, GROUP):
        group_copy(e, B, d).start()


def ph_payload_wait(e, B):
    for d in range(1, GROUP):
        group_copy(e, B, d).wait_recv()
    for d in range(1, e.nb):
        batch_copy(e, B, d).wait_send()
    for d in range(1, GROUP):
        group_copy(e, B, d).wait_send()


def lane_sum(blocks):
    total = blocks[0]
    for block in blocks[1:]:
        total = total + block
    return jnp.sum(total, -1, keepdims=True) * (1.0 / C)


def fold8(v):
    return jnp.sum(v.reshape(v.shape[0] // 8, 8, v.shape[1]), 0)


def ph_bwd_one(e, B):
    chunk = 256
    half = chunk // 16
    B.acc[...] = jnp.zeros_like(B.acc)
    B.acup[...] = jnp.zeros_like(B.acup)
    B.vs[...] = jnp.zeros_like(B.vs)

    def body(it, _):
        at = pl.multiple_of(it * chunk, chunk)
        m = it // (POS // chunk)
        keep = B.mask[m, e.i].astype(F32) * (1.0 / KEEP)
        span = pl.ds(at, chunk)
        lanes = [slice(LANES * j, LANES * (j + 1)) for j in range(J)]
        dg = [B.dnt[m, :, :, lanes[j]] * vec_row(B, 5, j) for j in range(J)]
        m1 = lane_sum(dg)
        hat = [B.v2[span, lanes[j]].reshape(half, 2, OWN, LANES) for j in range(J)]
        m2 = lane_sum([dg[j] * hat[j] for j in range(J)])
        scale = B.rs2[span, :].reshape(half, 2, OWN, LANES)
        for j in range(J):
            zspan = pl.ds(j * NPOS + at, chunk)
            dr = (scale * (dg[j] - m1 - hat[j] * m2)).reshape(chunk, LANES)
            B.vs[m, :, :, lanes[j]] += jnp.sum(hat[j], 0)
            dz = (dr * (vec_row(B, 4, j) * keep)).astype(BF16)
            B.dz[span, lanes[j]] = dz
            B.acc[3, :, lanes[j]] += fold8(dz.astype(F32))
            B.acc[4, :, lanes[j]] += fold8(dr * B.z[zspan, :]) * keep
            B.z[zspan, :] = dr
        return 0

    lax.fori_loop(0, NPOS // chunk, body, 0)
    for m in range(MICRO):
        B.acc[5] += B.dnt[m, 0] * B.vs[m, 0] + B.dnt[m, 1] * B.vs[m, 1]
        B.acc[6] += (B.dnt[m, 0] + B.dnt[m, 1]) * float(COLS // 2)


def ph_bwd_two(e, B, steps):
    chunk = 256
    width = 256

    def body(it, _):
        hooks(it, steps)
        at = pl.multiple_of(it * chunk, chunk)
        m = it // (POS // chunk)
        c0 = (it % (POS // chunk)) * (chunk // OWN)
        span = pl.ds(at, chunk)
        lanes = [slice(LANES * j, LANES * (j + 1)) for j in range(J)]
        dz = B.dz[span, :]
        for k in range(HID // width):
            hid = slice(width * k, width * (k + 1))
            du = lax.dot_general(dz, B.wdn[hid, :], (((1,), (1,)), ((), ())), preferred_element_type=F32)
            dh = (du * B.gp[span, hid].astype(F32)).astype(BF16)
            B.gp[span, hid] = dh
            B.acup[:, hid] += fold8(dh.astype(F32))
        dn = lax.dot_general(B.gp[span, :], B.wup[...], (((1,), (1,)), ((), ())), preferred_element_type=F32)
        dns = [dn[:, lanes[j]] for j in range(J)]
        dg = [dns[j] * vec_row(B, 1, j) for j in range(J)]
        hat = [B.v1[span, lanes[j]] for j in range(J)]
        m1 = lane_sum(dg)
        m2 = lane_sum([dg[j] * hat[j] for j in range(J)])
        scale = B.rs1[span, :]
        for j in range(J):
            dy = scale * (dg[j] - m1 - hat[j] * m2)
            B.acc[0, :, lanes[j]] += fold8(dy)
            B.acc[1, :, lanes[j]] += fold8(dns[j] * hat[j])
            B.acc[2, :, lanes[j]] += fold8(dns[j])
            for c in range(chunk // OWN):
                B.big[pl.ds(xrow(j, m) + (3 + c0 + c) * SUB + 3, OWN), :] = dy[OWN * c : OWN * (c + 1), :]
        return 0

    lax.fori_loop(0, NPOS // chunk, body, 0)


def ph_wgrad_down(e, B):
    for k in range(4):
        w = lax.dot_general(
            B.u[:, C * k : C * (k + 1)], B.dz[...], (((0,), (0,)), ((), ())), preferred_element_type=F32
        )
        w = w.reshape(24, 16, C)
        a, b = w[:, 0:8], w[:, 8:16]
        units = [v[:, :, LANES * j : LANES * (j + 1)] for v in (a, b) for j in range(J)]
        tiles = [jnp.concatenate(units[2 * t : 2 * t + 2], axis=1).astype(BF16) for t in range(3)]
        for q in range(24):
            piece, inner = divmod(12 * k + q // 2, 3)
            for t in range(3):
                B.gb[0, piece // 4, piece // 2 % 2, piece % 2, inner, 3 * (q % 2) + t] = tiles[t][q]


def ph_wgrad_up(e, B):
    width = 256
    for k in range(HID // width):
        w = lax.dot_general(
            B.n[...], B.gp[:, width * k : width * (k + 1)], (((0,), (0,)), ((), ())), preferred_element_type=F32
        )
        w = w.reshape(48, 8, width)
        w = jnp.concatenate([w[:, :, :LANES], w[:, :, LANES:]], axis=1).astype(BF16)
        B.gb[1, :, :, :, :, k] = w.reshape(4, 2, 2, 3, 16, LANES)


def dy_copy(e, B, m, up):
    if up:
        return remote(e, B.hs.at[m, 1], B.hr.at[m, 0], B.s_dy.at[1, m], B.r_dy.at[1, m], r=e.r + GROUP)
    return remote(e, B.hs.at[m, 0], B.hr.at[m, 1], B.s_dy.at[0, m], B.r_dy.at[0, m], r=e.r - GROUP)


def dy_send(e, B, m):
    zero = jnp.zeros((3 * SUB, LANES), F32)
    for j in range(J):
        B.big[pl.ds(xrow(j, m), 3 * SUB), :] = zero
        B.big[pl.ds(xrow(j, m) + (COLS + 3) * SUB, 3 * SUB), :] = zero
        for side in range(2):
            for k in range(3):
                row = 3 + k if side == 0 else 8 + k
                v = B.big[pl.ds(xrow(j, m) + 3 * SUB + row, COLS, stride=SUB), :]
                B.hs[m, side, k, :, LANES * j : LANES * (j + 1)] = v.astype(BF16)

    @pl.when(e.g > 0)
    def _():
        dy_copy(e, B, m, False).start()

    @pl.when(e.g < e.G - 1)
    def _():
        dy_copy(e, B, m, True).start()


def ph_dy_edges(e, B):
    zero = jnp.zeros((MICRO, 3, COLS, C), BF16)

    @pl.when(e.g == 0)
    def _():
        B.hr[:, 0] = zero

    @pl.when(e.g == e.G - 1)
    def _():
        B.hr[:, 1] = zero


def dy_take(e, B, m):
    @pl.when(e.g < e.G - 1)
    def _():
        dy_copy(e, B, m, False).wait_recv()

    @pl.when(e.g > 0)
    def _():
        dy_copy(e, B, m, True).wait_recv()

    for j in range(J):
        for side in range(2):
            for k in range(3):
                row = k if side == 0 else 11 + k
                v = B.hr[m, side, k, :, LANES * j : LANES * (j + 1)].astype(F32)
                B.big[pl.ds(xrow(j, m) + 3 * SUB + row, COLS, stride=SUB), :] = v


def ph_dy_done(e, B):
    for m in range(MICRO):

        @pl.when(e.g > 0)
        def _(m=m):
            dy_copy(e, B, m, False).wait_send()

        @pl.when(e.g < e.G - 1)
        def _(m=m):
            dy_copy(e, B, m, True).wait_send()


def ph_conv_kernel(e, B, steps):
    halves = COLS // TILE

    def taps(it, _):
        hooks(it, steps)
        j = it // 7
        a = it % 7

        def body(k, dk):
            m = k // halves
            c0 = k % halves * TILE
            dk = list(dk)
            at = j * NPOS + m * POS + c0 * OWN
            xs = [B.xc[pl.ds(pl.multiple_of(at + OWN * c, OWN), OWN), :] for c in range(TILE)]
            for c in range(TILE + 6):
                d = B.big[pl.ds(xrow(j, m) + (c0 + c) * SUB + a, OWN), :]
                for b in range(7):
                    if 0 <= c - b < TILE:
                        dk[b] = dk[b] + d * xs[c - b]
            return tuple(dk)

        zero = jnp.zeros((OWN, LANES), F32)
        dk = lax.fori_loop(0, MICRO * halves, body, (zero,) * 7)
        for b in range(7):
            tap = (6 - a) * 7 + 6 - b
            B.sg[pl.ds(tap * J + j, 1), :] = jnp.sum(dk[b], 0, keepdims=True)
        return 0

    lax.fori_loop(0, 7 * J, taps, 0)


def ph_conv_input(e, B, steps):
    halves = COLS // TILE

    def body(it, _):
        hooks(it, steps)
        m = it // (J * halves)
        j = it // halves % J
        c0 = it % halves * TILE
        at = j * NPOS + m * POS + c0 * OWN
        acc = [B.z[pl.ds(pl.multiple_of(at + OWN * c, OWN), OWN), :] for c in range(TILE)]
        acc = conv_tile(B, m, j, c0, TILE, acc, True)
        for c in range(TILE):
            B.dx[pl.ds(pl.multiple_of(at + OWN * c, OWN), OWN), :] = acc[c]
        return 0

    lax.fori_loop(0, MICRO * J * halves, body, 0)


def ph_small_fill(e, B):
    for k in range(HID // LANES):
        B.sg[SG_CUP + k : SG_CUP + k + 1, :] = jnp.sum(B.acup[:, LANES * k : LANES * (k + 1)], 0, keepdims=True)
    for v in range(7):
        for j in range(J):
            row = SG_VEC + v * J + j
            B.sg[row : row + 1, :] = jnp.sum(B.acc[v, :, LANES * j : LANES * (j + 1)], 0, keepdims=True)


def out_copy(e, B, m, d):
    j = lax.rem(e.i + d, GROUP)
    return remote(
        e,
        B.xg.at[m, pl.ds(3 + 2 * j, 2)],
        B.fo.at[m, e.i],
        B.s_out.at[m, d],
        B.r_out.at[m, d],
        r=e.g * GROUP + j,
    )


def own_out_copy(e, B, m):
    return pltpu.make_async_copy(B.xg.at[m, pl.ds(3 + 2 * e.i, 2)], B.fo.at[m, e.i], B.s_outown.at[m])


def out_send(e, B, m):
    for row in range(OWN):
        for j in range(J):
            v = B.dx[pl.ds(j * NPOS + m * POS + row, COLS, stride=OWN), :]
            B.xg[m, 3 + row, :, LANES * j : LANES * (j + 1)] = v.astype(BF16)
    own_out_copy(e, B, m).start()
    for d in (2, 1, 3):
        out_copy(e, B, m, d).start()


def ph_out_wait(e, B):
    for m in range(MICRO):
        own_out_copy(e, B, m).wait()
        for d in range(1, GROUP):
            out_copy(e, B, m, d).wait()


PIECE = C * HID // LANES // 16
START = (ROW_DOWN, ROW_UP)


def rs_first(e, B, f):
    c = e.i % 2
    return remote(e, B.gb.at[f, :, :, 1 - c], B.ra1.at[f], B.s_rs.at[f, 0], B.r_rs.at[f, 0], r=e.r + 1 - 2 * c)


def rs_second(e, B, f):
    to = e.g * GROUP + lax.rem(e.i + 2, GROUP)
    return remote(e, B.sa2.at[f], B.ra2.at[f], B.s_rs.at[f, 1], B.r_rs.at[f, 1], r=to)


def group_of(e, q):
    return q * (e.G // 4)


def rs_third(e, B, f, q):
    to = group_of(e, q)
    d = lax.rem(to - e.g + e.G, e.G)
    return remote(e, B.sc.at[f, q], B.rc.at[f, d], B.s_rc.at[f, q], B.r_rc.at[f, d], r=to * GROUP + e.i)


def rs_third_wait(e, B, f, d):
    return remote(e, B.sc.at[f, 0], B.rc.at[f, d], B.s_rc.at[f, 0], B.r_rc.at[f, d], r=lax.rem(e.r + GROUP, e.n))


def rs_fourth(e, B, f, d):
    return remote(e, B.rb.at[f, 0], B.rb.at[f, d], B.s_rb.at[f, d], B.r_rb.at[f, d], b=lax.rem(e.b + d, e.nb))


def ends_here(e, body):
    if e.G == 4:
        body()
    else:
        pl.when(e.g % (e.G // 4) == 0)(body)


def rs_step1(e, B, f):
    rs_first(e, B, f).start()


def rs_step2(e, B, f):
    x, c = e.i // 2, e.i % 2
    rs_first(e, B, f).wait_recv()
    for q in range(4):
        B.sa2[f, q] = (B.gb[f, q, 1 - x, c].astype(F32) + B.ra1[f, q, 1 - x].astype(F32)).astype(BF16)
    rs_second(e, B, f).start()
    for q in range(4):
        B.h1[f, q] = B.gb[f, q, x, c].astype(F32) + B.ra1[f, q, x].astype(F32)


def rs_step3(e, B, f):
    rs_second(e, B, f).wait_recv()
    for q in range(4):
        B.h1[f, q] = B.h1[f, q] + B.ra2[f, q].astype(F32)
        B.sc[f, q] = B.h1[f, q].astype(BF16)
    for q in range(4):

        @pl.when(e.g != group_of(e, q))
        def _(q=q):
            rs_third(e, B, f, q).start()


def rs_step4(e, B, f):
    def body():
        total = B.h1[f, e.g // (e.G // 4)]
        for d in range(1, e.G):
            rs_third_wait(e, B, f, d).wait_recv()
            total = total + B.rc[f, d].astype(F32)
        B.rb[f, 0] = total.astype(BF16)
        for d in range(1, e.nb):
            rs_fourth(e, B, f, d).start()

    ends_here(e, body)


def piece_owners(e, f):
    start = START[f] + PIECE * (e.g // (e.G // 4) * 4 + e.i)
    return start // e.slab, (start + PIECE - 1) // e.slab


def own_copy(e, B, f, k, owner):
    slot = lax.rem(e.g // (e.G // 4) * 4 + e.i, 8)
    return remote(e, B.fp.at[f], B.ro.at[f, slot], B.s_ro.at[f, k], B.r_ro.at[f, slot], r=owner)


def own_wait(e, B, f, slot, home):
    remote(e, B.fp.at[f], B.ro.at[f, slot], B.s_ro.at[f, 0], B.r_ro.at[f, slot], r=home).wait_recv()


def rs_step5(e, B, f):
    def body():
        for d in range(1, e.nb):
            rs_fourth(e, B, f, d).wait_recv()
        for k in range(3):
            total = None
            for b in range(e.nb):
                part = B.rb[f, lax.rem(e.b - b + e.nb, e.nb), k].astype(F32)
                total = part if total is None else total + part
            for t in range(6):
                for h in range(2):
                    unit = 2 * t + h
                    tile = total[t, 8 * h : 8 * h + 8, :]
                    if f == 1:
                        B.ft[pl.ds(96 * k + unit, 8, stride=12), :] = tile
                    else:
                        B.ft[pl.ds(96 * k + 24 * (unit // 3) + unit % 3, 8, stride=3), :] = tile
        B.fp[f] = B.ft[...].astype(BF16)
        lo, hi = piece_owners(e, f)

        @pl.when(lo != e.r)
        def _():
            own_copy(e, B, f, 0, lo).start()

        @pl.when(jnp.logical_and(hi != lo, hi != e.r))
        def _():
            own_copy(e, B, f, 1, hi).start()

    ends_here(e, body)


def rs_place(e, B, f):
    for p in range(16):
        off = START[f] + PIECE * p - e.slab * e.r
        home = group_of(e, p // 4) * GROUP + p % 4
        overlap = jnp.logical_and(off < e.slab, off + PIECE > 0)

        @pl.when(jnp.logical_and(overlap, e.r != home))
        def _(p=p, off=off, home=home):
            slot = p % 8
            own_wait(e, B, f, slot, home)
            B.gf[pl.ds(MARGIN + off, PIECE), :] = B.ro[f, slot].astype(F32)

        @pl.when(jnp.logical_and(overlap, e.r == home))
        def _(off=off):
            B.gf[pl.ds(MARGIN + off, PIECE), :] = B.fp[f].astype(F32)


def ph_rs_done(e, B):
    for f in range(2):
        rs_first(e, B, f).wait_send()
        rs_second(e, B, f).wait_send()
        for q in range(4):

            @pl.when(e.g != group_of(e, q))
            def _(f=f, q=q):
                rs_third(e, B, f, q).wait_send()

        def body(f=f):
            for d in range(1, e.nb):
                rs_fourth(e, B, f, d).wait_send()
            lo, hi = piece_owners(e, f)

            @pl.when(lo != e.r)
            def _():
                own_copy(e, B, f, 0, lo).wait_send()

            @pl.when(jnp.logical_and(hi != lo, hi != e.r))
            def _():
                own_copy(e, B, f, 1, hi).wait_send()

        ends_here(e, body)


MARGIN = 1792


QUARTER = SG_ROWS // 4


def quarter_of(i):
    return i % 2 * 2 + i // 2


def small_core(e, B):
    c = e.i % 2
    at = pl.ds(pl.multiple_of((1 - c) * 2 * QUARTER, QUARTER), 2 * QUARTER)
    return remote(e, B.sg.at[at], B.sg_core, B.s_sg.at[0], B.r_sg.at[0], r=e.r + 1 - 2 * c)


def small_pair(e, B):
    x = e.i // 2
    at = pl.ds(pl.multiple_of((1 - x) * QUARTER, QUARTER), QUARTER)
    to = e.g * GROUP + lax.rem(e.i + 2, GROUP)
    return remote(e, B.sg_half.at[at], B.sg_pair, B.s_sg.at[1], B.r_sg.at[1], r=to)


def small_line(e, B, d):
    to = lax.rem(e.g + d, e.G)
    return remote(e, B.sg_line.at[0], B.sg_line.at[d], B.s_sgl.at[d], B.r_sgl.at[d], r=to * GROUP + e.i)


def small_batch(e, B, d):
    return remote(e, B.sgb.at[0], B.sgb.at[d], B.s_sgb.at[d], B.r_sgb.at[d], b=lax.rem(e.b + d, e.nb))


def small_back(e, B, d):
    q = quarter_of(e.i)
    to = e.g * GROUP + lax.rem(e.i + d, GROUP)
    return remote(e, B.sga.at[q], B.sga.at[q], B.s_sgg.at[d], B.r_sgg.at[d], r=to)


def small_step1(e, B):
    small_core(e, B).start()


def small_step2(e, B):
    c = e.i % 2
    small_core(e, B).wait_recv()
    B.sg_half[...] = B.sg[pl.ds(pl.multiple_of(c * 2 * QUARTER, QUARTER), 2 * QUARTER), :] + B.sg_core[...]
    small_pair(e, B).start()


def small_step3(e, B):
    x = e.i // 2
    small_pair(e, B).wait_recv()
    B.sg_line[0] = B.sg_half[pl.ds(pl.multiple_of(x * QUARTER, QUARTER), QUARTER), :] + B.sg_pair[...]
    for d in range(1, e.G):
        small_line(e, B, d).start()


def small_step4(e, B):
    for d in range(1, e.G):
        small_line(e, B, d).wait_recv()
    total = None
    for level in range(e.G):
        part = B.sg_line[lax.rem(e.g - level + e.G, e.G)]
        total = part if total is None else total + part
    B.sgb[0] = total
    for d in range(1, e.nb):
        small_batch(e, B, d).start()


def small_step5(e, B):
    for d in range(1, e.nb):
        small_batch(e, B, d).wait_recv()
    total = None
    for b in range(e.nb):
        part = B.sgb[lax.rem(e.b - b + e.nb, e.nb)]
        total = part if total is None else total + part
    B.sga[quarter_of(e.i)] = total
    for d in range(1, GROUP):
        small_back(e, B, d).start()


def ph_small_place(e, B):
    for d in range(1, GROUP):
        small_back(e, B, d).wait_recv()
    for k in range(4):
        B.sg2[QUARTER * k : QUARTER * (k + 1), :] = B.sga[k]
    for first, at, count in ((ROW_K, 0, 49 * J), (ROW_CUP, SG_CUP, HID // LANES), (ROW_VEC, SG_VEC, 7 * J)):
        off = MARGIN + first % e.slab

        @pl.when(e.r == first // e.slab)
        def _(off=off, at=at, count=count):
            B.gf[off : off + count, :] = B.sg2[at : at + count, :]


def ph_small_done(e, B):
    small_core(e, B).wait_send()
    small_pair(e, B).wait_send()
    for d in range(1, e.G):
        small_line(e, B, d).wait_send()
    for d in range(1, e.nb):
        small_batch(e, B, d).wait_send()
    for d in range(1, GROUP):
        small_back(e, B, d).wait_send()


def ph_head_grads(e, B):
    parts = GROUP * e.nb
    rows = 16 * parts
    sums = None
    for p in range(parts):
        x = B.pall[p].astype(F32)
        sums = x if sums is None else sums + x
        dd = x[6:9, 0:DOUT]
        B.gp[16 * p : 16 * p + 16, 0:DOUT] = jnp.concatenate([dd, dd, jnp.zeros((10, DOUT), F32)], axis=0).astype(BF16)
        dl = x[9:12, 0:CLSP]
        B.gp[rows + 16 * p : rows + 16 * p + 16, 0:CLSP] = jnp.concatenate(
            [jnp.zeros((6, CLSP), F32), dl, jnp.zeros((7, CLSP), F32)], axis=0
        ).astype(BF16)
    B.psum[...] = sums
    for q in range(4):
        for p in range(parts):
            B.v2[16 * p : 16 * p + 16, :] = B.pall[p, :, C * q : C * (q + 1)].astype(F32)
        for j in range(J):
            t = J * q + j
            B.u[LANES * t : LANES * (t + 1), 0:rows] = B.v2[0:rows, LANES * j : LANES * (j + 1)].T.astype(BF16)
    per = DOUT // LANES
    base = MARGIN - e.slab * e.r

    kc = 288
    low = e.slab * e.r - ROW_DS

    @pl.when(jnp.logical_and(low < 4 * C * per, low + e.slab > 0))
    def _():
        k0 = jnp.clip(low // (16 * per) * 16, 0, 4 * C - kc)
        k0 = pl.multiple_of(k0, 16)
        w = jnp.dot(B.u[pl.ds(k0, kc), 0:rows], B.gp[0:rows, 0:DOUT], preferred_element_type=F32)
        for j in range(per):
            B.gf[pl.ds(base + ROW_DS + per * k0 + j, kc, stride=per), :] = w[:, LANES * j : LANES * (j + 1)]

    low2 = e.slab * e.r - ROW_HEAD

    @pl.when(jnp.logical_and(low2 < DOUT * CLS // LANES, low2 + e.slab > 0))
    def _():
        g0 = jnp.clip(low2 // 125, 0, DOUT // 16 - 16)
        k0 = pl.multiple_of(DOUT + 16 * g0, 16)
        for t in range(8):
            B.big[256 * t : 256 * (t + 1), :] = jnp.dot(
                B.u[pl.ds(k0, 256), 0:rows],
                B.gp[rows : 2 * rows, LANES * t : LANES * (t + 1)],
                preferred_element_type=F32,
            )
        lane = lax.broadcasted_iota(jnp.int32, (16, LANES), 1)
        held = None
        for kk in range(16):
            o = (-CLS * kk) % LANES
            tiles = [B.big[pl.ds(256 * t + kk, 16, stride=16), :] for t in range(8)]
            if o:
                tiles = [pltpu.roll(tile, LANES - o, 1) for tile in tiles]
            for s in range(CLS * kk // LANES, (CLS * kk + CLS - 1) // LANES + 1):
                t0 = (LANES * s - CLS * kk) // LANES
                if o == 0:
                    value = tiles[t0]
                elif t0 < 0:
                    value = tiles[0]
                elif t0 + 1 > 7:
                    value = tiles[t0]
                else:
                    value = jnp.where(lane < LANES - o, tiles[t0], tiles[t0 + 1])
                border = CLS * kk - LANES * s
                if border > 0:
                    value = jnp.where(lane < border, held, value)
                if LANES * (s + 1) > CLS * (kk + 1):
                    held = value
                else:
                    B.gf[pl.ds(base + ROW_HEAD + 125 * g0 + s, 16, stride=125), :] = value

    @pl.when(e.r == ROW_OUT // e.slab)
    def _():
        off = MARGIN + ROW_OUT % e.slab
        for j in range(per):
            at = slice(LANES * j, LANES * (j + 1))
            B.gf[off + j : off + j + 1, :] = B.psum[6:7, at] * e.positions + (
                B.psum[7:8, at] * e.positions + B.psum[8:9, at] * e.positions
            )
            gain = B.psum[12:13, at] + B.psum[13:14, at] + B.psum[14:15, at]
            B.gf[off + per + j : off + per + j + 1, :] = gain
            at = slice(DOUT + LANES * j, DOUT + LANES * (j + 1))
            shift = B.psum[12:13, at] + B.psum[13:14, at] + B.psum[14:15, at]
            B.gf[off + 2 * per + j : off + 2 * per + j + 1, :] = shift

    @pl.when(e.r == ROW_BH // e.slab)
    def _():
        off = MARGIN + ROW_BH % e.slab
        for j in range(CLSP // LANES):
            at = slice(LANES * j, LANES * (j + 1))
            B.gf[off + j : off + j + 1, :] = B.psum[9:10, at] + B.psum[10:11, at] + B.psum[11:12, at]
        rest = FLAT - ROW_BH - CLSP // LANES
        B.gf[off + CLSP // LANES : off + CLSP // LANES + rest, :] = jnp.zeros((rest, LANES), F32)


def norm_copy(e, B, d):
    return remote(e, B.nrm.at[0], B.nrm.at[d], B.s_nrm.at[d], B.r_nrm.at[d], r=lax.rem(e.r + d, e.n))


def squares(v):
    return jnp.sum((v * v).reshape(-1, 8, LANES), 0)


def ph_norm_local(e, B):
    size = 64
    whole = e.slab // size

    def body(k, acc):
        return acc + squares(B.gf[pl.ds(pl.multiple_of(MARGIN + size * k, 8), size), :])

    part = lax.fori_loop(0, whole, body, jnp.zeros((8, LANES), F32))
    v = B.gf[MARGIN + whole * size : MARGIN + e.slab, :]
    B.nrm[0] = part + jnp.broadcast_to(jnp.sum(v * v, 0, keepdims=True) * 0.125, (8, LANES))


def ph_norm(e, B):
    def pieces():
        B.nrm[0] += squares(B.fp[0].astype(F32)) + squares(B.fp[1].astype(F32))

    ends_here(e, pieces)

    @pl.when(e.g == 0)
    def _():
        B.nrm[0] += squares(B.sga[quarter_of(e.i)])

    for d in range(1, e.n):
        norm_copy(e, B, d).start()


def ph_norm_wait(e, B):
    for d in range(1, e.n):
        norm_copy(e, B, d).wait_recv()
    total = None
    for k in range(e.n):
        part = B.nrm[lax.rem(e.r - k + e.n, e.n)]
        total = part if total is None else total + part
    square = jnp.sum(jnp.sum(total, 0, keepdims=True), 1, keepdims=True)
    B.o_norm[...] = jnp.broadcast_to(jnp.sqrt(square), (8, LANES))
    loss = B.psum[15:16, :]
    loss = loss[:, 0:LANES] + loss[:, LANES : 2 * LANES] + loss[:, 2 * LANES : 3 * LANES]
    B.o_loss[...] = jnp.broadcast_to(loss, (8, LANES))
    for d in range(1, e.n):
        norm_copy(e, B, d).wait_send()


def buffers(e):
    n, G, nb, slab = e.n, e.G, e.nb, e.slab
    tiles = (3, 6, 16, LANES)
    parts = GROUP * nb
    V = pltpu.VMEM
    D = pltpu.SemaphoreType.DMA
    return dict(
        gw=V((n, 2, e.half, LANES), BF16),
        stage=V((TAB_ROWS, LANES), F32),
        tab=V((TAB_ROWS, LANES), F32),
        big=V((10816, LANES), F32),
        dx=V((8 * DOUT, LANES), F32),
        wup=V((C, HID), BF16),
        wdn=V((HID, C), BF16),
        wds=V((4 * C, DOUT), BF16),
        wh=V((DOUT, CLSP), BF16),
        xg=V((MICRO, 14, COLS, C), BF16),
        xc=V((J * NPOS, LANES), F32),
        kb=V((49 * J, 8, LANES), F32),
        v1=V((NPOS, C), F32),
        rs1=V((NPOS, LANES), F32),
        v2=V((NPOS, C), F32),
        rs2=V((NPOS, LANES), F32),
        n=V((NPOS, C), BF16),
        u=V((NPOS, HID), BF16),
        gp=V((NPOS, HID), BF16),
        z=V((J * NPOS, LANES), F32),
        dz=V((NPOS, C), BF16),
        ps=V((MICRO, 2, OWN, C), F32),
        vs=V((MICRO, 2, OWN, C), F32),
        sl=V((32, C), F32),
        sr=V((G, 32, C), F32),
        dn2=V((32, C), F32),
        dnt=V((MICRO, 2, OWN, C), F32),
        pb=V((16, 4 * C), F32),
        pall=V((parts, 16, 4 * C), BF16),
        psum=V((16, 4 * C), F32),
        acc=V((7, 8, C), F32),
        acup=V((8, HID), F32),
        hs=V((MICRO, 2, 3, COLS, C), BF16),
        hr=V((MICRO, 2, 3, COLS, C), BF16),
        gb=V((2, 4, 2, 2) + tiles, BF16),
        ra1=V((2, 4, 2) + tiles, BF16),
        sa2=V((2, 4) + tiles, BF16),
        ra2=V((2, 4) + tiles, BF16),
        h1=V((2, 4) + tiles, F32),
        sc=V((2, 4) + tiles, BF16),
        rc=V((2, G) + tiles, BF16),
        rb=V((2, nb) + tiles, BF16),
        ft=V((PIECE, LANES), F32),
        fp=V((2, PIECE, LANES), BF16),
        ro=V((2, 8, PIECE, LANES), BF16),
        gf=V((MARGIN + slab + MARGIN, LANES), F32),
        sg=V((SG_ROWS, LANES), F32),
        sg2=V((SG_ROWS, LANES), F32),
        sg_core=V((2 * QUARTER, LANES), F32),
        sg_half=V((2 * QUARTER, LANES), F32),
        sg_pair=V((QUARTER, LANES), F32),
        sg_line=V((G, QUARTER, LANES), F32),
        sgb=V((nb, QUARTER, LANES), F32),
        sga=V((4, QUARTER, LANES), F32),
        nrm=V((n, 8, LANES), F32),
        s_own=D((1,)),
        s_feat=D((MICRO, GROUP)),
        r_feat=D((MICRO, GROUP)),
        s_halo=D((2, MICRO)),
        r_halo=D((2, MICRO)),
        s_tab=D((len(TABLES), G)),
        s_tabg=D((len(TABLES), GROUP)),
        r_tab=D((len(TABLES),)),
        s_line=D((G,)),
        r_line=D((G,)),
        s_pair=D((G,)),
        r_pair=D((G,)),
        s_row=D((2, G)),
        r_row=D((2, G)),
        s_core=D((4, G)),
        r_core=D((4, G)),
        s_patch=D((G,)),
        r_patch=D((G,)),
        s_pb=D((nb,)),
        r_pb=D((nb,)),
        s_pg=D((GROUP,)),
        r_pg=D((GROUP,)),
        s_dy=D((2, MICRO)),
        r_dy=D((2, MICRO)),
        s_out=D((MICRO, GROUP)),
        r_out=D((MICRO, GROUP)),
        s_outown=D((MICRO,)),
        s_rs=D((2, 2)),
        r_rs=D((2, 2)),
        s_rc=D((2, 4)),
        r_rc=D((2, G)),
        s_rb=D((2, nb)),
        r_rb=D((2, nb)),
        s_ro=D((2, 2)),
        r_ro=D((2, 8)),
        s_sg=D((2,)),
        r_sg=D((2,)),
        s_sgl=D((G,)),
        r_sgl=D((G,)),
        s_sgg=D((GROUP,)),
        r_sgg=D((GROUP,)),
        s_sgb=D((nb,)),
        r_sgb=D((nb,)),
        s_nrm=D((n,)),
        r_nrm=D((n,)),
    )


def ph_clear(e, B):
    B.sg[...] = jnp.zeros_like(B.sg)
    B.gf[...] = jnp.zeros_like(B.gf)


def ph_result(e, B):
    B.o_grad[...] = B.gf[MARGIN : MARGIN + e.slab, :]


def schedule(e, B):
    def do(step, *args):
        return lambda: step(e, B, *args)

    def level_of(row):
        return row // e.slab // GROUP

    up = range(0, level_of(ROW_CUP - 1) + 1)
    down = range(up.stop, level_of(ROW_VEC - 1) + 1)
    rest = range(down.stop, e.G)
    ph_barrier_signal(e, B)
    ph_cast(e, B)
    ph_feat_zero(e, B)
    ph_clear(e, B)
    ph_barrier_wait(e, B)
    ph_feat_start(e, B)
    ph_tables_start(e, B)
    line_send(e, B, up)
    halo_start(e, B, 0)
    tables_forward(e, B, (0, 2))
    tables_wait(e, B, (0, 2))
    ph_taps(e, B)
    ph_conv_fwd(
        e,
        B,
        {
            0: [do(halo_wait, 0), do(transpose, 0)],
            1: [do(halo_start, 1), do(line_send, down)],
            3: [do(line_step, up)],
            4: [do(halo_start, 2), do(tables_forward, (1, 3, 4))],
            6: [do(halo_wait, 1), do(transpose, 1)],
            8: [do(line_step, down)],
            9: [do(line_send, rest)],
            11: [do(row_step, up)],
            12: [do(halo_wait, 2), do(transpose, 2)],
            15: [do(row_step, down)],
            17: [do(core_step, up)],
        },
    )
    ph_norm_one(e, B)
    tables_wait(e, B, (1, 3, 4))
    gather_ready(e, B, up)
    ph_weights_up(e, B)
    ph_mlp_up(e, B, {0: [do(line_step, rest)], 1: [do(core_step, down)], 4: [do(row_step, rest)]})
    gather_ready(e, B, down)
    ph_weights_down(e, B)
    ph_mlp_down(e, B, {4: [do(core_step, rest)]})
    ph_patch_local(e, B)
    patch_start(e, B)
    gather_ready(e, B, rest)
    ph_weights_head(e, B)
    patch_wait(e, B)
    ph_head(e, B)
    ph_payload_batch(e, B)
    ph_dy_edges(e, B)
    ph_bwd_one(e, B)
    ph_wgrad_down(e, B)
    rs_step1(e, B, 0)
    ph_bwd_two(
        e,
        B,
        {
            1: [do(ph_payload_group)],
            2: [do(dy_send, 0), do(rs_step2, 0)],
            4: [do(dy_send, 1)],
        },
    )
    dy_send(e, B, 2)
    ph_wgrad_up(e, B)
    rs_step1(e, B, 1)
    for m in range(MICRO):
        dy_take(e, B, m)
    ph_conv_kernel(
        e,
        B,
        {
            1: [do(rs_step3, 0)],
            5: [do(rs_step2, 1)],
            14: [do(rs_step4, 0)],
            18: [do(rs_step3, 1)],
        },
    )
    ph_small_fill(e, B)
    small_step1(e, B)
    ph_feat_done(e, B)
    ph_conv_input(
        e,
        B,
        {
            1: [do(rs_step5, 0)],
            3: [do(small_step2)],
            6: [do(out_send, 0)],
            8: [do(small_step3)],
            10: [do(rs_step4, 1)],
            12: [do(out_send, 1), do(small_step4)],
            13: [do(ph_payload_wait), do(ph_head_grads), do(ph_norm_local)],
            15: [do(rs_step5, 1)],
            17: [do(small_step5)],
        },
    )
    ph_norm(e, B)
    out_send(e, B, 2)
    rs_place(e, B, 0)
    ph_small_place(e, B)
    rs_place(e, B, 1)
    ph_result(e, B)
    ph_tables_done(e, B)
    ph_gather_done(e, B)
    ph_dy_done(e, B)
    ph_rs_done(e, B)
    ph_small_done(e, B)
    ph_norm_wait(e, B)
    ph_out_wait(e, B)


def step_kernel(e, names, *refs):
    B = Env()
    for name, ref in zip(names, refs):
        setattr(B, name, ref)
    here(e)
    schedule(e, B)


def train_step(e, features, mask, labels, params):
    bufs = buffers(e)
    names = ["mask", "labels", "features", "params", "o_grad", "o_norm", "o_loss", "fo"] + list(bufs)
    return pl.pallas_call(
        functools.partial(step_kernel, e, names),
        out_shape=(
            jax.ShapeDtypeStruct((e.slab, LANES), F32),
            jax.ShapeDtypeStruct((8, LANES), F32),
            jax.ShapeDtypeStruct((8, LANES), F32),
            jax.ShapeDtypeStruct((MICRO, GROUP, 2, COLS, C), BF16),
        ),
        in_specs=[
            pl.BlockSpec(memory_space=pltpu.SMEM),
            pl.BlockSpec(memory_space=pltpu.SMEM),
            pl.BlockSpec(memory_space=pl.ANY),
            pl.BlockSpec(memory_space=pltpu.VMEM),
        ],
        out_specs=(
            pl.BlockSpec(memory_space=pltpu.VMEM),
            pl.BlockSpec(memory_space=pltpu.VMEM),
            pl.BlockSpec(memory_space=pltpu.VMEM),
            pl.BlockSpec(memory_space=pl.ANY),
        ),
        scratch_shapes=list(bufs.values()),
        compiler_params=pltpu.CompilerParams(collective_id=0, has_side_effects=True, vmem_limit_bytes=64 * MB - 65536),
        name="train_step",
    )(mask, labels, features, params)


def update_kernel(e, norm, loss, grad, params, m1, m2, out, o_norm, o_loss, new_params, first, second, feats, *scratch):
    g, p, a, b, fin, fout, s_in, s_out, s_feat, s_fout = scratch
    parts = 4
    size = e.slab // parts // 8 * 8
    spans = [(k * size, size if k < parts - 1 else e.slab - k * size) for k in range(parts)]
    copy = pltpu.make_async_copy
    ins = []
    for k, (at, count) in enumerate(spans):
        for q, (src, dst) in enumerate(((grad, g), (params, p), (m1, a), (m2, b))):
            ins.append(copy(src.at[pl.ds(at, count)], dst.at[pl.ds(at, count)], s_in.at[k, q]))
            ins[-1].start()
    fins = [copy(out.at[k], fin.at[k], s_feat.at[k]) for k in range(MICRO)]
    for cp in fins:
        cp.start()
    o_norm[0, 0] = jnp.max(norm[...])
    o_loss[0, 0] = jnp.max(loss[...])
    scale = jnp.minimum(1.0, CLIP / (norm[0:1, 0:1] + 1e-06))
    outs = []
    for k, (at, count) in enumerate(spans):
        for q in range(4):
            ins[4 * k + q].wait()
        rows = slice(at, at + count)
        clipped = g[rows, :] * scale
        one = BETA_ONE * a[rows, :] + (1.0 - BETA_ONE) * clipped
        two = BETA_TWO * b[rows, :] + (1.0 - BETA_TWO) * clipped * clipped
        a[rows, :] = one
        b[rows, :] = two
        ratio = one / (1.0 - BETA_ONE**STEP) / (jnp.sqrt(two / (1.0 - BETA_TWO**STEP)) + EPS_ADAM)
        p[rows, :] = p[rows, :] - RATE * (ratio + DECAY * p[rows, :])
        for q, (src, dst) in enumerate(((p, new_params), (a, first), (b, second))):
            outs.append(copy(src.at[pl.ds(at, count)], dst.at[pl.ds(at, count)], s_out.at[k, q]))
            outs[-1].start()
        if k < MICRO:
            fins[k].wait()
            fout[k] = fin[k].astype(F32)
            outs.append(copy(fout.at[k], feats.at[k], s_fout.at[k]))
            outs[-1].start()
    for cp in outs:
        cp.wait()


def update(e, grad, norm, loss, params, m1, m2, out):
    flat = jax.ShapeDtypeStruct((e.slab, LANES), F32)
    scalar = jax.ShapeDtypeStruct((1, 1), F32)
    shape = (MICRO, GROUP, 2, COLS, C)
    near, far, one = (pl.BlockSpec(memory_space=k) for k in (pltpu.VMEM, pl.ANY, pltpu.SMEM))
    D = pltpu.SemaphoreType.DMA
    return pl.pallas_call(
        functools.partial(update_kernel, e),
        in_specs=[near, near, far, far, far, far, far],
        out_specs=(one, one, far, far, far, far),
        out_shape=(scalar, scalar, flat, flat, flat, jax.ShapeDtypeStruct(shape, F32)),
        scratch_shapes=[pltpu.VMEM((e.slab, LANES), F32)] * 4
        + [pltpu.VMEM(shape, BF16), pltpu.VMEM(shape, F32), D((4, 4)), D((4, 3)), D((MICRO,)), D((MICRO,))],
        compiler_params=pltpu.CompilerParams(vmem_limit_bytes=64 * MB - 65536),
        name="update",
    )(norm, loss, grad, params, m1, m2, out)


def local(e, features, drop_mask, labels, params, moment1, moment2):
    flat = [v.reshape(e.slab, LANES) for v in (params, moment1, moment2)]
    grad, norm, loss, out = train_step(e, features, drop_mask, labels, flat[0])
    norm, loss, new_params, first, second, feats = update(e, grad, norm, loss, *flat, out)
    size = e.slab * LANES
    return (
        new_params.reshape(size),
        first.reshape(size),
        second.reshape(size),
        loss.reshape(()),
        norm.reshape(()),
        feats,
    )


def solution(mesh):
    e = Env()
    e.n = mesh.shape["rows"]
    e.nb = mesh.shape["batch"]
    e.G = e.n // GROUP
    e.slab = FLAT // e.n
    e.half = (e.slab + 31) // 32 * 16
    e.positions = float(e.n * COLS // 2)
    e.inv_count = 1.0 / (MICRO * GROUP * e.nb)
    return jax.shard_map(
        functools.partial(local, e),
        mesh=mesh,
        in_specs=(
            P(None, "batch", "rows", None, None),
            P(None, "batch"),
            P(None, "batch"),
            P("rows"),
            P("rows"),
            P("rows"),
        ),
        out_specs=(P("rows"), P("rows"), P("rows"), P(), P(), P(None, "batch", "rows", None, None)),
        check_vma=False,
    )
```

```python
import functools

import jax
import jax.numpy as jnp
from jax import lax
from jax.experimental import pallas as pl
from jax.experimental.pallas import tpu as pltpu
from jax.sharding import PartitionSpec as P

C = 384
HID = 1536
DOUT = 768
CLS = 1000
MICRO = 3
STEP = 10
P_SIZE = 3153920
KEEP = 0.8
CLIP = 0.01
RATE = 0.05
BETA_ONE = 0.9
BETA_TWO = 0.999
DECAY = 0.05
EPS_ADAM = 1e-08
EPS_NORM = 1e-06

MESH = pl.DeviceIdType.MESH
F32 = jnp.float32
BF16 = jnp.bfloat16
MB = 1 << 20

LANES = 128
J = C // LANES
GROUP = 4
OWN = 8
COLS = 64
PADC = COLS + 6
SUB = 16
POS = COLS * OWN
NPOS = MICRO * POS
FLAT = P_SIZE // LANES
ROW_K = 0
ROW_UP = 49 * J
ROW_CUP = ROW_UP + C * HID // LANES
ROW_DOWN = ROW_CUP + HID // LANES
ROW_VEC = ROW_DOWN + C * HID // LANES
ROW_DS = ROW_VEC + 7 * J
ROW_OUT = ROW_DS + 4 * C * DOUT // LANES
ROW_HEAD = ROW_OUT + 3 * DOUT // LANES
ROW_BH = ROW_HEAD + DOUT * CLS // LANES
TABLES = (
    (ROW_K, 49 * J, 0),
    (ROW_CUP, HID // LANES, 152),
    (ROW_VEC, 7 * J, 168),
    (ROW_OUT, 3 * DOUT // LANES, 192),
    (ROW_BH, FLAT - ROW_BH, 216),
)
TAB_ROWS = 232
TAB_SPAN = (152, 16, 24, 24, 16)
T_CUP, T_VEC, T_OUT, T_BH = 152, 168, 192, 216
SG_ROWS = 256
SG_CUP, SG_VEC = 152, 168
CLSP = 1024


class Env:
    pass


def xrow(j, m):
    return (j * MICRO + m) * PADC * SUB


def rows_of(refs, row, count):
    return refs[row : row + count, :]


def lane_row(ref, row, count):
    return jnp.concatenate([ref[row + k : row + k + 1, :] for k in range(count)], axis=1)


def ln_parts(blocks, width):
    total = blocks[0]
    for block in blocks[1:]:
        total = total + block
    mean = jnp.sum(total, -1, keepdims=True) * (1.0 / width)
    centred = [block - mean for block in blocks]
    square = centred[0] * centred[0]
    for block in centred[1:]:
        square = square + block * block
    spread = jnp.sum(square, -1, keepdims=True) * (1.0 / width)
    scale = lax.rsqrt(spread + EPS_NORM)
    return [block * scale for block in centred], scale


def here(e):
    e.r = lax.axis_index("rows")
    e.b = lax.axis_index("batch")
    e.g = e.r // GROUP
    e.i = e.r % GROUP
    e.h = e.b % 2


def dev(e, r=None, b=None):
    return {"rows": e.r if r is None else r, "batch": e.b if b is None else b}


def remote(e, src, dst, send, recv, r=None, b=None):
    return pltpu.make_async_remote_copy(
        src, dst, send, recv, device_id=(e.r if r is None else r, e.b if b is None else b), device_id_type=MESH
    )


def ph_barrier_signal(e, B):
    barrier = pltpu.get_barrier_semaphore()
    for d in range(1, e.n):
        pl.semaphore_signal(barrier, inc=1, device_id=(lax.rem(e.r + d, e.n), e.b), device_id_type=MESH)
    for d in range(1, e.nb):
        pl.semaphore_signal(barrier, inc=1, device_id=(e.r, lax.rem(e.b + d, e.nb)), device_id_type=MESH)


def ph_barrier_wait(e, B):
    pl.semaphore_wait(pltpu.get_barrier_semaphore(), e.n - 1 + e.nb - 1)


def feat_copy(e, B, m, d):
    j = lax.rem(e.i + d, GROUP)
    return remote(
        e,
        B.features.at[m, j],
        B.xg.at[m, pl.ds(3 + 2 * e.i, 2)],
        B.s_feat.at[m, d],
        B.r_feat.at[m, d],
        r=e.g * GROUP + j,
    )


def feat_own(e, B):
    return pltpu.make_async_copy(B.features.at[:, e.i], B.xg.at[:, pl.ds(3 + 2 * e.i, 2)], B.s_own.at[0])


def feat_start(e, B, m):
    if m == 0:
        feat_own(e, B).start()
    for d in (2, 3, 1):
        feat_copy(e, B, m, d).start()


def ph_feat_zero(e, B):
    zero = jnp.zeros((MICRO, 3, COLS, C), BF16)

    @pl.when(e.g == 0)
    def _():
        B.xg[:, 0:3] = zero

    @pl.when(e.g == e.G - 1)
    def _():
        B.xg[:, 11:14] = zero


def halo_copy(e, B, m, up):
    if up:
        return remote(e, B.xg.at[m, 8:11], B.xg.at[m, 0:3], B.s_halo.at[1, m], B.r_halo.at[1, m], r=e.r + GROUP)
    return remote(e, B.xg.at[m, 3:6], B.xg.at[m, 11:14], B.s_halo.at[0, m], B.r_halo.at[0, m], r=e.r - GROUP)


def halo_start(e, B, m):
    if m == 0:
        feat_own(e, B).wait()
    for d in range(1, GROUP):
        feat_copy(e, B, m, d).wait_recv()

    @pl.when(e.g > 0)
    def _():
        halo_copy(e, B, m, False).start()

    @pl.when(e.g < e.G - 1)
    def _():
        halo_copy(e, B, m, True).start()


def halo_wait(e, B, m):
    @pl.when(e.g < e.G - 1)
    def _():
        halo_copy(e, B, m, False).wait_recv()

    @pl.when(e.g > 0)
    def _():
        halo_copy(e, B, m, True).wait_recv()


def ph_feat_done(e, B):
    for m in range(MICRO):
        for d in range(1, GROUP):
            feat_copy(e, B, m, d).wait_send()

        @pl.when(e.g > 0)
        def _(m=m):
            halo_copy(e, B, m, False).wait_send()

        @pl.when(e.g < e.G - 1)
        def _(m=m):
            halo_copy(e, B, m, True).wait_send()


def ph_cast(e, B):
    for h in range(2):
        count = e.half if h == 0 else e.slab - e.half
        whole = count // 16 * 16
        B.gw[e.r, h, 0:whole, :] = B.params[h * e.half : h * e.half + whole, :].astype(BF16)
        rest = count - whole
        if whole < e.half:
            parts = [jnp.zeros((e.half - whole - rest, LANES), F32)]
            if rest:
                parts = [B.params[e.slab - rest : e.slab, :]] + parts
            B.gw[e.r, h, whole : e.half, :] = jnp.concatenate(parts, axis=0).astype(BF16)
    for k, (first, count, place) in enumerate(TABLES):
        off = first % e.slab
        B.stage[place : place + count, :] = B.params[off : off + count, :]


def table_line(e, B, k, d):
    first, count, place = TABLES[k]
    owner = first // e.slab
    part = pl.ds(place, TAB_SPAN[k])
    return remote(e, B.stage.at[part], B.tab.at[part], B.s_tab.at[k, d], B.r_tab.at[k], r=lax.rem(owner + GROUP * d, e.n))


def table_group(e, B, k, d):
    first, count, place = TABLES[k]
    part = pl.ds(place, TAB_SPAN[k])
    to = e.g * GROUP + lax.rem(e.i + d, GROUP)
    return remote(e, B.tab.at[part], B.tab.at[part], B.s_tabg.at[k, d], B.r_tab.at[k], r=to)


def ph_tables_start(e, B):
    for k, (first, count, place) in enumerate(TABLES):
        owner = first // e.slab

        @pl.when(e.r == owner)
        def _(k=k, place=place):
            for d in range(1, e.G):
                table_line(e, B, k, d).start()
            B.tab[place : place + TAB_SPAN[k], :] = B.stage[place : place + TAB_SPAN[k], :]
            for d in range(1, GROUP):
                table_group(e, B, k, d).start()


def tables_forward(e, B, some):
    for k in some:
        owner = TABLES[k][0] // e.slab

        @pl.when(jnp.logical_and(e.i == owner % GROUP, e.r != owner))
        def _(k=k):
            table_line(e, B, k, 1).wait_recv()
            for d in range(1, GROUP):
                table_group(e, B, k, d).start()


def tables_wait(e, B, some):
    for k in some:
        owner = TABLES[k][0] // e.slab

        @pl.when(e.i != owner % GROUP)
        def _(k=k):
            table_group(e, B, k, 1).wait_recv()


def ph_tables_done(e, B):
    for k, (first, count, place) in enumerate(TABLES):
        owner = first // e.slab

        @pl.when(e.r == owner)
        def _(k=k):
            for d in range(1, e.G):
                table_line(e, B, k, d).wait_send()

        @pl.when(e.i == owner % GROUP)
        def _(k=k):
            for d in range(1, GROUP):
                table_group(e, B, k, d).wait_send()


CHUNKS = 4


def chunk_of(e, c):
    if c is None:
        return pl.ds(0, e.half)
    tiles = e.half // 16
    cuts = [(tiles * k + CHUNKS - 1) // CHUNKS * 16 for k in range(CHUNKS + 1)]
    return pl.ds(cuts[c], cuts[c + 1] - cuts[c])


def half_ref(e, B, slot, h, c):
    return B.gw.at[slot, h, chunk_of(e, c)]


def line_copy(e, B, level, up, c):
    ref = half_ref(e, B, level * GROUP + e.i, e.h, c)
    k = 0 if up else 1
    return remote(e, ref, ref, B.s_line.at[k, level], B.r_line.at[level, c or 0], r=e.r + GROUP if up else e.r - GROUP)


def pair_copy(e, B, level, c):
    ref = half_ref(e, B, level * GROUP + e.i, e.h, c)
    to = e.g * GROUP + lax.rem(e.i + 2, GROUP)
    return remote(e, ref, ref, B.s_pair.at[level], B.r_pair.at[level, c or 0], r=to)


def row_copy(e, B, level, other, c):
    i = lax.rem(e.i + 2, GROUP) if other else e.i
    ref = half_ref(e, B, level * GROUP + i, e.h, c)
    k = int(other)
    return remote(e, ref, ref, B.s_row.at[k, level], B.r_row.at[k, level, c or 0], b=e.b + 1 - 2 * e.h)


def core_copy(e, B, level, other, mine, c):
    i = lax.rem(e.i + 2, GROUP) if other else e.i
    ref = half_ref(e, B, level * GROUP + i, e.h if mine else 1 - e.h, c)
    k = 2 * int(other) + int(mine)
    sib = e.g * GROUP + e.i + 1 - 2 * (e.i % 2)
    return remote(e, ref, ref, B.s_core.at[k, level], B.r_core.at[k, level, c or 0], r=sib)


def line_out(e, B, level, c):
    @pl.when(jnp.logical_and(e.g >= level, e.g + 1 < e.G))
    def _():
        line_copy(e, B, level, True, c).start()

    @pl.when(jnp.logical_and(e.g <= level, e.g >= 1))
    def _():
        line_copy(e, B, level, False, c).start()


def at_hop(e, level, hop, body):
    if hop == 0:
        cond = e.g == level
    else:
        cond = jnp.logical_or(e.g == level + hop, e.g == level - hop)
    pl.when(cond)(body)


def line_send(e, B, levels, chunks):
    for level in levels:

        def body(level=level):
            for c in chunks:
                line_out(e, B, level, c)

        at_hop(e, level, 0, body)


def line_step(e, B, levels, hop, chunks):
    for level in levels:

        def body(level=level):
            for c in chunks:
                line_copy(e, B, level, True, c).wait_recv()
                line_out(e, B, level, c)
                row_copy(e, B, level, False, c).start()
                core_copy(e, B, level, False, True, c).start()

        at_hop(e, level, hop, body)


def pair_step(e, B, levels, hop, chunks):
    for level in levels:

        def body(level=level):
            for c in chunks:
                pair_copy(e, B, level, c).start()
                if hop == 0:
                    core_copy(e, B, level, False, True, c).start()
                    core_copy(e, B, level, False, False, c).start()

        at_hop(e, level, hop, body)


def row_step(e, B, levels, hop, chunks):
    for level in levels:

        def body(level=level):
            for c in chunks:
                pair_copy(e, B, level, c).wait_recv()
                row_copy(e, B, level, True, c).start()
                core_copy(e, B, level, True, True, c).start()

        at_hop(e, level, hop, body)


def core_step(e, B, levels, hop, chunks):
    for level in levels:

        def body(level=level):
            for c in chunks:
                if hop:
                    row_copy(e, B, level, False, c).wait_recv()
                    core_copy(e, B, level, False, False, c).start()
                row_copy(e, B, level, True, c).wait_recv()
                core_copy(e, B, level, True, False, c).start()

        at_hop(e, level, hop, body)


def gather_ready(e, B, levels):
    for level in levels:
        for other in (False, True):
            for mine in (False, True):
                for c in range(CHUNKS):
                    core_copy(e, B, level, other, mine, c).wait_recv()


def ph_gather_done(e, B):
    G = e.G
    for level in range(G):
        pair_copy(e, B, level, None).wait_send()
        row_copy(e, B, level, True, None).wait_send()

        @pl.when(e.g != level)
        def _(level=level):
            row_copy(e, B, level, False, None).wait_send()

        for other in (False, True):
            for mine in (False, True):
                core_copy(e, B, level, other, mine, None).wait_send()

        @pl.when(jnp.logical_and(e.g >= level, e.g + 1 < G))
        def _(level=level):
            line_copy(e, B, level, True, None).wait_send()

        @pl.when(jnp.logical_and(e.g <= level, e.g >= 1))
        def _(level=level):
            line_copy(e, B, level, False, None).wait_send()


def flatten(e, B, first, last):
    step = 112
    s0 = first // e.slab

    def slab(k, _):
        for h in range(2):
            count = e.half if h == 0 else e.slab - e.half
            whole = count // step
            left = (count - whole * step + 15) // 16 * 16
            base = e.slab * k + h * e.half

            def body(t, _, h=h, base=base):
                at = pl.multiple_of(t * step, 16)
                B.big[pl.ds(base + t * step, step), :] = B.gw[s0 + k, h, pl.ds(at, step), :].astype(F32)
                return 0

            lax.fori_loop(0, whole, body, 0)
            if left:
                last = B.gw[s0 + k, h, whole * step : whole * step + left, :]
                B.big[pl.ds(base + whole * step, left), :] = last.astype(F32)
        return 0

    lax.fori_loop(0, (last - 1) // e.slab - s0 + 1, slab, 0)
    return e.slab * s0


def ph_weights_up(e, B):
    base = flatten(e, B, ROW_UP, ROW_CUP)
    for j in range(HID // LANES):
        B.wup[:, LANES * j : LANES * (j + 1)] = B.big[pl.ds(ROW_UP - base + j, C, stride=HID // LANES), :].astype(BF16)


def ph_weights_down(e, B):
    base = flatten(e, B, ROW_DOWN, ROW_VEC)
    for j in range(J):
        B.wdn[:, LANES * j : LANES * (j + 1)] = B.big[pl.ds(ROW_DOWN - base + j, HID, stride=J), :].astype(BF16)


def ph_weights_head(e, B):
    base = flatten(e, B, ROW_DS, ROW_OUT)
    per = DOUT // LANES
    for j in range(per):
        B.wds[:, LANES * j : LANES * (j + 1)] = B.big[pl.ds(ROW_DS - base + j, 4 * C, stride=per), :].astype(BF16)
    base = flatten(e, B, ROW_HEAD, ROW_BH)
    lane = lax.broadcasted_iota(jnp.int32, (DOUT // 16, LANES), 1)
    for kk in range(16):
        first, off = divmod(CLS * kk, LANES)
        parts = [B.big[pl.ds(ROW_HEAD - base + first + t, DOUT // 16, stride=125), :] for t in range(9 if off else 8)]
        if off:
            parts = [pltpu.roll(part, LANES - off, 1) for part in parts]
        for t in range(8):
            tile = parts[t]
            if off:
                tile = jnp.where(lane < LANES - off, parts[t], parts[t + 1])
            if t == 7:
                tile = jnp.where(lane < CLS - 7 * LANES, tile, 0.0)
            B.dx[pl.ds(DOUT * t + kk, DOUT // 16, stride=16), :] = tile
    for t in range(8):
        B.wh[:, LANES * t : LANES * (t + 1)] = B.dx[DOUT * t : DOUT * (t + 1), :].astype(BF16)


def hooks(it, steps):
    if not steps:
        return
    bits = sum(1 << k for k in steps)

    @pl.when(lax.rem(lax.shift_right_logical(jnp.int32(bits), it), 2) == 1)
    def _():
        for k, some in steps.items():

            @pl.when(it == k)
            def _(some=some):
                for step in some:
                    step()


def transpose(e, B, m):
    pad = jnp.zeros((3 * SUB, LANES), F32)
    for j in range(J):
        B.big[pl.ds(xrow(j, m), 3 * SUB), :] = pad
        B.big[pl.ds(xrow(j, m) + (COLS + 3) * SUB, 3 * SUB), :] = pad
        for row in range(14):
            v = B.xg[m, row, :, LANES * j : LANES * (j + 1)].astype(F32)
            B.big[pl.ds(xrow(j, m) + 3 * SUB + row, COLS, stride=SUB), :] = v
            if 3 <= row < 11:
                B.xc[pl.ds(j * NPOS + m * POS + row - 3, COLS, stride=OWN), :] = v


def ph_taps(e, B):
    def body(t, _):
        B.kb[t] = jnp.broadcast_to(B.tab[pl.ds(t, 1), :], (8, LANES))
        return 0

    lax.fori_loop(0, 49 * J, body, 0)


def vec_row(B, v, j):
    row = T_VEC + v * J + j
    return B.tab[row : row + 1, :]


def conv_tile(B, m, j, c0, tile, acc, flip):
    for a in range(7):
        taps = [B.kb[((6 - a) * 7 + 6 - b if flip else a * 7 + b) * J + j] for b in range(7)]
        for c in range(tile + 6):
            d = B.big[pl.ds(xrow(j, m) + (c0 + c) * SUB + a, OWN), :]
            for b in range(7):
                if 0 <= c - b < tile:
                    acc[c - b] = acc[c - b] + d * taps[b]
    return acc


TILE = 32


def ph_conv_fwd(e, B, steps):
    halves = COLS // TILE

    def body(it, _):
        m = it // halves
        c0 = it % halves * TILE
        for j in range(J):
            hooks(it, {k // J: v for k, v in steps.items() if k % J == j})
            bias = jnp.broadcast_to(vec_row(B, 0, j), (OWN, LANES))
            acc = conv_tile(B, m, j, c0, TILE, [bias] * TILE, False)
            at = j * NPOS + m * POS + c0 * OWN
            for c in range(TILE):
                B.dx[pl.ds(pl.multiple_of(at + OWN * c, OWN), OWN), :] = acc[c]
        return 0

    lax.fori_loop(0, MICRO * halves, body, 0)


def ph_norm_one(e, B):
    size = 128

    def body(it, _):
        at = pl.multiple_of(it * size, size)
        hat, scale = ln_parts([B.dx[pl.ds(j * NPOS + at, size), :] for j in range(J)], C)
        B.rs1[pl.ds(at, size), :] = jnp.broadcast_to(scale, (size, LANES))
        for j in range(J):
            B.v1[pl.ds(at, size), LANES * j : LANES * (j + 1)] = hat[j]
            B.n[pl.ds(at, size), LANES * j : LANES * (j + 1)] = (
                hat[j] * vec_row(B, 1, j) + vec_row(B, 2, j)
            ).astype(BF16)
        return 0

    lax.fori_loop(0, NPOS // size, body, 0)


def ph_mlp_up(e, B, steps):
    chunk = 256
    width = 256
    c0 = 0.7978845608028654
    c1 = 0.044715 * c0

    def body(it, _):
        hooks(it, steps)
        at = pl.multiple_of(it * chunk, chunk)
        rows = B.n[pl.ds(at, chunk), :]
        for k in range(HID // width):
            lanes = slice(width * k, width * (k + 1))
            bias = lane_row(B.tab, T_CUP + k * width // LANES, width // LANES)
            h = jnp.dot(rows, B.wup[:, lanes], preferred_element_type=F32) + bias
            sq = h * h
            half = 0.5 * jnp.tanh(h * (c0 + c1 * sq)) + 0.5
            u = h * half
            B.u[pl.ds(at, chunk), lanes] = u.astype(BF16)
            slope = half + u * (1.0 - half) * (2.0 * c0 + 6.0 * c1 * sq)
            B.gp[pl.ds(at, chunk), lanes] = slope.astype(BF16)
        return 0

    lax.fori_loop(0, NPOS // chunk, body, 0)


def ph_mlp_down(e, B, steps):
    chunk = 256
    B.ps[...] = jnp.zeros_like(B.ps)

    def body(it, _):
        hooks(it, steps)
        at = pl.multiple_of(it * chunk, chunk)
        m = it // (POS // chunk)
        keep = B.mask[m, e.i].astype(F32) * (1.0 / KEEP)
        z = jnp.dot(B.u[pl.ds(at, chunk), :], B.wdn[...], preferred_element_type=F32)
        resid = []
        for j in range(J):
            zj = z[:, LANES * j : LANES * (j + 1)] + vec_row(B, 3, j)
            B.z[pl.ds(j * NPOS + at, chunk), :] = zj
            resid.append(B.xc[pl.ds(j * NPOS + at, chunk), :] + (vec_row(B, 4, j) * keep) * zj)
        hat, scale = ln_parts(resid, C)
        B.rs2[pl.ds(at, chunk), :] = jnp.broadcast_to(scale, (chunk, LANES))
        for j in range(J):
            B.v2[pl.ds(at, chunk), LANES * j : LANES * (j + 1)] = hat[j]
            low = (hat[j] * vec_row(B, 5, j) + vec_row(B, 6, j)).astype(BF16).astype(F32)
            low = jnp.sum(low.reshape(chunk // 16, 2, OWN, LANES), 0)
            B.ps[m, :, :, LANES * j : LANES * (j + 1)] += low
        return 0

    lax.fori_loop(0, NPOS // chunk, body, 0)


def ph_patch_local(e, B):
    even = lax.broadcasted_iota(jnp.int32, (OWN, C), 0) % 2 == 0
    pick = lax.broadcasted_iota(jnp.int32, (8, C), 0)
    for parity in range(2):
        for side in range(2):
            tile = jnp.zeros((8, C), F32)
            for m in range(MICRO):
                v = B.ps[m, side]
                part = jnp.sum(jnp.where(even if parity == 0 else jnp.logical_not(even), v, 0.0), 0, keepdims=True)
                tile = jnp.where(pick == m, part, tile)
            q = 2 * parity + side
            B.sl[8 * q : 8 * q + 8, :] = tile


def patch_copy(e, B, d):
    to = lax.rem(e.g + d, e.G)
    return remote(e, B.sl, B.sr.at[d], B.s_patch.at[d], B.r_patch.at[d], r=to * GROUP + e.i)


def patch_start(e, B):
    for d in range(1, e.G):
        patch_copy(e, B, d).start()
    B.sr[0] = B.sl[...]


def patch_wait(e, B):
    for d in range(1, e.G):
        patch_copy(e, B, d).wait_recv()
    for d in range(1, e.G):
        patch_copy(e, B, d).wait_send()


def split3(v):
    hi = v.astype(BF16).astype(F32)
    mid = (v - hi).astype(BF16).astype(F32)
    return hi, mid, v - hi - mid


def ph_head(e, B):
    total = None
    for level in range(e.G):
        part = B.sr[lax.rem(e.g - level + e.G, e.G)]
        total = part if total is None else total + part
    per = DOUT // LANES
    gain = lane_row(B.tab, T_OUT + per, per)
    shift = lane_row(B.tab, T_OUT + 2 * per, per)
    mean = total * (1.0 / e.positions)
    pooled = lane_row(B.tab, T_OUT, per)
    for q in range(4):
        parts = jnp.concatenate(split3(mean[8 * q : 8 * q + 8, :]), axis=0).astype(BF16)
        prod = jnp.dot(parts, B.wds[C * q : C * (q + 1), :], preferred_element_type=F32)
        pooled = pooled + (prod[0:8] + (prod[8:16] + prod[16:24]))
    rows = lax.broadcasted_iota(jnp.int32, (8, 1), 0)
    live = rows < MICRO
    (hat,), scale = ln_parts([pooled], DOUT)
    query = (hat * gain + shift).astype(BF16)
    lane = lax.broadcasted_iota(jnp.int32, (8, CLSP), 1)
    logits = jnp.dot(query, B.wh[...], preferred_element_type=F32) + lane_row(B.tab, T_BH, CLSP // LANES)
    logits = jnp.where(lane < CLS, logits, -1e30)
    top = jnp.max(logits, 1, keepdims=True)
    powers = jnp.exp(logits - top)
    expsum = jnp.sum(powers, 1, keepdims=True)
    label = jnp.zeros((8, 1), jnp.int32)
    for m in range(MICRO):
        label = jnp.where(rows == m, B.labels[m, e.i], label)
    onehot = (lane == label).astype(F32)
    own = jnp.sum(jnp.where(lane == label, logits, 0.0), 1, keepdims=True)
    loss = jnp.sum(jnp.where(live, top + jnp.log(expsum) - own, 0.0), 0, keepdims=True)
    grad = jnp.where(live, (powers / expsum - onehot) * e.inv_count, 0.0).astype(BF16)
    grad_query = lax.dot_general(grad, B.wh[...], (((1,), (1,)), ((), ())), preferred_element_type=F32)
    dn = grad_query * gain
    m1 = jnp.sum(dn, 1, keepdims=True) * (1.0 / DOUT)
    m2 = jnp.sum(dn * hat, 1, keepdims=True) * (1.0 / DOUT)
    grad_pool = scale * (dn - m1 - hat * m2)
    down = jnp.where(live, grad_pool * (1.0 / e.positions), 0.0).astype(BF16)
    for q in range(4):
        B.dn2[8 * q : 8 * q + 8, :] = lax.dot_general(
            down, B.wds[C * q : C * (q + 1), :], (((1,), (1,)), ((), ())), preferred_element_type=F32
        )
    low = grad.astype(F32)
    d32 = down.astype(F32)
    q32 = jnp.where(live, query.astype(F32), 0.0)
    zero3 = jnp.zeros((3, C), F32)
    g3 = jnp.sum(jnp.where(live, grad_query * hat, 0.0), 0, keepdims=True)
    s3 = jnp.sum(jnp.where(live, grad_query, 0.0), 0, keepdims=True)
    vec = jnp.concatenate([g3, s3], axis=1)
    vec_parts = split3(vec)
    loss_parts = split3(loss)
    for q in range(4):
        at = slice(C * q, C * (q + 1))
        s_hi, s_mid, _ = split3(total[8 * q : 8 * q + 8, :])
        B.pb[0:8, at] = jnp.zeros((8, C), F32)
        B.pb[8:16, at] = jnp.zeros((8, C), F32)
        B.pb[0:3, at] = s_hi[0:3]
        B.pb[3:6, at] = s_mid[0:3]
    B.pb[6:9, 0:DOUT] = d32[0:3]
    B.pb[6:9, DOUT : 2 * DOUT] = q32[0:3]
    B.pb[9:12, 0:CLSP] = low[0:3]
    for k in range(3):
        B.pb[12 + k : 13 + k, :] = vec_parts[k]
        B.pb[15:16, LANES * k : LANES * (k + 1)] = jnp.broadcast_to(loss_parts[k], (1, LANES))
    B.pall[e.i * e.nb + e.b] = B.pb[...].astype(BF16)
    even = lax.broadcasted_iota(jnp.int32, (OWN, C), 0) % 2 == 0
    for m in range(MICRO):
        for side in range(2):
            first = B.dn2[8 * side + m : 8 * side + m + 1, :]
            second = B.dn2[8 * (2 + side) + m : 8 * (2 + side) + m + 1, :]
            B.dnt[m, side] = jnp.where(even, first, second)


def batch_copy(e, B, d):
    slot = e.i * e.nb + e.b
    return remote(e, B.pall.at[slot], B.pall.at[slot], B.s_pb.at[d], B.r_pb.at[d], b=lax.rem(e.b + d, e.nb))


def group_copy(e, B, d):
    at = pl.ds(e.i * e.nb, e.nb)
    to = e.g * GROUP + lax.rem(e.i + d, GROUP)
    return remote(e, B.pall.at[at], B.pall.at[at], B.s_pg.at[d], B.r_pg.at[d], r=to)


def ph_payload_batch(e, B):
    for d in range(1, e.nb):
        batch_copy(e, B, d).start()


def ph_payload_group(e, B):
    for d in range(1, e.nb):
        batch_copy(e, B, d).wait_recv()
    for d in range(1, GROUP):
        group_copy(e, B, d).start()


def ph_payload_wait(e, B):
    for d in range(1, GROUP):
        group_copy(e, B, d).wait_recv()
    for d in range(1, e.nb):
        batch_copy(e, B, d).wait_send()
    for d in range(1, GROUP):
        group_copy(e, B, d).wait_send()


def lane_sum(blocks):
    total = blocks[0]
    for block in blocks[1:]:
        total = total + block
    return jnp.sum(total, -1, keepdims=True) * (1.0 / C)


def fold8(v):
    return jnp.sum(v.reshape(v.shape[0] // 8, 8, v.shape[1]), 0)


def ph_bwd_one(e, B):
    chunk = 256
    half = chunk // 16
    B.acc[...] = jnp.zeros_like(B.acc)
    B.acup[...] = jnp.zeros_like(B.acup)
    B.vs[...] = jnp.zeros_like(B.vs)

    def body(it, _):
        at = pl.multiple_of(it * chunk, chunk)
        m = it // (POS // chunk)
        keep = B.mask[m, e.i].astype(F32) * (1.0 / KEEP)
        span = pl.ds(at, chunk)
        lanes = [slice(LANES * j, LANES * (j + 1)) for j in range(J)]
        dg = [B.dnt[m, :, :, lanes[j]] * vec_row(B, 5, j) for j in range(J)]
        m1 = lane_sum(dg)
        hat = [B.v2[span, lanes[j]].reshape(half, 2, OWN, LANES) for j in range(J)]
        m2 = lane_sum([dg[j] * hat[j] for j in range(J)])
        scale = B.rs2[span, :].reshape(half, 2, OWN, LANES)
        for j in range(J):
            zspan = pl.ds(j * NPOS + at, chunk)
            dr = (scale * (dg[j] - m1 - hat[j] * m2)).reshape(chunk, LANES)
            B.vs[m, :, :, lanes[j]] += jnp.sum(hat[j], 0)
            dz = (dr * (vec_row(B, 4, j) * keep)).astype(BF16)
            B.dz[span, lanes[j]] = dz
            B.acc[3, :, lanes[j]] += fold8(dz.astype(F32))
            B.acc[4, :, lanes[j]] += fold8(dr * B.z[zspan, :]) * keep
            B.z[zspan, :] = dr
        return 0

    lax.fori_loop(0, NPOS // chunk, body, 0)
    for m in range(MICRO):
        B.acc[5] += B.dnt[m, 0] * B.vs[m, 0] + B.dnt[m, 1] * B.vs[m, 1]
        B.acc[6] += (B.dnt[m, 0] + B.dnt[m, 1]) * float(COLS // 2)


def ph_bwd_two(e, B, steps):
    chunk = 256
    width = 256

    def body(it, _):
        hooks(it, steps)
        at = pl.multiple_of(it * chunk, chunk)
        m = it // (POS // chunk)
        c0 = (it % (POS // chunk)) * (chunk // OWN)
        span = pl.ds(at, chunk)
        lanes = [slice(LANES * j, LANES * (j + 1)) for j in range(J)]
        dz = B.dz[span, :]
        for k in range(HID // width):
            hid = slice(width * k, width * (k + 1))
            du = lax.dot_general(dz, B.wdn[hid, :], (((1,), (1,)), ((), ())), preferred_element_type=F32)
            dh = (du * B.gp[span, hid].astype(F32)).astype(BF16)
            B.gp[span, hid] = dh
            B.acup[:, hid] += fold8(dh.astype(F32))
        dn = lax.dot_general(B.gp[span, :], B.wup[...], (((1,), (1,)), ((), ())), preferred_element_type=F32)
        dns = [dn[:, lanes[j]] for j in range(J)]
        dg = [dns[j] * vec_row(B, 1, j) for j in range(J)]
        hat = [B.v1[span, lanes[j]] for j in range(J)]
        m1 = lane_sum(dg)
        m2 = lane_sum([dg[j] * hat[j] for j in range(J)])
        scale = B.rs1[span, :]
        for j in range(J):
            dy = scale * (dg[j] - m1 - hat[j] * m2)
            B.acc[0, :, lanes[j]] += fold8(dy)
            B.acc[1, :, lanes[j]] += fold8(dns[j] * hat[j])
            B.acc[2, :, lanes[j]] += fold8(dns[j])
            for c in range(chunk // OWN):
                B.big[pl.ds(xrow(j, m) + (3 + c0 + c) * SUB + 3, OWN), :] = dy[OWN * c : OWN * (c + 1), :]
        return 0

    lax.fori_loop(0, NPOS // chunk, body, 0)


def ph_wgrad_down(e, B):
    for k in range(4):
        w = lax.dot_general(
            B.u[:, C * k : C * (k + 1)], B.dz[...], (((0,), (0,)), ((), ())), preferred_element_type=F32
        )
        w = w.reshape(24, 16, C)
        a, b = w[:, 0:8], w[:, 8:16]
        units = [v[:, :, LANES * j : LANES * (j + 1)] for v in (a, b) for j in range(J)]
        tiles = [jnp.concatenate(units[2 * t : 2 * t + 2], axis=1).astype(BF16) for t in range(3)]
        for q in range(24):
            piece, inner = divmod(12 * k + q // 2, 3)
            for t in range(3):
                B.gb[0, piece // 4, piece // 2 % 2, piece % 2, inner, 3 * (q % 2) + t] = tiles[t][q]


def ph_wgrad_up(e, B):
    width = 256
    for k in range(HID // width):
        w = lax.dot_general(
            B.n[...], B.gp[:, width * k : width * (k + 1)], (((0,), (0,)), ((), ())), preferred_element_type=F32
        )
        w = w.reshape(48, 8, width)
        w = jnp.concatenate([w[:, :, :LANES], w[:, :, LANES:]], axis=1).astype(BF16)
        B.gb[1, :, :, :, :, k] = w.reshape(4, 2, 2, 3, 16, LANES)


def dy_copy(e, B, m, up):
    if up:
        return remote(e, B.hs.at[m, 1], B.hr.at[m, 0], B.s_dy.at[1, m], B.r_dy.at[1, m], r=e.r + GROUP)
    return remote(e, B.hs.at[m, 0], B.hr.at[m, 1], B.s_dy.at[0, m], B.r_dy.at[0, m], r=e.r - GROUP)


def dy_send(e, B, m):
    zero = jnp.zeros((3 * SUB, LANES), F32)
    for j in range(J):
        B.big[pl.ds(xrow(j, m), 3 * SUB), :] = zero
        B.big[pl.ds(xrow(j, m) + (COLS + 3) * SUB, 3 * SUB), :] = zero
        for side in range(2):
            for k in range(3):
                row = 3 + k if side == 0 else 8 + k
                v = B.big[pl.ds(xrow(j, m) + 3 * SUB + row, COLS, stride=SUB), :]
                B.hs[m, side, k, :, LANES * j : LANES * (j + 1)] = v.astype(BF16)

    @pl.when(e.g > 0)
    def _():
        dy_copy(e, B, m, False).start()

    @pl.when(e.g < e.G - 1)
    def _():
        dy_copy(e, B, m, True).start()


def ph_dy_edges(e, B):
    zero = jnp.zeros((MICRO, 3, COLS, C), BF16)

    @pl.when(e.g == 0)
    def _():
        B.hr[:, 0] = zero

    @pl.when(e.g == e.G - 1)
    def _():
        B.hr[:, 1] = zero


def dy_take(e, B, m):
    @pl.when(e.g < e.G - 1)
    def _():
        dy_copy(e, B, m, False).wait_recv()

    @pl.when(e.g > 0)
    def _():
        dy_copy(e, B, m, True).wait_recv()

    for j in range(J):
        for side in range(2):
            for k in range(3):
                row = k if side == 0 else 11 + k
                v = B.hr[m, side, k, :, LANES * j : LANES * (j + 1)].astype(F32)
                B.big[pl.ds(xrow(j, m) + 3 * SUB + row, COLS, stride=SUB), :] = v


def ph_dy_done(e, B):
    for m in range(MICRO):

        @pl.when(e.g > 0)
        def _(m=m):
            dy_copy(e, B, m, False).wait_send()

        @pl.when(e.g < e.G - 1)
        def _(m=m):
            dy_copy(e, B, m, True).wait_send()


def ph_conv_kernel(e, B, steps):
    halves = COLS // TILE

    def taps(it, _):
        hooks(it, steps)
        j = it // 7
        a = it % 7

        def body(k, dk):
            m = k // halves
            c0 = k % halves * TILE
            dk = list(dk)
            at = j * NPOS + m * POS + c0 * OWN
            xs = [B.xc[pl.ds(pl.multiple_of(at + OWN * c, OWN), OWN), :] for c in range(TILE)]
            for c in range(TILE + 6):
                d = B.big[pl.ds(xrow(j, m) + (c0 + c) * SUB + a, OWN), :]
                for b in range(7):
                    if 0 <= c - b < TILE:
                        dk[b] = dk[b] + d * xs[c - b]
            return tuple(dk)

        zero = jnp.zeros((OWN, LANES), F32)
        dk = lax.fori_loop(0, MICRO * halves, body, (zero,) * 7)
        for b in range(7):
            tap = (6 - a) * 7 + 6 - b
            B.sg[pl.ds(tap * J + j, 1), :] = jnp.sum(dk[b], 0, keepdims=True)
        return 0

    lax.fori_loop(0, 7 * J, taps, 0)


def ph_conv_input(e, B, steps):
    halves = COLS // TILE

    def body(it, _):
        m = it // halves
        c0 = it % halves * TILE
        for j in range(J):
            hooks(it, {k // J: v for k, v in steps.items() if k % J == j})
            at = j * NPOS + m * POS + c0 * OWN
            acc = [B.z[pl.ds(pl.multiple_of(at + OWN * c, OWN), OWN), :] for c in range(TILE)]
            acc = conv_tile(B, m, j, c0, TILE, acc, True)
            for c in range(TILE):
                B.dx[pl.ds(pl.multiple_of(at + OWN * c, OWN), OWN), :] = acc[c]
        return 0

    lax.fori_loop(0, MICRO * halves, body, 0)


def ph_small_fill(e, B):
    for k in range(HID // LANES):
        B.sg[SG_CUP + k : SG_CUP + k + 1, :] = jnp.sum(B.acup[:, LANES * k : LANES * (k + 1)], 0, keepdims=True)
    for v in range(7):
        for j in range(J):
            row = SG_VEC + v * J + j
            B.sg[row : row + 1, :] = jnp.sum(B.acc[v, :, LANES * j : LANES * (j + 1)], 0, keepdims=True)


def out_copy(e, B, m, d):
    j = lax.rem(e.i + d, GROUP)
    return remote(
        e,
        B.xg.at[m, pl.ds(3 + 2 * j, 2)],
        B.fo.at[m, e.i],
        B.s_out.at[m, d],
        B.r_out.at[m, d],
        r=e.g * GROUP + j,
    )


def own_out_copy(e, B, m):
    return pltpu.make_async_copy(B.xg.at[m, pl.ds(3 + 2 * e.i, 2)], B.fo.at[m, e.i], B.s_outown.at[m])


def out_send(e, B, m):
    for row in range(OWN):
        for j in range(J):
            v = B.dx[pl.ds(j * NPOS + m * POS + row, COLS, stride=OWN), :]
            B.xg[m, 3 + row, :, LANES * j : LANES * (j + 1)] = v.astype(BF16)
    own_out_copy(e, B, m).start()
    for d in (2, 1, 3):
        out_copy(e, B, m, d).start()


def ph_out_wait(e, B):
    for m in range(MICRO):
        own_out_copy(e, B, m).wait()
        for d in range(1, GROUP):
            out_copy(e, B, m, d).wait()


PIECE = C * HID // LANES // 16
START = (ROW_DOWN, ROW_UP)


def rs_first(e, B, f):
    c = e.i % 2
    return remote(e, B.gb.at[f, :, :, 1 - c], B.ra1.at[f], B.s_rs.at[f, 0], B.r_rs.at[f, 0], r=e.r + 1 - 2 * c)


def rs_second(e, B, f):
    to = e.g * GROUP + lax.rem(e.i + 2, GROUP)
    return remote(e, B.sa2.at[f], B.ra2.at[f], B.s_rs.at[f, 1], B.r_rs.at[f, 1], r=to)


def group_of(e, q):
    return q * (e.G // 4)


def rs_third(e, B, f, q):
    to = group_of(e, q)
    d = lax.rem(to - e.g + e.G, e.G)
    return remote(e, B.sc.at[f, q], B.rc.at[f, d], B.s_rc.at[f, q], B.r_rc.at[f, d], r=to * GROUP + e.i)


def rs_third_wait(e, B, f, d):
    return remote(e, B.sc.at[f, 0], B.rc.at[f, d], B.s_rc.at[f, 0], B.r_rc.at[f, d], r=lax.rem(e.r + GROUP, e.n))


def rs_fourth(e, B, f, d):
    return remote(e, B.rb.at[f, 0], B.rb.at[f, d], B.s_rb.at[f, d], B.r_rb.at[f, d], b=lax.rem(e.b + d, e.nb))


def ends_here(e, body):
    if e.G == 4:
        body()
    else:
        pl.when(e.g % (e.G // 4) == 0)(body)


def rs_step1(e, B, f):
    rs_first(e, B, f).start()


def rs_step2(e, B, f):
    x, c = e.i // 2, e.i % 2
    rs_first(e, B, f).wait_recv()
    for q in range(4):
        B.sa2[f, q] = (B.gb[f, q, 1 - x, c].astype(F32) + B.ra1[f, q, 1 - x].astype(F32)).astype(BF16)
    rs_second(e, B, f).start()
    for q in range(4):
        B.h1[f, q] = B.gb[f, q, x, c].astype(F32) + B.ra1[f, q, x].astype(F32)


def rs_step3(e, B, f):
    rs_second(e, B, f).wait_recv()
    for q in range(4):
        B.h1[f, q] = B.h1[f, q] + B.ra2[f, q].astype(F32)
        B.sc[f, q] = B.h1[f, q].astype(BF16)
    for q in range(4):

        @pl.when(e.g != group_of(e, q))
        def _(q=q):
            rs_third(e, B, f, q).start()


def rs_step4(e, B, f):
    def body():
        total = B.h1[f, e.g // (e.G // 4)]
        for d in range(1, e.G):
            rs_third_wait(e, B, f, d).wait_recv()
            total = total + B.rc[f, d].astype(F32)
        B.rb[f, 0] = total.astype(BF16)
        for d in range(1, e.nb):
            rs_fourth(e, B, f, d).start()

    ends_here(e, body)


def piece_owners(e, f):
    start = START[f] + PIECE * (e.g // (e.G // 4) * 4 + e.i)
    return start // e.slab, (start + PIECE - 1) // e.slab


def own_copy(e, B, f, k, owner):
    slot = lax.rem(e.g // (e.G // 4) * 4 + e.i, 8)
    return remote(e, B.fp.at[f], B.ro.at[f, slot], B.s_ro.at[f, k], B.r_ro.at[f, slot], r=owner)


def own_wait(e, B, f, slot, home):
    remote(e, B.fp.at[f], B.ro.at[f, slot], B.s_ro.at[f, 0], B.r_ro.at[f, slot], r=home).wait_recv()


def rs_step5(e, B, f):
    def body():
        for d in range(1, e.nb):
            rs_fourth(e, B, f, d).wait_recv()
        for k in range(3):
            total = None
            for b in range(e.nb):
                part = B.rb[f, lax.rem(e.b - b + e.nb, e.nb), k].astype(F32)
                total = part if total is None else total + part
            for t in range(6):
                for h in range(2):
                    unit = 2 * t + h
                    tile = total[t, 8 * h : 8 * h + 8, :]
                    if f == 1:
                        B.ft[pl.ds(96 * k + unit, 8, stride=12), :] = tile
                    else:
                        B.ft[pl.ds(96 * k + 24 * (unit // 3) + unit % 3, 8, stride=3), :] = tile
        B.fp[f] = B.ft[...].astype(BF16)
        lo, hi = piece_owners(e, f)

        @pl.when(lo != e.r)
        def _():
            own_copy(e, B, f, 0, lo).start()

        @pl.when(jnp.logical_and(hi != lo, hi != e.r))
        def _():
            own_copy(e, B, f, 1, hi).start()

    ends_here(e, body)


def rs_place(e, B, f):
    for p in range(16):
        off = START[f] + PIECE * p - e.slab * e.r
        home = group_of(e, p // 4) * GROUP + p % 4
        overlap = jnp.logical_and(off < e.slab, off + PIECE > 0)

        @pl.when(jnp.logical_and(overlap, e.r != home))
        def _(p=p, off=off, home=home):
            slot = p % 8
            own_wait(e, B, f, slot, home)
            B.gf[pl.ds(MARGIN + off, PIECE), :] = B.ro[f, slot].astype(F32)

        @pl.when(jnp.logical_and(overlap, e.r == home))
        def _(off=off):
            B.gf[pl.ds(MARGIN + off, PIECE), :] = B.fp[f].astype(F32)


def ph_rs_done(e, B):
    for f in range(2):
        rs_first(e, B, f).wait_send()
        rs_second(e, B, f).wait_send()
        for q in range(4):

            @pl.when(e.g != group_of(e, q))
            def _(f=f, q=q):
                rs_third(e, B, f, q).wait_send()

        def body(f=f):
            for d in range(1, e.nb):
                rs_fourth(e, B, f, d).wait_send()
            lo, hi = piece_owners(e, f)

            @pl.when(lo != e.r)
            def _():
                own_copy(e, B, f, 0, lo).wait_send()

            @pl.when(jnp.logical_and(hi != lo, hi != e.r))
            def _():
                own_copy(e, B, f, 1, hi).wait_send()

        ends_here(e, body)


MARGIN = 1792


QUARTER = SG_ROWS // 4


def quarter_of(i):
    return i % 2 * 2 + i // 2


def small_core(e, B):
    c = e.i % 2
    at = pl.ds(pl.multiple_of((1 - c) * 2 * QUARTER, QUARTER), 2 * QUARTER)
    return remote(e, B.sg.at[at], B.sg_core, B.s_sg.at[0], B.r_sg.at[0], r=e.r + 1 - 2 * c)


def small_pair(e, B):
    x = e.i // 2
    at = pl.ds(pl.multiple_of((1 - x) * QUARTER, QUARTER), QUARTER)
    to = e.g * GROUP + lax.rem(e.i + 2, GROUP)
    return remote(e, B.sg_half.at[at], B.sg_pair, B.s_sg.at[1], B.r_sg.at[1], r=to)


def small_line(e, B, d):
    to = lax.rem(e.g + d, e.G)
    return remote(e, B.sg_line.at[0], B.sg_line.at[d], B.s_sgl.at[d], B.r_sgl.at[d], r=to * GROUP + e.i)


def small_batch(e, B, d):
    return remote(e, B.sgb.at[0], B.sgb.at[d], B.s_sgb.at[d], B.r_sgb.at[d], b=lax.rem(e.b + d, e.nb))


def small_back(e, B, d):
    q = quarter_of(e.i)
    to = e.g * GROUP + lax.rem(e.i + d, GROUP)
    return remote(e, B.sga.at[q], B.sga.at[q], B.s_sgg.at[d], B.r_sgg.at[d], r=to)


def small_step1(e, B):
    small_core(e, B).start()


def small_step2(e, B):
    c = e.i % 2
    small_core(e, B).wait_recv()
    B.sg_half[...] = B.sg[pl.ds(pl.multiple_of(c * 2 * QUARTER, QUARTER), 2 * QUARTER), :] + B.sg_core[...]
    small_pair(e, B).start()


def small_step3(e, B):
    x = e.i // 2
    small_pair(e, B).wait_recv()
    B.sg_line[0] = B.sg_half[pl.ds(pl.multiple_of(x * QUARTER, QUARTER), QUARTER), :] + B.sg_pair[...]
    for d in range(1, e.G):
        small_line(e, B, d).start()


def small_step4(e, B):
    for d in range(1, e.G):
        small_line(e, B, d).wait_recv()
    total = None
    for level in range(e.G):
        part = B.sg_line[lax.rem(e.g - level + e.G, e.G)]
        total = part if total is None else total + part
    B.sgb[0] = total
    for d in range(1, e.nb):
        small_batch(e, B, d).start()


def small_step5(e, B):
    for d in range(1, e.nb):
        small_batch(e, B, d).wait_recv()
    total = None
    for b in range(e.nb):
        part = B.sgb[lax.rem(e.b - b + e.nb, e.nb)]
        total = part if total is None else total + part
    B.sga[quarter_of(e.i)] = total
    for d in range(1, GROUP):
        small_back(e, B, d).start()


def ph_small_place(e, B):
    for d in range(1, GROUP):
        small_back(e, B, d).wait_recv()
    for k in range(4):
        B.sg2[QUARTER * k : QUARTER * (k + 1), :] = B.sga[k]
    for first, at, count in ((ROW_K, 0, 49 * J), (ROW_CUP, SG_CUP, HID // LANES), (ROW_VEC, SG_VEC, 7 * J)):
        off = MARGIN + first % e.slab

        @pl.when(e.r == first // e.slab)
        def _(off=off, at=at, count=count):
            B.gf[off : off + count, :] = B.sg2[at : at + count, :]


def ph_small_done(e, B):
    small_core(e, B).wait_send()
    small_pair(e, B).wait_send()
    for d in range(1, e.G):
        small_line(e, B, d).wait_send()
    for d in range(1, e.nb):
        small_batch(e, B, d).wait_send()
    for d in range(1, GROUP):
        small_back(e, B, d).wait_send()


def ph_head_grads(e, B):
    parts = GROUP * e.nb
    rows = 16 * parts
    sums = None
    for p in range(parts):
        x = B.pall[p].astype(F32)
        sums = x if sums is None else sums + x
        dd = x[6:9, 0:DOUT]
        B.gp[16 * p : 16 * p + 16, 0:DOUT] = jnp.concatenate([dd, dd, jnp.zeros((10, DOUT), F32)], axis=0).astype(BF16)
        dl = x[9:12, 0:CLSP]
        B.gp[rows + 16 * p : rows + 16 * p + 16, 0:CLSP] = jnp.concatenate(
            [jnp.zeros((6, CLSP), F32), dl, jnp.zeros((7, CLSP), F32)], axis=0
        ).astype(BF16)
    B.psum[...] = sums
    for q in range(4):
        for p in range(parts):
            B.v2[16 * p : 16 * p + 16, :] = B.pall[p, :, C * q : C * (q + 1)].astype(F32)
        for j in range(J):
            t = J * q + j
            B.u[LANES * t : LANES * (t + 1), 0:rows] = B.v2[0:rows, LANES * j : LANES * (j + 1)].T.astype(BF16)
    per = DOUT // LANES
    base = MARGIN - e.slab * e.r

    kc = 288
    low = e.slab * e.r - ROW_DS

    @pl.when(jnp.logical_and(low < 4 * C * per, low + e.slab > 0))
    def _():
        k0 = jnp.clip(low // (16 * per) * 16, 0, 4 * C - kc)
        k0 = pl.multiple_of(k0, 16)
        w = jnp.dot(B.u[pl.ds(k0, kc), 0:rows], B.gp[0:rows, 0:DOUT], preferred_element_type=F32)
        for j in range(per):
            B.gf[pl.ds(base + ROW_DS + per * k0 + j, kc, stride=per), :] = w[:, LANES * j : LANES * (j + 1)]

    low2 = e.slab * e.r - ROW_HEAD

    @pl.when(jnp.logical_and(low2 < DOUT * CLS // LANES, low2 + e.slab > 0))
    def _():
        g0 = jnp.clip(low2 // 125, 0, DOUT // 16 - 16)
        k0 = pl.multiple_of(DOUT + 16 * g0, 16)
        for t in range(8):
            B.big[256 * t : 256 * (t + 1), :] = jnp.dot(
                B.u[pl.ds(k0, 256), 0:rows],
                B.gp[rows : 2 * rows, LANES * t : LANES * (t + 1)],
                preferred_element_type=F32,
            )
        lane = lax.broadcasted_iota(jnp.int32, (16, LANES), 1)
        held = None
        for kk in range(16):
            o = (-CLS * kk) % LANES
            tiles = [B.big[pl.ds(256 * t + kk, 16, stride=16), :] for t in range(8)]
            if o:
                tiles = [pltpu.roll(tile, LANES - o, 1) for tile in tiles]
            for s in range(CLS * kk // LANES, (CLS * kk + CLS - 1) // LANES + 1):
                t0 = (LANES * s - CLS * kk) // LANES
                if o == 0:
                    value = tiles[t0]
                elif t0 < 0:
                    value = tiles[0]
                elif t0 + 1 > 7:
                    value = tiles[t0]
                else:
                    value = jnp.where(lane < LANES - o, tiles[t0], tiles[t0 + 1])
                border = CLS * kk - LANES * s
                if border > 0:
                    value = jnp.where(lane < border, held, value)
                if LANES * (s + 1) > CLS * (kk + 1):
                    held = value
                else:
                    B.gf[pl.ds(base + ROW_HEAD + 125 * g0 + s, 16, stride=125), :] = value

    @pl.when(e.r == ROW_OUT // e.slab)
    def _():
        off = MARGIN + ROW_OUT % e.slab
        for j in range(per):
            at = slice(LANES * j, LANES * (j + 1))
            B.gf[off + j : off + j + 1, :] = B.psum[6:7, at] * e.positions + (
                B.psum[7:8, at] * e.positions + B.psum[8:9, at] * e.positions
            )
            gain = B.psum[12:13, at] + B.psum[13:14, at] + B.psum[14:15, at]
            B.gf[off + per + j : off + per + j + 1, :] = gain
            at = slice(DOUT + LANES * j, DOUT + LANES * (j + 1))
            shift = B.psum[12:13, at] + B.psum[13:14, at] + B.psum[14:15, at]
            B.gf[off + 2 * per + j : off + 2 * per + j + 1, :] = shift

    @pl.when(e.r == ROW_BH // e.slab)
    def _():
        off = MARGIN + ROW_BH % e.slab
        for j in range(CLSP // LANES):
            at = slice(LANES * j, LANES * (j + 1))
            B.gf[off + j : off + j + 1, :] = B.psum[9:10, at] + B.psum[10:11, at] + B.psum[11:12, at]
        rest = FLAT - ROW_BH - CLSP // LANES
        B.gf[off + CLSP // LANES : off + CLSP // LANES + rest, :] = jnp.zeros((rest, LANES), F32)


def norm_copy(e, B, d):
    return remote(e, B.nrm.at[0], B.nrm.at[d], B.s_nrm.at[d], B.r_nrm.at[d], r=lax.rem(e.r + d, e.n))


def squares(v):
    return jnp.sum((v * v).reshape(-1, 8, LANES), 0)


def ph_norm_local(e, B):
    size = 64
    whole = e.slab // size

    def body(k, acc):
        return acc + squares(B.gf[pl.ds(pl.multiple_of(MARGIN + size * k, 8), size), :])

    part = lax.fori_loop(0, whole, body, jnp.zeros((8, LANES), F32))
    v = B.gf[MARGIN + whole * size : MARGIN + e.slab, :]
    B.nrm[0] = part + jnp.broadcast_to(jnp.sum(v * v, 0, keepdims=True) * 0.125, (8, LANES))


def ph_norm(e, B):
    def pieces():
        B.nrm[0] += squares(B.fp[0].astype(F32)) + squares(B.fp[1].astype(F32))

    ends_here(e, pieces)

    @pl.when(e.g == 0)
    def _():
        B.nrm[0] += squares(B.sga[quarter_of(e.i)])

    for d in range(1, e.n):
        norm_copy(e, B, d).start()


def ph_norm_wait(e, B):
    for d in range(1, e.n):
        norm_copy(e, B, d).wait_recv()
    total = None
    for k in range(e.n):
        part = B.nrm[lax.rem(e.r - k + e.n, e.n)]
        total = part if total is None else total + part
    square = jnp.sum(jnp.sum(total, 0, keepdims=True), 1, keepdims=True)
    B.o_norm[...] = jnp.broadcast_to(jnp.sqrt(square), (8, LANES))
    loss = B.psum[15:16, :]
    loss = loss[:, 0:LANES] + loss[:, LANES : 2 * LANES] + loss[:, 2 * LANES : 3 * LANES]
    B.o_loss[...] = jnp.broadcast_to(loss, (8, LANES))
    for d in range(1, e.n):
        norm_copy(e, B, d).wait_send()


def buffers(e):
    n, G, nb, slab = e.n, e.G, e.nb, e.slab
    tiles = (3, 6, 16, LANES)
    parts = GROUP * nb
    V = pltpu.VMEM
    D = pltpu.SemaphoreType.DMA
    return dict(
        gw=V((n, 2, e.half, LANES), BF16),
        stage=V((TAB_ROWS, LANES), F32),
        tab=V((TAB_ROWS, LANES), F32),
        big=V((10816, LANES), F32),
        dx=V((8 * DOUT, LANES), F32),
        wup=V((C, HID), BF16),
        wdn=V((HID, C), BF16),
        wds=V((4 * C, DOUT), BF16),
        wh=V((DOUT, CLSP), BF16),
        xg=V((MICRO, 14, COLS, C), BF16),
        xc=V((J * NPOS, LANES), F32),
        kb=V((49 * J, 8, LANES), F32),
        v1=V((NPOS, C), F32),
        rs1=V((NPOS, LANES), F32),
        v2=V((NPOS, C), F32),
        rs2=V((NPOS, LANES), F32),
        n=V((NPOS, C), BF16),
        u=V((NPOS, HID), BF16),
        gp=V((NPOS, HID), BF16),
        z=V((J * NPOS, LANES), F32),
        dz=V((NPOS, C), BF16),
        ps=V((MICRO, 2, OWN, C), F32),
        vs=V((MICRO, 2, OWN, C), F32),
        sl=V((32, C), F32),
        sr=V((G, 32, C), F32),
        dn2=V((32, C), F32),
        dnt=V((MICRO, 2, OWN, C), F32),
        pb=V((16, 4 * C), F32),
        pall=V((parts, 16, 4 * C), BF16),
        psum=V((16, 4 * C), F32),
        acc=V((7, 8, C), F32),
        acup=V((8, HID), F32),
        hs=V((MICRO, 2, 3, COLS, C), BF16),
        hr=V((MICRO, 2, 3, COLS, C), BF16),
        gb=V((2, 4, 2, 2) + tiles, BF16),
        ra1=V((2, 4, 2) + tiles, BF16),
        sa2=V((2, 4) + tiles, BF16),
        ra2=V((2, 4) + tiles, BF16),
        h1=V((2, 4) + tiles, F32),
        sc=V((2, 4) + tiles, BF16),
        rc=V((2, G) + tiles, BF16),
        rb=V((2, nb) + tiles, BF16),
        ft=V((PIECE, LANES), F32),
        fp=V((2, PIECE, LANES), BF16),
        ro=V((2, 8, PIECE, LANES), BF16),
        gf=V((MARGIN + slab + MARGIN, LANES), F32),
        sg=V((SG_ROWS, LANES), F32),
        sg2=V((SG_ROWS, LANES), F32),
        sg_core=V((2 * QUARTER, LANES), F32),
        sg_half=V((2 * QUARTER, LANES), F32),
        sg_pair=V((QUARTER, LANES), F32),
        sg_line=V((G, QUARTER, LANES), F32),
        sgb=V((nb, QUARTER, LANES), F32),
        sga=V((4, QUARTER, LANES), F32),
        nrm=V((n, 8, LANES), F32),
        s_own=D((1,)),
        s_feat=D((MICRO, GROUP)),
        r_feat=D((MICRO, GROUP)),
        s_halo=D((2, MICRO)),
        r_halo=D((2, MICRO)),
        s_tab=D((len(TABLES), G)),
        s_tabg=D((len(TABLES), GROUP)),
        r_tab=D((len(TABLES),)),
        s_line=D((2, G)),
        r_line=D((G, CHUNKS)),
        s_pair=D((G,)),
        r_pair=D((G, CHUNKS)),
        s_row=D((2, G)),
        r_row=D((2, G, CHUNKS)),
        s_core=D((4, G)),
        r_core=D((4, G, CHUNKS)),
        s_patch=D((G,)),
        r_patch=D((G,)),
        s_pb=D((nb,)),
        r_pb=D((nb,)),
        s_pg=D((GROUP,)),
        r_pg=D((GROUP,)),
        s_dy=D((2, MICRO)),
        r_dy=D((2, MICRO)),
        s_out=D((MICRO, GROUP)),
        r_out=D((MICRO, GROUP)),
        s_outown=D((MICRO,)),
        s_rs=D((2, 2)),
        r_rs=D((2, 2)),
        s_rc=D((2, 4)),
        r_rc=D((2, G)),
        s_rb=D((2, nb)),
        r_rb=D((2, nb)),
        s_ro=D((2, 2)),
        r_ro=D((2, 8)),
        s_sg=D((2,)),
        r_sg=D((2,)),
        s_sgl=D((G,)),
        r_sgl=D((G,)),
        s_sgg=D((GROUP,)),
        r_sgg=D((GROUP,)),
        s_sgb=D((nb,)),
        r_sgb=D((nb,)),
        s_nrm=D((n,)),
        r_nrm=D((n,)),
    )


def ph_clear(e, B):
    B.sg[...] = jnp.zeros_like(B.sg)
    B.gf[...] = jnp.zeros_like(B.gf)


def ph_result(e, B):
    B.o_grad[...] = B.gf[MARGIN : MARGIN + e.slab, :]


def schedule(e, B):
    def do(step, *args):
        return lambda: step(e, B, *args)

    def level_of(row):
        return row // e.slab // GROUP

    up = range(0, level_of(ROW_CUP - 1) + 1)
    down = range(up.stop, level_of(ROW_VEC - 1) + 1)
    rest = range(down.stop, e.G)
    ph_barrier_signal(e, B)
    ph_cast(e, B)
    ph_feat_zero(e, B)
    ph_clear(e, B)
    ph_barrier_wait(e, B)
    every = range(CHUNKS)
    one, two = range(0, CHUNKS // 2), range(CHUNKS // 2, CHUNKS)

    def hops(some):
        return range(max(max(level, e.G - 1 - level) for level in some) + 1)

    def steps(step, some, which, chunks):
        return [do(step, some, h, chunks) for h in which]

    ph_tables_start(e, B)
    feat_start(e, B, 0)
    line_send(e, B, up, every)
    tables_forward(e, B, (0, 2))
    feat_start(e, B, 1)
    line_step(e, B, up, 1, every)
    halo_start(e, B, 0)
    feat_start(e, B, 2)
    for h in hops(up)[2:]:
        line_step(e, B, up, h, every)
    for h in hops(up):
        pair_step(e, B, up, h, every)
    tables_wait(e, B, (0, 2))
    ph_taps(e, B)
    ph_conv_fwd(
        e,
        B,
        {
            0: [do(halo_wait, 0), do(transpose, 0)],
            1: [do(halo_start, 1), do(line_send, down, one)],
            2: [do(line_send, rest, one)],
            4: [do(halo_start, 2), do(line_send, down, two)] + steps(row_step, up, hops(up), one),
            5: [do(line_send, rest, two)],
            6: [do(halo_wait, 1), do(transpose, 1)],
            7: [do(tables_forward, (1, 3, 4))] + steps(row_step, up, hops(up), two),
            9: steps(line_step, down, [1], one),
            10: steps(core_step, up, hops(up), one) + steps(line_step, rest, [1], one),
            11: steps(line_step, down, [1], two),
            12: [do(halo_wait, 2), do(transpose, 2)] + steps(line_step, rest, [1], two),
            13: steps(core_step, up, hops(up), two) + steps(line_step, down, hops(down)[2:], one),
            14: steps(line_step, down, hops(down)[2:], two)
            + steps(pair_step, down, hops(down), every)
            + steps(pair_step, rest, hops(rest)[:2], every),
            15: steps(line_step, rest, hops(rest)[2:3], one),
            16: steps(line_step, rest, hops(rest)[2:3], two),
            17: steps(row_step, down, hops(down), one),
        },
    )
    ph_norm_one(e, B)
    tables_wait(e, B, (1, 3, 4))
    for h in hops(down):
        row_step(e, B, down, h, two)
    gather_ready(e, B, up)
    ph_weights_up(e, B)
    ph_mlp_up(
        e,
        B,
        {
            0: steps(core_step, down, hops(down), one)
            + steps(pair_step, rest, hops(rest)[2:3], every)
            + steps(line_step, rest, hops(rest)[3:], one),
            1: steps(core_step, down, hops(down), two)
            + steps(line_step, rest, hops(rest)[3:], two)
            + steps(pair_step, rest, hops(rest)[3:], every),
            2: steps(row_step, rest, hops(rest)[:2], one),
            3: steps(row_step, rest, hops(rest)[:2], two),
            4: steps(row_step, rest, hops(rest)[2:3], every),
            5: steps(core_step, rest, hops(rest)[:2], every),
        },
    )
    gather_ready(e, B, down)
    ph_weights_down(e, B)
    ph_mlp_down(
        e,
        B,
        {
            0: steps(row_step, rest, hops(rest)[3:], every),
            3: steps(core_step, rest, hops(rest)[2:3], every),
            5: steps(core_step, rest, hops(rest)[3:], every),
        },
    )
    ph_patch_local(e, B)
    patch_start(e, B)
    gather_ready(e, B, rest)
    ph_weights_head(e, B)
    patch_wait(e, B)
    ph_head(e, B)
    ph_payload_batch(e, B)
    ph_dy_edges(e, B)
    ph_bwd_one(e, B)
    ph_wgrad_down(e, B)
    rs_step1(e, B, 0)
    ph_bwd_two(
        e,
        B,
        {
            1: [do(ph_payload_group)],
            2: [do(dy_send, 0), do(rs_step2, 0)],
            4: [do(dy_send, 1)],
        },
    )
    dy_send(e, B, 2)
    ph_wgrad_up(e, B)
    rs_step1(e, B, 1)
    for m in range(MICRO):
        dy_take(e, B, m)
    ph_conv_kernel(
        e,
        B,
        {
            1: [do(rs_step3, 0)],
            5: [do(rs_step2, 1)],
            14: [do(rs_step4, 0)],
            18: [do(rs_step3, 1)],
        },
    )
    ph_small_fill(e, B)
    small_step1(e, B)
    ph_feat_done(e, B)
    ph_conv_input(
        e,
        B,
        {
            1: [do(rs_step5, 0)],
            3: [do(small_step2)],
            6: [do(out_send, 0)],
            8: [do(small_step3)],
            10: [do(rs_step4, 1)],
            12: [do(out_send, 1)],
            13: [do(ph_payload_wait), do(ph_head_grads), do(ph_norm_local)],
            14: [do(small_step4)],
            16: [do(rs_step5, 1)],
            17: [do(small_step5)],
        },
    )
    ph_norm(e, B)
    out_send(e, B, 2)
    rs_place(e, B, 0)
    ph_small_place(e, B)
    rs_place(e, B, 1)
    ph_result(e, B)
    ph_tables_done(e, B)
    ph_gather_done(e, B)
    ph_dy_done(e, B)
    ph_rs_done(e, B)
    ph_small_done(e, B)
    ph_norm_wait(e, B)
    ph_out_wait(e, B)


def step_kernel(e, names, *refs):
    B = Env()
    for name, ref in zip(names, refs):
        setattr(B, name, ref)
    here(e)
    schedule(e, B)


def train_step(e, features, mask, labels, params):
    bufs = buffers(e)
    names = ["mask", "labels", "features", "params", "o_grad", "o_norm", "o_loss", "fo"] + list(bufs)
    return pl.pallas_call(
        functools.partial(step_kernel, e, names),
        out_shape=(
            jax.ShapeDtypeStruct((e.slab, LANES), F32),
            jax.ShapeDtypeStruct((8, LANES), F32),
            jax.ShapeDtypeStruct((8, LANES), F32),
            jax.ShapeDtypeStruct((MICRO, GROUP, 2, COLS, C), BF16),
        ),
        in_specs=[
            pl.BlockSpec(memory_space=pltpu.SMEM),
            pl.BlockSpec(memory_space=pltpu.SMEM),
            pl.BlockSpec(memory_space=pl.ANY),
            pl.BlockSpec(memory_space=pltpu.VMEM),
        ],
        out_specs=(
            pl.BlockSpec(memory_space=pltpu.VMEM),
            pl.BlockSpec(memory_space=pltpu.VMEM),
            pl.BlockSpec(memory_space=pltpu.VMEM),
            pl.BlockSpec(memory_space=pl.ANY),
        ),
        scratch_shapes=list(bufs.values()),
        compiler_params=pltpu.CompilerParams(collective_id=0, has_side_effects=True, vmem_limit_bytes=64 * MB - 65536),
        name="train_step",
    )(mask, labels, features, params)


def update_kernel(e, norm, loss, grad, params, m1, m2, out, o_norm, o_loss, new_params, first, second, feats, *scratch):
    g, p, a, b, fin, fout, s_in, s_out, s_feat, s_fout = scratch
    parts = 4
    size = e.slab // parts // 8 * 8
    spans = [(k * size, size if k < parts - 1 else e.slab - k * size) for k in range(parts)]
    copy = pltpu.make_async_copy
    ins = []
    for k, (at, count) in enumerate(spans):
        for q, (src, dst) in enumerate(((grad, g), (params, p), (m1, a), (m2, b))):
            ins.append(copy(src.at[pl.ds(at, count)], dst.at[pl.ds(at, count)], s_in.at[k, q]))
            ins[-1].start()
    fins = [copy(out.at[k], fin.at[k], s_feat.at[k]) for k in range(MICRO)]
    for cp in fins:
        cp.start()
    o_norm[0, 0] = jnp.max(norm[...])
    o_loss[0, 0] = jnp.max(loss[...])
    scale = jnp.minimum(1.0, CLIP / (norm[0:1, 0:1] + 1e-06))
    outs = []
    for k, (at, count) in enumerate(spans):
        for q in range(4):
            ins[4 * k + q].wait()
        rows = slice(at, at + count)
        clipped = g[rows, :] * scale
        one = BETA_ONE * a[rows, :] + (1.0 - BETA_ONE) * clipped
        two = BETA_TWO * b[rows, :] + (1.0 - BETA_TWO) * clipped * clipped
        a[rows, :] = one
        b[rows, :] = two
        ratio = one / (1.0 - BETA_ONE**STEP) / (jnp.sqrt(two / (1.0 - BETA_TWO**STEP)) + EPS_ADAM)
        p[rows, :] = p[rows, :] - RATE * (ratio + DECAY * p[rows, :])
        for q, (src, dst) in enumerate(((p, new_params), (a, first), (b, second))):
            outs.append(copy(src.at[pl.ds(at, count)], dst.at[pl.ds(at, count)], s_out.at[k, q]))
            outs[-1].start()
        if k < MICRO:
            fins[k].wait()
            fout[k] = fin[k].astype(F32)
            outs.append(copy(fout.at[k], feats.at[k], s_fout.at[k]))
            outs[-1].start()
    for cp in outs:
        cp.wait()


def update(e, grad, norm, loss, params, m1, m2, out):
    flat = jax.ShapeDtypeStruct((e.slab, LANES), F32)
    scalar = jax.ShapeDtypeStruct((1, 1), F32)
    shape = (MICRO, GROUP, 2, COLS, C)
    near, far, one = (pl.BlockSpec(memory_space=k) for k in (pltpu.VMEM, pl.ANY, pltpu.SMEM))
    D = pltpu.SemaphoreType.DMA
    return pl.pallas_call(
        functools.partial(update_kernel, e),
        in_specs=[near, near, far, far, far, far, far],
        out_specs=(one, one, far, far, far, far),
        out_shape=(scalar, scalar, flat, flat, flat, jax.ShapeDtypeStruct(shape, F32)),
        scratch_shapes=[pltpu.VMEM((e.slab, LANES), F32)] * 4
        + [pltpu.VMEM(shape, BF16), pltpu.VMEM(shape, F32), D((4, 4)), D((4, 3)), D((MICRO,)), D((MICRO,))],
        compiler_params=pltpu.CompilerParams(vmem_limit_bytes=64 * MB - 65536),
        name="update",
    )(norm, loss, grad, params, m1, m2, out)


def local(e, features, drop_mask, labels, params, moment1, moment2):
    flat = [v.reshape(e.slab, LANES) for v in (params, moment1, moment2)]
    grad, norm, loss, out = train_step(e, features, drop_mask, labels, flat[0])
    norm, loss, new_params, first, second, feats = update(e, grad, norm, loss, *flat, out)
    size = e.slab * LANES
    return (
        new_params.reshape(size),
        first.reshape(size),
        second.reshape(size),
        loss.reshape(()),
        norm.reshape(()),
        feats,
    )


def solution(mesh):
    e = Env()
    e.n = mesh.shape["rows"]
    e.nb = mesh.shape["batch"]
    e.G = e.n // GROUP
    e.slab = FLAT // e.n
    e.half = (e.slab + 31) // 32 * 16
    e.positions = float(e.n * COLS // 2)
    e.inv_count = 1.0 / (MICRO * GROUP * e.nb)
    return jax.shard_map(
        functools.partial(local, e),
        mesh=mesh,
        in_specs=(
            P(None, "batch", "rows", None, None),
            P(None, "batch"),
            P(None, "batch"),
            P("rows"),
            P("rows"),
            P("rows"),
        ),
        out_specs=(P("rows"), P("rows"), P("rows"), P(), P(), P(None, "batch", "rows", None, None)),
        check_vma=False,
    )
```

```python
import functools

import jax
import jax.numpy as jnp
from jax import lax
from jax.experimental import pallas as pl
from jax.experimental.pallas import tpu as pltpu
from jax.sharding import PartitionSpec as P

C = 384
HID = 1536
DOUT = 768
CLS = 1000
MICRO = 3
STEP = 10
P_SIZE = 3153920
KEEP = 0.8
CLIP = 0.01
RATE = 0.05
BETA_ONE = 0.9
BETA_TWO = 0.999
DECAY = 0.05
EPS_ADAM = 1e-08
EPS_NORM = 1e-06

MESH = pl.DeviceIdType.MESH
F32 = jnp.float32
BF16 = jnp.bfloat16
MB = 1 << 20

LANES = 128
J = C // LANES
GROUP = 4
OWN = 8
COLS = 64
PADC = COLS + 6
SUB = 16
POS = COLS * OWN
NPOS = MICRO * POS
FLAT = P_SIZE // LANES
ROW_K = 0
ROW_UP = 49 * J
ROW_CUP = ROW_UP + C * HID // LANES
ROW_DOWN = ROW_CUP + HID // LANES
ROW_VEC = ROW_DOWN + C * HID // LANES
ROW_DS = ROW_VEC + 7 * J
ROW_OUT = ROW_DS + 4 * C * DOUT // LANES
ROW_HEAD = ROW_OUT + 3 * DOUT // LANES
ROW_BH = ROW_HEAD + DOUT * CLS // LANES
TABLES = (
    (ROW_K, 49 * J, 0),
    (ROW_CUP, HID // LANES, 152),
    (ROW_VEC, 7 * J, 168),
    (ROW_OUT, 3 * DOUT // LANES, 192),
    (ROW_BH, FLAT - ROW_BH, 216),
)
TAB_ROWS = 232
TAB_SPAN = (152, 16, 24, 24, 16)
T_CUP, T_VEC, T_OUT, T_BH = 152, 168, 192, 216
SG_ROWS = 256
SG_CUP, SG_VEC = 152, 168
CLSP = 1024


class Env:
    pass


def xrow(j, m):
    return (j * MICRO + m) * PADC * SUB


def rows_of(refs, row, count):
    return refs[row : row + count, :]


def lane_row(ref, row, count):
    return jnp.concatenate([ref[row + k : row + k + 1, :] for k in range(count)], axis=1)


def ln_parts(blocks, width):
    total = blocks[0]
    for block in blocks[1:]:
        total = total + block
    mean = jnp.sum(total, -1, keepdims=True) * (1.0 / width)
    centred = [block - mean for block in blocks]
    square = centred[0] * centred[0]
    for block in centred[1:]:
        square = square + block * block
    spread = jnp.sum(square, -1, keepdims=True) * (1.0 / width)
    scale = lax.rsqrt(spread + EPS_NORM)
    return [block * scale for block in centred], scale


def here(e):
    e.r = lax.axis_index("rows")
    e.b = lax.axis_index("batch")
    e.g = e.r // GROUP
    e.i = e.r % GROUP
    e.h = e.b % 2


def dev(e, r=None, b=None):
    return {"rows": e.r if r is None else r, "batch": e.b if b is None else b}


def remote(e, src, dst, send, recv, r=None, b=None):
    return pltpu.make_async_remote_copy(
        src, dst, send, recv, device_id=(e.r if r is None else r, e.b if b is None else b), device_id_type=MESH
    )


def ph_barrier_signal(e, B):
    barrier = pltpu.get_barrier_semaphore()
    for d in range(1, e.n):
        pl.semaphore_signal(barrier, inc=1, device_id=(lax.rem(e.r + d, e.n), e.b), device_id_type=MESH)
    for d in range(1, e.nb):
        pl.semaphore_signal(barrier, inc=1, device_id=(e.r, lax.rem(e.b + d, e.nb)), device_id_type=MESH)


def ph_barrier_wait(e, B):
    pl.semaphore_wait(pltpu.get_barrier_semaphore(), e.n - 1 + e.nb - 1)


def feat_copy(e, B, m, d):
    j = lax.rem(e.i + d, GROUP)
    return remote(
        e,
        B.features.at[m, j],
        B.xg.at[m, pl.ds(3 + 2 * e.i, 2)],
        B.s_feat.at[m, d],
        B.r_feat.at[m, d],
        r=e.g * GROUP + j,
    )


def feat_own(e, B):
    return pltpu.make_async_copy(B.features.at[:, e.i], B.xg.at[:, pl.ds(3 + 2 * e.i, 2)], B.s_own.at[0])


def feat_start(e, B, m):
    if m == 0:
        feat_own(e, B).start()
    for d in (2, 3, 1):
        feat_copy(e, B, m, d).start()


def ph_feat_zero(e, B):
    zero = jnp.zeros((MICRO, 3, COLS, C), BF16)

    @pl.when(e.g == 0)
    def _():
        B.xg[:, 0:3] = zero

    @pl.when(e.g == e.G - 1)
    def _():
        B.xg[:, 11:14] = zero


def halo_copy(e, B, m, up):
    if up:
        return remote(e, B.xg.at[m, 8:11], B.xg.at[m, 0:3], B.s_halo.at[1, m], B.r_halo.at[1, m], r=e.r + GROUP)
    return remote(e, B.xg.at[m, 3:6], B.xg.at[m, 11:14], B.s_halo.at[0, m], B.r_halo.at[0, m], r=e.r - GROUP)


def halo_start(e, B, m):
    if m == 0:
        feat_own(e, B).wait()
    for d in range(1, GROUP):
        feat_copy(e, B, m, d).wait_recv()

    @pl.when(e.g > 0)
    def _():
        halo_copy(e, B, m, False).start()

    @pl.when(e.g < e.G - 1)
    def _():
        halo_copy(e, B, m, True).start()


def halo_wait(e, B, m):
    @pl.when(e.g < e.G - 1)
    def _():
        halo_copy(e, B, m, False).wait_recv()

    @pl.when(e.g > 0)
    def _():
        halo_copy(e, B, m, True).wait_recv()


def ph_feat_done(e, B):
    for m in range(MICRO):
        for d in range(1, GROUP):
            feat_copy(e, B, m, d).wait_send()

        @pl.when(e.g > 0)
        def _(m=m):
            halo_copy(e, B, m, False).wait_send()

        @pl.when(e.g < e.G - 1)
        def _(m=m):
            halo_copy(e, B, m, True).wait_send()


def ph_cast(e, B):
    for h in range(2):
        count = e.half if h == 0 else e.slab - e.half
        whole = count // 16 * 16
        B.gw[e.r, h, 0:whole, :] = B.params[h * e.half : h * e.half + whole, :].astype(BF16)
        rest = count - whole
        if whole < e.half:
            parts = [jnp.zeros((e.half - whole - rest, LANES), F32)]
            if rest:
                parts = [B.params[e.slab - rest : e.slab, :]] + parts
            B.gw[e.r, h, whole : e.half, :] = jnp.concatenate(parts, axis=0).astype(BF16)
    for k, (first, count, place) in enumerate(TABLES):
        off = first % e.slab

        @pl.when(e.r == first // e.slab)
        def _(off=off, count=count, place=place):
            B.tab[place : place + count, :] = B.params[off : off + count, :]


def table_line(e, B, k, d):
    first, count, place = TABLES[k]
    owner = first // e.slab
    part = pl.ds(place, TAB_SPAN[k])
    return remote(e, B.tab.at[part], B.tab.at[part], B.s_tab.at[k, d], B.r_tab.at[k], r=lax.rem(owner + GROUP * d, e.n))


def table_group(e, B, k, d):
    first, count, place = TABLES[k]
    part = pl.ds(place, TAB_SPAN[k])
    to = e.g * GROUP + lax.rem(e.i + d, GROUP)
    return remote(e, B.tab.at[part], B.tab.at[part], B.s_tabg.at[k, d], B.r_tab.at[k], r=to)


def ph_tables_start(e, B):
    for k, (first, count, place) in enumerate(TABLES):
        owner = first // e.slab

        @pl.when(e.r == owner)
        def _(k=k):
            for d in range(1, e.G):
                table_line(e, B, k, d).start()
            for d in range(1, GROUP):
                table_group(e, B, k, d).start()


def tables_forward(e, B, some):
    for k in some:
        owner = TABLES[k][0] // e.slab

        @pl.when(jnp.logical_and(e.i == owner % GROUP, e.r != owner))
        def _(k=k):
            table_line(e, B, k, 1).wait_recv()
            for d in range(1, GROUP):
                table_group(e, B, k, d).start()


def tables_wait(e, B, some):
    for k in some:
        owner = TABLES[k][0] // e.slab

        @pl.when(e.i != owner % GROUP)
        def _(k=k):
            table_group(e, B, k, 1).wait_recv()


def ph_tables_done(e, B):
    for k, (first, count, place) in enumerate(TABLES):
        owner = first // e.slab

        @pl.when(e.r == owner)
        def _(k=k):
            for d in range(1, e.G):
                table_line(e, B, k, d).wait_send()

        @pl.when(e.i == owner % GROUP)
        def _(k=k):
            for d in range(1, GROUP):
                table_group(e, B, k, d).wait_send()


CHUNKS = 4


def chunk_of(e, c):
    if c is None:
        return pl.ds(0, e.half)
    tiles = e.half // 16
    cuts = [(tiles * k + CHUNKS - 1) // CHUNKS * 16 for k in range(CHUNKS + 1)]
    return pl.ds(cuts[c], cuts[c + 1] - cuts[c])


def half_ref(e, B, slot, h, c):
    return B.gw.at[slot, h, chunk_of(e, c)]


def line_copy(e, B, level, up, c):
    ref = half_ref(e, B, level * GROUP + e.i, e.h, c)
    k = 0 if up else 1
    return remote(e, ref, ref, B.s_line.at[k, level], B.r_line.at[level, c or 0], r=e.r + GROUP if up else e.r - GROUP)


def pair_copy(e, B, level, c):
    ref = half_ref(e, B, level * GROUP + e.i, e.h, c)
    to = e.g * GROUP + lax.rem(e.i + 2, GROUP)
    return remote(e, ref, ref, B.s_pair.at[level], B.r_pair.at[level, c or 0], r=to)


def row_copy(e, B, level, other, c):
    i = lax.rem(e.i + 2, GROUP) if other else e.i
    ref = half_ref(e, B, level * GROUP + i, e.h, c)
    k = int(other)
    return remote(e, ref, ref, B.s_row.at[k, level], B.r_row.at[k, level, c or 0], b=e.b + 1 - 2 * e.h)


def core_copy(e, B, level, other, mine, c):
    i = lax.rem(e.i + 2, GROUP) if other else e.i
    ref = half_ref(e, B, level * GROUP + i, e.h if mine else 1 - e.h, c)
    k = 2 * int(other) + int(mine)
    sib = e.g * GROUP + e.i + 1 - 2 * (e.i % 2)
    return remote(e, ref, ref, B.s_core.at[k, level], B.r_core.at[k, level, c or 0], r=sib)


def line_out(e, B, level, c):
    @pl.when(jnp.logical_and(e.g >= level, e.g + 1 < e.G))
    def _():
        line_copy(e, B, level, True, c).start()

    @pl.when(jnp.logical_and(e.g <= level, e.g >= 1))
    def _():
        line_copy(e, B, level, False, c).start()


def at_hop(e, level, hop, body):
    if hop == 0:
        cond = e.g == level
    else:
        cond = jnp.logical_or(e.g == level + hop, e.g == level - hop)
    pl.when(cond)(body)


def line_send(e, B, levels, chunks):
    for level in levels:

        def body(level=level):
            for c in chunks:
                line_out(e, B, level, c)

        at_hop(e, level, 0, body)


def line_step(e, B, levels, hop, chunks):
    for level in levels:

        def body(level=level):
            for c in chunks:
                line_copy(e, B, level, True, c).wait_recv()
                line_out(e, B, level, c)
                row_copy(e, B, level, False, c).start()
                core_copy(e, B, level, False, True, c).start()

        at_hop(e, level, hop, body)


def pair_step(e, B, levels, hop, chunks):
    for level in levels:

        def body(level=level):
            for c in chunks:
                pair_copy(e, B, level, c).start()
                if hop == 0:
                    core_copy(e, B, level, False, True, c).start()
                    core_copy(e, B, level, False, False, c).start()

        at_hop(e, level, hop, body)


def row_step(e, B, levels, hop, chunks):
    for level in levels:

        def body(level=level):
            for c in chunks:
                pair_copy(e, B, level, c).wait_recv()
                row_copy(e, B, level, True, c).start()
                core_copy(e, B, level, True, True, c).start()

        at_hop(e, level, hop, body)


def core_step(e, B, levels, hop, chunks):
    for level in levels:

        def body(level=level):
            for c in chunks:
                if hop:
                    row_copy(e, B, level, False, c).wait_recv()
                    core_copy(e, B, level, False, False, c).start()
                row_copy(e, B, level, True, c).wait_recv()
                core_copy(e, B, level, True, False, c).start()

        at_hop(e, level, hop, body)


def gather_ready(e, B, levels):
    for level in levels:
        for other in (False, True):
            for mine in (False, True):
                for c in range(CHUNKS):
                    core_copy(e, B, level, other, mine, c).wait_recv()


def ph_gather_done(e, B):
    G = e.G
    for level in range(G):
        pair_copy(e, B, level, None).wait_send()
        row_copy(e, B, level, True, None).wait_send()

        @pl.when(e.g != level)
        def _(level=level):
            row_copy(e, B, level, False, None).wait_send()

        for other in (False, True):
            for mine in (False, True):
                core_copy(e, B, level, other, mine, None).wait_send()

        @pl.when(jnp.logical_and(e.g >= level, e.g + 1 < G))
        def _(level=level):
            line_copy(e, B, level, True, None).wait_send()

        @pl.when(jnp.logical_and(e.g <= level, e.g >= 1))
        def _(level=level):
            line_copy(e, B, level, False, None).wait_send()


def flatten(e, B, first, last):
    step = 112
    s0 = first // e.slab

    def slab(k, _):
        for h in range(2):
            count = e.half if h == 0 else e.slab - e.half
            whole = count // step
            left = (count - whole * step + 15) // 16 * 16
            base = e.slab * k + h * e.half

            def body(t, _, h=h, base=base):
                at = pl.multiple_of(t * step, 16)
                B.big[pl.ds(base + t * step, step), :] = B.gw[s0 + k, h, pl.ds(at, step), :].astype(F32)
                return 0

            lax.fori_loop(0, whole, body, 0)
            if left:
                last = B.gw[s0 + k, h, whole * step : whole * step + left, :]
                B.big[pl.ds(base + whole * step, left), :] = last.astype(F32)
        return 0

    lax.fori_loop(0, (last - 1) // e.slab - s0 + 1, slab, 0)
    return e.slab * s0


def ph_weights_up(e, B):
    base = flatten(e, B, ROW_UP, ROW_CUP)
    for j in range(HID // LANES):
        B.wup[:, LANES * j : LANES * (j + 1)] = B.big[pl.ds(ROW_UP - base + j, C, stride=HID // LANES), :].astype(BF16)


def ph_weights_down(e, B):
    base = flatten(e, B, ROW_DOWN, ROW_VEC)
    for j in range(J):
        B.wdn[:, LANES * j : LANES * (j + 1)] = B.big[pl.ds(ROW_DOWN - base + j, HID, stride=J), :].astype(BF16)


def ph_weights_head(e, B):
    base = flatten(e, B, ROW_DS, ROW_OUT)
    per = DOUT // LANES
    for j in range(per):
        B.wds[:, LANES * j : LANES * (j + 1)] = B.big[pl.ds(ROW_DS - base + j, 4 * C, stride=per), :].astype(BF16)
    base = flatten(e, B, ROW_HEAD, ROW_BH)
    lane = lax.broadcasted_iota(jnp.int32, (DOUT // 16, LANES), 1)
    for kk in range(16):
        first, off = divmod(CLS * kk, LANES)
        parts = [B.big[pl.ds(ROW_HEAD - base + first + t, DOUT // 16, stride=125), :] for t in range(9 if off else 8)]
        if off:
            parts = [pltpu.roll(part, LANES - off, 1) for part in parts]
        for t in range(8):
            tile = parts[t]
            if off:
                tile = jnp.where(lane < LANES - off, parts[t], parts[t + 1])
            if t == 7:
                tile = jnp.where(lane < CLS - 7 * LANES, tile, 0.0)
            B.dx[pl.ds(DOUT * t + kk, DOUT // 16, stride=16), :] = tile
    for t in range(8):
        B.wh[:, LANES * t : LANES * (t + 1)] = B.dx[DOUT * t : DOUT * (t + 1), :].astype(BF16)


def hooks(it, steps, also=None):
    if not steps:
        return
    bits = sum(1 << k for k in steps)
    due = lax.rem(lax.shift_right_logical(jnp.int32(bits), it), 2) == 1
    if also is not None:
        due = jnp.logical_and(due, also)

    @pl.when(due)
    def _():
        for k, some in steps.items():

            @pl.when(it == k)
            def _(some=some):
                for step in some:
                    step()


def transpose(e, B, m):
    pad = jnp.zeros((3 * SUB, LANES), F32)
    for j in range(J):
        B.big[pl.ds(xrow(j, m), 3 * SUB), :] = pad
        B.big[pl.ds(xrow(j, m) + (COLS + 3) * SUB, 3 * SUB), :] = pad
        for row in range(14):
            v = B.xg[m, row, :, LANES * j : LANES * (j + 1)].astype(F32)
            B.big[pl.ds(xrow(j, m) + 3 * SUB + row, COLS, stride=SUB), :] = v
            if 3 <= row < 11:
                B.xc[pl.ds(j * NPOS + m * POS + row - 3, COLS, stride=OWN), :] = v


def ph_taps(e, B):
    def body(t, _):
        B.kb[t] = jnp.broadcast_to(B.tab[pl.ds(t, 1), :], (8, LANES))
        return 0

    lax.fori_loop(0, 49 * J, body, 0)


def vec_row(B, v, j):
    row = T_VEC + v * J + j
    return B.tab[row : row + 1, :]


def conv_tile(B, m, j, c0, tile, acc, flip):
    for a in range(7):
        taps = [B.kb[((6 - a) * 7 + 6 - b if flip else a * 7 + b) * J + j] for b in range(7)]
        for c in range(tile + 6):
            d = B.big[pl.ds(xrow(j, m) + (c0 + c) * SUB + a, OWN), :]
            for b in range(7):
                if 0 <= c - b < tile:
                    acc[c - b] = acc[c - b] + d * taps[b]
    return acc


TILE = 32


def ph_conv_fwd(e, B, steps):
    halves = COLS // TILE

    def body(it, _):
        m = it // halves
        c0 = it % halves * TILE
        for j in range(J):
            hooks(it, {k // J: v for k, v in steps.items() if k % J == j})
            bias = jnp.broadcast_to(vec_row(B, 0, j), (OWN, LANES))
            acc = conv_tile(B, m, j, c0, TILE, [bias] * TILE, False)
            at = j * NPOS + m * POS + c0 * OWN
            for c in range(TILE):
                B.dx[pl.ds(pl.multiple_of(at + OWN * c, OWN), OWN), :] = acc[c]
        return 0

    lax.fori_loop(0, MICRO * halves, body, 0)


def ph_norm_one(e, B):
    size = 128

    def body(it, _):
        at = pl.multiple_of(it * size, size)
        hat, scale = ln_parts([B.dx[pl.ds(j * NPOS + at, size), :] for j in range(J)], C)
        B.rs1[pl.ds(at, size), :] = jnp.broadcast_to(scale, (size, LANES))
        for j in range(J):
            B.v1[pl.ds(at, size), LANES * j : LANES * (j + 1)] = hat[j]
            B.n[pl.ds(at, size), LANES * j : LANES * (j + 1)] = (
                hat[j] * vec_row(B, 1, j) + vec_row(B, 2, j)
            ).astype(BF16)
        return 0

    lax.fori_loop(0, NPOS // size, body, 0)


def ph_mlp_up(e, B, steps):
    chunk = 256
    width = 256
    c0 = 0.7978845608028654
    c1 = 0.044715 * c0

    def body(it, _):
        hooks(it, steps)
        at = pl.multiple_of(it * chunk, chunk)
        rows = B.n[pl.ds(at, chunk), :]
        for k in range(HID // width):
            lanes = slice(width * k, width * (k + 1))
            bias = lane_row(B.tab, T_CUP + k * width // LANES, width // LANES)
            h = jnp.dot(rows, B.wup[:, lanes], preferred_element_type=F32) + bias
            sq = h * h
            half = 0.5 * jnp.tanh(h * (c0 + c1 * sq)) + 0.5
            u = h * half
            B.u[pl.ds(at, chunk), lanes] = u.astype(BF16)
            slope = half + u * (1.0 - half) * (2.0 * c0 + 6.0 * c1 * sq)
            B.gp[pl.ds(at, chunk), lanes] = slope.astype(BF16)
        return 0

    lax.fori_loop(0, NPOS // chunk, body, 0)


def ph_mlp_down(e, B, steps):
    chunk = 256
    B.ps[...] = jnp.zeros_like(B.ps)

    def body(it, _):
        hooks(it, steps)
        at = pl.multiple_of(it * chunk, chunk)
        m = it // (POS // chunk)
        keep = B.mask[m, e.i].astype(F32) * (1.0 / KEEP)
        z = jnp.dot(B.u[pl.ds(at, chunk), :], B.wdn[...], preferred_element_type=F32)
        resid = []
        for j in range(J):
            zj = z[:, LANES * j : LANES * (j + 1)] + vec_row(B, 3, j)
            B.z[pl.ds(j * NPOS + at, chunk), :] = zj
            resid.append(B.xc[pl.ds(j * NPOS + at, chunk), :] + (vec_row(B, 4, j) * keep) * zj)
        hat, scale = ln_parts(resid, C)
        B.rs2[pl.ds(at, chunk), :] = jnp.broadcast_to(scale, (chunk, LANES))
        for j in range(J):
            B.v2[pl.ds(at, chunk), LANES * j : LANES * (j + 1)] = hat[j]
            low = (hat[j] * vec_row(B, 5, j) + vec_row(B, 6, j)).astype(BF16).astype(F32)
            low = jnp.sum(low.reshape(chunk // 16, 2, OWN, LANES), 0)
            B.ps[m, :, :, LANES * j : LANES * (j + 1)] += low
        return 0

    lax.fori_loop(0, NPOS // chunk, body, 0)


def ph_patch_local(e, B):
    even = lax.broadcasted_iota(jnp.int32, (OWN, C), 0) % 2 == 0
    pick = lax.broadcasted_iota(jnp.int32, (8, C), 0)
    for parity in range(2):
        for side in range(2):
            tile = jnp.zeros((8, C), F32)
            for m in range(MICRO):
                v = B.ps[m, side]
                part = jnp.sum(jnp.where(even if parity == 0 else jnp.logical_not(even), v, 0.0), 0, keepdims=True)
                tile = jnp.where(pick == m, part, tile)
            q = 2 * parity + side
            B.sl[8 * q : 8 * q + 8, :] = tile


def patch_copy(e, B, d):
    to = lax.rem(e.g + d, e.G)
    return remote(e, B.sl, B.sr.at[d], B.s_patch.at[d], B.r_patch.at[d], r=to * GROUP + e.i)


def patch_start(e, B):
    for d in range(1, e.G):
        patch_copy(e, B, d).start()
    B.sr[0] = B.sl[...]


def patch_wait(e, B):
    for d in range(1, e.G):
        patch_copy(e, B, d).wait_recv()
    for d in range(1, e.G):
        patch_copy(e, B, d).wait_send()


def split3(v):
    hi = v.astype(BF16).astype(F32)
    mid = (v - hi).astype(BF16).astype(F32)
    return hi, mid, v - hi - mid


def ph_head(e, B):
    total = None
    for level in range(e.G):
        part = B.sr[lax.rem(e.g - level + e.G, e.G)]
        total = part if total is None else total + part
    per = DOUT // LANES
    gain = lane_row(B.tab, T_OUT + per, per)
    shift = lane_row(B.tab, T_OUT + 2 * per, per)
    mean = total * (1.0 / e.positions)
    pooled = lane_row(B.tab, T_OUT, per)
    for q in range(4):
        parts = jnp.concatenate(split3(mean[8 * q : 8 * q + 8, :]), axis=0).astype(BF16)
        prod = jnp.dot(parts, B.wds[C * q : C * (q + 1), :], preferred_element_type=F32)
        pooled = pooled + (prod[0:8] + (prod[8:16] + prod[16:24]))
    rows = lax.broadcasted_iota(jnp.int32, (8, 1), 0)
    live = rows < MICRO
    (hat,), scale = ln_parts([pooled], DOUT)
    query = (hat * gain + shift).astype(BF16)
    lane = lax.broadcasted_iota(jnp.int32, (8, CLSP), 1)
    logits = jnp.dot(query, B.wh[...], preferred_element_type=F32) + lane_row(B.tab, T_BH, CLSP // LANES)
    logits = jnp.where(lane < CLS, logits, -1e30)
    top = jnp.max(logits, 1, keepdims=True)
    powers = jnp.exp(logits - top)
    expsum = jnp.sum(powers, 1, keepdims=True)
    label = jnp.zeros((8, 1), jnp.int32)
    for m in range(MICRO):
        label = jnp.where(rows == m, B.labels[m, e.i], label)
    onehot = (lane == label).astype(F32)
    own = jnp.sum(jnp.where(lane == label, logits, 0.0), 1, keepdims=True)
    loss = jnp.sum(jnp.where(live, top + jnp.log(expsum) - own, 0.0), 0, keepdims=True)
    grad = jnp.where(live, (powers / expsum - onehot) * e.inv_count, 0.0).astype(BF16)
    grad_query = lax.dot_general(grad, B.wh[...], (((1,), (1,)), ((), ())), preferred_element_type=F32)
    dn = grad_query * gain
    m1 = jnp.sum(dn, 1, keepdims=True) * (1.0 / DOUT)
    m2 = jnp.sum(dn * hat, 1, keepdims=True) * (1.0 / DOUT)
    grad_pool = scale * (dn - m1 - hat * m2)
    down = jnp.where(live, grad_pool * (1.0 / e.positions), 0.0).astype(BF16)
    for q in range(4):
        B.dn2[8 * q : 8 * q + 8, :] = lax.dot_general(
            down, B.wds[C * q : C * (q + 1), :], (((1,), (1,)), ((), ())), preferred_element_type=F32
        )
    low = grad.astype(F32)
    d32 = down.astype(F32)
    q32 = jnp.where(live, query.astype(F32), 0.0)
    zero3 = jnp.zeros((3, C), F32)
    g3 = jnp.sum(jnp.where(live, grad_query * hat, 0.0), 0, keepdims=True)
    s3 = jnp.sum(jnp.where(live, grad_query, 0.0), 0, keepdims=True)
    vec = jnp.concatenate([g3, s3], axis=1)
    vec_parts = split3(vec)
    loss_parts = split3(loss)
    for q in range(4):
        at = slice(C * q, C * (q + 1))
        s_hi, s_mid, _ = split3(total[8 * q : 8 * q + 8, :])
        B.pb[0:8, at] = jnp.zeros((8, C), F32)
        B.pb[8:16, at] = jnp.zeros((8, C), F32)
        B.pb[0:3, at] = s_hi[0:3]
        B.pb[3:6, at] = s_mid[0:3]
    B.pb[6:9, 0:DOUT] = d32[0:3]
    B.pb[6:9, DOUT : 2 * DOUT] = q32[0:3]
    B.pb[9:12, 0:CLSP] = low[0:3]
    for k in range(3):
        B.pb[12 + k : 13 + k, :] = vec_parts[k]
        B.pb[15:16, LANES * k : LANES * (k + 1)] = jnp.broadcast_to(loss_parts[k], (1, LANES))
    B.pall[e.i * e.nb + e.b] = B.pb[...].astype(BF16)
    even = lax.broadcasted_iota(jnp.int32, (OWN, C), 0) % 2 == 0
    for m in range(MICRO):
        for side in range(2):
            first = B.dn2[8 * side + m : 8 * side + m + 1, :]
            second = B.dn2[8 * (2 + side) + m : 8 * (2 + side) + m + 1, :]
            B.dnt[m, side] = jnp.where(even, first, second)


def batch_copy(e, B, d):
    slot = e.i * e.nb + e.b
    return remote(e, B.pall.at[slot], B.pall.at[slot], B.s_pb.at[d], B.r_pb.at[d], b=lax.rem(e.b + d, e.nb))


def group_copy(e, B, d):
    at = pl.ds(e.i * e.nb, e.nb)
    to = e.g * GROUP + lax.rem(e.i + d, GROUP)
    return remote(e, B.pall.at[at], B.pall.at[at], B.s_pg.at[d], B.r_pg.at[d], r=to)


def ph_payload_batch(e, B):
    for d in range(1, e.nb):
        batch_copy(e, B, d).start()


def ph_payload_group(e, B):
    for d in range(1, e.nb):
        batch_copy(e, B, d).wait_recv()
    for d in range(1, GROUP):
        group_copy(e, B, d).start()


def ph_payload_wait(e, B):
    for d in range(1, GROUP):
        group_copy(e, B, d).wait_recv()
    for d in range(1, e.nb):
        batch_copy(e, B, d).wait_send()
    for d in range(1, GROUP):
        group_copy(e, B, d).wait_send()


def lane_sum(blocks):
    total = blocks[0]
    for block in blocks[1:]:
        total = total + block
    return jnp.sum(total, -1, keepdims=True) * (1.0 / C)


def fold8(v):
    return jnp.sum(v.reshape(v.shape[0] // 8, 8, v.shape[1]), 0)


def ph_bwd_one(e, B):
    chunk = 256
    half = chunk // 16
    B.acc[...] = jnp.zeros_like(B.acc)
    B.acup[...] = jnp.zeros_like(B.acup)
    B.vs[...] = jnp.zeros_like(B.vs)

    def body(it, _):
        at = pl.multiple_of(it * chunk, chunk)
        m = it // (POS // chunk)
        keep = B.mask[m, e.i].astype(F32) * (1.0 / KEEP)
        span = pl.ds(at, chunk)
        lanes = [slice(LANES * j, LANES * (j + 1)) for j in range(J)]
        dg = [B.dnt[m, :, :, lanes[j]] * vec_row(B, 5, j) for j in range(J)]
        m1 = lane_sum(dg)
        hat = [B.v2[span, lanes[j]].reshape(half, 2, OWN, LANES) for j in range(J)]
        m2 = lane_sum([dg[j] * hat[j] for j in range(J)])
        scale = B.rs2[span, :].reshape(half, 2, OWN, LANES)
        for j in range(J):
            zspan = pl.ds(j * NPOS + at, chunk)
            dr = (scale * (dg[j] - m1 - hat[j] * m2)).reshape(chunk, LANES)
            B.vs[m, :, :, lanes[j]] += jnp.sum(hat[j], 0)
            dz = (dr * (vec_row(B, 4, j) * keep)).astype(BF16)
            B.dz[span, lanes[j]] = dz
            B.acc[3, :, lanes[j]] += fold8(dz.astype(F32))
            B.acc[4, :, lanes[j]] += fold8(dr * B.z[zspan, :]) * keep
            B.z[zspan, :] = dr
        return 0

    lax.fori_loop(0, NPOS // chunk, body, 0)
    for m in range(MICRO):
        B.acc[5] += B.dnt[m, 0] * B.vs[m, 0] + B.dnt[m, 1] * B.vs[m, 1]
        B.acc[6] += (B.dnt[m, 0] + B.dnt[m, 1]) * float(COLS // 2)


def ph_bwd_two(e, B, steps):
    chunk = 256
    width = 256

    def body(it, _):
        hooks(it, steps)
        at = pl.multiple_of(it * chunk, chunk)
        m = it // (POS // chunk)
        c0 = (it % (POS // chunk)) * (chunk // OWN)
        span = pl.ds(at, chunk)
        lanes = [slice(LANES * j, LANES * (j + 1)) for j in range(J)]
        dz = B.dz[span, :]
        for k in range(HID // width):
            hid = slice(width * k, width * (k + 1))
            du = lax.dot_general(dz, B.wdn[hid, :], (((1,), (1,)), ((), ())), preferred_element_type=F32)
            dh = (du * B.gp[span, hid].astype(F32)).astype(BF16)
            B.gp[span, hid] = dh
            B.acup[:, hid] += fold8(dh.astype(F32))
        dn = lax.dot_general(B.gp[span, :], B.wup[...], (((1,), (1,)), ((), ())), preferred_element_type=F32)
        dns = [dn[:, lanes[j]] for j in range(J)]
        dg = [dns[j] * vec_row(B, 1, j) for j in range(J)]
        hat = [B.v1[span, lanes[j]] for j in range(J)]
        m1 = lane_sum(dg)
        m2 = lane_sum([dg[j] * hat[j] for j in range(J)])
        scale = B.rs1[span, :]
        for j in range(J):
            dy = scale * (dg[j] - m1 - hat[j] * m2)
            B.acc[0, :, lanes[j]] += fold8(dy)
            B.acc[1, :, lanes[j]] += fold8(dns[j] * hat[j])
            B.acc[2, :, lanes[j]] += fold8(dns[j])
            for c in range(chunk // OWN):
                B.big[pl.ds(xrow(j, m) + (3 + c0 + c) * SUB + 3, OWN), :] = dy[OWN * c : OWN * (c + 1), :]
        return 0

    lax.fori_loop(0, NPOS // chunk, body, 0)


def wgrad_down(e, B, f):
    for k in range(2):
        first = 2 * C * f + C * k
        w = lax.dot_general(
            B.u[:, first : first + C], B.dz[...], (((0,), (0,)), ((), ())), preferred_element_type=F32
        )
        w = w.reshape(24, 16, C)
        a, b = w[:, 0:8], w[:, 8:16]
        units = [v[:, :, LANES * j : LANES * (j + 1)] for v in (a, b) for j in range(J)]
        tiles = [jnp.concatenate(units[2 * t : 2 * t + 2], axis=1).astype(BF16) for t in range(3)]
        for q in range(24):
            piece, inner = divmod(24 * k + q, 3)
            for t in range(3):
                B.gb[f, piece // 4, piece // 2 % 2, piece % 2, inner, t] = tiles[t][q]


def wgrad_up(e, B, f):
    width = 256
    for k in range(3):
        first = 768 * (f - 2) + width * k
        w = lax.dot_general(
            B.n[...], B.gp[:, first : first + width], (((0,), (0,)), ((), ())), preferred_element_type=F32
        )
        w = w.reshape(48, 8, width)
        w = jnp.concatenate([w[:, :, :LANES], w[:, :, LANES:]], axis=1).astype(BF16)
        B.gb[f, :, :, :, :, k] = w.reshape(4, 2, 2, 3, 16, LANES)


def dy_copy(e, B, m, up):
    if up:
        return remote(e, B.hs.at[m, 1], B.hr.at[m, 0], B.s_dy.at[1, m], B.r_dy.at[1, m], r=e.r + GROUP)
    return remote(e, B.hs.at[m, 0], B.hr.at[m, 1], B.s_dy.at[0, m], B.r_dy.at[0, m], r=e.r - GROUP)


def dy_send(e, B, m):
    zero = jnp.zeros((3 * SUB, LANES), F32)
    for j in range(J):
        B.big[pl.ds(xrow(j, m), 3 * SUB), :] = zero
        B.big[pl.ds(xrow(j, m) + (COLS + 3) * SUB, 3 * SUB), :] = zero
        for side in range(2):
            for k in range(3):
                row = 3 + k if side == 0 else 8 + k
                v = B.big[pl.ds(xrow(j, m) + 3 * SUB + row, COLS, stride=SUB), :]
                B.hs[m, side, k, :, LANES * j : LANES * (j + 1)] = v.astype(BF16)

    @pl.when(e.g > 0)
    def _():
        dy_copy(e, B, m, False).start()

    @pl.when(e.g < e.G - 1)
    def _():
        dy_copy(e, B, m, True).start()


def ph_dy_edges(e, B):
    zero = jnp.zeros((MICRO, 3, COLS, C), BF16)

    @pl.when(e.g == 0)
    def _():
        B.hr[:, 0] = zero

    @pl.when(e.g == e.G - 1)
    def _():
        B.hr[:, 1] = zero


def dy_take(e, B, m):
    @pl.when(e.g < e.G - 1)
    def _():
        dy_copy(e, B, m, False).wait_recv()

    @pl.when(e.g > 0)
    def _():
        dy_copy(e, B, m, True).wait_recv()

    for j in range(J):
        for side in range(2):
            for k in range(3):
                row = k if side == 0 else 11 + k
                v = B.hr[m, side, k, :, LANES * j : LANES * (j + 1)].astype(F32)
                B.big[pl.ds(xrow(j, m) + 3 * SUB + row, COLS, stride=SUB), :] = v


def ph_dy_done(e, B):
    for m in range(MICRO):

        @pl.when(e.g > 0)
        def _(m=m):
            dy_copy(e, B, m, False).wait_send()

        @pl.when(e.g < e.G - 1)
        def _(m=m):
            dy_copy(e, B, m, True).wait_send()


def ph_conv_kernel(e, B, parts, steps):
    halves = COLS // TILE

    def taps(it, _):
        hooks(it, steps)
        j = it // 7
        a = it % 7

        def body(k, dk):
            m = parts.start + k // halves
            c0 = k % halves * TILE
            dk = list(dk)
            at = j * NPOS + m * POS + c0 * OWN
            xs = [B.xc[pl.ds(pl.multiple_of(at + OWN * c, OWN), OWN), :] for c in range(TILE)]
            for c in range(TILE + 6):
                d = B.big[pl.ds(xrow(j, m) + (c0 + c) * SUB + a, OWN), :]
                for b in range(7):
                    if 0 <= c - b < TILE:
                        dk[b] = dk[b] + d * xs[c - b]
            return tuple(dk)

        zero = jnp.zeros((OWN, LANES), F32)
        dk = lax.fori_loop(0, halves * len(parts), body, (zero,) * 7)
        for b in range(7):
            tap = (6 - a) * 7 + 6 - b
            B.sg[pl.ds(tap * J + j, 1), :] += jnp.sum(dk[b], 0, keepdims=True)
        return 0

    lax.fori_loop(0, 7 * J, taps, 0)


def ph_conv_input(e, B, steps):
    halves = COLS // TILE

    def body(it, _):
        m = it // halves
        c0 = it % halves * TILE
        for j in range(J):
            hooks(it, {k // J: v for k, v in steps.items() if k % J == j})
            at = j * NPOS + m * POS + c0 * OWN
            acc = [B.z[pl.ds(pl.multiple_of(at + OWN * c, OWN), OWN), :] for c in range(TILE)]
            acc = conv_tile(B, m, j, c0, TILE, acc, True)
            for c in range(TILE):
                B.dx[pl.ds(pl.multiple_of(at + OWN * c, OWN), OWN), :] = acc[c]
        return 0

    lax.fori_loop(0, MICRO * halves, body, 0)


def ph_small_fill(e, B):
    for k in range(HID // LANES):
        B.sg[SG_CUP + k : SG_CUP + k + 1, :] = jnp.sum(B.acup[:, LANES * k : LANES * (k + 1)], 0, keepdims=True)
    for v in range(7):
        for j in range(J):
            row = SG_VEC + v * J + j
            B.sg[row : row + 1, :] = jnp.sum(B.acc[v, :, LANES * j : LANES * (j + 1)], 0, keepdims=True)


def out_copy(e, B, m, k, d):
    j = lax.rem(e.i + d, GROUP)
    cols = pl.ds(TILE * k, TILE)
    return remote(
        e,
        B.xg.at[m, pl.ds(3 + 2 * j, 2), cols],
        B.fo.at[m, e.i, :, cols],
        B.s_out.at[m, k, d],
        B.r_out.at[m, k, d],
        r=e.g * GROUP + j,
    )


def own_out_copy(e, B, m, k):
    cols = pl.ds(TILE * k, TILE)
    return pltpu.make_async_copy(
        B.xg.at[m, pl.ds(3 + 2 * e.i, 2), cols], B.fo.at[m, e.i, :, cols], B.s_outown.at[m, k]
    )


def out_send(e, B, m, k):
    for row in range(OWN):
        for j in range(J):
            v = B.dx[pl.ds(j * NPOS + m * POS + k * TILE * OWN + row, TILE, stride=OWN), :]
            B.xg[m, 3 + row, TILE * k : TILE * (k + 1), LANES * j : LANES * (j + 1)] = v.astype(BF16)
    own_out_copy(e, B, m, k).start()
    for d in (2, 3, 1):
        out_copy(e, B, m, k, d).start()


def ph_out_wait(e, B):
    for m in range(MICRO):
        for k in range(COLS // TILE):
            own_out_copy(e, B, m, k).wait()
            for d in range(1, GROUP):
                out_copy(e, B, m, k, d).wait()


PARTS = 4
PIECE = (144, 144, 288, 288)
START = (ROW_DOWN, ROW_DOWN + 16 * 144, ROW_UP, ROW_UP)


def rs_first(e, B, f):
    c = e.i % 2
    return remote(e, B.gb.at[f, :, :, 1 - c], B.ra1.at[f], B.s_rs.at[f, 0], B.r_rs.at[f, 0], r=e.r + 1 - 2 * c)


def rs_second(e, B, f):
    to = e.g * GROUP + lax.rem(e.i + 2, GROUP)
    return remote(e, B.sa2.at[f], B.ra2.at[f], B.s_rs.at[f, 1], B.r_rs.at[f, 1], r=to)


def group_of(e, q):
    return q * (e.G // 4)


def rs_third(e, B, f, q):
    to = group_of(e, q)
    d = lax.rem(to - e.g + e.G, e.G)
    return remote(e, B.sc.at[f, q], B.rc.at[f, d], B.s_rc.at[f, q], B.r_rc.at[f, d], r=to * GROUP + e.i)


def rs_third_wait(e, B, f, d):
    return remote(e, B.sc.at[f, 0], B.rc.at[f, d], B.s_rc.at[f, 0], B.r_rc.at[f, d], r=lax.rem(e.r + GROUP, e.n))


def rs_fourth(e, B, f, d):
    return remote(e, B.rb.at[f, 0], B.rb.at[f, d], B.s_rb.at[f, d], B.r_rb.at[f, d], b=lax.rem(e.b + d, e.nb))


def ends_here(e, body):
    if e.G == 4:
        body()
    else:
        pl.when(e.g % (e.G // 4) == 0)(body)


def rs_step1(e, B, f):
    rs_first(e, B, f).start()


def rs_step2(e, B, f):
    x, c = e.i // 2, e.i % 2
    rs_first(e, B, f).wait_recv()
    for q in range(4):
        B.sa2[f, q] = (B.gb[f, q, 1 - x, c].astype(F32) + B.ra1[f, q, 1 - x].astype(F32)).astype(BF16)
    rs_second(e, B, f).start()
    for q in range(4):
        B.h1[f, q] = B.gb[f, q, x, c].astype(F32) + B.ra1[f, q, x].astype(F32)


def rs_step3(e, B, f):
    rs_second(e, B, f).wait_recv()
    for q in range(4):
        B.h1[f, q] = B.h1[f, q] + B.ra2[f, q].astype(F32)
        B.sc[f, q] = B.h1[f, q].astype(BF16)
    for q in range(4):

        @pl.when(e.g != group_of(e, q))
        def _(q=q):
            rs_third(e, B, f, q).start()


def rs_step4(e, B, f):
    def body():
        total = B.h1[f, e.g // (e.G // 4)]
        for d in range(1, e.G):
            rs_third_wait(e, B, f, d).wait_recv()
            total = total + B.rc[f, d].astype(F32)
        B.rb[f, 0] = total.astype(BF16)
        for d in range(1, e.nb):
            rs_fourth(e, B, f, d).start()

    ends_here(e, body)


def piece_owners(e, f):
    start = START[f] + PIECE[f] * (e.g // (e.G // 4) * 4 + e.i)
    return start // e.slab, (start + PIECE[f] - 1) // e.slab


def own_slot(B, f, slot):
    return B.ro.at[f, slot] if f < 2 else B.ro_up.at[f - 2, slot]


def own_copy(e, B, f, k, owner):
    slot = lax.rem(e.g // (e.G // 4) * 4 + e.i, 16 if f < 2 else 8)
    return remote(e, B.fp.at[f], own_slot(B, f, slot), B.s_ro.at[f, k], B.r_ro.at[f, slot], r=owner)


def own_wait(e, B, f, slot, home):
    remote(e, B.fp.at[f], own_slot(B, f, slot), B.s_ro.at[f, 0], B.r_ro.at[f, slot], r=home).wait_recv()


def rs_step5(e, B, f):
    def body():
        for d in range(1, e.nb):
            rs_fourth(e, B, f, d).wait_recv()
        total = None
        for b in range(e.nb):
            part = B.rb[f, lax.rem(e.b - b + e.nb, e.nb)].astype(F32)
            total = part if total is None else total + part
        B.fp[f] = total.astype(BF16)
        lo, hi = piece_owners(e, f)

        @pl.when(lo != e.r)
        def _():
            own_copy(e, B, f, 0, lo).start()

        @pl.when(jnp.logical_and(hi != lo, hi != e.r))
        def _():
            own_copy(e, B, f, 1, hi).start()

    ends_here(e, body)


def place(B, f, off, tiles):
    for k in range(3):
        for t in range(3):
            for h in range(2):
                unit = 2 * t + h
                tile = tiles[k, t, 8 * h : 8 * h + 8, :].astype(F32)
                if f >= 2:
                    at = pl.ds(MARGIN + off + 96 * k + 6 * (f - 2) + unit, 8, stride=12)
                else:
                    at = pl.ds(MARGIN + off + 48 * k + 24 * (unit // 3) + unit % 3, 8, stride=3)
                B.gf[at, :] = tile


def rs_place(e, B, f):
    for p in range(16):
        off = START[f] + PIECE[f] * p - e.slab * e.r
        home = group_of(e, p // 4) * GROUP + p % 4

        @pl.when(jnp.logical_and(off < e.slab, off + PIECE[f] > 0))
        def _(p=p, off=off, home=home):
            slot = p % (16 if f < 2 else 8)

            @pl.when(e.r != home)
            def _():
                own_wait(e, B, f, slot, home)
                place(B, f, off, B.ro[f, slot] if f < 2 else B.ro_up[f - 2, slot])

            @pl.when(e.r == home)
            def _():
                place(B, f, off, B.fp[f])


def ph_rs_done(e, B):
    for f in range(PARTS):
        rs_first(e, B, f).wait_send()
        rs_second(e, B, f).wait_send()
        for q in range(4):

            @pl.when(e.g != group_of(e, q))
            def _(f=f, q=q):
                rs_third(e, B, f, q).wait_send()

        def body(f=f):
            for d in range(1, e.nb):
                rs_fourth(e, B, f, d).wait_send()
            lo, hi = piece_owners(e, f)

            @pl.when(lo != e.r)
            def _():
                own_copy(e, B, f, 0, lo).wait_send()

            @pl.when(jnp.logical_and(hi != lo, hi != e.r))
            def _():
                own_copy(e, B, f, 1, hi).wait_send()

        ends_here(e, body)


MARGIN = 1792


QUARTER = SG_ROWS // 4


def quarter_of(i):
    return i % 2 * 2 + i // 2


def small_core(e, B):
    c = e.i % 2
    at = pl.ds(pl.multiple_of((1 - c) * 2 * QUARTER, QUARTER), 2 * QUARTER)
    return remote(e, B.sg.at[at], B.sg_core, B.s_sg.at[0], B.r_sg.at[0], r=e.r + 1 - 2 * c)


def small_pair(e, B):
    x = e.i // 2
    at = pl.ds(pl.multiple_of((1 - x) * QUARTER, QUARTER), QUARTER)
    to = e.g * GROUP + lax.rem(e.i + 2, GROUP)
    return remote(e, B.sg_half.at[at], B.sg_pair, B.s_sg.at[1], B.r_sg.at[1], r=to)


def small_line(e, B, d):
    to = lax.rem(e.g + d, e.G)
    return remote(e, B.sg_line.at[0], B.sg_line.at[d], B.s_sgl.at[d], B.r_sgl.at[d], r=to * GROUP + e.i)


def small_batch(e, B, d):
    return remote(e, B.sgb.at[0], B.sgb.at[d], B.s_sgb.at[d], B.r_sgb.at[d], b=lax.rem(e.b + d, e.nb))


def small_back(e, B, d):
    q = quarter_of(e.i)
    to = e.g * GROUP + lax.rem(e.i + d, GROUP)
    at = pl.ds(pl.multiple_of(q * QUARTER, QUARTER), QUARTER)
    return remote(e, B.sga.at[at], B.sga.at[at], B.s_sgg.at[d], B.r_sgg.at[d], r=to)


def small_step1(e, B):
    small_core(e, B).start()


def small_step2(e, B):
    c = e.i % 2
    small_core(e, B).wait_recv()
    B.sg_half[...] = B.sg[pl.ds(pl.multiple_of(c * 2 * QUARTER, QUARTER), 2 * QUARTER), :] + B.sg_core[...]
    small_pair(e, B).start()


def small_step3(e, B):
    x = e.i // 2
    small_pair(e, B).wait_recv()
    B.sg_line[0] = B.sg_half[pl.ds(pl.multiple_of(x * QUARTER, QUARTER), QUARTER), :] + B.sg_pair[...]
    for d in range(1, e.G):
        small_line(e, B, d).start()


def small_step4(e, B):
    for d in range(1, e.G):
        small_line(e, B, d).wait_recv()
    total = None
    for level in range(e.G):
        part = B.sg_line[lax.rem(e.g - level + e.G, e.G)]
        total = part if total is None else total + part
    B.sgb[0] = total
    for d in range(1, e.nb):
        small_batch(e, B, d).start()


def small_step5(e, B):
    for d in range(1, e.nb):
        small_batch(e, B, d).wait_recv()
    total = None
    for b in range(e.nb):
        part = B.sgb[lax.rem(e.b - b + e.nb, e.nb)]
        total = part if total is None else total + part
    B.sga[pl.ds(pl.multiple_of(quarter_of(e.i) * QUARTER, QUARTER), QUARTER), :] = total
    for d in range(1, GROUP):
        small_back(e, B, d).start()


def ph_small_place(e, B):
    for d in range(1, GROUP):
        small_back(e, B, d).wait_recv()
    for first, at, count in ((ROW_K, 0, 49 * J), (ROW_CUP, SG_CUP, HID // LANES), (ROW_VEC, SG_VEC, 7 * J)):
        off = MARGIN + first % e.slab

        @pl.when(e.r == first // e.slab)
        def _(off=off, at=at, count=count):
            B.gf[off : off + count, :] = B.sga[at : at + count, :]


def ph_small_done(e, B):
    small_core(e, B).wait_send()
    small_pair(e, B).wait_send()
    for d in range(1, e.G):
        small_line(e, B, d).wait_send()
    for d in range(1, e.nb):
        small_batch(e, B, d).wait_send()
    for d in range(1, GROUP):
        small_back(e, B, d).wait_send()


def ph_head_grads(e, B):
    parts = GROUP * e.nb
    rows = 16 * parts
    sums = None
    for p in range(parts):
        x = B.pall[p].astype(F32)
        sums = x if sums is None else sums + x
        dd = x[6:9, 0:DOUT]
        B.gp[16 * p : 16 * p + 16, 0:DOUT] = jnp.concatenate([dd, dd, jnp.zeros((10, DOUT), F32)], axis=0).astype(BF16)
        dl = x[9:12, 0:CLSP]
        B.gp[rows + 16 * p : rows + 16 * p + 16, 0:CLSP] = jnp.concatenate(
            [jnp.zeros((6, CLSP), F32), dl, jnp.zeros((7, CLSP), F32)], axis=0
        ).astype(BF16)
    B.psum[...] = sums
    for q in range(4):
        for p in range(parts):
            B.v2[16 * p : 16 * p + 16, :] = B.pall[p, :, C * q : C * (q + 1)].astype(F32)
        for j in range(J):
            t = J * q + j
            B.u[LANES * t : LANES * (t + 1), 0:rows] = B.v2[0:rows, LANES * j : LANES * (j + 1)].T.astype(BF16)
    per = DOUT // LANES
    base = MARGIN - e.slab * e.r

    kc = 288
    low = e.slab * e.r - ROW_DS

    @pl.when(jnp.logical_and(low < 4 * C * per, low + e.slab > 0))
    def _():
        k0 = jnp.clip(low // (16 * per) * 16, 0, 4 * C - kc)
        k0 = pl.multiple_of(k0, 16)
        w = jnp.dot(B.u[pl.ds(k0, kc), 0:rows], B.gp[0:rows, 0:DOUT], preferred_element_type=F32)
        for j in range(per):
            B.gf[pl.ds(base + ROW_DS + per * k0 + j, kc, stride=per), :] = w[:, LANES * j : LANES * (j + 1)]

    low2 = e.slab * e.r - ROW_HEAD

    @pl.when(jnp.logical_and(low2 < DOUT * CLS // LANES, low2 + e.slab > 0))
    def _():
        g0 = jnp.clip(low2 // 125, 0, DOUT // 16 - 16)
        k0 = pl.multiple_of(DOUT + 16 * g0, 16)
        for t in range(8):
            B.big[256 * t : 256 * (t + 1), :] = jnp.dot(
                B.u[pl.ds(k0, 256), 0:rows],
                B.gp[rows : 2 * rows, LANES * t : LANES * (t + 1)],
                preferred_element_type=F32,
            )
        lane = lax.broadcasted_iota(jnp.int32, (16, LANES), 1)
        held = None
        for kk in range(16):
            o = (-CLS * kk) % LANES
            tiles = [B.big[pl.ds(256 * t + kk, 16, stride=16), :] for t in range(8)]
            if o:
                tiles = [pltpu.roll(tile, LANES - o, 1) for tile in tiles]
            for s in range(CLS * kk // LANES, (CLS * kk + CLS - 1) // LANES + 1):
                t0 = (LANES * s - CLS * kk) // LANES
                if o == 0:
                    value = tiles[t0]
                elif t0 < 0:
                    value = tiles[0]
                elif t0 + 1 > 7:
                    value = tiles[t0]
                else:
                    value = jnp.where(lane < LANES - o, tiles[t0], tiles[t0 + 1])
                border = CLS * kk - LANES * s
                if border > 0:
                    value = jnp.where(lane < border, held, value)
                if LANES * (s + 1) > CLS * (kk + 1):
                    held = value
                else:
                    B.gf[pl.ds(base + ROW_HEAD + 125 * g0 + s, 16, stride=125), :] = value

    @pl.when(e.r == ROW_OUT // e.slab)
    def _():
        off = MARGIN + ROW_OUT % e.slab
        for j in range(per):
            at = slice(LANES * j, LANES * (j + 1))
            B.gf[off + j : off + j + 1, :] = B.psum[6:7, at] * e.positions + (
                B.psum[7:8, at] * e.positions + B.psum[8:9, at] * e.positions
            )
            gain = B.psum[12:13, at] + B.psum[13:14, at] + B.psum[14:15, at]
            B.gf[off + per + j : off + per + j + 1, :] = gain
            at = slice(DOUT + LANES * j, DOUT + LANES * (j + 1))
            shift = B.psum[12:13, at] + B.psum[13:14, at] + B.psum[14:15, at]
            B.gf[off + 2 * per + j : off + 2 * per + j + 1, :] = shift

    @pl.when(e.r == ROW_BH // e.slab)
    def _():
        off = MARGIN + ROW_BH % e.slab
        for j in range(CLSP // LANES):
            at = slice(LANES * j, LANES * (j + 1))
            B.gf[off + j : off + j + 1, :] = B.psum[9:10, at] + B.psum[10:11, at] + B.psum[11:12, at]
        rest = FLAT - ROW_BH - CLSP // LANES
        B.gf[off + CLSP // LANES : off + CLSP // LANES + rest, :] = jnp.zeros((rest, LANES), F32)


def norm_copy(e, B, d):
    return remote(e, B.nrm.at[0], B.nrm.at[d], B.s_nrm.at[d], B.r_nrm.at[d], r=lax.rem(e.r + d, e.n))


def squares(v):
    return jnp.sum((v * v).reshape(-1, 8, LANES), 0)


def ph_norm_local(e, B):
    size = 64
    whole = e.slab // size

    def body(k, acc):
        return acc + squares(B.gf[pl.ds(pl.multiple_of(MARGIN + size * k, 8), size), :])

    part = lax.fori_loop(0, whole, body, jnp.zeros((8, LANES), F32))
    v = B.gf[MARGIN + whole * size : MARGIN + e.slab, :]
    B.nrm[0] = part + jnp.broadcast_to(jnp.sum(v * v, 0, keepdims=True) * 0.125, (8, LANES))


def ph_norm(e, B):
    def pieces():
        B.nrm[0] += squares(B.fp[...].astype(F32))

    ends_here(e, pieces)

    @pl.when(e.g == 0)
    def _():
        B.nrm[0] += squares(B.sga[pl.ds(pl.multiple_of(quarter_of(e.i) * QUARTER, QUARTER), QUARTER), :])

    for d in range(1, e.n):
        norm_copy(e, B, d).start()


def ph_norm_wait(e, B):
    for d in range(1, e.n):
        norm_copy(e, B, d).wait_recv()
    total = None
    for k in range(e.n):
        part = B.nrm[lax.rem(e.r - k + e.n, e.n)]
        total = part if total is None else total + part
    square = jnp.sum(jnp.sum(total, 0, keepdims=True), 1, keepdims=True)
    B.o_norm[...] = jnp.broadcast_to(jnp.sqrt(square), (8, LANES))
    loss = B.psum[15:16, :]
    loss = loss[:, 0:LANES] + loss[:, LANES : 2 * LANES] + loss[:, 2 * LANES : 3 * LANES]
    B.o_loss[...] = jnp.broadcast_to(loss, (8, LANES))
    for d in range(1, e.n):
        norm_copy(e, B, d).wait_send()


def buffers(e):
    n, G, nb, slab = e.n, e.G, e.nb, e.slab
    tiles = (3, 3, 16, LANES)
    parts = GROUP * nb
    V = pltpu.VMEM
    D = pltpu.SemaphoreType.DMA
    return dict(
        gw=V((n, 2, e.half, LANES), BF16),
        tab=V((TAB_ROWS, LANES), F32),
        big=V((10816, LANES), F32),
        dx=V((8 * DOUT, LANES), F32),
        wup=V((C, HID), BF16),
        wdn=V((HID, C), BF16),
        wds=V((4 * C, DOUT), BF16),
        wh=V((DOUT, CLSP), BF16),
        xg=V((MICRO, 14, COLS, C), BF16),
        xc=V((J * NPOS, LANES), F32),
        kb=V((49 * J, 8, LANES), F32),
        v1=V((NPOS, C), F32),
        rs1=V((NPOS, LANES), F32),
        v2=V((NPOS, C), F32),
        rs2=V((NPOS, LANES), F32),
        n=V((NPOS, C), BF16),
        u=V((NPOS, HID), BF16),
        gp=V((NPOS, HID), BF16),
        z=V((J * NPOS, LANES), F32),
        dz=V((NPOS, C), BF16),
        ps=V((MICRO, 2, OWN, C), F32),
        vs=V((MICRO, 2, OWN, C), F32),
        sl=V((32, C), F32),
        sr=V((G, 32, C), F32),
        dn2=V((32, C), F32),
        dnt=V((MICRO, 2, OWN, C), F32),
        pb=V((16, 4 * C), F32),
        pall=V((parts, 16, 4 * C), BF16),
        psum=V((16, 4 * C), F32),
        acc=V((7, 8, C), F32),
        acup=V((8, HID), F32),
        hs=V((MICRO, 2, 3, COLS, C), BF16),
        hr=V((MICRO, 2, 3, COLS, C), BF16),
        gb=V((PARTS, 4, 2, 2) + tiles, BF16),
        ra1=V((PARTS, 4, 2) + tiles, BF16),
        sa2=V((PARTS, 4) + tiles, BF16),
        ra2=V((PARTS, 4) + tiles, BF16),
        h1=V((PARTS, 4) + tiles, F32),
        sc=V((PARTS, 4) + tiles, BF16),
        rc=V((PARTS, G) + tiles, BF16),
        rb=V((PARTS, nb) + tiles, BF16),
        fp=V((PARTS,) + tiles, BF16),
        ro=V((2, 16) + tiles, BF16),
        ro_up=V((2, 8) + tiles, BF16),
        gf=V((MARGIN + slab + MARGIN, LANES), F32),
        sg=V((SG_ROWS, LANES), F32),
        sg_core=V((2 * QUARTER, LANES), F32),
        sg_half=V((2 * QUARTER, LANES), F32),
        sg_pair=V((QUARTER, LANES), F32),
        sg_line=V((G, QUARTER, LANES), F32),
        sgb=V((nb, QUARTER, LANES), F32),
        sga=V((SG_ROWS, LANES), F32),
        nrm=V((n, 8, LANES), F32),
        s_own=D((1,)),
        s_feat=D((MICRO, GROUP)),
        r_feat=D((MICRO, GROUP)),
        s_halo=D((2, MICRO)),
        r_halo=D((2, MICRO)),
        s_tab=D((len(TABLES), G)),
        s_tabg=D((len(TABLES), GROUP)),
        r_tab=D((len(TABLES),)),
        s_line=D((2, G)),
        r_line=D((G, CHUNKS)),
        s_pair=D((G,)),
        r_pair=D((G, CHUNKS)),
        s_row=D((2, G)),
        r_row=D((2, G, CHUNKS)),
        s_core=D((4, G)),
        r_core=D((4, G, CHUNKS)),
        s_patch=D((G,)),
        r_patch=D((G,)),
        s_pb=D((nb,)),
        r_pb=D((nb,)),
        s_pg=D((GROUP,)),
        r_pg=D((GROUP,)),
        s_dy=D((2, MICRO)),
        r_dy=D((2, MICRO)),
        s_out=D((MICRO, 2, GROUP)),
        r_out=D((MICRO, 2, GROUP)),
        s_outown=D((MICRO, 2)),
        s_rs=D((PARTS, 2)),
        r_rs=D((PARTS, 2)),
        s_rc=D((PARTS, 4)),
        r_rc=D((PARTS, G)),
        s_rb=D((PARTS, nb)),
        r_rb=D((PARTS, nb)),
        s_ro=D((PARTS, 2)),
        r_ro=D((PARTS, 16)),
        s_sg=D((2,)),
        r_sg=D((2,)),
        s_sgl=D((G,)),
        r_sgl=D((G,)),
        s_sgg=D((GROUP,)),
        r_sgg=D((GROUP,)),
        s_sgb=D((nb,)),
        r_sgb=D((nb,)),
        s_nrm=D((n,)),
        r_nrm=D((n,)),
    )


def ph_clear(e, B):
    B.sg[...] = jnp.zeros_like(B.sg)
    B.gf[...] = jnp.zeros_like(B.gf)


def ph_result(e, B):
    B.o_grad[...] = B.gf[MARGIN : MARGIN + e.slab, :]


def schedule(e, B):
    def do(step, *args):
        return lambda: step(e, B, *args)

    def level_of(row):
        return row // e.slab // GROUP

    up = range(0, level_of(ROW_CUP - 1) + 1)
    down = range(up.stop, level_of(ROW_VEC - 1) + 1)
    rest = range(down.stop, e.G)
    ph_barrier_signal(e, B)
    ph_cast(e, B)
    ph_feat_zero(e, B)
    ph_clear(e, B)
    ph_barrier_wait(e, B)
    every = range(CHUNKS)
    one, two = range(0, CHUNKS // 2), range(CHUNKS // 2, CHUNKS)

    def hops(some):
        return range(max(max(level, e.G - 1 - level) for level in some) + 1)

    def steps(step, some, which, chunks):
        return [do(step, some, h, chunks) for h in which]

    ph_tables_start(e, B)
    feat_start(e, B, 0)
    line_send(e, B, range(e.G), every)
    tables_forward(e, B, (0, 2))
    feat_start(e, B, 1)
    line_step(e, B, up, 1, every)
    halo_start(e, B, 0)
    feat_start(e, B, 2)
    for h in hops(up)[2:3]:
        line_step(e, B, up, h, every)
    for h in hops(up)[:3]:
        pair_step(e, B, up, h, every)
    tables_wait(e, B, (0, 2))
    ph_taps(e, B)
    ph_conv_fwd(
        e,
        B,
        {
            0: [do(halo_wait, 0), do(transpose, 0)],
            1: [do(halo_start, 1)] + steps(line_step, rest, [1], one),
            2: steps(line_step, rest, [1], two) + steps(line_step, up, hops(up)[3:], every) + steps(pair_step, up, hops(up)[3:], every),
            4: [do(halo_start, 2)] + steps(line_step, down, [1], every) + steps(pair_step, down, hops(down)[:2], every),
            6: [do(halo_wait, 1), do(transpose, 1)],
            7: [do(tables_forward, (1, 3, 4))] + steps(row_step, up, hops(up), one),
            8: steps(line_step, rest, hops(rest)[2:3], one) + steps(pair_step, rest, hops(rest)[:2], every),
            9: steps(row_step, up, hops(up), two),
            10: steps(line_step, rest, hops(rest)[2:3], two),
            11: steps(line_step, down, hops(down)[2:], every)
            + steps(pair_step, down, hops(down)[2:], every)
            + steps(pair_step, rest, hops(rest)[2:3], every),
            12: [do(halo_wait, 2), do(transpose, 2)],
            13: steps(core_step, up, hops(up), one) + steps(row_step, down, hops(down)[:2], every),
            15: steps(line_step, rest, hops(rest)[3:], every) + steps(pair_step, rest, hops(rest)[3:], every),
            16: steps(row_step, rest, [0], every),
            17: steps(core_step, up, hops(up), two),
        },
    )
    ph_norm_one(e, B)
    tables_wait(e, B, (1, 3, 4))
    for h in hops(down)[2:]:
        row_step(e, B, down, h, every)
    row_step(e, B, rest, 1, every)
    gather_ready(e, B, up)
    ph_weights_up(e, B)
    ph_mlp_up(
        e,
        B,
        {
            0: steps(row_step, rest, hops(rest)[2:3], every),
            2: steps(core_step, down, hops(down)[:2], every) + steps(core_step, rest, [0], every),
            3: steps(row_step, rest, hops(rest)[3:], every),
            4: steps(core_step, down, hops(down)[2:], every),
            5: steps(core_step, rest, [1], every),
        },
    )
    gather_ready(e, B, down)
    ph_weights_down(e, B)
    ph_mlp_down(
        e,
        B,
        {
            1: steps(core_step, rest, hops(rest)[2:3], every),
            4: steps(core_step, rest, hops(rest)[3:], every),
        },
    )
    ph_patch_local(e, B)
    patch_start(e, B)
    gather_ready(e, B, rest)
    ph_weights_head(e, B)
    patch_wait(e, B)
    ph_head(e, B)
    ph_payload_batch(e, B)
    ph_dy_edges(e, B)
    ph_bwd_one(e, B)
    for f in (0, 1):
        wgrad_down(e, B, f)
        rs_step1(e, B, f)
    ph_bwd_two(
        e,
        B,
        {
            1: [do(ph_payload_group)],
            2: [do(dy_send, 0), do(rs_step2, 0)],
            3: [do(rs_step2, 1)],
            4: [do(dy_send, 1)],
        },
    )
    dy_send(e, B, 2)
    for f in (2, 3):
        wgrad_up(e, B, f)
        rs_step1(e, B, f)
    dy_take(e, B, 0)
    dy_take(e, B, 1)
    rs_step3(e, B, 0)
    ph_conv_kernel(
        e,
        B,
        range(0, MICRO - 1),
        {
            4: [do(rs_step3, 1)],
            7: [do(rs_step2, 2)],
            10: [do(rs_step2, 3)],
            13: [do(rs_step4, 0)],
            18: [do(rs_step4, 1)],
        },
    )
    dy_take(e, B, MICRO - 1)
    ph_conv_kernel(
        e,
        B,
        range(MICRO - 1, MICRO),
        {
            2: [do(rs_step3, 2)],
            10: [do(rs_step5, 0)],
            18: [do(rs_step3, 3)],
        },
    )
    ph_small_fill(e, B)
    small_step1(e, B)
    ph_feat_done(e, B)
    ph_conv_input(
        e,
        B,
        {
            0: [do(rs_step5, 1)],
            4: [do(small_step2), do(out_send, 0, 0)],
            6: [do(rs_step4, 2), do(out_send, 0, 1)],
            8: [do(small_step3)],
            9: [do(rs_step4, 3), do(out_send, 1, 0)],
            10: [do(rs_step5, 2)],
            11: [do(ph_payload_wait), do(ph_head_grads), do(ph_norm_local)],
            12: [do(small_step4), do(out_send, 1, 1)],
            13: [do(rs_place, 0), do(rs_place, 1), do(rs_step5, 3)],
            15: [do(out_send, 2, 0)],
            16: [do(small_step5), do(ph_norm), do(rs_place, 2)],
        },
    )
    rs_place(e, B, 3)
    out_send(e, B, 2, 1)
    ph_small_place(e, B)
    ph_result(e, B)
    ph_tables_done(e, B)
    ph_gather_done(e, B)
    ph_dy_done(e, B)
    ph_rs_done(e, B)
    ph_small_done(e, B)
    ph_norm_wait(e, B)
    ph_out_wait(e, B)


def step_kernel(e, names, *refs):
    B = Env()
    for name, ref in zip(names, refs):
        setattr(B, name, ref)
    here(e)
    schedule(e, B)


def train_step(e, features, mask, labels, params):
    bufs = buffers(e)
    names = ["mask", "labels", "features", "params", "o_grad", "o_norm", "o_loss", "fo"] + list(bufs)
    return pl.pallas_call(
        functools.partial(step_kernel, e, names),
        out_shape=(
            jax.ShapeDtypeStruct((e.slab, LANES), F32),
            jax.ShapeDtypeStruct((8, LANES), F32),
            jax.ShapeDtypeStruct((8, LANES), F32),
            jax.ShapeDtypeStruct((MICRO, GROUP, 2, COLS, C), BF16),
        ),
        in_specs=[
            pl.BlockSpec(memory_space=pltpu.SMEM),
            pl.BlockSpec(memory_space=pltpu.SMEM),
            pl.BlockSpec(memory_space=pl.ANY),
            pl.BlockSpec(memory_space=pltpu.VMEM),
        ],
        out_specs=(
            pl.BlockSpec(memory_space=pltpu.VMEM),
            pl.BlockSpec(memory_space=pltpu.VMEM),
            pl.BlockSpec(memory_space=pltpu.VMEM),
            pl.BlockSpec(memory_space=pl.ANY),
        ),
        scratch_shapes=list(bufs.values()),
        compiler_params=pltpu.CompilerParams(collective_id=0, has_side_effects=True, vmem_limit_bytes=64 * MB - 65536),
        name="train_step",
    )(mask, labels, features, params)


def update_kernel(e, norm, loss, grad, params, m1, m2, out, o_norm, o_loss, new_params, first, second, feats, *scratch):
    g, p, a, b, fin, fout, s_in, s_out, s_feat, s_fout = scratch
    parts = 4
    size = e.slab // parts // 8 * 8
    spans = [(k * size, size if k < parts - 1 else e.slab - k * size) for k in range(parts)]
    copy = pltpu.make_async_copy
    ins = []
    for k, (at, count) in enumerate(spans):
        for q, (src, dst) in enumerate(((grad, g), (params, p), (m1, a), (m2, b))):
            ins.append(copy(src.at[pl.ds(at, count)], dst.at[pl.ds(at, count)], s_in.at[k, q]))
            ins[-1].start()
    fins = [copy(out.at[k], fin.at[k], s_feat.at[k]) for k in range(MICRO)]
    for cp in fins:
        cp.start()
    o_norm[0, 0] = jnp.max(norm[...])
    o_loss[0, 0] = jnp.max(loss[...])
    scale = jnp.minimum(1.0, CLIP / (norm[0:1, 0:1] + 1e-06))
    outs = []
    for k, (at, count) in enumerate(spans):
        for q in range(4):
            ins[4 * k + q].wait()
        rows = slice(at, at + count)
        clipped = g[rows, :] * scale
        one = BETA_ONE * a[rows, :] + (1.0 - BETA_ONE) * clipped
        two = BETA_TWO * b[rows, :] + (1.0 - BETA_TWO) * clipped * clipped
        a[rows, :] = one
        b[rows, :] = two
        ratio = one / (1.0 - BETA_ONE**STEP) / (jnp.sqrt(two / (1.0 - BETA_TWO**STEP)) + EPS_ADAM)
        p[rows, :] = p[rows, :] - RATE * (ratio + DECAY * p[rows, :])
        for q, (src, dst) in enumerate(((p, new_params), (a, first), (b, second))):
            outs.append(copy(src.at[pl.ds(at, count)], dst.at[pl.ds(at, count)], s_out.at[k, q]))
            outs[-1].start()
        if k < MICRO:
            fins[k].wait()
            fout[k] = fin[k].astype(F32)
            outs.append(copy(fout.at[k], feats.at[k], s_fout.at[k]))
            outs[-1].start()
    for cp in outs:
        cp.wait()


def update(e, grad, norm, loss, params, m1, m2, out):
    flat = jax.ShapeDtypeStruct((e.slab, LANES), F32)
    scalar = jax.ShapeDtypeStruct((1, 1), F32)
    shape = (MICRO, GROUP, 2, COLS, C)
    near, far, one = (pl.BlockSpec(memory_space=k) for k in (pltpu.VMEM, pl.ANY, pltpu.SMEM))
    D = pltpu.SemaphoreType.DMA
    return pl.pallas_call(
        functools.partial(update_kernel, e),
        in_specs=[near, near, far, far, far, far, far],
        out_specs=(one, one, far, far, far, far),
        out_shape=(scalar, scalar, flat, flat, flat, jax.ShapeDtypeStruct(shape, F32)),
        scratch_shapes=[pltpu.VMEM((e.slab, LANES), F32)] * 4
        + [pltpu.VMEM(shape, BF16), pltpu.VMEM(shape, F32), D((4, 4)), D((4, 3)), D((MICRO,)), D((MICRO,))],
        compiler_params=pltpu.CompilerParams(vmem_limit_bytes=64 * MB - 65536),
        name="update",
    )(norm, loss, grad, params, m1, m2, out)


def local(e, features, drop_mask, labels, params, moment1, moment2):
    flat = [v.reshape(e.slab, LANES) for v in (params, moment1, moment2)]
    grad, norm, loss, out = train_step(e, features, drop_mask, labels, flat[0])
    norm, loss, new_params, first, second, feats = update(e, grad, norm, loss, *flat, out)
    size = e.slab * LANES
    return (
        new_params.reshape(size),
        first.reshape(size),
        second.reshape(size),
        loss.reshape(()),
        norm.reshape(()),
        feats,
    )


def solution(mesh):
    e = Env()
    e.n = mesh.shape["rows"]
    e.nb = mesh.shape["batch"]
    e.G = e.n // GROUP
    e.slab = FLAT // e.n
    e.half = (e.slab + 31) // 32 * 16
    e.positions = float(e.n * COLS // 2)
    e.inv_count = 1.0 / (MICRO * GROUP * e.nb)
    return jax.shard_map(
        functools.partial(local, e),
        mesh=mesh,
        in_specs=(
            P(None, "batch", "rows", None, None),
            P(None, "batch"),
            P(None, "batch"),
            P("rows"),
            P("rows"),
            P("rows"),
        ),
        out_specs=(P("rows"), P("rows"), P("rows"), P(), P(), P(None, "batch", "rows", None, None)),
        check_vma=False,
    )
```

```python
import functools

import jax
import jax.numpy as jnp
from jax import lax
from jax.experimental import pallas as pl
from jax.experimental.pallas import tpu as pltpu
from jax.sharding import PartitionSpec as P

C = 384
HID = 1536
DOUT = 768
CLS = 1000
MICRO = 3
STEP = 10
P_SIZE = 3153920
KEEP = 0.8
CLIP = 0.01
RATE = 0.05
BETA_ONE = 0.9
BETA_TWO = 0.999
DECAY = 0.05
EPS_ADAM = 1e-08
EPS_NORM = 1e-06

MESH = pl.DeviceIdType.MESH
F32 = jnp.float32
BF16 = jnp.bfloat16
MB = 1 << 20

LANES = 128
J = C // LANES
GROUP = 4
OWN = 8
COLS = 64
PADC = COLS + 6
SUB = 16
POS = COLS * OWN
NPOS = MICRO * POS
FLAT = P_SIZE // LANES
ROW_K = 0
ROW_UP = 49 * J
ROW_CUP = ROW_UP + C * HID // LANES
ROW_DOWN = ROW_CUP + HID // LANES
ROW_VEC = ROW_DOWN + C * HID // LANES
ROW_DS = ROW_VEC + 7 * J
ROW_OUT = ROW_DS + 4 * C * DOUT // LANES
ROW_HEAD = ROW_OUT + 3 * DOUT // LANES
ROW_BH = ROW_HEAD + DOUT * CLS // LANES
TABLES = (
    (ROW_K, 49 * J, 0),
    (ROW_CUP, HID // LANES, 152),
    (ROW_VEC, 7 * J, 168),
    (ROW_OUT, 3 * DOUT // LANES, 192),
    (ROW_BH, FLAT - ROW_BH, 216),
)
TAB_ROWS = 232
TAB_SPAN = (152, 16, 24, 24, 16)
T_CUP, T_VEC, T_OUT, T_BH = 152, 168, 192, 216
SG_ROWS = 320
SG_VEC, SG_CUP = 160, 240
CLSP = 1024


class Env:
    pass


def xrow(j, m):
    return (j * MICRO + m) * PADC * SUB


def rows_of(refs, row, count):
    return refs[row : row + count, :]


def lane_row(ref, row, count):
    return jnp.concatenate([ref[row + k : row + k + 1, :] for k in range(count)], axis=1)


def ln_parts(blocks, width):
    total = blocks[0]
    for block in blocks[1:]:
        total = total + block
    mean = jnp.sum(total, -1, keepdims=True) * (1.0 / width)
    centred = [block - mean for block in blocks]
    square = centred[0] * centred[0]
    for block in centred[1:]:
        square = square + block * block
    spread = jnp.sum(square, -1, keepdims=True) * (1.0 / width)
    scale = lax.rsqrt(spread + EPS_NORM)
    return [block * scale for block in centred], scale


def here(e):
    e.r = lax.axis_index("rows")
    e.b = lax.axis_index("batch")
    e.g = e.r // GROUP
    e.i = e.r % GROUP
    e.h = e.b % 2


def dev(e, r=None, b=None):
    return {"rows": e.r if r is None else r, "batch": e.b if b is None else b}


def remote(e, src, dst, send, recv, r=None, b=None):
    return pltpu.make_async_remote_copy(
        src, dst, send, recv, device_id=(e.r if r is None else r, e.b if b is None else b), device_id_type=MESH
    )


def ph_barrier_signal(e, B):
    barrier = pltpu.get_barrier_semaphore()
    for d in range(1, e.n):
        pl.semaphore_signal(barrier, inc=1, device_id=(lax.rem(e.r + d, e.n), e.b), device_id_type=MESH)
    for d in range(1, e.nb):
        pl.semaphore_signal(barrier, inc=1, device_id=(e.r, lax.rem(e.b + d, e.nb)), device_id_type=MESH)


def ph_barrier_wait(e, B):
    pl.semaphore_wait(pltpu.get_barrier_semaphore(), e.n - 1 + e.nb - 1)


def feat_copy(e, B, m, d):
    j = lax.rem(e.i + d, GROUP)
    return remote(
        e,
        B.features.at[m, j],
        B.xg.at[m, pl.ds(3 + 2 * e.i, 2)],
        B.s_feat.at[m, d],
        B.r_feat.at[m, d],
        r=e.g * GROUP + j,
    )


def feat_own(e, B):
    return pltpu.make_async_copy(B.features.at[:, e.i], B.xg.at[:, pl.ds(3 + 2 * e.i, 2)], B.s_own.at[0])


def feat_start(e, B, m):
    if m == 0:
        feat_own(e, B).start()
    for d in (2, 3, 1):
        feat_copy(e, B, m, d).start()


def ph_feat_zero(e, B):
    zero = jnp.zeros((MICRO, 3, COLS, C), BF16)

    @pl.when(e.g == 0)
    def _():
        B.xg[:, 0:3] = zero

    @pl.when(e.g == e.G - 1)
    def _():
        B.xg[:, 11:14] = zero


def halo_copy(e, B, m, up):
    if up:
        return remote(e, B.xg.at[m, 8:11], B.xg.at[m, 0:3], B.s_halo.at[1, m], B.r_halo.at[1, m], r=e.r + GROUP)
    return remote(e, B.xg.at[m, 3:6], B.xg.at[m, 11:14], B.s_halo.at[0, m], B.r_halo.at[0, m], r=e.r - GROUP)


def halo_start(e, B, m):
    if m == 0:
        feat_own(e, B).wait()
    for d in range(1, GROUP):
        feat_copy(e, B, m, d).wait_recv()

    @pl.when(e.g > 0)
    def _():
        halo_copy(e, B, m, False).start()

    @pl.when(e.g < e.G - 1)
    def _():
        halo_copy(e, B, m, True).start()


def halo_wait(e, B, m):
    @pl.when(e.g < e.G - 1)
    def _():
        halo_copy(e, B, m, False).wait_recv()

    @pl.when(e.g > 0)
    def _():
        halo_copy(e, B, m, True).wait_recv()


def ph_feat_done(e, B):
    for m in range(MICRO):
        for d in range(1, GROUP):
            feat_copy(e, B, m, d).wait_send()

        @pl.when(e.g > 0)
        def _(m=m):
            halo_copy(e, B, m, False).wait_send()

        @pl.when(e.g < e.G - 1)
        def _(m=m):
            halo_copy(e, B, m, True).wait_send()


def ph_cast(e, B):
    for h in range(2):
        count = e.half if h == 0 else e.slab - e.half
        whole = count // 16 * 16
        B.gw[e.r, h, 0:whole, :] = B.params[h * e.half : h * e.half + whole, :].astype(BF16)
        rest = count - whole
        if whole < e.half:
            parts = [jnp.zeros((e.half - whole - rest, LANES), F32)]
            if rest:
                parts = [B.params[e.slab - rest : e.slab, :]] + parts
            B.gw[e.r, h, whole : e.half, :] = jnp.concatenate(parts, axis=0).astype(BF16)
    for k, (first, count, place) in enumerate(TABLES):
        off = first % e.slab

        @pl.when(e.r == first // e.slab)
        def _(off=off, count=count, place=place):
            B.tab[place : place + count, :] = B.params[off : off + count, :]


def table_line(e, B, k, d):
    first, count, place = TABLES[k]
    owner = first // e.slab
    part = pl.ds(place, TAB_SPAN[k])
    return remote(e, B.tab.at[part], B.tab.at[part], B.s_tab.at[k, d], B.r_tab.at[k], r=lax.rem(owner + GROUP * d, e.n))


def table_group(e, B, k, d):
    first, count, place = TABLES[k]
    part = pl.ds(place, TAB_SPAN[k])
    to = e.g * GROUP + lax.rem(e.i + d, GROUP)
    return remote(e, B.tab.at[part], B.tab.at[part], B.s_tabg.at[k, d], B.r_tab.at[k], r=to)


def ph_tables_start(e, B):
    for k, (first, count, place) in enumerate(TABLES):
        owner = first // e.slab

        @pl.when(e.r == owner)
        def _(k=k):
            for d in range(1, e.G):
                table_line(e, B, k, d).start()
            for d in range(1, GROUP):
                table_group(e, B, k, d).start()


def tables_forward(e, B, some):
    for k in some:
        owner = TABLES[k][0] // e.slab

        @pl.when(jnp.logical_and(e.i == owner % GROUP, e.r != owner))
        def _(k=k):
            table_line(e, B, k, 1).wait_recv()
            for d in range(1, GROUP):
                table_group(e, B, k, d).start()


def tables_wait(e, B, some):
    for k in some:
        owner = TABLES[k][0] // e.slab

        @pl.when(e.i != owner % GROUP)
        def _(k=k):
            table_group(e, B, k, 1).wait_recv()


def ph_tables_done(e, B):
    for k, (first, count, place) in enumerate(TABLES):
        owner = first // e.slab

        @pl.when(e.r == owner)
        def _(k=k):
            for d in range(1, e.G):
                table_line(e, B, k, d).wait_send()

        @pl.when(e.i == owner % GROUP)
        def _(k=k):
            for d in range(1, GROUP):
                table_group(e, B, k, d).wait_send()


CHUNKS = 4


def chunk_of(e, c):
    if c is None:
        return pl.ds(0, e.half)
    tiles = e.half // 16
    cuts = [(tiles * k + CHUNKS - 1) // CHUNKS * 16 for k in range(CHUNKS + 1)]
    return pl.ds(cuts[c], cuts[c + 1] - cuts[c])


def half_ref(e, B, slot, h, c):
    return B.gw.at[slot, h, chunk_of(e, c)]


def line_copy(e, B, level, up, c):
    ref = half_ref(e, B, level * GROUP + e.i, e.h, c)
    k = 0 if up else 1
    return remote(e, ref, ref, B.s_line.at[k, level], B.r_line.at[level, c or 0], r=e.r + GROUP if up else e.r - GROUP)


def pair_copy(e, B, level, c):
    ref = half_ref(e, B, level * GROUP + e.i, e.h, c)
    to = e.g * GROUP + lax.rem(e.i + 2, GROUP)
    return remote(e, ref, ref, B.s_pair.at[level], B.r_pair.at[level, c or 0], r=to)


def row_copy(e, B, level, other, c):
    i = lax.rem(e.i + 2, GROUP) if other else e.i
    ref = half_ref(e, B, level * GROUP + i, e.h, c)
    k = int(other)
    return remote(e, ref, ref, B.s_row.at[k, level], B.r_row.at[k, level, c or 0], b=e.b + 1 - 2 * e.h)


def core_copy(e, B, level, other, mine, c):
    i = lax.rem(e.i + 2, GROUP) if other else e.i
    ref = half_ref(e, B, level * GROUP + i, e.h if mine else 1 - e.h, c)
    k = 2 * int(other) + int(mine)
    sib = e.g * GROUP + e.i + 1 - 2 * (e.i % 2)
    return remote(e, ref, ref, B.s_core.at[k, level], B.r_core.at[k, level, c or 0], r=sib)


def line_out(e, B, level, c):
    @pl.when(jnp.logical_and(e.g >= level, e.g + 1 < e.G))
    def _():
        line_copy(e, B, level, True, c).start()

    @pl.when(jnp.logical_and(e.g <= level, e.g >= 1))
    def _():
        line_copy(e, B, level, False, c).start()


def at_hop(e, level, hop, body):
    if hop == 0:
        cond = e.g == level
    else:
        cond = jnp.logical_or(e.g == level + hop, e.g == level - hop)
    pl.when(cond)(body)


def line_send(e, B, levels, chunks):
    for level in levels:

        def body(level=level):
            for c in chunks:
                line_out(e, B, level, c)

        at_hop(e, level, 0, body)


def line_step(e, B, levels, hop, chunks):
    for level in levels:

        def body(level=level):
            for c in chunks:
                line_copy(e, B, level, True, c).wait_recv()
                line_out(e, B, level, c)
                row_copy(e, B, level, False, c).start()
                core_copy(e, B, level, False, True, c).start()

        at_hop(e, level, hop, body)


def pair_step(e, B, levels, hop, chunks):
    for level in levels:

        def body(level=level):
            for c in chunks:
                pair_copy(e, B, level, c).start()
                if hop == 0:
                    core_copy(e, B, level, False, True, c).start()
                    core_copy(e, B, level, False, False, c).start()

        at_hop(e, level, hop, body)


def row_step(e, B, levels, hop, chunks):
    for level in levels:

        def body(level=level):
            for c in chunks:
                pair_copy(e, B, level, c).wait_recv()
                row_copy(e, B, level, True, c).start()
                core_copy(e, B, level, True, True, c).start()

        at_hop(e, level, hop, body)


def core_step(e, B, levels, hop, chunks):
    for level in levels:

        def body(level=level):
            for c in chunks:
                if hop:
                    row_copy(e, B, level, False, c).wait_recv()
                    core_copy(e, B, level, False, False, c).start()
                row_copy(e, B, level, True, c).wait_recv()
                core_copy(e, B, level, True, False, c).start()

        at_hop(e, level, hop, body)


def gather_ready(e, B, levels):
    for level in levels:
        for other in (False, True):
            for mine in (False, True):
                for c in range(CHUNKS):
                    core_copy(e, B, level, other, mine, c).wait_recv()


def ph_gather_done(e, B):
    G = e.G
    for level in range(G):
        pair_copy(e, B, level, None).wait_send()
        row_copy(e, B, level, True, None).wait_send()

        @pl.when(e.g != level)
        def _(level=level):
            row_copy(e, B, level, False, None).wait_send()

        for other in (False, True):
            for mine in (False, True):
                core_copy(e, B, level, other, mine, None).wait_send()

        @pl.when(jnp.logical_and(e.g >= level, e.g + 1 < G))
        def _(level=level):
            line_copy(e, B, level, True, None).wait_send()

        @pl.when(jnp.logical_and(e.g <= level, e.g >= 1))
        def _(level=level):
            line_copy(e, B, level, False, None).wait_send()


def flatten(e, B, first, last):
    step = 112
    s0 = first // e.slab

    def slab(k, _):
        for h in range(2):
            count = e.half if h == 0 else e.slab - e.half
            whole = count // step
            left = (count - whole * step + 15) // 16 * 16
            base = e.slab * k + h * e.half

            def body(t, _, h=h, base=base):
                at = pl.multiple_of(t * step, 16)
                B.big[pl.ds(base + t * step, step), :] = B.gw[s0 + k, h, pl.ds(at, step), :].astype(F32)
                return 0

            lax.fori_loop(0, whole, body, 0)
            if left:
                last = B.gw[s0 + k, h, whole * step : whole * step + left, :]
                B.big[pl.ds(base + whole * step, left), :] = last.astype(F32)
        return 0

    lax.fori_loop(0, (last - 1) // e.slab - s0 + 1, slab, 0)
    return e.slab * s0


def ph_weights_up(e, B):
    base = flatten(e, B, ROW_UP, ROW_CUP)
    for j in range(HID // LANES):
        B.wup[:, LANES * j : LANES * (j + 1)] = B.big[pl.ds(ROW_UP - base + j, C, stride=HID // LANES), :].astype(BF16)


def ph_weights_down(e, B):
    base = flatten(e, B, ROW_DOWN, ROW_VEC)
    for j in range(J):
        B.wdn[:, LANES * j : LANES * (j + 1)] = B.big[pl.ds(ROW_DOWN - base + j, HID, stride=J), :].astype(BF16)


def ph_weights_head(e, B):
    base = flatten(e, B, ROW_DS, ROW_OUT)
    per = DOUT // LANES
    for j in range(per):
        B.wds[:, LANES * j : LANES * (j + 1)] = B.big[pl.ds(ROW_DS - base + j, 4 * C, stride=per), :].astype(BF16)
    base = flatten(e, B, ROW_HEAD, ROW_BH)
    lane = lax.broadcasted_iota(jnp.int32, (DOUT // 16, LANES), 1)
    for kk in range(16):
        first, off = divmod(CLS * kk, LANES)
        parts = [B.big[pl.ds(ROW_HEAD - base + first + t, DOUT // 16, stride=125), :] for t in range(9 if off else 8)]
        if off:
            parts = [pltpu.roll(part, LANES - off, 1) for part in parts]
        for t in range(8):
            tile = parts[t]
            if off:
                tile = jnp.where(lane < LANES - off, parts[t], parts[t + 1])
            if t == 7:
                tile = jnp.where(lane < CLS - 7 * LANES, tile, 0.0)
            B.dx[pl.ds(DOUT * t + kk, DOUT // 16, stride=16), :] = tile
    for t in range(8):
        B.wh[:, LANES * t : LANES * (t + 1)] = B.dx[DOUT * t : DOUT * (t + 1), :].astype(BF16)


def hooks(it, steps, also=None):
    if not steps:
        return
    bits = sum(1 << k for k in steps)
    due = lax.rem(lax.shift_right_logical(jnp.int32(bits), it), 2) == 1
    if also is not None:
        due = jnp.logical_and(due, also)

    @pl.when(due)
    def _():
        for k, some in steps.items():

            @pl.when(it == k)
            def _(some=some):
                for step in some:
                    step()


def transpose(e, B, m):
    pad = jnp.zeros((3 * SUB, LANES), F32)
    for j in range(J):
        B.big[pl.ds(xrow(j, m), 3 * SUB), :] = pad
        B.big[pl.ds(xrow(j, m) + (COLS + 3) * SUB, 3 * SUB), :] = pad
        for row in range(14):
            v = B.xg[m, row, :, LANES * j : LANES * (j + 1)].astype(F32)
            B.big[pl.ds(xrow(j, m) + 3 * SUB + row, COLS, stride=SUB), :] = v
            if 3 <= row < 11:
                B.xc[pl.ds(j * NPOS + m * POS + row - 3, COLS, stride=OWN), :] = v


def ph_taps(e, B):
    def body(t, _):
        B.kb[t] = jnp.broadcast_to(B.tab[pl.ds(t, 1), :], (8, LANES))
        return 0

    lax.fori_loop(0, 49 * J, body, 0)


def vec_row(B, v, j):
    row = T_VEC + v * J + j
    return B.tab[row : row + 1, :]


def conv_tile(B, m, j, c0, tile, acc, flip):
    for a in range(7):
        taps = [B.kb[((6 - a) * 7 + 6 - b if flip else a * 7 + b) * J + j] for b in range(7)]
        for c in range(tile + 6):
            d = B.big[pl.ds(xrow(j, m) + (c0 + c) * SUB + a, OWN), :]
            for b in range(7):
                if 0 <= c - b < tile:
                    acc[c - b] = acc[c - b] + d * taps[b]
    return acc


TILE = 32


def ph_conv_fwd(e, B, steps):
    halves = COLS // TILE

    def body(it, _):
        m = it // halves
        c0 = it % halves * TILE
        for j in range(J):
            hooks(it, {k // J: v for k, v in steps.items() if k % J == j})
            bias = jnp.broadcast_to(vec_row(B, 0, j), (OWN, LANES))
            acc = conv_tile(B, m, j, c0, TILE, [bias] * TILE, False)
            at = j * NPOS + m * POS + c0 * OWN
            for c in range(TILE):
                B.dx[pl.ds(pl.multiple_of(at + OWN * c, OWN), OWN), :] = acc[c]
        return 0

    lax.fori_loop(0, MICRO * halves, body, 0)


def ph_norm_one(e, B):
    size = 128

    def body(it, _):
        at = pl.multiple_of(it * size, size)
        hat, scale = ln_parts([B.dx[pl.ds(j * NPOS + at, size), :] for j in range(J)], C)
        B.rs1[pl.ds(at, size), :] = jnp.broadcast_to(scale, (size, LANES))
        for j in range(J):
            B.v1[pl.ds(at, size), LANES * j : LANES * (j + 1)] = hat[j]
            B.n[pl.ds(at, size), LANES * j : LANES * (j + 1)] = (
                hat[j] * vec_row(B, 1, j) + vec_row(B, 2, j)
            ).astype(BF16)
        return 0

    lax.fori_loop(0, NPOS // size, body, 0)


def ph_mlp_up(e, B, steps):
    chunk = 256
    width = 256
    c0 = 0.7978845608028654
    c1 = 0.044715 * c0

    def body(it, _):
        hooks(it, steps)
        at = pl.multiple_of(it * chunk, chunk)
        rows = B.n[pl.ds(at, chunk), :]
        for k in range(HID // width):
            lanes = slice(width * k, width * (k + 1))
            bias = lane_row(B.tab, T_CUP + k * width // LANES, width // LANES)
            h = jnp.dot(rows, B.wup[:, lanes], preferred_element_type=F32) + bias
            sq = h * h
            half = 0.5 * jnp.tanh(h * (c0 + c1 * sq)) + 0.5
            u = h * half
            B.u[pl.ds(at, chunk), lanes] = u.astype(BF16)
            slope = half + u * (1.0 - half) * (2.0 * c0 + 6.0 * c1 * sq)
            B.gp[pl.ds(at, chunk), lanes] = slope.astype(BF16)
        return 0

    lax.fori_loop(0, NPOS // chunk, body, 0)


def ph_mlp_down(e, B, steps):
    chunk = 256
    B.ps[...] = jnp.zeros_like(B.ps)

    def body(it, _):
        hooks(it, steps)
        at = pl.multiple_of(it * chunk, chunk)
        m = it // (POS // chunk)
        keep = B.mask[m, e.i].astype(F32) * (1.0 / KEEP)
        z = jnp.dot(B.u[pl.ds(at, chunk), :], B.wdn[...], preferred_element_type=F32)
        resid = []
        for j in range(J):
            zj = z[:, LANES * j : LANES * (j + 1)] + vec_row(B, 3, j)
            B.z[pl.ds(j * NPOS + at, chunk), :] = zj
            resid.append(B.xc[pl.ds(j * NPOS + at, chunk), :] + (vec_row(B, 4, j) * keep) * zj)
        hat, scale = ln_parts(resid, C)
        B.rs2[pl.ds(at, chunk), :] = jnp.broadcast_to(scale, (chunk, LANES))
        for j in range(J):
            B.v2[pl.ds(at, chunk), LANES * j : LANES * (j + 1)] = hat[j]
            low = (hat[j] * vec_row(B, 5, j) + vec_row(B, 6, j)).astype(BF16).astype(F32)
            low = jnp.sum(low.reshape(chunk // 16, 2, OWN, LANES), 0)
            B.ps[m, :, :, LANES * j : LANES * (j + 1)] += low
        return 0

    lax.fori_loop(0, NPOS // chunk, body, 0)


def ph_patch_local(e, B):
    even = lax.broadcasted_iota(jnp.int32, (OWN, C), 0) % 2 == 0
    pick = lax.broadcasted_iota(jnp.int32, (8, C), 0)
    for parity in range(2):
        for side in range(2):
            tile = jnp.zeros((8, C), F32)
            for m in range(MICRO):
                v = B.ps[m, side]
                part = jnp.sum(jnp.where(even if parity == 0 else jnp.logical_not(even), v, 0.0), 0, keepdims=True)
                tile = jnp.where(pick == m, part, tile)
            q = 2 * parity + side
            B.sl[8 * q : 8 * q + 8, :] = tile


def patch_copy(e, B, d):
    to = lax.rem(e.g + d, e.G)
    return remote(e, B.sl, B.sr.at[d], B.s_patch.at[d], B.r_patch.at[d], r=to * GROUP + e.i)


def patch_start(e, B):
    for d in range(1, e.G):
        patch_copy(e, B, d).start()
    B.sr[0] = B.sl[...]


def patch_wait(e, B):
    for d in range(1, e.G):
        patch_copy(e, B, d).wait_recv()
    for d in range(1, e.G):
        patch_copy(e, B, d).wait_send()


def split3(v):
    hi = v.astype(BF16).astype(F32)
    mid = (v - hi).astype(BF16).astype(F32)
    return hi, mid, v - hi - mid


def ph_head(e, B):
    total = None
    for level in range(e.G):
        part = B.sr[lax.rem(e.g - level + e.G, e.G)]
        total = part if total is None else total + part
    per = DOUT // LANES
    gain = lane_row(B.tab, T_OUT + per, per)
    shift = lane_row(B.tab, T_OUT + 2 * per, per)
    mean = total * (1.0 / e.positions)
    pooled = lane_row(B.tab, T_OUT, per)
    for q in range(4):
        parts = jnp.concatenate(split3(mean[8 * q : 8 * q + 8, :]), axis=0).astype(BF16)
        prod = jnp.dot(parts, B.wds[C * q : C * (q + 1), :], preferred_element_type=F32)
        pooled = pooled + (prod[0:8] + (prod[8:16] + prod[16:24]))
    rows = lax.broadcasted_iota(jnp.int32, (8, 1), 0)
    live = rows < MICRO
    (hat,), scale = ln_parts([pooled], DOUT)
    query = (hat * gain + shift).astype(BF16)
    lane = lax.broadcasted_iota(jnp.int32, (8, CLSP), 1)
    logits = jnp.dot(query, B.wh[...], preferred_element_type=F32) + lane_row(B.tab, T_BH, CLSP // LANES)
    logits = jnp.where(lane < CLS, logits, -1e30)
    top = jnp.max(logits, 1, keepdims=True)
    powers = jnp.exp(logits - top)
    expsum = jnp.sum(powers, 1, keepdims=True)
    label = jnp.zeros((8, 1), jnp.int32)
    for m in range(MICRO):
        label = jnp.where(rows == m, B.labels[m, e.i], label)
    onehot = (lane == label).astype(F32)
    own = jnp.sum(jnp.where(lane == label, logits, 0.0), 1, keepdims=True)
    loss = jnp.sum(jnp.where(live, top + jnp.log(expsum) - own, 0.0), 0, keepdims=True)
    grad = jnp.where(live, (powers / expsum - onehot) * e.inv_count, 0.0).astype(BF16)
    grad_query = lax.dot_general(grad, B.wh[...], (((1,), (1,)), ((), ())), preferred_element_type=F32)
    dn = grad_query * gain
    m1 = jnp.sum(dn, 1, keepdims=True) * (1.0 / DOUT)
    m2 = jnp.sum(dn * hat, 1, keepdims=True) * (1.0 / DOUT)
    grad_pool = scale * (dn - m1 - hat * m2)
    down = jnp.where(live, grad_pool * (1.0 / e.positions), 0.0).astype(BF16)
    for q in range(4):
        B.dn2[8 * q : 8 * q + 8, :] = lax.dot_general(
            down, B.wds[C * q : C * (q + 1), :], (((1,), (1,)), ((), ())), preferred_element_type=F32
        )
    low = grad.astype(F32)
    d32 = down.astype(F32)
    q32 = jnp.where(live, query.astype(F32), 0.0)
    zero3 = jnp.zeros((3, C), F32)
    g3 = jnp.sum(jnp.where(live, grad_query * hat, 0.0), 0, keepdims=True)
    s3 = jnp.sum(jnp.where(live, grad_query, 0.0), 0, keepdims=True)
    vec = jnp.concatenate([g3, s3], axis=1)
    vec_parts = split3(vec)
    loss_parts = split3(loss)
    for q in range(4):
        at = slice(C * q, C * (q + 1))
        s_hi, s_mid, _ = split3(total[8 * q : 8 * q + 8, :])
        B.pb[0:8, at] = jnp.zeros((8, C), F32)
        B.pb[8:16, at] = jnp.zeros((8, C), F32)
        B.pb[0:3, at] = s_hi[0:3]
        B.pb[3:6, at] = s_mid[0:3]
    B.pb[6:9, 0:DOUT] = d32[0:3]
    B.pb[6:9, DOUT : 2 * DOUT] = q32[0:3]
    B.pb[9:12, 0:CLSP] = low[0:3]
    for k in range(3):
        B.pb[12 + k : 13 + k, :] = vec_parts[k]
        B.pb[15:16, LANES * k : LANES * (k + 1)] = jnp.broadcast_to(loss_parts[k], (1, LANES))
    B.pall[e.i * e.nb + e.b] = B.pb[...].astype(BF16)
    even = lax.broadcasted_iota(jnp.int32, (OWN, C), 0) % 2 == 0
    for m in range(MICRO):
        for side in range(2):
            first = B.dn2[8 * side + m : 8 * side + m + 1, :]
            second = B.dn2[8 * (2 + side) + m : 8 * (2 + side) + m + 1, :]
            B.dnt[m, side] = jnp.where(even, first, second)


def batch_copy(e, B, d):
    slot = e.i * e.nb + e.b
    return remote(e, B.pall.at[slot], B.pall.at[slot], B.s_pb.at[d], B.r_pb.at[d], b=lax.rem(e.b + d, e.nb))


def group_copy(e, B, d):
    at = pl.ds(e.i * e.nb, e.nb)
    to = e.g * GROUP + lax.rem(e.i + d, GROUP)
    return remote(e, B.pall.at[at], B.pall.at[at], B.s_pg.at[d], B.r_pg.at[d], r=to)


def ph_payload_batch(e, B):
    for d in range(1, e.nb):
        batch_copy(e, B, d).start()


def ph_payload_group(e, B):
    for d in range(1, e.nb):
        batch_copy(e, B, d).wait_recv()
    for d in range(1, GROUP):
        group_copy(e, B, d).start()


def ph_payload_wait(e, B):
    for d in range(1, GROUP):
        group_copy(e, B, d).wait_recv()
    for d in range(1, e.nb):
        batch_copy(e, B, d).wait_send()
    for d in range(1, GROUP):
        group_copy(e, B, d).wait_send()


def lane_sum(blocks):
    total = blocks[0]
    for block in blocks[1:]:
        total = total + block
    return jnp.sum(total, -1, keepdims=True) * (1.0 / C)


def fold8(v):
    return jnp.sum(v.reshape(v.shape[0] // 8, 8, v.shape[1]), 0)


def ph_bwd_one(e, B):
    chunk = 256
    half = chunk // 16
    B.acc[...] = jnp.zeros_like(B.acc)
    B.acup[...] = jnp.zeros_like(B.acup)
    B.ps[...] = jnp.zeros_like(B.ps)

    def body(it, _):
        at = pl.multiple_of(it * chunk, chunk)
        m = it // (POS // chunk)
        keep = B.mask[m, e.i].astype(F32) * (1.0 / KEEP)
        span = pl.ds(at, chunk)
        lanes = [slice(LANES * j, LANES * (j + 1)) for j in range(J)]
        dg = [B.dnt[m, :, :, lanes[j]] * vec_row(B, 5, j) for j in range(J)]
        m1 = lane_sum(dg)
        hat = [B.v2[span, lanes[j]].reshape(half, 2, OWN, LANES) for j in range(J)]
        m2 = lane_sum([dg[j] * hat[j] for j in range(J)])
        scale = B.rs2[span, :].reshape(half, 2, OWN, LANES)
        for j in range(J):
            zspan = pl.ds(j * NPOS + at, chunk)
            dr = (scale * (dg[j] - m1 - hat[j] * m2)).reshape(chunk, LANES)
            B.ps[m, :, :, lanes[j]] += jnp.sum(hat[j], 0)
            dz = (dr * (vec_row(B, 4, j) * keep)).astype(BF16)
            B.dz[span, lanes[j]] = dz
            B.acc[3, :, lanes[j]] += fold8(dz.astype(F32))
            B.acc[4, :, lanes[j]] += fold8(dr * B.z[zspan, :]) * keep
            B.z[zspan, :] = dr
        return 0

    lax.fori_loop(0, NPOS // chunk, body, 0)
    for m in range(MICRO):
        B.acc[5] += B.dnt[m, 0] * B.ps[m, 0] + B.dnt[m, 1] * B.ps[m, 1]
        B.acc[6] += (B.dnt[m, 0] + B.dnt[m, 1]) * float(COLS // 2)


def ph_bwd_two(e, B, steps):
    chunk = 256
    width = 256

    def body(it, _):
        hooks(it, steps)
        at = pl.multiple_of(it * chunk, chunk)
        m = it // (POS // chunk)
        c0 = (it % (POS // chunk)) * (chunk // OWN)
        span = pl.ds(at, chunk)
        lanes = [slice(LANES * j, LANES * (j + 1)) for j in range(J)]
        dz = B.dz[span, :]
        for k in range(HID // width):
            hid = slice(width * k, width * (k + 1))
            du = lax.dot_general(dz, B.wdn[hid, :], (((1,), (1,)), ((), ())), preferred_element_type=F32)
            dh = (du * B.gp[span, hid].astype(F32)).astype(BF16)
            B.gp[span, hid] = dh
            B.acup[:, hid] += fold8(dh.astype(F32))
        dn = lax.dot_general(B.gp[span, :], B.wup[...], (((1,), (1,)), ((), ())), preferred_element_type=F32)
        dns = [dn[:, lanes[j]] for j in range(J)]
        dg = [dns[j] * vec_row(B, 1, j) for j in range(J)]
        hat = [B.v1[span, lanes[j]] for j in range(J)]
        m1 = lane_sum(dg)
        m2 = lane_sum([dg[j] * hat[j] for j in range(J)])
        scale = B.rs1[span, :]
        for j in range(J):
            dy = scale * (dg[j] - m1 - hat[j] * m2)
            B.acc[0, :, lanes[j]] += fold8(dy)
            B.acc[1, :, lanes[j]] += fold8(dns[j] * hat[j])
            B.acc[2, :, lanes[j]] += fold8(dns[j])
            for c in range(chunk // OWN):
                B.big[pl.ds(xrow(j, m) + (3 + c0 + c) * SUB + 3, OWN), :] = dy[OWN * c : OWN * (c + 1), :]
        return 0

    lax.fori_loop(0, NPOS // chunk, body, 0)


def wgrad_down(e, B, f):
    for k in range(2):
        first = 2 * C * f + C * k
        w = lax.dot_general(
            B.u[:, first : first + C], B.dz[...], (((0,), (0,)), ((), ())), preferred_element_type=F32
        )
        w = w.reshape(24, 16, C)
        a, b = w[:, 0:8], w[:, 8:16]
        units = [v[:, :, LANES * j : LANES * (j + 1)] for v in (a, b) for j in range(J)]
        tiles = [jnp.concatenate(units[2 * t : 2 * t + 2], axis=1).astype(BF16) for t in range(3)]
        for q in range(24):
            piece, inner = divmod(24 * k + q, 3)
            for t in range(3):
                B.gb[f, piece // 4, piece // 2 % 2, piece % 2, inner, t] = tiles[t][q]


def wgrad_up(e, B, f):
    width = 256
    for k in range(3):
        first = 768 * (f - 2) + width * k
        w = lax.dot_general(
            B.n[...], B.gp[:, first : first + width], (((0,), (0,)), ((), ())), preferred_element_type=F32
        )
        w = w.reshape(48, 8, width)
        w = jnp.concatenate([w[:, :, :LANES], w[:, :, LANES:]], axis=1).astype(BF16)
        B.gb[f, :, :, :, :, k] = w.reshape(4, 2, 2, 3, 16, LANES)


def dy_copy(e, B, m, up):
    if up:
        return remote(e, B.hs.at[m, 1], B.hr.at[m, 0], B.s_dy.at[1, m], B.r_dy.at[1, m], r=e.r + GROUP)
    return remote(e, B.hs.at[m, 0], B.hr.at[m, 1], B.s_dy.at[0, m], B.r_dy.at[0, m], r=e.r - GROUP)


def dy_send(e, B, m):
    zero = jnp.zeros((3 * SUB, LANES), F32)
    for j in range(J):
        B.big[pl.ds(xrow(j, m), 3 * SUB), :] = zero
        B.big[pl.ds(xrow(j, m) + (COLS + 3) * SUB, 3 * SUB), :] = zero
        for side in range(2):
            for k in range(3):
                row = 3 + k if side == 0 else 8 + k
                v = B.big[pl.ds(xrow(j, m) + 3 * SUB + row, COLS, stride=SUB), :]
                B.hs[m, side, k, :, LANES * j : LANES * (j + 1)] = v.astype(BF16)

    @pl.when(e.g > 0)
    def _():
        dy_copy(e, B, m, False).start()

    @pl.when(e.g < e.G - 1)
    def _():
        dy_copy(e, B, m, True).start()


def ph_dy_edges(e, B):
    zero = jnp.zeros((MICRO, 3, COLS, C), BF16)

    @pl.when(e.g == 0)
    def _():
        B.hr[:, 0] = zero

    @pl.when(e.g == e.G - 1)
    def _():
        B.hr[:, 1] = zero


def dy_take(e, B, m):
    @pl.when(e.g < e.G - 1)
    def _():
        dy_copy(e, B, m, False).wait_recv()

    @pl.when(e.g > 0)
    def _():
        dy_copy(e, B, m, True).wait_recv()

    for j in range(J):
        for side in range(2):
            for k in range(3):
                row = k if side == 0 else 11 + k
                v = B.hr[m, side, k, :, LANES * j : LANES * (j + 1)].astype(F32)
                B.big[pl.ds(xrow(j, m) + 3 * SUB + row, COLS, stride=SUB), :] = v


def ph_dy_done(e, B):
    for m in range(MICRO):

        @pl.when(e.g > 0)
        def _(m=m):
            dy_copy(e, B, m, False).wait_send()

        @pl.when(e.g < e.G - 1)
        def _(m=m):
            dy_copy(e, B, m, True).wait_send()


def ph_conv_kernel(e, B, parts, steps):
    halves = COLS // TILE

    def taps(it, _):
        hooks(it, steps)
        j = it // 7
        a = it % 7

        def body(k, dk):
            m = parts.start + k // halves
            c0 = k % halves * TILE
            dk = list(dk)
            at = j * NPOS + m * POS + c0 * OWN
            xs = [B.xc[pl.ds(pl.multiple_of(at + OWN * c, OWN), OWN), :] for c in range(TILE)]
            for c in range(TILE + 6):
                d = B.big[pl.ds(xrow(j, m) + (c0 + c) * SUB + a, OWN), :]
                for b in range(7):
                    if 0 <= c - b < TILE:
                        dk[b] = dk[b] + d * xs[c - b]
            return tuple(dk)

        zero = jnp.zeros((OWN, LANES), F32)
        dk = lax.fori_loop(0, halves * len(parts), body, (zero,) * 7)
        for b in range(7):
            tap = (6 - a) * 7 + 6 - b
            B.sg[pl.ds(tap * J + j, 1), :] += jnp.sum(dk[b], 0, keepdims=True)
        return 0

    lax.fori_loop(0, 7 * J, taps, 0)


def tap_low(B, t):
    return B.wh[16 * (t // 8) : 16 * (t // 8) + 16, LANES * (t % 8) : LANES * (t % 8 + 1)]


def ph_taps_low(e, B):
    for t in range(49 * J):
        row = B.kb[t]
        B.wh[16 * (t // 8) : 16 * (t // 8) + 16, LANES * (t % 8) : LANES * (t % 8 + 1)] = jnp.concatenate(
            [row, row], axis=0
        ).astype(BF16)


def ph_conv_input(e, B, steps):
    halves = COLS // TILE
    half = TILE // 2

    def body(it, _):
        m = it // halves
        c0 = it % halves * TILE
        for j in range(J):
            hooks(it, {k // J: v for k, v in steps.items() if k % J == j})
            acc = [None] * half
            for a in range(7):
                cols = []
                for c in range(half + 6):
                    at = xrow(j, m) + (c0 + c) * SUB + a
                    pair = [B.big[pl.ds(at, OWN), :], B.big[pl.ds(at + half * SUB, OWN), :]]
                    cols.append(jnp.concatenate(pair, axis=0).astype(BF16))
                for some in (range(0, 4), range(4, 7)):
                    taps = {b: tap_low(B, ((6 - a) * 7 + 6 - b) * J + j) for b in some}
                    for c in range(half):
                        part = [cols[c + b] * taps[b] for b in some]
                        while len(part) > 1:
                            part = [part[k] + part[k + 1] for k in range(0, len(part) - 1, 2)] + part[len(part) // 2 * 2 :]
                        low = part[0].astype(F32)
                        acc[c] = low if acc[c] is None else acc[c] + low
            at = j * NPOS + m * POS + c0 * OWN
            for c in range(half):
                for k in range(2):
                    span = pl.ds(pl.multiple_of(at + OWN * (c + half * k), OWN), OWN)
                    B.dx[span, :] = B.z[span, :] + acc[c][OWN * k : OWN * (k + 1), :]
        return 0

    lax.fori_loop(0, MICRO * halves, body, 0)


def ph_small_fill(e, B):
    for k in range(HID // LANES):
        B.sg[SG_CUP + k : SG_CUP + k + 1, :] = jnp.sum(B.acup[:, LANES * k : LANES * (k + 1)], 0, keepdims=True)
    for v in range(7):
        for j in range(J):
            row = SG_VEC + v * J + j
            B.sg[row : row + 1, :] = jnp.sum(B.acc[v, :, LANES * j : LANES * (j + 1)], 0, keepdims=True)


def out_copy(e, B, m, k, d):
    j = lax.rem(e.i + d, GROUP)
    cols = pl.ds(TILE * k, TILE)
    return remote(
        e,
        B.xg.at[m, pl.ds(3 + 2 * j, 2), cols],
        B.fo.at[m, e.i, :, cols],
        B.s_out.at[m, k, d],
        B.r_out.at[m, k, d],
        r=e.g * GROUP + j,
    )


def own_out_copy(e, B, m, k):
    cols = pl.ds(TILE * k, TILE)
    return pltpu.make_async_copy(
        B.xg.at[m, pl.ds(3 + 2 * e.i, 2), cols], B.fo.at[m, e.i, :, cols], B.s_outown.at[m, k]
    )


def out_send(e, B, m, k):
    for row in range(OWN):
        for j in range(J):
            v = B.dx[pl.ds(j * NPOS + m * POS + k * TILE * OWN + row, TILE, stride=OWN), :]
            B.xg[m, 3 + row, TILE * k : TILE * (k + 1), LANES * j : LANES * (j + 1)] = v.astype(BF16)
    own_out_copy(e, B, m, k).start()
    for d in (2, 3, 1):
        out_copy(e, B, m, k, d).start()


def ph_out_wait(e, B):
    for m in range(MICRO):
        for k in range(COLS // TILE):
            own_out_copy(e, B, m, k).wait()
            for d in range(1, GROUP):
                out_copy(e, B, m, k, d).wait()


PARTS = 4
PIECE = (144, 144, 288, 288)
START = (ROW_DOWN, ROW_DOWN + 16 * 144, ROW_UP, ROW_UP)


def rs_first(e, B, f):
    c = e.i % 2
    return remote(e, B.gb.at[f, :, :, 1 - c], B.ra1.at[f], B.s_rs.at[f, 0], B.r_rs.at[f, 0], r=e.r + 1 - 2 * c)


def rs_second(e, B, f):
    to = e.g * GROUP + lax.rem(e.i + 2, GROUP)
    return remote(e, B.sa2.at[f], B.ra2.at[f], B.s_rs.at[f, 1], B.r_rs.at[f, 1], r=to)


def group_of(e, q):
    return q * (e.G // 4)


def rs_third(e, B, f, q):
    to = group_of(e, q)
    d = lax.rem(to - e.g + e.G, e.G)
    return remote(e, B.sc.at[f, q], B.rc.at[f, d], B.s_rc.at[f, q], B.r_rc.at[f, d], r=to * GROUP + e.i)


def rs_third_wait(e, B, f, d):
    return remote(e, B.sc.at[f, 0], B.rc.at[f, d], B.s_rc.at[f, 0], B.r_rc.at[f, d], r=lax.rem(e.r + GROUP, e.n))


def rs_fourth(e, B, f, d):
    return remote(e, B.rb.at[f, 0], B.rb.at[f, d], B.s_rb.at[f, d], B.r_rb.at[f, d], b=lax.rem(e.b + d, e.nb))


def ends_here(e, body):
    if e.G == 4:
        body()
    else:
        pl.when(e.g % (e.G // 4) == 0)(body)


def rs_step1(e, B, f):
    rs_first(e, B, f).start()


def rs_step2(e, B, f):
    x, c = e.i // 2, e.i % 2
    rs_first(e, B, f).wait_recv()
    for q in range(4):
        B.sa2[f, q] = (B.gb[f, q, 1 - x, c].astype(F32) + B.ra1[f, q, 1 - x].astype(F32)).astype(BF16)
    rs_second(e, B, f).start()
    for q in range(4):
        B.h1[f, q] = B.gb[f, q, x, c].astype(F32) + B.ra1[f, q, x].astype(F32)


def rs_step3(e, B, f):
    rs_second(e, B, f).wait_recv()
    for q in range(4):
        B.h1[f, q] = B.h1[f, q] + B.ra2[f, q].astype(F32)
        B.sc[f, q] = B.h1[f, q].astype(BF16)
    for q in range(4):

        @pl.when(e.g != group_of(e, q))
        def _(q=q):
            rs_third(e, B, f, q).start()


def rs_step4(e, B, f):
    def body():
        total = B.h1[f, e.g // (e.G // 4)]
        for d in range(1, e.G):
            rs_third_wait(e, B, f, d).wait_recv()
            total = total + B.rc[f, d].astype(F32)
        B.rb[f, 0] = total.astype(BF16)
        for d in range(1, e.nb):
            rs_fourth(e, B, f, d).start()

    ends_here(e, body)


def piece_owners(e, f):
    start = START[f] + PIECE[f] * (e.g // (e.G // 4) * 4 + e.i)
    return start // e.slab, (start + PIECE[f] - 1) // e.slab


def own_slot(B, f, slot):
    return B.ro.at[f, slot] if f < 2 else B.ro_up.at[f - 2, slot]


def own_copy(e, B, f, k, owner):
    slot = lax.rem(e.g // (e.G // 4) * 4 + e.i, 16 if f < 2 else 8)
    return remote(e, B.fp.at[f], own_slot(B, f, slot), B.s_ro.at[f, k], B.r_ro.at[f, slot], r=owner)


def own_wait(e, B, f, slot, home):
    remote(e, B.fp.at[f], own_slot(B, f, slot), B.s_ro.at[f, 0], B.r_ro.at[f, slot], r=home).wait_recv()


def rs_step5(e, B, f):
    def body():
        for d in range(1, e.nb):
            rs_fourth(e, B, f, d).wait_recv()
        total = None
        for b in range(e.nb):
            part = B.rb[f, lax.rem(e.b - b + e.nb, e.nb)].astype(F32)
            total = part if total is None else total + part
        B.fp[f] = total.astype(BF16)
        lo, hi = piece_owners(e, f)

        @pl.when(lo != e.r)
        def _():
            own_copy(e, B, f, 0, lo).start()

        @pl.when(jnp.logical_and(hi != lo, hi != e.r))
        def _():
            own_copy(e, B, f, 1, hi).start()

    ends_here(e, body)


def place(B, f, off, tiles):
    for k in range(3):
        for t in range(3):
            for h in range(2):
                unit = 2 * t + h
                tile = tiles[k, t, 8 * h : 8 * h + 8, :].astype(F32)
                if f >= 2:
                    at = pl.ds(MARGIN + off + 96 * k + 6 * (f - 2) + unit, 8, stride=12)
                else:
                    at = pl.ds(MARGIN + off + 48 * k + 24 * (unit // 3) + unit % 3, 8, stride=3)
                B.gf[at, :] = tile


def rs_place(e, B, f):
    for p in range(16):
        off = START[f] + PIECE[f] * p - e.slab * e.r
        home = group_of(e, p // 4) * GROUP + p % 4

        @pl.when(jnp.logical_and(off < e.slab, off + PIECE[f] > 0))
        def _(p=p, off=off, home=home):
            slot = p % (16 if f < 2 else 8)

            @pl.when(e.r != home)
            def _():
                own_wait(e, B, f, slot, home)
                place(B, f, off, B.ro[f, slot] if f < 2 else B.ro_up[f - 2, slot])

            @pl.when(e.r == home)
            def _():
                place(B, f, off, B.fp[f])


def ph_rs_done(e, B):
    for f in range(PARTS):
        rs_first(e, B, f).wait_send()
        rs_second(e, B, f).wait_send()
        for q in range(4):

            @pl.when(e.g != group_of(e, q))
            def _(f=f, q=q):
                rs_third(e, B, f, q).wait_send()

        def body(f=f):
            for d in range(1, e.nb):
                rs_fourth(e, B, f, d).wait_send()
            lo, hi = piece_owners(e, f)

            @pl.when(lo != e.r)
            def _():
                own_copy(e, B, f, 0, lo).wait_send()

            @pl.when(jnp.logical_and(hi != lo, hi != e.r))
            def _():
                own_copy(e, B, f, 1, hi).wait_send()

        ends_here(e, body)


MARGIN = 1792


QUARTER = 80
SEGMENTS = (
    (0, 0, QUARTER, ROW_K),
    (1, 0, 49 * J - QUARTER, ROW_K + QUARTER),
    (2, 0, 7 * J, ROW_VEC),
    (3, 0, HID // LANES, ROW_CUP),
)


def small_group(e, B, d):
    j = lax.rem(e.i + d, GROUP)
    at = pl.ds(pl.multiple_of(j * QUARTER, QUARTER), QUARTER)
    return remote(e, B.sg.at[at], B.sg_group.at[d - 1], B.s_sg.at[d], B.r_sg.at[d], r=e.g * GROUP + j)


def small_line(e, B, d):
    to = lax.rem(e.g + d, e.G)
    return remote(e, B.sg_line.at[0], B.sg_line.at[d], B.s_sgl.at[d], B.r_sgl.at[d], r=to * GROUP + e.i)


def small_batch(e, B, d):
    return remote(e, B.sgb.at[0], B.sgb.at[d], B.s_sgb.at[d], B.r_sgb.at[d], b=lax.rem(e.b + d, e.nb))


def small_back(e, B, q, owner):
    at = pl.ds(q * QUARTER, QUARTER)
    return remote(e, B.sga.at[at], B.sga.at[at], B.s_sgg.at[q], B.r_sgg.at[q], r=owner)


def small_moves(e):
    for q, row, count, flat in SEGMENTS:
        owner = flat // e.slab
        holder = owner // GROUP * GROUP + q
        if owner != holder:
            yield q, holder, owner


def small_step1(e, B):
    for d in (2, 3, 1):
        small_group(e, B, d).start()


def small_step2(e, B):
    total = B.sg[pl.ds(pl.multiple_of(e.i * QUARTER, QUARTER), QUARTER), :]
    for d in range(1, GROUP):
        small_group(e, B, d).wait_recv()
        total = total + B.sg_group[d - 1]
    B.sg_line[0] = total
    for d in range(1, e.G):
        small_line(e, B, d).start()


def small_step3(e, B):
    for d in range(1, e.G):
        small_line(e, B, d).wait_recv()
    total = None
    for level in range(e.G):
        part = B.sg_line[lax.rem(e.g - level + e.G, e.G)]
        total = part if total is None else total + part
    B.sgb[0] = total
    for d in range(1, e.nb):
        small_batch(e, B, d).start()


def small_step4(e, B):
    for d in range(1, e.nb):
        small_batch(e, B, d).wait_recv()
    total = None
    for b in range(e.nb):
        part = B.sgb[lax.rem(e.b - b + e.nb, e.nb)]
        total = part if total is None else total + part
    B.sga[pl.ds(pl.multiple_of(e.i * QUARTER, QUARTER), QUARTER), :] = total
    for q, holder, owner in small_moves(e):

        @pl.when(e.r == holder)
        def _(q=q, owner=owner):
            small_back(e, B, q, owner).start()


def ph_small_place(e, B):
    for q, holder, owner in small_moves(e):

        @pl.when(e.r == owner)
        def _(q=q, holder=holder):
            small_back(e, B, q, holder).wait_recv()

    for q, row, count, flat in SEGMENTS:
        off = MARGIN + flat % e.slab
        at = q * QUARTER + row

        @pl.when(e.r == flat // e.slab)
        def _(off=off, at=at, count=count):
            B.gf[off : off + count, :] = B.sga[at : at + count, :]


def ph_small_done(e, B):
    for d in range(1, GROUP):
        small_group(e, B, d).wait_send()
    for d in range(1, e.G):
        small_line(e, B, d).wait_send()
    for d in range(1, e.nb):
        small_batch(e, B, d).wait_send()
    for q, holder, owner in small_moves(e):

        @pl.when(e.r == holder)
        def _(q=q, owner=owner):
            small_back(e, B, q, owner).wait_send()


def ph_head_grads(e, B):
    parts = GROUP * e.nb
    rows = 16 * parts
    sums = None
    for p in range(parts):
        x = B.pall[p].astype(F32)
        sums = x if sums is None else sums + x
        dd = x[6:9, 0:DOUT]
        B.gp[16 * p : 16 * p + 16, 0:DOUT] = jnp.concatenate([dd, dd, jnp.zeros((10, DOUT), F32)], axis=0).astype(BF16)
        dl = x[9:12, 0:CLSP]
        B.gp[rows + 16 * p : rows + 16 * p + 16, 0:CLSP] = jnp.concatenate(
            [jnp.zeros((6, CLSP), F32), dl, jnp.zeros((7, CLSP), F32)], axis=0
        ).astype(BF16)
    B.pb[...] = sums
    for q in range(4):
        for p in range(parts):
            B.v2[16 * p : 16 * p + 16, :] = B.pall[p, :, C * q : C * (q + 1)].astype(F32)
        for j in range(J):
            t = J * q + j
            B.u[LANES * t : LANES * (t + 1), 0:rows] = B.v2[0:rows, LANES * j : LANES * (j + 1)].T.astype(BF16)
    per = DOUT // LANES
    base = MARGIN - e.slab * e.r

    kc = 288
    low = e.slab * e.r - ROW_DS

    @pl.when(jnp.logical_and(low < 4 * C * per, low + e.slab > 0))
    def _():
        k0 = jnp.clip(low // (16 * per) * 16, 0, 4 * C - kc)
        k0 = pl.multiple_of(k0, 16)
        w = jnp.dot(B.u[pl.ds(k0, kc), 0:rows], B.gp[0:rows, 0:DOUT], preferred_element_type=F32)
        for j in range(per):
            B.gf[pl.ds(base + ROW_DS + per * k0 + j, kc, stride=per), :] = w[:, LANES * j : LANES * (j + 1)]

    low2 = e.slab * e.r - ROW_HEAD

    @pl.when(jnp.logical_and(low2 < DOUT * CLS // LANES, low2 + e.slab > 0))
    def _():
        g0 = jnp.clip(low2 // 125, 0, DOUT // 16 - 16)
        k0 = pl.multiple_of(DOUT + 16 * g0, 16)
        for t in range(8):
            B.big[256 * t : 256 * (t + 1), :] = jnp.dot(
                B.u[pl.ds(k0, 256), 0:rows],
                B.gp[rows : 2 * rows, LANES * t : LANES * (t + 1)],
                preferred_element_type=F32,
            )
        lane = lax.broadcasted_iota(jnp.int32, (16, LANES), 1)
        held = None
        for kk in range(16):
            o = (-CLS * kk) % LANES
            tiles = [B.big[pl.ds(256 * t + kk, 16, stride=16), :] for t in range(8)]
            if o:
                tiles = [pltpu.roll(tile, LANES - o, 1) for tile in tiles]
            for s in range(CLS * kk // LANES, (CLS * kk + CLS - 1) // LANES + 1):
                t0 = (LANES * s - CLS * kk) // LANES
                if o == 0:
                    value = tiles[t0]
                elif t0 < 0:
                    value = tiles[0]
                elif t0 + 1 > 7:
                    value = tiles[t0]
                else:
                    value = jnp.where(lane < LANES - o, tiles[t0], tiles[t0 + 1])
                border = CLS * kk - LANES * s
                if border > 0:
                    value = jnp.where(lane < border, held, value)
                if LANES * (s + 1) > CLS * (kk + 1):
                    held = value
                else:
                    B.gf[pl.ds(base + ROW_HEAD + 125 * g0 + s, 16, stride=125), :] = value

    @pl.when(e.r == ROW_OUT // e.slab)
    def _():
        off = MARGIN + ROW_OUT % e.slab
        for j in range(per):
            at = slice(LANES * j, LANES * (j + 1))
            B.gf[off + j : off + j + 1, :] = B.pb[6:7, at] * e.positions + (
                B.pb[7:8, at] * e.positions + B.pb[8:9, at] * e.positions
            )
            gain = B.pb[12:13, at] + B.pb[13:14, at] + B.pb[14:15, at]
            B.gf[off + per + j : off + per + j + 1, :] = gain
            at = slice(DOUT + LANES * j, DOUT + LANES * (j + 1))
            shift = B.pb[12:13, at] + B.pb[13:14, at] + B.pb[14:15, at]
            B.gf[off + 2 * per + j : off + 2 * per + j + 1, :] = shift

    @pl.when(e.r == ROW_BH // e.slab)
    def _():
        off = MARGIN + ROW_BH % e.slab
        for j in range(CLSP // LANES):
            at = slice(LANES * j, LANES * (j + 1))
            B.gf[off + j : off + j + 1, :] = B.pb[9:10, at] + B.pb[10:11, at] + B.pb[11:12, at]
        rest = FLAT - ROW_BH - CLSP // LANES
        B.gf[off + CLSP // LANES : off + CLSP // LANES + rest, :] = jnp.zeros((rest, LANES), F32)


def norm_copy(e, B, d):
    return remote(e, B.nrm.at[0], B.nrm.at[d], B.s_nrm.at[d], B.r_nrm.at[d], r=lax.rem(e.r + d, e.n))


def squares(v):
    return jnp.sum((v * v).reshape(-1, 8, LANES), 0)


def ph_norm_local(e, B):
    size = 64
    whole = e.slab // size

    def body(k, acc):
        return acc + squares(B.gf[pl.ds(pl.multiple_of(MARGIN + size * k, 8), size), :])

    part = lax.fori_loop(0, whole, body, jnp.zeros((8, LANES), F32))
    v = B.gf[MARGIN + whole * size : MARGIN + e.slab, :]
    B.nrm[0] = part + jnp.broadcast_to(jnp.sum(v * v, 0, keepdims=True) * 0.125, (8, LANES))


def ph_norm(e, B):
    def pieces():
        B.nrm[0] += squares(B.fp[...].astype(F32))

    ends_here(e, pieces)

    @pl.when(e.g == 0)
    def _():
        B.nrm[0] += squares(B.sga[pl.ds(pl.multiple_of(e.i * QUARTER, QUARTER), QUARTER), :])

    for d in range(1, e.n):
        norm_copy(e, B, d).start()


def ph_norm_wait(e, B):
    for d in range(1, e.n):
        norm_copy(e, B, d).wait_recv()
    total = None
    for k in range(e.n):
        part = B.nrm[lax.rem(e.r - k + e.n, e.n)]
        total = part if total is None else total + part
    square = jnp.sum(jnp.sum(total, 0, keepdims=True), 1, keepdims=True)
    B.o_norm[...] = jnp.broadcast_to(jnp.sqrt(square), (8, LANES))
    loss = B.pb[15:16, :]
    loss = loss[:, 0:LANES] + loss[:, LANES : 2 * LANES] + loss[:, 2 * LANES : 3 * LANES]
    B.o_loss[...] = jnp.broadcast_to(loss, (8, LANES))
    for d in range(1, e.n):
        norm_copy(e, B, d).wait_send()


def buffers(e):
    n, G, nb, slab = e.n, e.G, e.nb, e.slab
    tiles = (3, 3, 16, LANES)
    parts = GROUP * nb
    V = pltpu.VMEM
    D = pltpu.SemaphoreType.DMA
    return dict(
        gw=V((n, 2, e.half, LANES), BF16),
        tab=V((TAB_ROWS, LANES), F32),
        big=V((10816, LANES), F32),
        dx=V((8 * DOUT, LANES), F32),
        wup=V((C, HID), BF16),
        wdn=V((HID, C), BF16),
        wds=V((4 * C, DOUT), BF16),
        wh=V((DOUT, CLSP), BF16),
        xg=V((MICRO, 14, COLS, C), BF16),
        xc=V((J * NPOS, LANES), F32),
        kb=V((49 * J, 8, LANES), F32),
        v1=V((NPOS, C), F32),
        rs1=V((NPOS, LANES), F32),
        v2=V((NPOS, C), F32),
        rs2=V((NPOS, LANES), F32),
        n=V((NPOS, C), BF16),
        u=V((NPOS, HID), BF16),
        gp=V((NPOS, HID), BF16),
        z=V((J * NPOS, LANES), F32),
        dz=V((NPOS, C), BF16),
        ps=V((MICRO, 2, OWN, C), F32),
        sl=V((32, C), F32),
        sr=V((G, 32, C), F32),
        dn2=V((32, C), F32),
        dnt=V((MICRO, 2, OWN, C), F32),
        pb=V((16, 4 * C), F32),
        pall=V((parts, 16, 4 * C), BF16),
        acc=V((7, 8, C), F32),
        acup=V((8, HID), F32),
        hs=V((MICRO, 2, 3, COLS, C), BF16),
        hr=V((MICRO, 2, 3, COLS, C), BF16),
        gb=V((PARTS, 4, 2, 2) + tiles, BF16),
        ra1=V((PARTS, 4, 2) + tiles, BF16),
        sa2=V((PARTS, 4) + tiles, BF16),
        ra2=V((PARTS, 4) + tiles, BF16),
        h1=V((PARTS, 4) + tiles, F32),
        sc=V((PARTS, 4) + tiles, BF16),
        rc=V((PARTS, G) + tiles, BF16),
        rb=V((PARTS, nb) + tiles, BF16),
        fp=V((PARTS,) + tiles, BF16),
        ro=V((2, 16) + tiles, BF16),
        ro_up=V((2, 8) + tiles, BF16),
        gf=V((MARGIN + slab + MARGIN, LANES), F32),
        sg=V((SG_ROWS, LANES), F32),
        sg_group=V((GROUP - 1, QUARTER, LANES), F32),
        sg_line=V((G, QUARTER, LANES), F32),
        sgb=V((nb, QUARTER, LANES), F32),
        sga=V((SG_ROWS, LANES), F32),
        nrm=V((n, 8, LANES), F32),
        s_own=D((1,)),
        s_feat=D((MICRO, GROUP)),
        r_feat=D((MICRO, GROUP)),
        s_halo=D((2, MICRO)),
        r_halo=D((2, MICRO)),
        s_tab=D((len(TABLES), G)),
        s_tabg=D((len(TABLES), GROUP)),
        r_tab=D((len(TABLES),)),
        s_line=D((2, G)),
        r_line=D((G, CHUNKS)),
        s_pair=D((G,)),
        r_pair=D((G, CHUNKS)),
        s_row=D((2, G)),
        r_row=D((2, G, CHUNKS)),
        s_core=D((4, G)),
        r_core=D((4, G, CHUNKS)),
        s_patch=D((G,)),
        r_patch=D((G,)),
        s_pb=D((nb,)),
        r_pb=D((nb,)),
        s_pg=D((GROUP,)),
        r_pg=D((GROUP,)),
        s_dy=D((2, MICRO)),
        r_dy=D((2, MICRO)),
        s_out=D((MICRO, 2, GROUP)),
        r_out=D((MICRO, 2, GROUP)),
        s_outown=D((MICRO, 2)),
        s_rs=D((PARTS, 2)),
        r_rs=D((PARTS, 2)),
        s_rc=D((PARTS, 4)),
        r_rc=D((PARTS, G)),
        s_rb=D((PARTS, nb)),
        r_rb=D((PARTS, nb)),
        s_ro=D((PARTS, 2)),
        r_ro=D((PARTS, 16)),
        s_sg=D((GROUP,)),
        r_sg=D((GROUP,)),
        s_sgl=D((G,)),
        r_sgl=D((G,)),
        s_sgg=D((GROUP,)),
        r_sgg=D((GROUP,)),
        s_sgb=D((nb,)),
        r_sgb=D((nb,)),
        s_nrm=D((n,)),
        r_nrm=D((n,)),
    )


def ph_clear(e, B):
    B.sg[...] = jnp.zeros_like(B.sg)
    B.gf[...] = jnp.zeros_like(B.gf)


def ph_result(e, B):
    B.o_grad[...] = B.gf[MARGIN : MARGIN + e.slab, :]


def schedule(e, B):
    def do(step, *args):
        return lambda: step(e, B, *args)

    def level_of(row):
        return row // e.slab // GROUP

    up = range(0, level_of(ROW_CUP - 1) + 1)
    down = range(up.stop, level_of(ROW_VEC - 1) + 1)
    rest = range(down.stop, e.G)
    ph_barrier_signal(e, B)
    ph_cast(e, B)
    ph_feat_zero(e, B)
    ph_clear(e, B)
    ph_barrier_wait(e, B)
    every = range(CHUNKS)
    one, two = range(0, CHUNKS // 2), range(CHUNKS // 2, CHUNKS)

    def hops(some):
        return range(max(max(level, e.G - 1 - level) for level in some) + 1)

    def steps(step, some, which, chunks):
        return [do(step, some, h, chunks) for h in which]

    ph_tables_start(e, B)
    feat_start(e, B, 0)
    line_send(e, B, range(e.G), every)
    tables_forward(e, B, (0, 2))
    feat_start(e, B, 1)
    line_step(e, B, up, 1, every)
    halo_start(e, B, 0)
    feat_start(e, B, 2)
    for h in hops(up)[2:3]:
        line_step(e, B, up, h, every)
    for h in hops(up)[:3]:
        pair_step(e, B, up, h, every)
    tables_wait(e, B, (0, 2))
    ph_taps(e, B)
    ph_conv_fwd(
        e,
        B,
        {
            0: [do(halo_wait, 0), do(transpose, 0)],
            1: [do(halo_start, 1)] + steps(line_step, rest, [1], one),
            2: steps(line_step, rest, [1], two) + steps(line_step, up, hops(up)[3:], every) + steps(pair_step, up, hops(up)[3:], every),
            4: [do(halo_start, 2)] + steps(line_step, down, [1], every) + steps(pair_step, down, hops(down)[:2], every),
            6: [do(halo_wait, 1), do(transpose, 1)],
            7: [do(tables_forward, (1, 3, 4))] + steps(row_step, up, hops(up), one),
            8: steps(line_step, rest, hops(rest)[2:3], one) + steps(pair_step, rest, hops(rest)[:2], every),
            9: steps(row_step, up, hops(up), two),
            10: steps(line_step, rest, hops(rest)[2:3], two),
            11: steps(line_step, down, hops(down)[2:], every)
            + steps(pair_step, down, hops(down)[2:], every)
            + steps(pair_step, rest, hops(rest)[2:3], every),
            12: [do(halo_wait, 2), do(transpose, 2)],
            13: steps(core_step, up, hops(up), one) + steps(row_step, down, hops(down)[:2], every),
            15: steps(line_step, rest, hops(rest)[3:], every) + steps(pair_step, rest, hops(rest)[3:], every),
            16: steps(row_step, rest, [0], every),
            17: steps(core_step, up, hops(up), two),
        },
    )
    ph_norm_one(e, B)
    tables_wait(e, B, (1, 3, 4))
    for h in hops(down)[2:]:
        row_step(e, B, down, h, every)
    row_step(e, B, rest, 1, every)
    gather_ready(e, B, up)
    ph_weights_up(e, B)
    ph_mlp_up(
        e,
        B,
        {
            0: steps(row_step, rest, hops(rest)[2:3], every),
            2: steps(core_step, down, hops(down)[:2], every) + steps(core_step, rest, [0], every),
            3: steps(row_step, rest, hops(rest)[3:], every),
            4: steps(core_step, down, hops(down)[2:], every),
            5: steps(core_step, rest, [1], every),
        },
    )
    gather_ready(e, B, down)
    ph_weights_down(e, B)
    ph_mlp_down(
        e,
        B,
        {
            1: steps(core_step, rest, hops(rest)[2:3], every),
            4: steps(core_step, rest, hops(rest)[3:], every),
        },
    )
    ph_patch_local(e, B)
    patch_start(e, B)
    gather_ready(e, B, rest)
    ph_weights_head(e, B)
    patch_wait(e, B)
    ph_head(e, B)
    ph_payload_batch(e, B)
    ph_dy_edges(e, B)
    ph_bwd_one(e, B)
    for f in (0, 1):
        wgrad_down(e, B, f)
        rs_step1(e, B, f)
    ph_bwd_two(
        e,
        B,
        {
            1: [do(ph_payload_group)],
            2: [do(dy_send, 0), do(rs_step2, 0)],
            3: [do(rs_step2, 1)],
            4: [do(dy_send, 1)],
        },
    )
    dy_send(e, B, 2)
    for f in (2, 3):
        wgrad_up(e, B, f)
        rs_step1(e, B, f)
    dy_take(e, B, 0)
    dy_take(e, B, 1)
    rs_step3(e, B, 0)
    ph_conv_kernel(
        e,
        B,
        range(0, MICRO - 1),
        {
            4: [do(rs_step3, 1)],
            6: [do(rs_step2, 2)],
            9: [do(rs_step2, 3)],
            20: [do(rs_step3, 2)],
        },
    )
    dy_take(e, B, MICRO - 1)
    ph_conv_kernel(
        e,
        B,
        range(MICRO - 1, MICRO),
        {
            7: [do(rs_step3, 3)],
            12: [do(rs_step4, 0)],
            17: [do(rs_step4, 1)],
        },
    )
    ph_small_fill(e, B)
    small_step1(e, B)
    ph_feat_done(e, B)
    ph_taps_low(e, B)
    ph_conv_input(
        e,
        B,
        {
            3: [do(out_send, 0, 0)],
            5: [do(rs_step4, 2)],
            6: [do(small_step2), do(out_send, 0, 1)],
            7: [do(rs_step5, 0), do(rs_step4, 3)],
            8: [do(rs_step5, 1)],
            9: [do(rs_step5, 2), do(out_send, 1, 0)],
            11: [do(rs_step5, 3)],
            12: [do(out_send, 1, 1)],
            13: [do(ph_payload_wait), do(ph_head_grads), do(ph_norm_local)],
            14: [do(small_step3)],
            15: [do(out_send, 2, 0)],
        },
    )
    small_step4(e, B)
    ph_norm(e, B)
    out_send(e, B, 2, 1)
    for f in range(PARTS):
        rs_place(e, B, f)
    ph_small_place(e, B)
    ph_result(e, B)
    ph_tables_done(e, B)
    ph_gather_done(e, B)
    ph_dy_done(e, B)
    ph_rs_done(e, B)
    ph_small_done(e, B)
    ph_norm_wait(e, B)
    ph_out_wait(e, B)


def step_kernel(e, names, *refs):
    B = Env()
    for name, ref in zip(names, refs):
        setattr(B, name, ref)
    here(e)
    schedule(e, B)


def train_step(e, features, mask, labels, params):
    bufs = buffers(e)
    names = ["mask", "labels", "features", "params", "o_grad", "o_norm", "o_loss", "fo"] + list(bufs)
    return pl.pallas_call(
        functools.partial(step_kernel, e, names),
        out_shape=(
            jax.ShapeDtypeStruct((e.slab, LANES), F32),
            jax.ShapeDtypeStruct((8, LANES), F32),
            jax.ShapeDtypeStruct((8, LANES), F32),
            jax.ShapeDtypeStruct((MICRO, GROUP, 2, COLS, C), BF16),
        ),
        in_specs=[
            pl.BlockSpec(memory_space=pltpu.SMEM),
            pl.BlockSpec(memory_space=pltpu.SMEM),
            pl.BlockSpec(memory_space=pl.ANY),
            pl.BlockSpec(memory_space=pltpu.VMEM),
        ],
        out_specs=(
            pl.BlockSpec(memory_space=pltpu.VMEM),
            pl.BlockSpec(memory_space=pltpu.VMEM),
            pl.BlockSpec(memory_space=pltpu.VMEM),
            pl.BlockSpec(memory_space=pl.ANY),
        ),
        scratch_shapes=list(bufs.values()),
        compiler_params=pltpu.CompilerParams(collective_id=0, has_side_effects=True, vmem_limit_bytes=64 * MB - 65536),
        name="train_step",
    )(mask, labels, features, params)


def update_kernel(e, norm, loss, grad, params, m1, m2, out, o_norm, o_loss, new_params, first, second, feats, *scratch):
    g, p, a, b, fin, fout, s_in, s_out, s_feat, s_fout = scratch
    parts = 4
    size = e.slab // parts // 8 * 8
    spans = [(k * size, size if k < parts - 1 else e.slab - k * size) for k in range(parts)]
    copy = pltpu.make_async_copy
    ins = []
    for k, (at, count) in enumerate(spans):
        for q, (src, dst) in enumerate(((grad, g), (params, p), (m1, a), (m2, b))):
            ins.append(copy(src.at[pl.ds(at, count)], dst.at[pl.ds(at, count)], s_in.at[k, q]))
            ins[-1].start()
    fins = [copy(out.at[k], fin.at[k], s_feat.at[k]) for k in range(MICRO)]
    for cp in fins:
        cp.start()
    o_norm[0, 0] = jnp.max(norm[...])
    o_loss[0, 0] = jnp.max(loss[...])
    scale = jnp.minimum(1.0, CLIP / (norm[0:1, 0:1] + 1e-06))
    outs = []
    for k, (at, count) in enumerate(spans):
        for q in range(4):
            ins[4 * k + q].wait()
        rows = slice(at, at + count)
        clipped = g[rows, :] * scale
        one = BETA_ONE * a[rows, :] + (1.0 - BETA_ONE) * clipped
        two = BETA_TWO * b[rows, :] + (1.0 - BETA_TWO) * clipped * clipped
        a[rows, :] = one
        b[rows, :] = two
        ratio = one / (1.0 - BETA_ONE**STEP) / (jnp.sqrt(two / (1.0 - BETA_TWO**STEP)) + EPS_ADAM)
        p[rows, :] = p[rows, :] - RATE * (ratio + DECAY * p[rows, :])
        for q, (src, dst) in enumerate(((p, new_params), (a, first), (b, second))):
            outs.append(copy(src.at[pl.ds(at, count)], dst.at[pl.ds(at, count)], s_out.at[k, q]))
            outs[-1].start()
        if k < MICRO:
            fins[k].wait()
            fout[k] = fin[k].astype(F32)
            outs.append(copy(fout.at[k], feats.at[k], s_fout.at[k]))
            outs[-1].start()
    for cp in outs:
        cp.wait()


def update(e, grad, norm, loss, params, m1, m2, out):
    flat = jax.ShapeDtypeStruct((e.slab, LANES), F32)
    scalar = jax.ShapeDtypeStruct((1, 1), F32)
    shape = (MICRO, GROUP, 2, COLS, C)
    near, far, one = (pl.BlockSpec(memory_space=k) for k in (pltpu.VMEM, pl.ANY, pltpu.SMEM))
    D = pltpu.SemaphoreType.DMA
    return pl.pallas_call(
        functools.partial(update_kernel, e),
        in_specs=[near, near, far, far, far, far, far],
        out_specs=(one, one, far, far, far, far),
        out_shape=(scalar, scalar, flat, flat, flat, jax.ShapeDtypeStruct(shape, F32)),
        scratch_shapes=[pltpu.VMEM((e.slab, LANES), F32)] * 4
        + [pltpu.VMEM(shape, BF16), pltpu.VMEM(shape, F32), D((4, 4)), D((4, 3)), D((MICRO,)), D((MICRO,))],
        compiler_params=pltpu.CompilerParams(vmem_limit_bytes=64 * MB - 65536),
        name="update",
    )(norm, loss, grad, params, m1, m2, out)


def local(e, features, drop_mask, labels, params, moment1, moment2):
    flat = [v.reshape(e.slab, LANES) for v in (params, moment1, moment2)]
    grad, norm, loss, out = train_step(e, features, drop_mask, labels, flat[0])
    norm, loss, new_params, first, second, feats = update(e, grad, norm, loss, *flat, out)
    size = e.slab * LANES
    return (
        new_params.reshape(size),
        first.reshape(size),
        second.reshape(size),
        loss.reshape(()),
        norm.reshape(()),
        feats,
    )


def solution(mesh):
    e = Env()
    e.n = mesh.shape["rows"]
    e.nb = mesh.shape["batch"]
    e.G = e.n // GROUP
    e.slab = FLAT // e.n
    e.half = (e.slab + 31) // 32 * 16
    e.positions = float(e.n * COLS // 2)
    e.inv_count = 1.0 / (MICRO * GROUP * e.nb)
    return jax.shard_map(
        functools.partial(local, e),
        mesh=mesh,
        in_specs=(
            P(None, "batch", "rows", None, None),
            P(None, "batch"),
            P(None, "batch"),
            P("rows"),
            P("rows"),
            P("rows"),
        ),
        out_specs=(P("rows"), P("rows"), P("rows"), P(), P(), P(None, "batch", "rows", None, None)),
        check_vma=False,
    )
```

```python
import functools

import jax
import jax.numpy as jnp
from jax import lax
from jax.experimental import pallas as pl
from jax.experimental.pallas import tpu as pltpu
from jax.sharding import PartitionSpec as P

C = 384
HID = 1536
DOUT = 768
CLS = 1000
MICRO = 3
STEP = 10
P_SIZE = 3153920
KEEP = 0.8
CLIP = 0.01
RATE = 0.05
BETA_ONE = 0.9
BETA_TWO = 0.999
DECAY = 0.05
EPS_ADAM = 1e-08
EPS_NORM = 1e-06

MESH = pl.DeviceIdType.MESH
F32 = jnp.float32
BF16 = jnp.bfloat16
MB = 1 << 20

LANES = 128
J = C // LANES
GROUP = 4
OWN = 8
COLS = 64
PADC = COLS + 6
SUB = 16
POS = COLS * OWN
NPOS = MICRO * POS
FLAT = P_SIZE // LANES
ROW_K = 0
ROW_UP = 49 * J
ROW_CUP = ROW_UP + C * HID // LANES
ROW_DOWN = ROW_CUP + HID // LANES
ROW_VEC = ROW_DOWN + C * HID // LANES
ROW_DS = ROW_VEC + 7 * J
ROW_OUT = ROW_DS + 4 * C * DOUT // LANES
ROW_HEAD = ROW_OUT + 3 * DOUT // LANES
ROW_BH = ROW_HEAD + DOUT * CLS // LANES
TABLES = (
    (ROW_K, 49 * J, 0),
    (ROW_CUP, HID // LANES, 152),
    (ROW_VEC, 7 * J, 168),
    (ROW_OUT, 3 * DOUT // LANES, 192),
    (ROW_BH, FLAT - ROW_BH, 216),
)
TAB_ROWS = 232
TAB_SPAN = (152, 16, 24, 24, 16)
T_CUP, T_VEC, T_OUT, T_BH = 152, 168, 192, 216
SG_ROWS = 320
SG_VEC, SG_CUP = 160, 240
CLSP = 1024


class Env:
    pass


def xrow(j, m):
    return (j * MICRO + m) * PADC * SUB


def rows_of(refs, row, count):
    return refs[row : row + count, :]


def lane_row(ref, row, count):
    return jnp.concatenate([ref[row + k : row + k + 1, :] for k in range(count)], axis=1)


def ln_parts(blocks, width):
    total = blocks[0]
    for block in blocks[1:]:
        total = total + block
    mean = jnp.sum(total, -1, keepdims=True) * (1.0 / width)
    centred = [block - mean for block in blocks]
    square = centred[0] * centred[0]
    for block in centred[1:]:
        square = square + block * block
    spread = jnp.sum(square, -1, keepdims=True) * (1.0 / width)
    scale = lax.rsqrt(spread + EPS_NORM)
    return [block * scale for block in centred], scale


def here(e):
    e.r = lax.axis_index("rows")
    e.b = lax.axis_index("batch")
    e.g = e.r // GROUP
    e.i = e.r % GROUP
    e.h = e.b % 2


def dev(e, r=None, b=None):
    return {"rows": e.r if r is None else r, "batch": e.b if b is None else b}


def remote(e, src, dst, send, recv, r=None, b=None):
    return pltpu.make_async_remote_copy(
        src, dst, send, recv, device_id=(e.r if r is None else r, e.b if b is None else b), device_id_type=MESH
    )


def ph_barrier_signal(e, B):
    barrier = pltpu.get_barrier_semaphore()
    for d in range(1, e.n):
        pl.semaphore_signal(barrier, inc=1, device_id=(lax.rem(e.r + d, e.n), e.b), device_id_type=MESH)
    for d in range(1, e.nb):
        pl.semaphore_signal(barrier, inc=1, device_id=(e.r, lax.rem(e.b + d, e.nb)), device_id_type=MESH)


def ph_barrier_wait(e, B):
    pl.semaphore_wait(pltpu.get_barrier_semaphore(), e.n - 1 + e.nb - 1)


def feat_copy(e, B, m, d):
    j = lax.rem(e.i + d, GROUP)
    return remote(
        e,
        B.features.at[m, j],
        B.xg.at[m, pl.ds(3 + 2 * e.i, 2)],
        B.s_feat.at[m, d],
        B.r_feat.at[m, d],
        r=e.g * GROUP + j,
    )


def feat_own(e, B):
    return pltpu.make_async_copy(B.features.at[:, e.i], B.xg.at[:, pl.ds(3 + 2 * e.i, 2)], B.s_own.at[0])


def feat_start(e, B, m):
    if m == 0:
        feat_own(e, B).start()
    for d in (2, 3, 1):
        feat_copy(e, B, m, d).start()


def ph_feat_zero(e, B):
    zero = jnp.zeros((MICRO, 3, COLS, C), BF16)

    @pl.when(e.g == 0)
    def _():
        B.xg[:, 0:3] = zero

    @pl.when(e.g == e.G - 1)
    def _():
        B.xg[:, 11:14] = zero


def halo_copy(e, B, m, up):
    if up:
        return remote(e, B.xg.at[m, 8:11], B.xg.at[m, 0:3], B.s_halo.at[1, m], B.r_halo.at[1, m], r=e.r + GROUP)
    return remote(e, B.xg.at[m, 3:6], B.xg.at[m, 11:14], B.s_halo.at[0, m], B.r_halo.at[0, m], r=e.r - GROUP)


def halo_start(e, B, m):
    if m == 0:
        feat_own(e, B).wait()
    for d in range(1, GROUP):
        feat_copy(e, B, m, d).wait_recv()

    @pl.when(e.g > 0)
    def _():
        halo_copy(e, B, m, False).start()

    @pl.when(e.g < e.G - 1)
    def _():
        halo_copy(e, B, m, True).start()


def halo_wait(e, B, m):
    @pl.when(e.g < e.G - 1)
    def _():
        halo_copy(e, B, m, False).wait_recv()

    @pl.when(e.g > 0)
    def _():
        halo_copy(e, B, m, True).wait_recv()


def ph_feat_done(e, B):
    for m in range(MICRO):
        for d in range(1, GROUP):
            feat_copy(e, B, m, d).wait_send()

        @pl.when(e.g > 0)
        def _(m=m):
            halo_copy(e, B, m, False).wait_send()

        @pl.when(e.g < e.G - 1)
        def _(m=m):
            halo_copy(e, B, m, True).wait_send()


def ph_cast(e, B):
    for h in range(2):
        count = e.half if h == 0 else e.slab - e.half
        whole = count // 16 * 16
        B.gw[e.r, h, 0:whole, :] = B.params[h * e.half : h * e.half + whole, :].astype(BF16)
        rest = count - whole
        if whole < e.half:
            parts = [jnp.zeros((e.half - whole - rest, LANES), F32)]
            if rest:
                parts = [B.params[e.slab - rest : e.slab, :]] + parts
            B.gw[e.r, h, whole : e.half, :] = jnp.concatenate(parts, axis=0).astype(BF16)
    for k, (first, count, place) in enumerate(TABLES):
        off = first % e.slab

        @pl.when(e.r == first // e.slab)
        def _(off=off, count=count, place=place):
            B.tab[place : place + count, :] = B.params[off : off + count, :]


def table_line(e, B, k, d):
    first, count, place = TABLES[k]
    owner = first // e.slab
    part = pl.ds(place, TAB_SPAN[k])
    return remote(e, B.tab.at[part], B.tab.at[part], B.s_tab.at[k, d], B.r_tab.at[k], r=lax.rem(owner + GROUP * d, e.n))


def table_group(e, B, k, d):
    first, count, place = TABLES[k]
    part = pl.ds(place, TAB_SPAN[k])
    to = e.g * GROUP + lax.rem(e.i + d, GROUP)
    return remote(e, B.tab.at[part], B.tab.at[part], B.s_tabg.at[k, d], B.r_tab.at[k], r=to)


def ph_tables_start(e, B):
    for k, (first, count, place) in enumerate(TABLES):
        owner = first // e.slab

        @pl.when(e.r == owner)
        def _(k=k):
            for d in range(1, e.G):
                table_line(e, B, k, d).start()
            for d in range(1, GROUP):
                table_group(e, B, k, d).start()


def tables_forward(e, B, some):
    for k in some:
        owner = TABLES[k][0] // e.slab

        @pl.when(jnp.logical_and(e.i == owner % GROUP, e.r != owner))
        def _(k=k):
            table_line(e, B, k, 1).wait_recv()
            for d in range(1, GROUP):
                table_group(e, B, k, d).start()


def tables_wait(e, B, some):
    for k in some:
        owner = TABLES[k][0] // e.slab

        @pl.when(e.i != owner % GROUP)
        def _(k=k):
            table_group(e, B, k, 1).wait_recv()


def ph_tables_done(e, B):
    for k, (first, count, place) in enumerate(TABLES):
        owner = first // e.slab

        @pl.when(e.r == owner)
        def _(k=k):
            for d in range(1, e.G):
                table_line(e, B, k, d).wait_send()

        @pl.when(e.i == owner % GROUP)
        def _(k=k):
            for d in range(1, GROUP):
                table_group(e, B, k, d).wait_send()


CHUNKS = 4


def chunk_of(e, c):
    if c is None:
        return pl.ds(0, e.half)
    tiles = e.half // 16
    cuts = [(tiles * k + CHUNKS - 1) // CHUNKS * 16 for k in range(CHUNKS + 1)]
    return pl.ds(cuts[c], cuts[c + 1] - cuts[c])


def half_ref(e, B, slot, h, c):
    return B.gw.at[slot, h, chunk_of(e, c)]


def line_copy(e, B, level, up, c):
    ref = half_ref(e, B, level * GROUP + e.i, e.h, c)
    k = 0 if up else 1
    return remote(e, ref, ref, B.s_line.at[k, level], B.r_line.at[level, c or 0], r=e.r + GROUP if up else e.r - GROUP)


def pair_copy(e, B, level, c):
    ref = half_ref(e, B, level * GROUP + e.i, e.h, c)
    to = e.g * GROUP + lax.rem(e.i + 2, GROUP)
    return remote(e, ref, ref, B.s_pair.at[level], B.r_pair.at[level, c or 0], r=to)


def row_copy(e, B, level, other, c):
    i = lax.rem(e.i + 2, GROUP) if other else e.i
    ref = half_ref(e, B, level * GROUP + i, e.h, c)
    k = int(other)
    return remote(e, ref, ref, B.s_row.at[k, level], B.r_row.at[k, level, c or 0], b=e.b + 1 - 2 * e.h)


def core_copy(e, B, level, other, mine, c):
    i = lax.rem(e.i + 2, GROUP) if other else e.i
    ref = half_ref(e, B, level * GROUP + i, e.h if mine else 1 - e.h, c)
    k = 2 * int(other) + int(mine)
    sib = e.g * GROUP + e.i + 1 - 2 * (e.i % 2)
    return remote(e, ref, ref, B.s_core.at[k, level], B.r_core.at[k, level, c or 0], r=sib)


def line_out(e, B, level, c):
    @pl.when(jnp.logical_and(e.g >= level, e.g + 1 < e.G))
    def _():
        line_copy(e, B, level, True, c).start()

    @pl.when(jnp.logical_and(e.g <= level, e.g >= 1))
    def _():
        line_copy(e, B, level, False, c).start()


def at_hop(e, level, hop, body):
    if hop == 0:
        cond = e.g == level
    else:
        cond = jnp.logical_or(e.g == level + hop, e.g == level - hop)
    pl.when(cond)(body)


def line_send(e, B, levels, chunks):
    for level in levels:

        def body(level=level):
            for c in chunks:
                line_out(e, B, level, c)

        at_hop(e, level, 0, body)


def line_step(e, B, levels, hop, chunks):
    for level in levels:

        def body(level=level):
            for c in chunks:
                line_copy(e, B, level, True, c).wait_recv()
                line_out(e, B, level, c)
                row_copy(e, B, level, False, c).start()
                core_copy(e, B, level, False, True, c).start()

        at_hop(e, level, hop, body)


def pair_step(e, B, levels, hop, chunks):
    for level in levels:

        def body(level=level):
            for c in chunks:
                pair_copy(e, B, level, c).start()
                if hop == 0:
                    core_copy(e, B, level, False, True, c).start()
                    core_copy(e, B, level, False, False, c).start()

        at_hop(e, level, hop, body)


def row_step(e, B, levels, hop, chunks):
    for level in levels:

        def body(level=level):
            for c in chunks:
                pair_copy(e, B, level, c).wait_recv()
                row_copy(e, B, level, True, c).start()
                core_copy(e, B, level, True, True, c).start()

        at_hop(e, level, hop, body)


def core_step(e, B, levels, hop, chunks):
    for level in levels:

        def body(level=level):
            for c in chunks:
                if hop:
                    row_copy(e, B, level, False, c).wait_recv()
                    core_copy(e, B, level, False, False, c).start()
                row_copy(e, B, level, True, c).wait_recv()
                core_copy(e, B, level, True, False, c).start()

        at_hop(e, level, hop, body)


def gather_ready(e, B, levels):
    for level in levels:
        for other in (False, True):
            for mine in (False, True):
                for c in range(CHUNKS):
                    core_copy(e, B, level, other, mine, c).wait_recv()


def ph_gather_done(e, B):
    G = e.G
    for level in range(G):
        pair_copy(e, B, level, None).wait_send()
        row_copy(e, B, level, True, None).wait_send()

        @pl.when(e.g != level)
        def _(level=level):
            row_copy(e, B, level, False, None).wait_send()

        for other in (False, True):
            for mine in (False, True):
                core_copy(e, B, level, other, mine, None).wait_send()

        @pl.when(jnp.logical_and(e.g >= level, e.g + 1 < G))
        def _(level=level):
            line_copy(e, B, level, True, None).wait_send()

        @pl.when(jnp.logical_and(e.g <= level, e.g >= 1))
        def _(level=level):
            line_copy(e, B, level, False, None).wait_send()


def flatten(e, B, first, last):
    s0 = first // e.slab

    def slab(k, _):
        for h in range(2):
            count = (e.half if h == 0 else e.slab - e.half + 15) // 16 * 16
            base = e.slab * k + h * e.half
            B.big[pl.ds(base, count), :] = B.gw[s0 + k, h, 0:count, :].astype(F32)
        return 0

    lax.fori_loop(0, (last - 1) // e.slab - s0 + 1, slab, 0)
    return e.slab * s0


def ph_weights_up(e, B):
    base = flatten(e, B, ROW_UP, ROW_CUP)
    for j in range(HID // LANES):
        B.wup[:, LANES * j : LANES * (j + 1)] = B.big[pl.ds(ROW_UP - base + j, C, stride=HID // LANES), :].astype(BF16)


def ph_weights_down(e, B):
    base = flatten(e, B, ROW_DOWN, ROW_VEC)
    for j in range(J):
        B.wdn[:, LANES * j : LANES * (j + 1)] = B.big[pl.ds(ROW_DOWN - base + j, HID, stride=J), :].astype(BF16)


def ph_weights_head(e, B):
    base = flatten(e, B, ROW_DS, ROW_OUT)
    per = DOUT // LANES
    for j in range(per):
        B.wds[:, LANES * j : LANES * (j + 1)] = B.big[pl.ds(ROW_DS - base + j, 4 * C, stride=per), :].astype(BF16)
    base = flatten(e, B, ROW_HEAD, ROW_BH)
    lane = lax.broadcasted_iota(jnp.int32, (DOUT // 16, LANES), 1)
    for kk in range(16):
        first, off = divmod(CLS * kk, LANES)
        parts = [B.big[pl.ds(ROW_HEAD - base + first + t, DOUT // 16, stride=125), :] for t in range(9 if off else 8)]
        if off:
            parts = [pltpu.roll(part, LANES - off, 1) for part in parts]
        for t in range(8):
            tile = parts[t]
            if off:
                tile = jnp.where(lane < LANES - off, parts[t], parts[t + 1])
            if t == 7:
                tile = jnp.where(lane < CLS - 7 * LANES, tile, 0.0)
            B.dx[pl.ds(DOUT * t + kk, DOUT // 16, stride=16), :] = tile
    for t in range(8):
        B.wh[:, LANES * t : LANES * (t + 1)] = B.dx[DOUT * t : DOUT * (t + 1), :].astype(BF16)


def hooks(it, steps, also=None):
    if not steps:
        return
    bits = sum(1 << k for k in steps)
    due = lax.rem(lax.shift_right_logical(jnp.int32(bits), it), 2) == 1
    if also is not None:
        due = jnp.logical_and(due, also)

    @pl.when(due)
    def _():
        for k, some in steps.items():

            @pl.when(it == k)
            def _(some=some):
                for step in some:
                    step()


def transpose(e, B, m):
    pad = jnp.zeros((3 * SUB, LANES), F32)
    for j in range(J):
        B.big[pl.ds(xrow(j, m), 3 * SUB), :] = pad
        B.big[pl.ds(xrow(j, m) + (COLS + 3) * SUB, 3 * SUB), :] = pad
        for row in range(14):
            v = B.xg[m, row, :, LANES * j : LANES * (j + 1)].astype(F32)
            B.big[pl.ds(xrow(j, m) + 3 * SUB + row, COLS, stride=SUB), :] = v
            if 3 <= row < 11:
                B.xc[pl.ds(j * NPOS + m * POS + row - 3, COLS, stride=OWN), :] = v


def ph_taps(e, B):
    def body(t, _):
        B.kb[t] = jnp.broadcast_to(B.tab[pl.ds(t, 1), :], (8, LANES))
        return 0

    lax.fori_loop(0, 49 * J, body, 0)


def vec_row(B, v, j):
    row = T_VEC + v * J + j
    return B.tab[row : row + 1, :]


def conv_tile(B, m, j, c0, tile, acc, flip):
    for a in range(7):
        taps = [B.kb[((6 - a) * 7 + 6 - b if flip else a * 7 + b) * J + j] for b in range(7)]
        for c in range(tile + 6):
            d = B.big[pl.ds(xrow(j, m) + (c0 + c) * SUB + a, OWN), :]
            for b in range(7):
                if 0 <= c - b < tile:
                    acc[c - b] = acc[c - b] + d * taps[b]
    return acc


TILE = 32


def ph_conv_fwd(e, B, steps):
    halves = COLS // TILE

    def body(it, _):
        m = it // halves
        c0 = it % halves * TILE
        for j in range(J):
            hooks(it, {k // J: v for k, v in steps.items() if k % J == j})
            bias = jnp.broadcast_to(vec_row(B, 0, j), (OWN, LANES))
            acc = conv_tile(B, m, j, c0, TILE, [bias] * TILE, False)
            at = j * NPOS + m * POS + c0 * OWN
            for c in range(TILE):
                B.dx[pl.ds(pl.multiple_of(at + OWN * c, OWN), OWN), :] = acc[c]
        return 0

    lax.fori_loop(0, MICRO * halves, body, 0)


def ph_norm_one(e, B):
    size = 256

    def body(it, _):
        at = pl.multiple_of(it * size, size)
        hat, scale = ln_parts([B.dx[pl.ds(j * NPOS + at, size), :] for j in range(J)], C)
        B.rs1[pl.ds(at, size), :] = jnp.broadcast_to(scale, (size, LANES))
        for j in range(J):
            B.v1[pl.ds(at, size), LANES * j : LANES * (j + 1)] = hat[j]
            B.n[pl.ds(at, size), LANES * j : LANES * (j + 1)] = (
                hat[j] * vec_row(B, 1, j) + vec_row(B, 2, j)
            ).astype(BF16)
        return 0

    lax.fori_loop(0, NPOS // size, body, 0)


def ph_mlp_up(e, B, steps):
    chunk = 256
    width = 256
    c0 = 0.7978845608028654
    c1 = 0.044715 * c0

    def body(it, _):
        hooks(it, steps)
        at = pl.multiple_of(it * chunk, chunk)
        rows = B.n[pl.ds(at, chunk), :]
        for k in range(HID // width):
            lanes = slice(width * k, width * (k + 1))
            bias = lane_row(B.tab, T_CUP + k * width // LANES, width // LANES)
            h = jnp.dot(rows, B.wup[:, lanes], preferred_element_type=F32) + bias
            sq = h * h
            half = 0.5 * jnp.tanh(h * (c0 + c1 * sq)) + 0.5
            u = h * half
            B.u[pl.ds(at, chunk), lanes] = u.astype(BF16)
            slope = half + u * (1.0 - half) * (2.0 * c0 + 6.0 * c1 * sq)
            B.gp[pl.ds(at, chunk), lanes] = slope.astype(BF16)
        return 0

    lax.fori_loop(0, NPOS // chunk, body, 0)


def ph_mlp_down(e, B, steps):
    chunk = 256
    B.ps[...] = jnp.zeros_like(B.ps)

    def body(it, _):
        hooks(it, steps)
        at = pl.multiple_of(it * chunk, chunk)
        m = it // (POS // chunk)
        keep = B.mask[m, e.i].astype(F32) * (1.0 / KEEP)
        z = jnp.dot(B.u[pl.ds(at, chunk), :], B.wdn[...], preferred_element_type=F32)
        resid = []
        for j in range(J):
            zj = z[:, LANES * j : LANES * (j + 1)] + vec_row(B, 3, j)
            B.z[pl.ds(j * NPOS + at, chunk), :] = zj
            resid.append(B.xc[pl.ds(j * NPOS + at, chunk), :] + (vec_row(B, 4, j) * keep) * zj)
        hat, scale = ln_parts(resid, C)
        B.rs2[pl.ds(at, chunk), :] = jnp.broadcast_to(scale, (chunk, LANES))
        for j in range(J):
            B.v2[pl.ds(at, chunk), LANES * j : LANES * (j + 1)] = hat[j]
            low = (hat[j] * vec_row(B, 5, j) + vec_row(B, 6, j)).astype(BF16).astype(F32)
            low = jnp.sum(low.reshape(chunk // 16, 2, OWN, LANES), 0)
            B.ps[m, :, :, LANES * j : LANES * (j + 1)] += low
        return 0

    lax.fori_loop(0, NPOS // chunk, body, 0)


def ph_patch_local(e, B):
    even = lax.broadcasted_iota(jnp.int32, (OWN, C), 0) % 2 == 0
    pick = lax.broadcasted_iota(jnp.int32, (8, C), 0)
    for parity in range(2):
        tile = jnp.zeros((8, C), F32)
        for side in range(2):
            for m in range(MICRO):
                v = B.ps[m, side]
                part = jnp.sum(jnp.where(even if parity == 0 else jnp.logical_not(even), v, 0.0), 0, keepdims=True)
                tile = jnp.where(pick == m + 4 * side, part, tile)
        B.sl[8 * parity : 8 * parity + 8, :] = tile


def place_rows(sums, q):
    tile = sums[8 * (q // 2) : 8 * (q // 2) + 8, :]
    return pltpu.roll(tile, 4, 0) if q % 2 else tile


def patch_copy(e, B, d):
    to = lax.rem(e.g + d, e.G)
    return remote(e, B.sl, B.sr.at[d], B.s_patch.at[d], B.r_patch.at[d], r=to * GROUP + e.i)


def patch_start(e, B):
    for d in range(1, e.G):
        patch_copy(e, B, d).start()
    B.sr[0] = B.sl[...]


def patch_wait(e, B):
    for d in range(1, e.G):
        patch_copy(e, B, d).wait_recv()
    for d in range(1, e.G):
        patch_copy(e, B, d).wait_send()


def split3(v):
    hi = v.astype(BF16).astype(F32)
    mid = (v - hi).astype(BF16).astype(F32)
    return hi, mid, v - hi - mid


def ph_head(e, B):
    total = None
    for level in range(e.G):
        part = B.sr[lax.rem(e.g - level + e.G, e.G)]
        total = part if total is None else total + part
    per = DOUT // LANES
    gain = lane_row(B.tab, T_OUT + per, per)
    shift = lane_row(B.tab, T_OUT + 2 * per, per)
    mean = total * (1.0 / e.positions)
    pooled = lane_row(B.tab, T_OUT, per)
    for q in range(4):
        parts = jnp.concatenate(split3(place_rows(mean, q)), axis=0).astype(BF16)
        prod = jnp.dot(parts, B.wds[C * q : C * (q + 1), :], preferred_element_type=F32)
        pooled = pooled + (prod[0:8] + (prod[8:16] + prod[16:24]))
    rows = lax.broadcasted_iota(jnp.int32, (8, 1), 0)
    live = rows < MICRO
    (hat,), scale = ln_parts([pooled], DOUT)
    query = (hat * gain + shift).astype(BF16)
    lane = lax.broadcasted_iota(jnp.int32, (8, CLSP), 1)
    logits = jnp.dot(query, B.wh[...], preferred_element_type=F32) + lane_row(B.tab, T_BH, CLSP // LANES)
    logits = jnp.where(lane < CLS, logits, -1e30)
    top = jnp.max(logits, 1, keepdims=True)
    powers = jnp.exp(logits - top)
    expsum = jnp.sum(powers, 1, keepdims=True)
    label = jnp.zeros((8, 1), jnp.int32)
    for m in range(MICRO):
        label = jnp.where(rows == m, B.labels[m, e.i], label)
    onehot = (lane == label).astype(F32)
    own = jnp.sum(jnp.where(lane == label, logits, 0.0), 1, keepdims=True)
    loss = jnp.sum(jnp.where(live, top + jnp.log(expsum) - own, 0.0), 0, keepdims=True)
    grad = jnp.where(live, (powers / expsum - onehot) * e.inv_count, 0.0).astype(BF16)
    grad_query = lax.dot_general(grad, B.wh[...], (((1,), (1,)), ((), ())), preferred_element_type=F32)
    dn = grad_query * gain
    m1 = jnp.sum(dn, 1, keepdims=True) * (1.0 / DOUT)
    m2 = jnp.sum(dn * hat, 1, keepdims=True) * (1.0 / DOUT)
    grad_pool = scale * (dn - m1 - hat * m2)
    down = jnp.where(live, grad_pool * (1.0 / e.positions), 0.0).astype(BF16)
    for q in range(4):
        B.dn2[8 * q : 8 * q + 8, :] = lax.dot_general(
            down, B.wds[C * q : C * (q + 1), :], (((1,), (1,)), ((), ())), preferred_element_type=F32
        )
    low = grad.astype(F32)
    d32 = down.astype(F32)
    q32 = jnp.where(live, query.astype(F32), 0.0)
    zero3 = jnp.zeros((3, C), F32)
    g3 = jnp.sum(jnp.where(live, grad_query * hat, 0.0), 0, keepdims=True)
    s3 = jnp.sum(jnp.where(live, grad_query, 0.0), 0, keepdims=True)
    vec = jnp.concatenate([g3, s3], axis=1)
    vec_parts = split3(vec)
    loss_parts = split3(loss)
    for q in range(4):
        at = slice(C * q, C * (q + 1))
        s_hi, s_mid, _ = split3(place_rows(total, q))
        B.pb[0:8, at] = jnp.zeros((8, C), F32)
        B.pb[8:16, at] = jnp.zeros((8, C), F32)
        B.pb[0:3, at] = s_hi[0:3]
        B.pb[3:6, at] = s_mid[0:3]
    B.pb[6:9, 0:DOUT] = d32[0:3]
    B.pb[6:9, DOUT : 2 * DOUT] = q32[0:3]
    B.pb[9:12, 0:CLSP] = low[0:3]
    for k in range(3):
        B.pb[12 + k : 13 + k, :] = vec_parts[k]
        B.pb[15:16, LANES * k : LANES * (k + 1)] = jnp.broadcast_to(loss_parts[k], (1, LANES))
    B.pall[e.i * e.nb + e.b] = B.pb[...].astype(BF16)
    even = lax.broadcasted_iota(jnp.int32, (OWN, C), 0) % 2 == 0
    for m in range(MICRO):
        for side in range(2):
            first = B.dn2[8 * side + m : 8 * side + m + 1, :]
            second = B.dn2[8 * (2 + side) + m : 8 * (2 + side) + m + 1, :]
            B.dnt[m, side] = jnp.where(even, first, second)


def batch_copy(e, B, d):
    slot = e.i * e.nb + e.b
    return remote(e, B.pall.at[slot], B.pall.at[slot], B.s_pb.at[d], B.r_pb.at[d], b=lax.rem(e.b + d, e.nb))


def group_copy(e, B, d):
    at = pl.ds(e.i * e.nb, e.nb)
    to = e.g * GROUP + lax.rem(e.i + d, GROUP)
    return remote(e, B.pall.at[at], B.pall.at[at], B.s_pg.at[d], B.r_pg.at[d], r=to)


def ph_payload_batch(e, B):
    for d in range(1, e.nb):
        batch_copy(e, B, d).start()


def ph_payload_group(e, B):
    for d in range(1, e.nb):
        batch_copy(e, B, d).wait_recv()
    for d in range(1, GROUP):
        group_copy(e, B, d).start()


def ph_payload_wait(e, B):
    for d in range(1, GROUP):
        group_copy(e, B, d).wait_recv()
    for d in range(1, e.nb):
        batch_copy(e, B, d).wait_send()
    for d in range(1, GROUP):
        group_copy(e, B, d).wait_send()


def lane_sum(blocks):
    total = blocks[0]
    for block in blocks[1:]:
        total = total + block
    return jnp.sum(total, -1, keepdims=True) * (1.0 / C)


def fold8(v):
    return jnp.sum(v.reshape(v.shape[0] // 8, 8, v.shape[1]), 0)


def ph_bwd_one(e, B):
    chunk = 256
    half = chunk // 16
    B.acc[...] = jnp.zeros_like(B.acc)
    B.acup[...] = jnp.zeros_like(B.acup)
    B.ps[...] = jnp.zeros_like(B.ps)

    def body(it, _):
        at = pl.multiple_of(it * chunk, chunk)
        m = it // (POS // chunk)
        keep = B.mask[m, e.i].astype(F32) * (1.0 / KEEP)
        span = pl.ds(at, chunk)
        lanes = [slice(LANES * j, LANES * (j + 1)) for j in range(J)]
        dg = [B.dnt[m, :, :, lanes[j]] * vec_row(B, 5, j) for j in range(J)]
        m1 = lane_sum(dg)
        hat = [B.v2[span, lanes[j]].reshape(half, 2, OWN, LANES) for j in range(J)]
        m2 = lane_sum([dg[j] * hat[j] for j in range(J)])
        scale = B.rs2[span, :].reshape(half, 2, OWN, LANES)
        for j in range(J):
            zspan = pl.ds(j * NPOS + at, chunk)
            dr = (scale * (dg[j] - m1 - hat[j] * m2)).reshape(chunk, LANES)
            B.ps[m, :, :, lanes[j]] += jnp.sum(hat[j], 0)
            dz = (dr * (vec_row(B, 4, j) * keep)).astype(BF16)
            B.dz[span, lanes[j]] = dz
            B.acc[3, :, lanes[j]] += fold8(dz.astype(F32))
            B.acc[4, :, lanes[j]] += fold8(dr * B.z[zspan, :]) * keep
            B.z[zspan, :] = dr
        return 0

    lax.fori_loop(0, NPOS // chunk, body, 0)
    for m in range(MICRO):
        B.acc[5] += B.dnt[m, 0] * B.ps[m, 0] + B.dnt[m, 1] * B.ps[m, 1]
        B.acc[6] += (B.dnt[m, 0] + B.dnt[m, 1]) * float(COLS // 2)


def ph_bwd_two(e, B, steps):
    chunk = 256
    width = 256

    def body(it, _):
        hooks(it, steps)
        at = pl.multiple_of(it * chunk, chunk)
        m = it // (POS // chunk)
        c0 = (it % (POS // chunk)) * (chunk // OWN)
        span = pl.ds(at, chunk)
        lanes = [slice(LANES * j, LANES * (j + 1)) for j in range(J)]
        dz = B.dz[span, :]
        for k in range(HID // width):
            hid = slice(width * k, width * (k + 1))
            du = lax.dot_general(dz, B.wdn[hid, :], (((1,), (1,)), ((), ())), preferred_element_type=F32)
            dh = (du * B.gp[span, hid].astype(F32)).astype(BF16)
            B.gp[span, hid] = dh
            B.acup[:, hid] += fold8(dh.astype(F32))
        dn = lax.dot_general(B.gp[span, :], B.wup[...], (((1,), (1,)), ((), ())), preferred_element_type=F32)
        dns = [dn[:, lanes[j]] for j in range(J)]
        dg = [dns[j] * vec_row(B, 1, j) for j in range(J)]
        hat = [B.v1[span, lanes[j]] for j in range(J)]
        m1 = lane_sum(dg)
        m2 = lane_sum([dg[j] * hat[j] for j in range(J)])
        scale = B.rs1[span, :]
        for j in range(J):
            dy = scale * (dg[j] - m1 - hat[j] * m2)
            B.acc[0, :, lanes[j]] += fold8(dy)
            B.acc[1, :, lanes[j]] += fold8(dns[j] * hat[j])
            B.acc[2, :, lanes[j]] += fold8(dns[j])
            for c in range(chunk // OWN):
                B.big[pl.ds(xrow(j, m) + (3 + c0 + c) * SUB + 3, OWN), :] = dy[OWN * c : OWN * (c + 1), :]
        return 0

    lax.fori_loop(0, NPOS // chunk, body, 0)


def wgrad_down(e, B, f):
    for k in range(2):
        first = 2 * C * f + C * k
        w = lax.dot_general(
            B.u[:, first : first + C], B.dz[...], (((0,), (0,)), ((), ())), preferred_element_type=F32
        )
        w = w.reshape(24, 16, C)
        a, b = w[:, 0:8], w[:, 8:16]
        units = [v[:, :, LANES * j : LANES * (j + 1)] for v in (a, b) for j in range(J)]
        tiles = [jnp.concatenate(units[2 * t : 2 * t + 2], axis=1).astype(BF16) for t in range(3)]
        for q in range(24):
            piece, inner = divmod(24 * k + q, 3)
            for t in range(3):
                B.gb[f, piece // 4, piece // 2 % 2, piece % 2, inner, t] = tiles[t][q]


def wgrad_up(e, B, f):
    width = 256
    for k in range(3):
        first = 768 * (f - 2) + width * k
        w = lax.dot_general(
            B.n[...], B.gp[:, first : first + width], (((0,), (0,)), ((), ())), preferred_element_type=F32
        )
        w = w.reshape(48, 8, width)
        w = jnp.concatenate([w[:, :, :LANES], w[:, :, LANES:]], axis=1).astype(BF16)
        B.gb[f, :, :, :, :, k] = w.reshape(4, 2, 2, 3, 16, LANES)


def dy_copy(e, B, m, up):
    if up:
        return remote(e, B.hs.at[m, 1], B.hr.at[m, 0], B.s_dy.at[1, m], B.r_dy.at[1, m], r=e.r + GROUP)
    return remote(e, B.hs.at[m, 0], B.hr.at[m, 1], B.s_dy.at[0, m], B.r_dy.at[0, m], r=e.r - GROUP)


def dy_send(e, B, m):
    zero = jnp.zeros((3 * SUB, LANES), F32)
    for j in range(J):
        B.big[pl.ds(xrow(j, m), 3 * SUB), :] = zero
        B.big[pl.ds(xrow(j, m) + (COLS + 3) * SUB, 3 * SUB), :] = zero
        for side in range(2):
            for k in range(3):
                row = 3 + k if side == 0 else 8 + k
                v = B.big[pl.ds(xrow(j, m) + 3 * SUB + row, COLS, stride=SUB), :]
                B.hs[m, side, k, :, LANES * j : LANES * (j + 1)] = v.astype(BF16)

    @pl.when(e.g > 0)
    def _():
        dy_copy(e, B, m, False).start()

    @pl.when(e.g < e.G - 1)
    def _():
        dy_copy(e, B, m, True).start()


def ph_dy_edges(e, B):
    zero = jnp.zeros((MICRO, 3, COLS, C), BF16)

    @pl.when(e.g == 0)
    def _():
        B.hr[:, 0] = zero

    @pl.when(e.g == e.G - 1)
    def _():
        B.hr[:, 1] = zero


def dy_take(e, B, m):
    @pl.when(e.g < e.G - 1)
    def _():
        dy_copy(e, B, m, False).wait_recv()

    @pl.when(e.g > 0)
    def _():
        dy_copy(e, B, m, True).wait_recv()

    for j in range(J):
        for side in range(2):
            for k in range(3):
                row = k if side == 0 else 11 + k
                v = B.hr[m, side, k, :, LANES * j : LANES * (j + 1)].astype(F32)
                B.big[pl.ds(xrow(j, m) + 3 * SUB + row, COLS, stride=SUB), :] = v


def ph_dy_done(e, B):
    for m in range(MICRO):

        @pl.when(e.g > 0)
        def _(m=m):
            dy_copy(e, B, m, False).wait_send()

        @pl.when(e.g < e.G - 1)
        def _(m=m):
            dy_copy(e, B, m, True).wait_send()


def ph_conv_kernel(e, B, parts, steps):
    halves = COLS // TILE

    def taps(it, _):
        hooks(it, steps)
        j = it // 7
        a = it % 7

        def body(k, dk):
            m = parts.start + k // halves
            c0 = k % halves * TILE
            dk = list(dk)
            at = j * NPOS + m * POS + c0 * OWN
            xs = [B.xc[pl.ds(pl.multiple_of(at + OWN * c, OWN), OWN), :] for c in range(TILE)]
            for c in range(TILE + 6):
                d = B.big[pl.ds(xrow(j, m) + (c0 + c) * SUB + a, OWN), :]
                for b in range(7):
                    if 0 <= c - b < TILE:
                        dk[b] = dk[b] + d * xs[c - b]
            return tuple(dk)

        zero = jnp.zeros((OWN, LANES), F32)
        dk = lax.fori_loop(0, halves * len(parts), body, (zero,) * 7)
        for b in range(7):
            tap = (6 - a) * 7 + 6 - b
            B.sg[pl.ds(tap * J + j, 1), :] += jnp.sum(dk[b], 0, keepdims=True)
        return 0

    lax.fori_loop(0, 7 * J, taps, 0)


def tap_low(B, t):
    return B.wh[16 * (t // 8) : 16 * (t // 8) + 16, LANES * (t % 8) : LANES * (t % 8 + 1)]


def ph_taps_low(e, B):
    for t in range(49 * J):
        row = B.kb[t]
        B.wh[16 * (t // 8) : 16 * (t // 8) + 16, LANES * (t % 8) : LANES * (t % 8 + 1)] = jnp.concatenate(
            [row, row], axis=0
        ).astype(BF16)


def ph_conv_input(e, B, steps):
    halves = COLS // TILE
    half = TILE // 2

    def body(it, _):
        m = it // halves
        c0 = it % halves * TILE
        for j in range(J):
            hooks(it, {k // J: v for k, v in steps.items() if k % J == j})
            acc = [None] * half
            for a in range(7):
                cols = []
                for c in range(half + 6):
                    at = xrow(j, m) + (c0 + c) * SUB + a
                    pair = [B.big[pl.ds(at, OWN), :], B.big[pl.ds(at + half * SUB, OWN), :]]
                    cols.append(jnp.concatenate(pair, axis=0).astype(BF16))
                for some in (range(0, 4), range(4, 7)):
                    taps = {b: tap_low(B, ((6 - a) * 7 + 6 - b) * J + j) for b in some}
                    for c in range(half):
                        part = [cols[c + b] * taps[b] for b in some]
                        while len(part) > 1:
                            part = [part[k] + part[k + 1] for k in range(0, len(part) - 1, 2)] + part[len(part) // 2 * 2 :]
                        low = part[0].astype(F32)
                        acc[c] = low if acc[c] is None else acc[c] + low
            at = j * NPOS + m * POS + c0 * OWN
            for c in range(half):
                for k in range(2):
                    span = pl.ds(pl.multiple_of(at + OWN * (c + half * k), OWN), OWN)
                    B.dx[span, :] = B.z[span, :] + acc[c][OWN * k : OWN * (k + 1), :]
        return 0

    lax.fori_loop(0, MICRO * halves, body, 0)


def ph_small_fill(e, B):
    for k in range(HID // LANES):
        B.sg[SG_CUP + k : SG_CUP + k + 1, :] = jnp.sum(B.acup[:, LANES * k : LANES * (k + 1)], 0, keepdims=True)
    for v in range(7):
        for j in range(J):
            row = SG_VEC + v * J + j
            B.sg[row : row + 1, :] = jnp.sum(B.acc[v, :, LANES * j : LANES * (j + 1)], 0, keepdims=True)


def out_copy(e, B, m, k, d):
    j = lax.rem(e.i + d, GROUP)
    cols = pl.ds(TILE * k, TILE)
    return remote(
        e,
        B.xg.at[m, pl.ds(3 + 2 * j, 2), cols],
        B.fo.at[m, e.i, :, cols],
        B.s_out.at[m, k, d],
        B.r_out.at[m, k, d],
        r=e.g * GROUP + j,
    )


def own_out_copy(e, B, m, k):
    cols = pl.ds(TILE * k, TILE)
    return pltpu.make_async_copy(
        B.xg.at[m, pl.ds(3 + 2 * e.i, 2), cols], B.fo.at[m, e.i, :, cols], B.s_outown.at[m, k]
    )


def out_send(e, B, m, k):
    for row in range(OWN):
        for j in range(J):
            v = B.dx[pl.ds(j * NPOS + m * POS + k * TILE * OWN + row, TILE, stride=OWN), :]
            B.xg[m, 3 + row, TILE * k : TILE * (k + 1), LANES * j : LANES * (j + 1)] = v.astype(BF16)
    own_out_copy(e, B, m, k).start()
    for d in (2, 3, 1):
        out_copy(e, B, m, k, d).start()


def ph_out_wait(e, B):
    for m in range(MICRO):
        for k in range(COLS // TILE):
            own_out_copy(e, B, m, k).wait()
            for d in range(1, GROUP):
                out_copy(e, B, m, k, d).wait()


PARTS = 4
PIECE = (144, 144, 288, 288)
START = (ROW_DOWN, ROW_DOWN + 16 * 144, ROW_UP, ROW_UP)


def rs_first(e, B, f):
    c = e.i % 2
    return remote(e, B.gb.at[f, :, :, 1 - c], B.ra1.at[f], B.s_rs.at[f, 0], B.r_rs.at[f, 0], r=e.r + 1 - 2 * c)


def rs_second(e, B, f):
    to = e.g * GROUP + lax.rem(e.i + 2, GROUP)
    return remote(e, B.sa2.at[f], B.ra2.at[f], B.s_rs.at[f, 1], B.r_rs.at[f, 1], r=to)


def group_of(e, q):
    return q * (e.G // 4)


def rs_third(e, B, f, q):
    to = group_of(e, q)
    d = lax.rem(to - e.g + e.G, e.G)
    return remote(e, B.sc.at[f, q], B.rc.at[f, d], B.s_rc.at[f, q], B.r_rc.at[f, d], r=to * GROUP + e.i)


def rs_third_wait(e, B, f, d):
    return remote(e, B.sc.at[f, 0], B.rc.at[f, d], B.s_rc.at[f, 0], B.r_rc.at[f, d], r=lax.rem(e.r + GROUP, e.n))


def rs_fourth(e, B, f, d):
    return remote(e, B.rb.at[f, 0], B.rb.at[f, d], B.s_rb.at[f, d], B.r_rb.at[f, d], b=lax.rem(e.b + d, e.nb))


def ends_here(e, body):
    if e.G == 4:
        body()
    else:
        pl.when(e.g % (e.G // 4) == 0)(body)


def rs_step1(e, B, f):
    rs_first(e, B, f).start()


def rs_step2(e, B, f):
    x, c = e.i // 2, e.i % 2
    rs_first(e, B, f).wait_recv()
    for q in range(4):
        B.sa2[f, q] = (B.gb[f, q, 1 - x, c].astype(F32) + B.ra1[f, q, 1 - x].astype(F32)).astype(BF16)
    rs_second(e, B, f).start()
    for q in range(4):
        B.h1[f, q] = B.gb[f, q, x, c].astype(F32) + B.ra1[f, q, x].astype(F32)


def rs_step3(e, B, f):
    rs_second(e, B, f).wait_recv()
    for q in range(4):
        B.h1[f, q] = B.h1[f, q] + B.ra2[f, q].astype(F32)
        B.sc[f, q] = B.h1[f, q].astype(BF16)
    for q in range(4):

        @pl.when(e.g != group_of(e, q))
        def _(q=q):
            rs_third(e, B, f, q).start()


def rs_step4(e, B, f):
    def body():
        total = B.h1[f, e.g // (e.G // 4)]
        for d in range(1, e.G):
            rs_third_wait(e, B, f, d).wait_recv()
            total = total + B.rc[f, d].astype(F32)
        B.rb[f, 0] = total.astype(BF16)
        for d in range(1, e.nb):
            rs_fourth(e, B, f, d).start()

    ends_here(e, body)


def piece_owners(e, f):
    start = START[f] + PIECE[f] * (e.g // (e.G // 4) * 4 + e.i)
    return start // e.slab, (start + PIECE[f] - 1) // e.slab


def own_slot(B, f, slot):
    return B.ro.at[f, slot] if f < 2 else B.ro_up.at[f - 2, slot]


def own_copy(e, B, f, k, owner):
    slot = lax.rem(e.g // (e.G // 4) * 4 + e.i, 16 if f < 2 else 8)
    return remote(e, B.fp.at[f], own_slot(B, f, slot), B.s_ro.at[f, k], B.r_ro.at[f, slot], r=owner)


def own_wait(e, B, f, slot, home):
    remote(e, B.fp.at[f], own_slot(B, f, slot), B.s_ro.at[f, 0], B.r_ro.at[f, slot], r=home).wait_recv()


def rs_step5(e, B, f):
    def body():
        for d in range(1, e.nb):
            rs_fourth(e, B, f, d).wait_recv()
        total = None
        for b in range(e.nb):
            part = B.rb[f, lax.rem(e.b - b + e.nb, e.nb)].astype(F32)
            total = part if total is None else total + part
        B.fp[f] = total.astype(BF16)
        lo, hi = piece_owners(e, f)

        @pl.when(lo != e.r)
        def _():
            own_copy(e, B, f, 0, lo).start()

        @pl.when(jnp.logical_and(hi != lo, hi != e.r))
        def _():
            own_copy(e, B, f, 1, hi).start()

    ends_here(e, body)


def place(B, f, off, tiles):
    for k in range(3):
        for t in range(3):
            for h in range(2):
                unit = 2 * t + h
                tile = tiles[k, t, 8 * h : 8 * h + 8, :].astype(F32)
                if f >= 2:
                    at = pl.ds(MARGIN + off + 96 * k + 6 * (f - 2) + unit, 8, stride=12)
                else:
                    at = pl.ds(MARGIN + off + 48 * k + 24 * (unit // 3) + unit % 3, 8, stride=3)
                B.gf[at, :] = tile


def rs_place(e, B, f):
    for p in range(16):
        off = START[f] + PIECE[f] * p - e.slab * e.r
        home = group_of(e, p // 4) * GROUP + p % 4

        @pl.when(jnp.logical_and(off < e.slab, off + PIECE[f] > 0))
        def _(p=p, off=off, home=home):
            slot = p % (16 if f < 2 else 8)

            @pl.when(e.r != home)
            def _():
                own_wait(e, B, f, slot, home)
                place(B, f, off, B.ro[f, slot] if f < 2 else B.ro_up[f - 2, slot])

            @pl.when(e.r == home)
            def _():
                place(B, f, off, B.fp[f])


def ph_rs_done(e, B):
    for f in range(PARTS):
        rs_first(e, B, f).wait_send()
        rs_second(e, B, f).wait_send()
        for q in range(4):

            @pl.when(e.g != group_of(e, q))
            def _(f=f, q=q):
                rs_third(e, B, f, q).wait_send()

        def body(f=f):
            for d in range(1, e.nb):
                rs_fourth(e, B, f, d).wait_send()
            lo, hi = piece_owners(e, f)

            @pl.when(lo != e.r)
            def _():
                own_copy(e, B, f, 0, lo).wait_send()

            @pl.when(jnp.logical_and(hi != lo, hi != e.r))
            def _():
                own_copy(e, B, f, 1, hi).wait_send()

        ends_here(e, body)


MARGIN = 1792


QUARTER = 80
SEGMENTS = (
    (0, 0, QUARTER, ROW_K),
    (1, 0, 49 * J - QUARTER, ROW_K + QUARTER),
    (2, 0, 7 * J, ROW_VEC),
    (3, 0, HID // LANES, ROW_CUP),
)


def small_group(e, B, d):
    j = lax.rem(e.i + d, GROUP)
    at = pl.ds(pl.multiple_of(j * QUARTER, QUARTER), QUARTER)
    return remote(e, B.sg.at[at], B.sg_group.at[d - 1], B.s_sg.at[d], B.r_sg.at[d], r=e.g * GROUP + j)


def small_line(e, B, d):
    to = lax.rem(e.g + d, e.G)
    return remote(e, B.sg_line.at[0], B.sg_line.at[d], B.s_sgl.at[d], B.r_sgl.at[d], r=to * GROUP + e.i)


def small_batch(e, B, d):
    return remote(e, B.sgb.at[0], B.sgb.at[d], B.s_sgb.at[d], B.r_sgb.at[d], b=lax.rem(e.b + d, e.nb))


def small_back(e, B, q, owner):
    at = pl.ds(q * QUARTER, QUARTER)
    return remote(e, B.sga.at[at], B.sga.at[at], B.s_sgg.at[q], B.r_sgg.at[q], r=owner)


def small_moves(e):
    for q, row, count, flat in SEGMENTS:
        owner = flat // e.slab
        holder = owner // GROUP * GROUP + q
        if owner != holder:
            yield q, holder, owner


def small_step1(e, B):
    for d in (2, 3, 1):
        small_group(e, B, d).start()


def small_step2(e, B):
    total = B.sg[pl.ds(pl.multiple_of(e.i * QUARTER, QUARTER), QUARTER), :]
    for d in range(1, GROUP):
        small_group(e, B, d).wait_recv()
        total = total + B.sg_group[d - 1]
    B.sg_line[0] = total
    for d in range(1, e.G):
        small_line(e, B, d).start()


def small_step3(e, B):
    for d in range(1, e.G):
        small_line(e, B, d).wait_recv()
    total = None
    for level in range(e.G):
        part = B.sg_line[lax.rem(e.g - level + e.G, e.G)]
        total = part if total is None else total + part
    B.sgb[0] = total
    for d in range(1, e.nb):
        small_batch(e, B, d).start()


def small_step4(e, B):
    for d in range(1, e.nb):
        small_batch(e, B, d).wait_recv()
    total = None
    for b in range(e.nb):
        part = B.sgb[lax.rem(e.b - b + e.nb, e.nb)]
        total = part if total is None else total + part
    B.sga[pl.ds(pl.multiple_of(e.i * QUARTER, QUARTER), QUARTER), :] = total
    for q, holder, owner in small_moves(e):

        @pl.when(e.r == holder)
        def _(q=q, owner=owner):
            small_back(e, B, q, owner).start()


def ph_small_place(e, B):
    for q, holder, owner in small_moves(e):

        @pl.when(e.r == owner)
        def _(q=q, holder=holder):
            small_back(e, B, q, holder).wait_recv()

    for q, row, count, flat in SEGMENTS:
        off = MARGIN + flat % e.slab
        at = q * QUARTER + row

        @pl.when(e.r == flat // e.slab)
        def _(off=off, at=at, count=count):
            B.gf[off : off + count, :] = B.sga[at : at + count, :]


def ph_small_done(e, B):
    for d in range(1, GROUP):
        small_group(e, B, d).wait_send()
    for d in range(1, e.G):
        small_line(e, B, d).wait_send()
    for d in range(1, e.nb):
        small_batch(e, B, d).wait_send()
    for q, holder, owner in small_moves(e):

        @pl.when(e.r == holder)
        def _(q=q, owner=owner):
            small_back(e, B, q, owner).wait_send()


def ph_head_grads(e, B):
    parts = GROUP * e.nb
    rows = 16 * parts
    sums = None
    for p in range(parts):
        x = B.pall[p].astype(F32)
        sums = x if sums is None else sums + x
        dd = x[6:9, 0:DOUT]
        B.gp[16 * p : 16 * p + 16, 0:DOUT] = jnp.concatenate([dd, dd, jnp.zeros((10, DOUT), F32)], axis=0).astype(BF16)
        dl = x[9:12, 0:CLSP]
        B.gp[rows + 16 * p : rows + 16 * p + 16, 0:CLSP] = jnp.concatenate(
            [jnp.zeros((6, CLSP), F32), dl, jnp.zeros((7, CLSP), F32)], axis=0
        ).astype(BF16)
    B.pb[...] = sums
    for q in range(4):
        for p in range(parts):
            B.v2[16 * p : 16 * p + 16, :] = B.pall[p, :, C * q : C * (q + 1)].astype(F32)
        for j in range(J):
            t = J * q + j
            B.u[LANES * t : LANES * (t + 1), 0:rows] = B.v2[0:rows, LANES * j : LANES * (j + 1)].T.astype(BF16)
    per = DOUT // LANES
    base = MARGIN - e.slab * e.r

    kc = 288
    low = e.slab * e.r - ROW_DS

    @pl.when(jnp.logical_and(low < 4 * C * per, low + e.slab > 0))
    def _():
        k0 = jnp.clip(low // (16 * per) * 16, 0, 4 * C - kc)
        k0 = pl.multiple_of(k0, 16)
        w = jnp.dot(B.u[pl.ds(k0, kc), 0:rows], B.gp[0:rows, 0:DOUT], preferred_element_type=F32)
        for j in range(per):
            B.gf[pl.ds(base + ROW_DS + per * k0 + j, kc, stride=per), :] = w[:, LANES * j : LANES * (j + 1)]

    low2 = e.slab * e.r - ROW_HEAD

    @pl.when(jnp.logical_and(low2 < DOUT * CLS // LANES, low2 + e.slab > 0))
    def _():
        g0 = jnp.clip(low2 // 125, 0, DOUT // 16 - 16)
        k0 = pl.multiple_of(DOUT + 16 * g0, 16)
        for t in range(8):
            B.big[256 * t : 256 * (t + 1), :] = jnp.dot(
                B.u[pl.ds(k0, 256), 0:rows],
                B.gp[rows : 2 * rows, LANES * t : LANES * (t + 1)],
                preferred_element_type=F32,
            )
        lane = lax.broadcasted_iota(jnp.int32, (16, LANES), 1)
        held = None
        for kk in range(16):
            o = (-CLS * kk) % LANES
            tiles = [B.big[pl.ds(256 * t + kk, 16, stride=16), :] for t in range(8)]
            if o:
                tiles = [pltpu.roll(tile, LANES - o, 1) for tile in tiles]
            for s in range(CLS * kk // LANES, (CLS * kk + CLS - 1) // LANES + 1):
                t0 = (LANES * s - CLS * kk) // LANES
                if o == 0:
                    value = tiles[t0]
                elif t0 < 0:
                    value = tiles[0]
                elif t0 + 1 > 7:
                    value = tiles[t0]
                else:
                    value = jnp.where(lane < LANES - o, tiles[t0], tiles[t0 + 1])
                border = CLS * kk - LANES * s
                if border > 0:
                    value = jnp.where(lane < border, held, value)
                if LANES * (s + 1) > CLS * (kk + 1):
                    held = value
                else:
                    B.gf[pl.ds(base + ROW_HEAD + 125 * g0 + s, 16, stride=125), :] = value

    @pl.when(e.r == ROW_OUT // e.slab)
    def _():
        off = MARGIN + ROW_OUT % e.slab
        for j in range(per):
            at = slice(LANES * j, LANES * (j + 1))
            B.gf[off + j : off + j + 1, :] = B.pb[6:7, at] * e.positions + (
                B.pb[7:8, at] * e.positions + B.pb[8:9, at] * e.positions
            )
            gain = B.pb[12:13, at] + B.pb[13:14, at] + B.pb[14:15, at]
            B.gf[off + per + j : off + per + j + 1, :] = gain
            at = slice(DOUT + LANES * j, DOUT + LANES * (j + 1))
            shift = B.pb[12:13, at] + B.pb[13:14, at] + B.pb[14:15, at]
            B.gf[off + 2 * per + j : off + 2 * per + j + 1, :] = shift

    @pl.when(e.r == ROW_BH // e.slab)
    def _():
        off = MARGIN + ROW_BH % e.slab
        for j in range(CLSP // LANES):
            at = slice(LANES * j, LANES * (j + 1))
            B.gf[off + j : off + j + 1, :] = B.pb[9:10, at] + B.pb[10:11, at] + B.pb[11:12, at]
        rest = FLAT - ROW_BH - CLSP // LANES
        B.gf[off + CLSP // LANES : off + CLSP // LANES + rest, :] = jnp.zeros((rest, LANES), F32)


def norm_copy(e, B, d):
    return remote(e, B.nrm.at[0], B.nrm.at[d], B.s_nrm.at[d], B.r_nrm.at[d], r=lax.rem(e.r + d, e.n))


def squares(v):
    return jnp.sum((v * v).reshape(-1, 8, LANES), 0)


def ph_norm_local(e, B):
    size = 64
    whole = e.slab // size

    def body(k, acc):
        return acc + squares(B.gf[pl.ds(pl.multiple_of(MARGIN + size * k, 8), size), :])

    part = lax.fori_loop(0, whole, body, jnp.zeros((8, LANES), F32))
    v = B.gf[MARGIN + whole * size : MARGIN + e.slab, :]
    B.nrm[0] = part + jnp.broadcast_to(jnp.sum(v * v, 0, keepdims=True) * 0.125, (8, LANES))


def ph_norm(e, B):
    def pieces():
        B.nrm[0] += squares(B.fp[...].astype(F32))

    ends_here(e, pieces)

    @pl.when(e.g == 0)
    def _():
        B.nrm[0] += squares(B.sga[pl.ds(pl.multiple_of(e.i * QUARTER, QUARTER), QUARTER), :])

    for d in range(1, e.n):
        norm_copy(e, B, d).start()


def ph_norm_wait(e, B):
    for d in range(1, e.n):
        norm_copy(e, B, d).wait_recv()
    total = None
    for k in range(e.n):
        part = B.nrm[lax.rem(e.r - k + e.n, e.n)]
        total = part if total is None else total + part
    square = jnp.sum(jnp.sum(total, 0, keepdims=True), 1, keepdims=True)
    B.o_norm[...] = jnp.broadcast_to(jnp.sqrt(square), (8, LANES))
    loss = B.pb[15:16, :]
    loss = loss[:, 0:LANES] + loss[:, LANES : 2 * LANES] + loss[:, 2 * LANES : 3 * LANES]
    B.o_loss[...] = jnp.broadcast_to(loss, (8, LANES))
    for d in range(1, e.n):
        norm_copy(e, B, d).wait_send()


def buffers(e):
    n, G, nb, slab = e.n, e.G, e.nb, e.slab
    tiles = (3, 3, 16, LANES)
    parts = GROUP * nb
    V = pltpu.VMEM
    D = pltpu.SemaphoreType.DMA
    return dict(
        gw=V((n, 2, e.half, LANES), BF16),
        tab=V((TAB_ROWS, LANES), F32),
        big=V((10816, LANES), F32),
        dx=V((8 * DOUT, LANES), F32),
        wup=V((C, HID), BF16),
        wdn=V((HID, C), BF16),
        wds=V((4 * C, DOUT), BF16),
        wh=V((DOUT, CLSP), BF16),
        xg=V((MICRO, 14, COLS, C), BF16),
        xc=V((J * NPOS, LANES), F32),
        kb=V((49 * J, 8, LANES), F32),
        v1=V((NPOS, C), F32),
        rs1=V((NPOS, LANES), F32),
        v2=V((NPOS, C), F32),
        rs2=V((NPOS, LANES), F32),
        n=V((NPOS, C), BF16),
        u=V((NPOS, HID), BF16),
        gp=V((NPOS, HID), BF16),
        z=V((J * NPOS, LANES), F32),
        dz=V((NPOS, C), BF16),
        ps=V((MICRO, 2, OWN, C), F32),
        sl=V((16, C), F32),
        sr=V((G, 16, C), F32),
        dn2=V((32, C), F32),
        dnt=V((MICRO, 2, OWN, C), F32),
        pb=V((16, 4 * C), F32),
        pall=V((parts, 16, 4 * C), BF16),
        acc=V((7, 8, C), F32),
        acup=V((8, HID), F32),
        hs=V((MICRO, 2, 3, COLS, C), BF16),
        hr=V((MICRO, 2, 3, COLS, C), BF16),
        gb=V((PARTS, 4, 2, 2) + tiles, BF16),
        ra1=V((PARTS, 4, 2) + tiles, BF16),
        sa2=V((PARTS, 4) + tiles, BF16),
        ra2=V((PARTS, 4) + tiles, BF16),
        h1=V((PARTS, 4) + tiles, F32),
        sc=V((PARTS, 4) + tiles, BF16),
        rc=V((PARTS, G) + tiles, BF16),
        rb=V((PARTS, nb) + tiles, BF16),
        fp=V((PARTS,) + tiles, BF16),
        ro=V((2, 16) + tiles, BF16),
        ro_up=V((2, 8) + tiles, BF16),
        gf=V((MARGIN + slab + MARGIN, LANES), F32),
        sg=V((SG_ROWS, LANES), F32),
        sg_group=V((GROUP - 1, QUARTER, LANES), F32),
        sg_line=V((G, QUARTER, LANES), F32),
        sgb=V((nb, QUARTER, LANES), F32),
        sga=V((SG_ROWS, LANES), F32),
        nrm=V((n, 8, LANES), F32),
        s_own=D((1,)),
        s_feat=D((MICRO, GROUP)),
        r_feat=D((MICRO, GROUP)),
        s_halo=D((2, MICRO)),
        r_halo=D((2, MICRO)),
        s_tab=D((len(TABLES), G)),
        s_tabg=D((len(TABLES), GROUP)),
        r_tab=D((len(TABLES),)),
        s_line=D((2, G)),
        r_line=D((G, CHUNKS)),
        s_pair=D((G,)),
        r_pair=D((G, CHUNKS)),
        s_row=D((2, G)),
        r_row=D((2, G, CHUNKS)),
        s_core=D((4, G)),
        r_core=D((4, G, CHUNKS)),
        s_patch=D((G,)),
        r_patch=D((G,)),
        s_pb=D((nb,)),
        r_pb=D((nb,)),
        s_pg=D((GROUP,)),
        r_pg=D((GROUP,)),
        s_dy=D((2, MICRO)),
        r_dy=D((2, MICRO)),
        s_out=D((MICRO, 2, GROUP)),
        r_out=D((MICRO, 2, GROUP)),
        s_outown=D((MICRO, 2)),
        s_rs=D((PARTS, 2)),
        r_rs=D((PARTS, 2)),
        s_rc=D((PARTS, 4)),
        r_rc=D((PARTS, G)),
        s_rb=D((PARTS, nb)),
        r_rb=D((PARTS, nb)),
        s_ro=D((PARTS, 2)),
        r_ro=D((PARTS, 16)),
        s_sg=D((GROUP,)),
        r_sg=D((GROUP,)),
        s_sgl=D((G,)),
        r_sgl=D((G,)),
        s_sgg=D((GROUP,)),
        r_sgg=D((GROUP,)),
        s_sgb=D((nb,)),
        r_sgb=D((nb,)),
        s_nrm=D((n,)),
        r_nrm=D((n,)),
    )


def ph_clear(e, B):
    B.sg[...] = jnp.zeros_like(B.sg)
    B.gf[...] = jnp.zeros_like(B.gf)


def ph_result(e, B):
    B.o_grad[...] = B.gf[MARGIN : MARGIN + e.slab, :]


def schedule(e, B):
    def do(step, *args):
        return lambda: step(e, B, *args)

    def level_of(row):
        return row // e.slab // GROUP

    up = range(0, level_of(ROW_CUP - 1) + 1)
    down = range(up.stop, level_of(ROW_VEC - 1) + 1)
    rest = range(down.stop, e.G)
    ph_barrier_signal(e, B)
    ph_cast(e, B)
    ph_feat_zero(e, B)
    ph_clear(e, B)
    ph_barrier_wait(e, B)
    every = range(CHUNKS)
    one, two = range(0, CHUNKS // 2), range(CHUNKS // 2, CHUNKS)

    def hops(some):
        return range(max(max(level, e.G - 1 - level) for level in some) + 1)

    def steps(step, some, which, chunks):
        return [do(step, some, h, chunks) for h in which]

    ph_tables_start(e, B)
    feat_start(e, B, 0)
    line_send(e, B, range(e.G), every)
    tables_forward(e, B, (0, 2))
    feat_start(e, B, 1)
    line_step(e, B, up, 1, every)
    halo_start(e, B, 0)
    feat_start(e, B, 2)
    for h in hops(up)[2:3]:
        line_step(e, B, up, h, every)
    for h in hops(up)[:3]:
        pair_step(e, B, up, h, every)
    tables_wait(e, B, (0, 2))
    ph_taps(e, B)
    ph_conv_fwd(
        e,
        B,
        {
            0: [do(halo_wait, 0), do(transpose, 0)],
            1: [do(halo_start, 1)] + steps(line_step, rest, [1], one),
            2: steps(line_step, rest, [1], two) + steps(line_step, up, hops(up)[3:], every) + steps(pair_step, up, hops(up)[3:], every),
            4: [do(halo_start, 2)] + steps(line_step, down, [1], every) + steps(pair_step, down, hops(down)[:2], every),
            6: [do(halo_wait, 1), do(transpose, 1)],
            7: [do(tables_forward, (1, 3, 4))] + steps(row_step, up, hops(up), one),
            8: steps(line_step, rest, hops(rest)[2:3], one) + steps(pair_step, rest, hops(rest)[:2], every),
            9: steps(row_step, up, hops(up), two),
            10: steps(line_step, rest, hops(rest)[2:3], two),
            11: steps(pair_step, rest, hops(rest)[2:3], every),
            12: [do(halo_wait, 2), do(transpose, 2)]
            + steps(line_step, down, hops(down)[2:], every)
            + steps(pair_step, down, hops(down)[2:], every),
            13: steps(row_step, down, hops(down)[:2], every),
            14: steps(core_step, up, hops(up), one),
            15: steps(line_step, rest, hops(rest)[3:], every) + steps(pair_step, rest, hops(rest)[3:], every),
            16: steps(row_step, rest, [0], every),
            17: steps(core_step, up, hops(up), two),
        },
    )
    ph_norm_one(e, B)
    tables_wait(e, B, (1, 3, 4))
    row_step(e, B, rest, 1, every)
    gather_ready(e, B, up)
    ph_weights_up(e, B)
    ph_mlp_up(
        e,
        B,
        {
            0: steps(row_step, down, hops(down)[2:], every),
            1: steps(row_step, rest, hops(rest)[2:3], every),
            2: steps(core_step, down, hops(down)[:2], every),
            3: steps(row_step, rest, hops(rest)[3:], every) + steps(core_step, rest, [0], every),
            5: steps(core_step, down, hops(down)[2:], every),
        },
    )
    gather_ready(e, B, down)
    ph_weights_down(e, B)
    ph_mlp_down(
        e,
        B,
        {
            0: steps(core_step, rest, [1], every),
            2: steps(core_step, rest, hops(rest)[2:3], every),
            5: steps(core_step, rest, hops(rest)[3:], every),
        },
    )
    ph_patch_local(e, B)
    patch_start(e, B)
    gather_ready(e, B, rest)
    ph_weights_head(e, B)
    patch_wait(e, B)
    ph_head(e, B)
    ph_payload_batch(e, B)
    ph_dy_edges(e, B)
    ph_bwd_one(e, B)
    for f in (0, 1):
        wgrad_down(e, B, f)
        rs_step1(e, B, f)
    ph_bwd_two(
        e,
        B,
        {
            1: [do(ph_payload_group)],
            2: [do(dy_send, 0), do(rs_step2, 0)],
            3: [do(rs_step2, 1)],
            4: [do(dy_send, 1)],
        },
    )
    dy_send(e, B, 2)
    for f in (2, 3):
        wgrad_up(e, B, f)
        rs_step1(e, B, f)
    dy_take(e, B, 0)
    dy_take(e, B, 1)
    rs_step3(e, B, 0)
    ph_conv_kernel(
        e,
        B,
        range(0, MICRO - 1),
        {
            4: [do(rs_step3, 1)],
            6: [do(rs_step2, 2)],
            9: [do(rs_step2, 3)],
            20: [do(rs_step3, 2)],
        },
    )
    dy_take(e, B, MICRO - 1)
    ph_conv_kernel(
        e,
        B,
        range(MICRO - 1, MICRO),
        {
            7: [do(rs_step3, 3)],
            12: [do(rs_step4, 0)],
            17: [do(rs_step4, 1)],
        },
    )
    ph_small_fill(e, B)
    small_step1(e, B)
    ph_feat_done(e, B)
    ph_taps_low(e, B)
    ph_conv_input(
        e,
        B,
        {
            3: [do(out_send, 0, 0)],
            5: [do(rs_step4, 2)],
            6: [do(small_step2), do(out_send, 0, 1)],
            7: [do(rs_step5, 0), do(rs_step4, 3)],
            8: [do(rs_step5, 1)],
            9: [do(rs_step5, 2), do(out_send, 1, 0)],
            11: [do(rs_step5, 3)],
            12: [do(out_send, 1, 1)],
            13: [do(ph_payload_wait), do(ph_head_grads), do(ph_norm_local)],
            14: [do(small_step3)],
            15: [do(out_send, 2, 0)],
        },
    )
    small_step4(e, B)
    ph_norm(e, B)
    out_send(e, B, 2, 1)
    for f in range(PARTS):
        rs_place(e, B, f)
    ph_small_place(e, B)
    ph_result(e, B)
    ph_tables_done(e, B)
    ph_gather_done(e, B)
    ph_dy_done(e, B)
    ph_rs_done(e, B)
    ph_small_done(e, B)
    ph_norm_wait(e, B)
    ph_out_wait(e, B)


def step_kernel(e, names, *refs):
    B = Env()
    for name, ref in zip(names, refs):
        setattr(B, name, ref)
    here(e)
    schedule(e, B)


def train_step(e, features, mask, labels, params):
    bufs = buffers(e)
    names = ["mask", "labels", "features", "params", "o_grad", "o_norm", "o_loss", "fo"] + list(bufs)
    return pl.pallas_call(
        functools.partial(step_kernel, e, names),
        out_shape=(
            jax.ShapeDtypeStruct((e.slab, LANES), F32),
            jax.ShapeDtypeStruct((8, LANES), F32),
            jax.ShapeDtypeStruct((8, LANES), F32),
            jax.ShapeDtypeStruct((MICRO, GROUP, 2, COLS, C), BF16),
        ),
        in_specs=[
            pl.BlockSpec(memory_space=pltpu.SMEM),
            pl.BlockSpec(memory_space=pltpu.SMEM),
            pl.BlockSpec(memory_space=pl.ANY),
            pl.BlockSpec(memory_space=pltpu.VMEM),
        ],
        out_specs=(
            pl.BlockSpec(memory_space=pltpu.VMEM),
            pl.BlockSpec(memory_space=pltpu.VMEM),
            pl.BlockSpec(memory_space=pltpu.VMEM),
            pl.BlockSpec(memory_space=pl.ANY),
        ),
        scratch_shapes=list(bufs.values()),
        compiler_params=pltpu.CompilerParams(collective_id=0, has_side_effects=True, vmem_limit_bytes=64 * MB - 65536),
        name="train_step",
    )(mask, labels, features, params)


def update_kernel(e, norm, loss, grad, params, m1, m2, out, o_norm, o_loss, new_params, first, second, feats, *scratch):
    g, p, a, b, fin, fout, s_in, s_out, s_feat, s_fout = scratch
    parts = 4
    size = e.slab // parts // 8 * 8
    spans = [(k * size, size if k < parts - 1 else e.slab - k * size) for k in range(parts)]
    copy = pltpu.make_async_copy
    ins = []
    for k, (at, count) in enumerate(spans):
        for q, (src, dst) in enumerate(((grad, g), (params, p), (m1, a), (m2, b))):
            ins.append(copy(src.at[pl.ds(at, count)], dst.at[pl.ds(at, count)], s_in.at[k, q]))
            ins[-1].start()
    fins = [copy(out.at[k], fin.at[k], s_feat.at[k]) for k in range(MICRO)]
    for cp in fins:
        cp.start()
    o_norm[0, 0] = jnp.max(norm[...])
    o_loss[0, 0] = jnp.max(loss[...])
    scale = jnp.minimum(1.0, CLIP / (norm[0:1, 0:1] + 1e-06))
    outs = []
    for k, (at, count) in enumerate(spans):
        for q in range(4):
            ins[4 * k + q].wait()
        rows = slice(at, at + count)
        clipped = g[rows, :] * scale
        one = BETA_ONE * a[rows, :] + (1.0 - BETA_ONE) * clipped
        two = BETA_TWO * b[rows, :] + (1.0 - BETA_TWO) * clipped * clipped
        a[rows, :] = one
        b[rows, :] = two
        ratio = one / (1.0 - BETA_ONE**STEP) / (jnp.sqrt(two / (1.0 - BETA_TWO**STEP)) + EPS_ADAM)
        p[rows, :] = p[rows, :] - RATE * (ratio + DECAY * p[rows, :])
        for q, (src, dst) in enumerate(((p, new_params), (a, first), (b, second))):
            outs.append(copy(src.at[pl.ds(at, count)], dst.at[pl.ds(at, count)], s_out.at[k, q]))
            outs[-1].start()
        if k < MICRO:
            fins[k].wait()
            fout[k] = fin[k].astype(F32)
            outs.append(copy(fout.at[k], feats.at[k], s_fout.at[k]))
            outs[-1].start()
    for cp in outs:
        cp.wait()


def update(e, grad, norm, loss, params, m1, m2, out):
    flat = jax.ShapeDtypeStruct((e.slab, LANES), F32)
    scalar = jax.ShapeDtypeStruct((1, 1), F32)
    shape = (MICRO, GROUP, 2, COLS, C)
    near, far, one = (pl.BlockSpec(memory_space=k) for k in (pltpu.VMEM, pl.ANY, pltpu.SMEM))
    D = pltpu.SemaphoreType.DMA
    return pl.pallas_call(
        functools.partial(update_kernel, e),
        in_specs=[near, near, far, far, far, far, far],
        out_specs=(one, one, far, far, far, far),
        out_shape=(scalar, scalar, flat, flat, flat, jax.ShapeDtypeStruct(shape, F32)),
        scratch_shapes=[pltpu.VMEM((e.slab, LANES), F32)] * 4
        + [pltpu.VMEM(shape, BF16), pltpu.VMEM(shape, F32), D((4, 4)), D((4, 3)), D((MICRO,)), D((MICRO,))],
        compiler_params=pltpu.CompilerParams(vmem_limit_bytes=64 * MB - 65536),
        name="update",
    )(norm, loss, grad, params, m1, m2, out)


def local(e, features, drop_mask, labels, params, moment1, moment2):
    flat = [v.reshape(e.slab, LANES) for v in (params, moment1, moment2)]
    grad, norm, loss, out = train_step(e, features, drop_mask, labels, flat[0])
    norm, loss, new_params, first, second, feats = update(e, grad, norm, loss, *flat, out)
    size = e.slab * LANES
    return (
        new_params.reshape(size),
        first.reshape(size),
        second.reshape(size),
        loss.reshape(()),
        norm.reshape(()),
        feats,
    )


def solution(mesh):
    e = Env()
    e.n = mesh.shape["rows"]
    e.nb = mesh.shape["batch"]
    e.G = e.n // GROUP
    e.slab = FLAT // e.n
    e.half = (e.slab + 31) // 32 * 16
    e.positions = float(e.n * COLS // 2)
    e.inv_count = 1.0 / (MICRO * GROUP * e.nb)
    return jax.shard_map(
        functools.partial(local, e),
        mesh=mesh,
        in_specs=(
            P(None, "batch", "rows", None, None),
            P(None, "batch"),
            P(None, "batch"),
            P("rows"),
            P("rows"),
            P("rows"),
        ),
        out_specs=(P("rows"), P("rows"), P("rows"), P(), P(), P(None, "batch", "rows", None, None)),
        check_vma=False,
    )
```

```python
import functools

import jax
import jax.numpy as jnp
from jax import lax
from jax.experimental import pallas as pl
from jax.experimental.pallas import tpu as pltpu
from jax.sharding import PartitionSpec as P

C = 384
HID = 1536
DOUT = 768
CLS = 1000
MICRO = 3
STEP = 10
P_SIZE = 3153920
KEEP = 0.8
CLIP = 0.01
RATE = 0.05
BETA_ONE = 0.9
BETA_TWO = 0.999
DECAY = 0.05
EPS_ADAM = 1e-08
EPS_NORM = 1e-06

MESH = pl.DeviceIdType.MESH
F32 = jnp.float32
BF16 = jnp.bfloat16
MB = 1 << 20

LANES = 128
J = C // LANES
GROUP = 4
OWN = 8
COLS = 64
PADC = COLS + 6
SUB = 16
POS = COLS * OWN
NPOS = MICRO * POS
FLAT = P_SIZE // LANES
ROW_K = 0
ROW_UP = 49 * J
ROW_CUP = ROW_UP + C * HID // LANES
ROW_DOWN = ROW_CUP + HID // LANES
ROW_VEC = ROW_DOWN + C * HID // LANES
ROW_DS = ROW_VEC + 7 * J
ROW_OUT = ROW_DS + 4 * C * DOUT // LANES
ROW_HEAD = ROW_OUT + 3 * DOUT // LANES
ROW_BH = ROW_HEAD + DOUT * CLS // LANES
TABLES = (
    (ROW_K, 49 * J, 0),
    (ROW_CUP, HID // LANES, 152),
    (ROW_VEC, 7 * J, 168),
    (ROW_OUT, 3 * DOUT // LANES, 192),
    (ROW_BH, FLAT - ROW_BH, 216),
)
TAB_ROWS = 232
TAB_SPAN = (152, 16, 24, 24, 16)
T_CUP, T_VEC, T_OUT, T_BH = 152, 168, 192, 216
SG_ROWS = 320
SG_VEC, SG_CUP = 160, 240
CLSP = 1024


class Env:
    pass


def xrow(j, m):
    return (j * MICRO + m) * PADC * SUB


def rows_of(refs, row, count):
    return refs[row : row + count, :]


def lane_row(ref, row, count):
    return jnp.concatenate([ref[row + k : row + k + 1, :] for k in range(count)], axis=1)


def ln_parts(blocks, width):
    total = blocks[0]
    for block in blocks[1:]:
        total = total + block
    mean = jnp.sum(total, -1, keepdims=True) * (1.0 / width)
    centred = [block - mean for block in blocks]
    square = centred[0] * centred[0]
    for block in centred[1:]:
        square = square + block * block
    spread = jnp.sum(square, -1, keepdims=True) * (1.0 / width)
    scale = lax.rsqrt(spread + EPS_NORM)
    return [block * scale for block in centred], scale


def here(e):
    e.r = lax.axis_index("rows")
    e.b = lax.axis_index("batch")
    e.g = e.r // GROUP
    e.i = e.r % GROUP
    e.h = e.b % 2


def dev(e, r=None, b=None):
    return {"rows": e.r if r is None else r, "batch": e.b if b is None else b}


def remote(e, src, dst, send, recv, r=None, b=None):
    return pltpu.make_async_remote_copy(
        src, dst, send, recv, device_id=(e.r if r is None else r, e.b if b is None else b), device_id_type=MESH
    )


def ph_barrier_signal(e, B):
    barrier = pltpu.get_barrier_semaphore()
    for d in range(1, e.n):
        pl.semaphore_signal(barrier, inc=1, device_id=(lax.rem(e.r + d, e.n), e.b), device_id_type=MESH)
    for d in range(1, e.nb):
        pl.semaphore_signal(barrier, inc=1, device_id=(e.r, lax.rem(e.b + d, e.nb)), device_id_type=MESH)


def ph_barrier_wait(e, B):
    pl.semaphore_wait(pltpu.get_barrier_semaphore(), e.n - 1 + e.nb - 1)


def feat_copy(e, B, m, d):
    j = lax.rem(e.i + d, GROUP)
    return remote(
        e,
        B.features.at[m, j],
        B.xg.at[m, pl.ds(3 + 2 * e.i, 2)],
        B.s_feat.at[m, d],
        B.r_feat.at[m, d],
        r=e.g * GROUP + j,
    )


def feat_own(e, B):
    return pltpu.make_async_copy(B.features.at[:, e.i], B.xg.at[:, pl.ds(3 + 2 * e.i, 2)], B.s_own.at[0])


def feat_start(e, B, m):
    if m == 0:
        feat_own(e, B).start()
    for d in (2, 3, 1):
        feat_copy(e, B, m, d).start()


def ph_feat_zero(e, B):
    zero = jnp.zeros((MICRO, 3, COLS, C), BF16)

    @pl.when(e.g == 0)
    def _():
        B.xg[:, 0:3] = zero

    @pl.when(e.g == e.G - 1)
    def _():
        B.xg[:, 11:14] = zero


def halo_copy(e, B, m, up):
    if up:
        return remote(e, B.xg.at[m, 8:11], B.xg.at[m, 0:3], B.s_halo.at[1, m], B.r_halo.at[1, m], r=e.r + GROUP)
    return remote(e, B.xg.at[m, 3:6], B.xg.at[m, 11:14], B.s_halo.at[0, m], B.r_halo.at[0, m], r=e.r - GROUP)


def halo_start(e, B, m):
    if m == 0:
        feat_own(e, B).wait()
    for d in range(1, GROUP):
        feat_copy(e, B, m, d).wait_recv()

    @pl.when(e.g > 0)
    def _():
        halo_copy(e, B, m, False).start()

    @pl.when(e.g < e.G - 1)
    def _():
        halo_copy(e, B, m, True).start()


def halo_wait(e, B, m):
    @pl.when(e.g < e.G - 1)
    def _():
        halo_copy(e, B, m, False).wait_recv()

    @pl.when(e.g > 0)
    def _():
        halo_copy(e, B, m, True).wait_recv()


def ph_feat_done(e, B):
    for m in range(MICRO):
        for d in range(1, GROUP):
            feat_copy(e, B, m, d).wait_send()

        @pl.when(e.g > 0)
        def _(m=m):
            halo_copy(e, B, m, False).wait_send()

        @pl.when(e.g < e.G - 1)
        def _(m=m):
            halo_copy(e, B, m, True).wait_send()


def ph_cast(e, B):
    for h in range(2):
        count = e.half if h == 0 else e.slab - e.half
        whole = count // 16 * 16
        B.gw[e.r, h, 0:whole, :] = B.params[h * e.half : h * e.half + whole, :].astype(BF16)
        rest = count - whole
        if whole < e.half:
            parts = [jnp.zeros((e.half - whole - rest, LANES), F32)]
            if rest:
                parts = [B.params[e.slab - rest : e.slab, :]] + parts
            B.gw[e.r, h, whole : e.half, :] = jnp.concatenate(parts, axis=0).astype(BF16)
    for k, (first, count, place) in enumerate(TABLES):
        off = first % e.slab

        @pl.when(e.r == first // e.slab)
        def _(off=off, count=count, place=place):
            B.tab[place : place + count, :] = B.params[off : off + count, :]


def table_line(e, B, k, d):
    first, count, place = TABLES[k]
    owner = first // e.slab
    part = pl.ds(place, TAB_SPAN[k])
    return remote(e, B.tab.at[part], B.tab.at[part], B.s_tab.at[k, d], B.r_tab.at[k], r=lax.rem(owner + GROUP * d, e.n))


def table_group(e, B, k, d):
    first, count, place = TABLES[k]
    part = pl.ds(place, TAB_SPAN[k])
    to = e.g * GROUP + lax.rem(e.i + d, GROUP)
    return remote(e, B.tab.at[part], B.tab.at[part], B.s_tabg.at[k, d], B.r_tab.at[k], r=to)


def ph_tables_start(e, B):
    for k, (first, count, place) in enumerate(TABLES):
        owner = first // e.slab

        @pl.when(e.r == owner)
        def _(k=k):
            for d in range(1, e.G):
                table_line(e, B, k, d).start()
            for d in range(1, GROUP):
                table_group(e, B, k, d).start()


def tables_forward(e, B, some):
    for k in some:
        owner = TABLES[k][0] // e.slab

        @pl.when(jnp.logical_and(e.i == owner % GROUP, e.r != owner))
        def _(k=k):
            table_line(e, B, k, 1).wait_recv()
            for d in range(1, GROUP):
                table_group(e, B, k, d).start()


def tables_wait(e, B, some):
    for k in some:
        owner = TABLES[k][0] // e.slab

        @pl.when(e.i != owner % GROUP)
        def _(k=k):
            table_group(e, B, k, 1).wait_recv()


def ph_tables_done(e, B):
    for k, (first, count, place) in enumerate(TABLES):
        owner = first // e.slab

        @pl.when(e.r == owner)
        def _(k=k):
            for d in range(1, e.G):
                table_line(e, B, k, d).wait_send()

        @pl.when(e.i == owner % GROUP)
        def _(k=k):
            for d in range(1, GROUP):
                table_group(e, B, k, d).wait_send()


CHUNKS = 2


def chunk_of(e, c):
    if c is None:
        return pl.ds(0, e.half)
    tiles = e.half // 16
    cuts = [(tiles * k + CHUNKS - 1) // CHUNKS * 16 for k in range(CHUNKS + 1)]
    return pl.ds(cuts[c], cuts[c + 1] - cuts[c])


def half_ref(e, B, slot, h, c):
    return B.gw.at[slot, h, chunk_of(e, c)]


def line_copy(e, B, level, up, c):
    ref = half_ref(e, B, level * GROUP + e.i, e.h, c)
    k = 0 if up else 1
    return remote(e, ref, ref, B.s_line.at[k, level], B.r_line.at[level, c or 0], r=e.r + GROUP if up else e.r - GROUP)


def pair_copy(e, B, level, c):
    ref = half_ref(e, B, level * GROUP + e.i, e.h, c)
    to = e.g * GROUP + lax.rem(e.i + 2, GROUP)
    return remote(e, ref, ref, B.s_pair.at[level], B.r_pair.at[level, c or 0], r=to)


def row_copy(e, B, level, other, c):
    i = lax.rem(e.i + 2, GROUP) if other else e.i
    ref = half_ref(e, B, level * GROUP + i, e.h, c)
    k = int(other)
    return remote(e, ref, ref, B.s_row.at[k, level], B.r_row.at[k, level, c or 0], b=e.b + 1 - 2 * e.h)


def core_copy(e, B, level, other, mine, c):
    i = lax.rem(e.i + 2, GROUP) if other else e.i
    ref = half_ref(e, B, level * GROUP + i, e.h if mine else 1 - e.h, c)
    k = 2 * int(other) + int(mine)
    sib = e.g * GROUP + e.i + 1 - 2 * (e.i % 2)
    return remote(e, ref, ref, B.s_core.at[k, level], B.r_core.at[k, level, c or 0], r=sib)


def line_out(e, B, level, c):
    @pl.when(jnp.logical_and(e.g >= level, e.g + 1 < e.G))
    def _():
        line_copy(e, B, level, True, c).start()

    @pl.when(jnp.logical_and(e.g <= level, e.g >= 1))
    def _():
        line_copy(e, B, level, False, c).start()


def at_hop(e, level, hop, body):
    if hop == 0:
        cond = e.g == level
    else:
        cond = jnp.logical_or(e.g == level + hop, e.g == level - hop)
    pl.when(cond)(body)


def line_send(e, B, levels, chunks):
    for level in levels:

        def body(level=level):
            for c in chunks:
                line_out(e, B, level, c)

        at_hop(e, level, 0, body)


def line_step(e, B, levels, hop, chunks):
    for level in levels:

        def body(level=level):
            for c in chunks:
                line_copy(e, B, level, True, c).wait_recv()
                line_out(e, B, level, c)
                row_copy(e, B, level, False, c).start()
                core_copy(e, B, level, False, True, c).start()

        at_hop(e, level, hop, body)


def pair_step(e, B, levels, hop, chunks):
    for level in levels:

        def body(level=level):
            for c in chunks:
                pair_copy(e, B, level, c).start()
                if hop == 0:
                    core_copy(e, B, level, False, True, c).start()
                    core_copy(e, B, level, False, False, c).start()

        at_hop(e, level, hop, body)


def row_step(e, B, levels, hop, chunks):
    for level in levels:

        def body(level=level):
            for c in chunks:
                pair_copy(e, B, level, c).wait_recv()
                row_copy(e, B, level, True, c).start()
                core_copy(e, B, level, True, True, c).start()

        at_hop(e, level, hop, body)


def core_step(e, B, levels, hop, chunks):
    for level in levels:

        def body(level=level):
            for c in chunks:
                if hop:
                    row_copy(e, B, level, False, c).wait_recv()
                    core_copy(e, B, level, False, False, c).start()
                row_copy(e, B, level, True, c).wait_recv()
                core_copy(e, B, level, True, False, c).start()

        at_hop(e, level, hop, body)


def gather_ready(e, B, levels):
    for level in levels:
        for other in (False, True):
            for mine in (False, True):
                for c in range(CHUNKS):
                    core_copy(e, B, level, other, mine, c).wait_recv()


def ph_gather_done(e, B):
    G = e.G
    for level in range(G):
        pair_copy(e, B, level, None).wait_send()
        row_copy(e, B, level, True, None).wait_send()

        @pl.when(e.g != level)
        def _(level=level):
            row_copy(e, B, level, False, None).wait_send()

        for other in (False, True):
            for mine in (False, True):
                core_copy(e, B, level, other, mine, None).wait_send()

        @pl.when(jnp.logical_and(e.g >= level, e.g + 1 < G))
        def _(level=level):
            line_copy(e, B, level, True, None).wait_send()

        @pl.when(jnp.logical_and(e.g <= level, e.g >= 1))
        def _(level=level):
            line_copy(e, B, level, False, None).wait_send()


def flatten(e, B, first, last):
    s0 = first // e.slab

    def slab(k, _):
        for h in range(2):
            count = (e.half if h == 0 else e.slab - e.half + 15) // 16 * 16
            base = e.slab * k + h * e.half
            B.big[pl.ds(base, count), :] = B.gw[s0 + k, h, 0:count, :].astype(F32)
        return 0

    lax.fori_loop(0, (last - 1) // e.slab - s0 + 1, slab, 0)
    return e.slab * s0


def ph_weights_up(e, B):
    base = flatten(e, B, ROW_UP, ROW_CUP)
    for j in range(HID // LANES):
        B.wup[:, LANES * j : LANES * (j + 1)] = B.big[pl.ds(ROW_UP - base + j, C, stride=HID // LANES), :].astype(BF16)


def ph_weights_down(e, B):
    base = flatten(e, B, ROW_DOWN, ROW_VEC)
    for j in range(J):
        B.wdn[:, LANES * j : LANES * (j + 1)] = B.big[pl.ds(ROW_DOWN - base + j, HID, stride=J), :].astype(BF16)


def ph_weights_head(e, B):
    base = flatten(e, B, ROW_DS, ROW_OUT)
    per = DOUT // LANES
    for j in range(per):
        B.wds[:, LANES * j : LANES * (j + 1)] = B.big[pl.ds(ROW_DS - base + j, 4 * C, stride=per), :].astype(BF16)
    base = flatten(e, B, ROW_HEAD, ROW_BH)
    lane = lax.broadcasted_iota(jnp.int32, (DOUT // 16, LANES), 1)
    for kk in range(16):
        first, off = divmod(CLS * kk, LANES)
        parts = [B.big[pl.ds(ROW_HEAD - base + first + t, DOUT // 16, stride=125), :] for t in range(9 if off else 8)]
        if off:
            parts = [pltpu.roll(part, LANES - off, 1) for part in parts]
        for t in range(8):
            tile = parts[t]
            if off:
                tile = jnp.where(lane < LANES - off, parts[t], parts[t + 1])
            if t == 7:
                tile = jnp.where(lane < CLS - 7 * LANES, tile, 0.0)
            B.dx[pl.ds(DOUT * t + kk, DOUT // 16, stride=16), :] = tile
    for t in range(8):
        B.wh[:, LANES * t : LANES * (t + 1)] = B.dx[DOUT * t : DOUT * (t + 1), :].astype(BF16)


def hooks(it, steps, also=None):
    if not steps:
        return
    bits = sum(1 << k for k in steps)
    due = lax.rem(lax.shift_right_logical(jnp.int32(bits), it), 2) == 1
    if also is not None:
        due = jnp.logical_and(due, also)

    @pl.when(due)
    def _():
        for k, some in steps.items():

            @pl.when(it == k)
            def _(some=some):
                for step in some:
                    step()


def transpose(e, B, m):
    pad = jnp.zeros((3 * SUB, LANES), F32)
    for j in range(J):
        B.big[pl.ds(xrow(j, m), 3 * SUB), :] = pad
        B.big[pl.ds(xrow(j, m) + (COLS + 3) * SUB, 3 * SUB), :] = pad
        for row in range(14):
            v = B.xg[m, row, :, LANES * j : LANES * (j + 1)].astype(F32)
            B.big[pl.ds(xrow(j, m) + 3 * SUB + row, COLS, stride=SUB), :] = v
            if 3 <= row < 11:
                B.xc[pl.ds(j * NPOS + m * POS + row - 3, COLS, stride=OWN), :] = v


def ph_taps(e, B):
    def body(t, _):
        B.kb[t] = jnp.broadcast_to(B.tab[pl.ds(t, 1), :], (8, LANES))
        return 0

    lax.fori_loop(0, 49 * J, body, 0)


def vec_row(B, v, j):
    row = T_VEC + v * J + j
    return B.tab[row : row + 1, :]


def conv_tile(B, m, j, c0, tile, acc, flip):
    for a in range(7):
        taps = [B.kb[((6 - a) * 7 + 6 - b if flip else a * 7 + b) * J + j] for b in range(7)]
        for c in range(tile + 6):
            d = B.big[pl.ds(xrow(j, m) + (c0 + c) * SUB + a, OWN), :]
            for b in range(7):
                if 0 <= c - b < tile:
                    acc[c - b] = acc[c - b] + d * taps[b]
    return acc


TILE = 32


def ph_conv_fwd(e, B, steps):
    halves = COLS // TILE

    def body(it, _):
        m = it // halves
        c0 = it % halves * TILE
        for j in range(J):
            hooks(it, {k // J: v for k, v in steps.items() if k % J == j})
            bias = jnp.broadcast_to(vec_row(B, 0, j), (OWN, LANES))
            acc = conv_tile(B, m, j, c0, TILE, [bias] * TILE, False)
            at = j * NPOS + m * POS + c0 * OWN
            for c in range(TILE):
                B.dx[pl.ds(pl.multiple_of(at + OWN * c, OWN), OWN), :] = acc[c]
        return 0

    lax.fori_loop(0, MICRO * halves, body, 0)


def ph_norm_one(e, B):
    size = 256

    def body(it, _):
        at = pl.multiple_of(it * size, size)
        hat, scale = ln_parts([B.dx[pl.ds(j * NPOS + at, size), :] for j in range(J)], C)
        B.rs1[pl.ds(at, size), :] = jnp.broadcast_to(scale, (size, LANES))
        for j in range(J):
            B.v1[pl.ds(at, size), LANES * j : LANES * (j + 1)] = hat[j]
            B.n[pl.ds(at, size), LANES * j : LANES * (j + 1)] = (
                hat[j] * vec_row(B, 1, j) + vec_row(B, 2, j)
            ).astype(BF16)
        return 0

    lax.fori_loop(0, NPOS // size, body, 0)


def ph_mlp_up(e, B, steps):
    chunk = 256
    width = 256
    c0 = 0.7978845608028654
    c1 = 0.044715 * c0

    def body(it, _):
        hooks(it, steps)
        at = pl.multiple_of(it * chunk, chunk)
        rows = B.n[pl.ds(at, chunk), :]
        for k in range(HID // width):
            lanes = slice(width * k, width * (k + 1))
            bias = lane_row(B.tab, T_CUP + k * width // LANES, width // LANES)
            h = jnp.dot(rows, B.wup[:, lanes], preferred_element_type=F32) + bias
            sq = h * h
            half = 0.5 * jnp.tanh(h * (c0 + c1 * sq)) + 0.5
            u = h * half
            B.u[pl.ds(at, chunk), lanes] = u.astype(BF16)
            slope = half + u * (1.0 - half) * (2.0 * c0 + 6.0 * c1 * sq)
            B.gp[pl.ds(at, chunk), lanes] = slope.astype(BF16)
        return 0

    lax.fori_loop(0, NPOS // chunk, body, 0)


def ph_mlp_down(e, B, steps):
    chunk = 256
    B.ps[...] = jnp.zeros_like(B.ps)

    def body(it, _):
        hooks(it, steps)
        at = pl.multiple_of(it * chunk, chunk)
        m = it // (POS // chunk)
        keep = B.mask[m, e.i].astype(F32) * (1.0 / KEEP)
        z = jnp.dot(B.u[pl.ds(at, chunk), :], B.wdn[...], preferred_element_type=F32)
        resid = []
        for j in range(J):
            zj = z[:, LANES * j : LANES * (j + 1)] + vec_row(B, 3, j)
            B.z[pl.ds(j * NPOS + at, chunk), :] = zj
            resid.append(B.xc[pl.ds(j * NPOS + at, chunk), :] + (vec_row(B, 4, j) * keep) * zj)
        hat, scale = ln_parts(resid, C)
        B.rs2[pl.ds(at, chunk), :] = jnp.broadcast_to(scale, (chunk, LANES))
        for j in range(J):
            B.v2[pl.ds(at, chunk), LANES * j : LANES * (j + 1)] = hat[j]
            low = (hat[j] * vec_row(B, 5, j) + vec_row(B, 6, j)).astype(BF16).astype(F32)
            low = jnp.sum(low.reshape(chunk // 16, 2, OWN, LANES), 0)
            B.ps[m, :, :, LANES * j : LANES * (j + 1)] += low
        return 0

    lax.fori_loop(0, NPOS // chunk, body, 0)


def ph_patch_local(e, B):
    even = lax.broadcasted_iota(jnp.int32, (OWN, C), 0) % 2 == 0
    pick = lax.broadcasted_iota(jnp.int32, (8, C), 0)
    for parity in range(2):
        tile = jnp.zeros((8, C), F32)
        for side in range(2):
            for m in range(MICRO):
                v = B.ps[m, side]
                part = jnp.sum(jnp.where(even if parity == 0 else jnp.logical_not(even), v, 0.0), 0, keepdims=True)
                tile = jnp.where(pick == m + 4 * side, part, tile)
        B.sl[8 * parity : 8 * parity + 8, :] = tile


def place_rows(sums, q):
    tile = sums[8 * (q // 2) : 8 * (q // 2) + 8, :]
    return pltpu.roll(tile, 4, 0) if q % 2 else tile


def patch_copy(e, B, d):
    to = lax.rem(e.g + d, e.G)
    return remote(e, B.sl, B.sr.at[d], B.s_patch.at[d], B.r_patch.at[d], r=to * GROUP + e.i)


def patch_start(e, B):
    for d in range(1, e.G):
        patch_copy(e, B, d).start()
    B.sr[0] = B.sl[...]


def patch_wait(e, B):
    for d in range(1, e.G):
        patch_copy(e, B, d).wait_recv()
    for d in range(1, e.G):
        patch_copy(e, B, d).wait_send()


def split3(v):
    hi = v.astype(BF16).astype(F32)
    mid = (v - hi).astype(BF16).astype(F32)
    return hi, mid, v - hi - mid


def ph_head(e, B):
    total = None
    for level in range(e.G):
        part = B.sr[lax.rem(e.g - level + e.G, e.G)]
        total = part if total is None else total + part
    per = DOUT // LANES
    gain = lane_row(B.tab, T_OUT + per, per)
    shift = lane_row(B.tab, T_OUT + 2 * per, per)
    mean = total * (1.0 / e.positions)
    pooled = lane_row(B.tab, T_OUT, per)
    for q in range(4):
        parts = jnp.concatenate(split3(place_rows(mean, q)), axis=0).astype(BF16)
        prod = jnp.dot(parts, B.wds[C * q : C * (q + 1), :], preferred_element_type=F32)
        pooled = pooled + (prod[0:8] + (prod[8:16] + prod[16:24]))
    rows = lax.broadcasted_iota(jnp.int32, (8, 1), 0)
    live = rows < MICRO
    (hat,), scale = ln_parts([pooled], DOUT)
    query = (hat * gain + shift).astype(BF16)
    lane = lax.broadcasted_iota(jnp.int32, (8, CLSP), 1)
    logits = jnp.dot(query, B.wh[...], preferred_element_type=F32) + lane_row(B.tab, T_BH, CLSP // LANES)
    logits = jnp.where(lane < CLS, logits, -1e30)
    top = jnp.max(logits, 1, keepdims=True)
    powers = jnp.exp(logits - top)
    expsum = jnp.sum(powers, 1, keepdims=True)
    label = jnp.zeros((8, 1), jnp.int32)
    for m in range(MICRO):
        label = jnp.where(rows == m, B.labels[m, e.i], label)
    onehot = (lane == label).astype(F32)
    own = jnp.sum(jnp.where(lane == label, logits, 0.0), 1, keepdims=True)
    loss = jnp.sum(jnp.where(live, top + jnp.log(expsum) - own, 0.0), 0, keepdims=True)
    grad = jnp.where(live, (powers / expsum - onehot) * e.inv_count, 0.0).astype(BF16)
    grad_query = lax.dot_general(grad, B.wh[...], (((1,), (1,)), ((), ())), preferred_element_type=F32)
    dn = grad_query * gain
    m1 = jnp.sum(dn, 1, keepdims=True) * (1.0 / DOUT)
    m2 = jnp.sum(dn * hat, 1, keepdims=True) * (1.0 / DOUT)
    grad_pool = scale * (dn - m1 - hat * m2)
    down = jnp.where(live, grad_pool * (1.0 / e.positions), 0.0).astype(BF16)
    for q in range(4):
        B.dn2[8 * q : 8 * q + 8, :] = lax.dot_general(
            down, B.wds[C * q : C * (q + 1), :], (((1,), (1,)), ((), ())), preferred_element_type=F32
        )
    low = grad.astype(F32)
    d32 = down.astype(F32)
    q32 = jnp.where(live, query.astype(F32), 0.0)
    zero3 = jnp.zeros((3, C), F32)
    g3 = jnp.sum(jnp.where(live, grad_query * hat, 0.0), 0, keepdims=True)
    s3 = jnp.sum(jnp.where(live, grad_query, 0.0), 0, keepdims=True)
    vec = jnp.concatenate([g3, s3], axis=1)
    vec_parts = split3(vec)
    loss_parts = split3(loss)
    for q in range(4):
        at = slice(C * q, C * (q + 1))
        s_hi, s_mid, _ = split3(place_rows(total, q))
        B.pb[0:8, at] = jnp.zeros((8, C), F32)
        B.pb[8:16, at] = jnp.zeros((8, C), F32)
        B.pb[0:3, at] = s_hi[0:3]
        B.pb[3:6, at] = s_mid[0:3]
    B.pb[6:9, 0:DOUT] = d32[0:3]
    B.pb[6:9, DOUT : 2 * DOUT] = q32[0:3]
    B.pb[9:12, 0:CLSP] = low[0:3]
    for k in range(3):
        B.pb[12 + k : 13 + k, :] = vec_parts[k]
        B.pb[15:16, LANES * k : LANES * (k + 1)] = jnp.broadcast_to(loss_parts[k], (1, LANES))
    B.pall[e.i * e.nb + e.b] = B.pb[...].astype(BF16)
    even = lax.broadcasted_iota(jnp.int32, (OWN, C), 0) % 2 == 0
    for m in range(MICRO):
        for side in range(2):
            first = B.dn2[8 * side + m : 8 * side + m + 1, :]
            second = B.dn2[8 * (2 + side) + m : 8 * (2 + side) + m + 1, :]
            B.dnt[m, side] = jnp.where(even, first, second)


def batch_copy(e, B, d):
    slot = e.i * e.nb + e.b
    return remote(e, B.pall.at[slot], B.pall.at[slot], B.s_pb.at[d], B.r_pb.at[d], b=lax.rem(e.b + d, e.nb))


def group_copy(e, B, d):
    at = pl.ds(e.i * e.nb, e.nb)
    to = e.g * GROUP + lax.rem(e.i + d, GROUP)
    return remote(e, B.pall.at[at], B.pall.at[at], B.s_pg.at[d], B.r_pg.at[d], r=to)


def ph_payload_batch(e, B):
    for d in range(1, e.nb):
        batch_copy(e, B, d).start()


def ph_payload_group(e, B):
    for d in range(1, e.nb):
        batch_copy(e, B, d).wait_recv()
    for d in range(1, GROUP):
        group_copy(e, B, d).start()


def ph_payload_wait(e, B):
    for d in range(1, GROUP):
        group_copy(e, B, d).wait_recv()
    for d in range(1, e.nb):
        batch_copy(e, B, d).wait_send()
    for d in range(1, GROUP):
        group_copy(e, B, d).wait_send()


def lane_sum(blocks):
    total = blocks[0]
    for block in blocks[1:]:
        total = total + block
    return jnp.sum(total, -1, keepdims=True) * (1.0 / C)


def fold8(v):
    return jnp.sum(v.reshape(v.shape[0] // 8, 8, v.shape[1]), 0)


def ph_bwd_one(e, B):
    chunk = 256
    half = chunk // 16
    B.acc[...] = jnp.zeros_like(B.acc)
    B.acup[...] = jnp.zeros_like(B.acup)
    B.ps[...] = jnp.zeros_like(B.ps)

    def body(it, _):
        at = pl.multiple_of(it * chunk, chunk)
        m = it // (POS // chunk)
        keep = B.mask[m, e.i].astype(F32) * (1.0 / KEEP)
        span = pl.ds(at, chunk)
        lanes = [slice(LANES * j, LANES * (j + 1)) for j in range(J)]
        dg = [B.dnt[m, :, :, lanes[j]] * vec_row(B, 5, j) for j in range(J)]
        m1 = lane_sum(dg)
        hat = [B.v2[span, lanes[j]].reshape(half, 2, OWN, LANES) for j in range(J)]
        m2 = lane_sum([dg[j] * hat[j] for j in range(J)])
        scale = B.rs2[span, :].reshape(half, 2, OWN, LANES)
        for j in range(J):
            zspan = pl.ds(j * NPOS + at, chunk)
            dr = (scale * (dg[j] - m1 - hat[j] * m2)).reshape(chunk, LANES)
            B.ps[m, :, :, lanes[j]] += jnp.sum(hat[j], 0)
            dz = (dr * (vec_row(B, 4, j) * keep)).astype(BF16)
            B.dz[span, lanes[j]] = dz
            B.acc[3, :, lanes[j]] += fold8(dz.astype(F32))
            B.acc[4, :, lanes[j]] += fold8(dr * B.z[zspan, :]) * keep
            B.z[zspan, :] = dr
        return 0

    lax.fori_loop(0, NPOS // chunk, body, 0)
    for m in range(MICRO):
        B.acc[5] += B.dnt[m, 0] * B.ps[m, 0] + B.dnt[m, 1] * B.ps[m, 1]
        B.acc[6] += (B.dnt[m, 0] + B.dnt[m, 1]) * float(COLS // 2)


def ph_bwd_two(e, B, steps):
    chunk = 256
    width = 256

    def body(it, _):
        hooks(it, steps)
        at = pl.multiple_of(it * chunk, chunk)
        m = it // (POS // chunk)
        c0 = (it % (POS // chunk)) * (chunk // OWN)
        span = pl.ds(at, chunk)
        lanes = [slice(LANES * j, LANES * (j + 1)) for j in range(J)]
        dz = B.dz[span, :]
        for k in range(HID // width):
            hid = slice(width * k, width * (k + 1))
            du = lax.dot_general(dz, B.wdn[hid, :], (((1,), (1,)), ((), ())), preferred_element_type=F32)
            dh = (du * B.gp[span, hid].astype(F32)).astype(BF16)
            B.gp[span, hid] = dh
            B.acup[:, hid] += fold8(dh.astype(F32))
        dn = lax.dot_general(B.gp[span, :], B.wup[...], (((1,), (1,)), ((), ())), preferred_element_type=F32)
        dns = [dn[:, lanes[j]] for j in range(J)]
        dg = [dns[j] * vec_row(B, 1, j) for j in range(J)]
        hat = [B.v1[span, lanes[j]] for j in range(J)]
        m1 = lane_sum(dg)
        m2 = lane_sum([dg[j] * hat[j] for j in range(J)])
        scale = B.rs1[span, :]
        for j in range(J):
            dy = scale * (dg[j] - m1 - hat[j] * m2)
            B.acc[0, :, lanes[j]] += fold8(dy)
            B.acc[1, :, lanes[j]] += fold8(dns[j] * hat[j])
            B.acc[2, :, lanes[j]] += fold8(dns[j])
            for c in range(chunk // OWN):
                B.big[pl.ds(xrow(j, m) + (3 + c0 + c) * SUB + 3, OWN), :] = dy[OWN * c : OWN * (c + 1), :]
        return 0

    lax.fori_loop(0, NPOS // chunk, body, 0)


def wgrad_down(e, B, f):
    for k in range(2):
        first = 2 * C * f + C * k
        w = lax.dot_general(
            B.u[:, first : first + C], B.dz[...], (((0,), (0,)), ((), ())), preferred_element_type=F32
        )
        w = w.reshape(24, 16, C)
        a, b = w[:, 0:8], w[:, 8:16]
        units = [v[:, :, LANES * j : LANES * (j + 1)] for v in (a, b) for j in range(J)]
        tiles = [jnp.concatenate(units[2 * t : 2 * t + 2], axis=1).astype(BF16) for t in range(3)]
        for q in range(24):
            piece, inner = divmod(24 * k + q, 3)
            for t in range(3):
                B.gb[f, piece // 4, piece // 2 % 2, piece % 2, inner, t] = tiles[t][q]


def wgrad_up(e, B, f):
    width = 256
    for k in range(3):
        first = 768 * (f - 2) + width * k
        w = lax.dot_general(
            B.n[...], B.gp[:, first : first + width], (((0,), (0,)), ((), ())), preferred_element_type=F32
        )
        w = w.reshape(48, 8, width)
        w = jnp.concatenate([w[:, :, :LANES], w[:, :, LANES:]], axis=1).astype(BF16)
        B.gb[f, :, :, :, :, k] = w.reshape(4, 2, 2, 3, 16, LANES)


def dy_copy(e, B, m, up):
    if up:
        return remote(e, B.hs.at[m, 1], B.hr.at[m, 0], B.s_dy.at[1, m], B.r_dy.at[1, m], r=e.r + GROUP)
    return remote(e, B.hs.at[m, 0], B.hr.at[m, 1], B.s_dy.at[0, m], B.r_dy.at[0, m], r=e.r - GROUP)


def dy_send(e, B, m):
    zero = jnp.zeros((3 * SUB, LANES), F32)
    for j in range(J):
        B.big[pl.ds(xrow(j, m), 3 * SUB), :] = zero
        B.big[pl.ds(xrow(j, m) + (COLS + 3) * SUB, 3 * SUB), :] = zero
        for side in range(2):
            for k in range(3):
                row = 3 + k if side == 0 else 8 + k
                v = B.big[pl.ds(xrow(j, m) + 3 * SUB + row, COLS, stride=SUB), :]
                B.hs[m, side, k, :, LANES * j : LANES * (j + 1)] = v.astype(BF16)

    @pl.when(e.g > 0)
    def _():
        dy_copy(e, B, m, False).start()

    @pl.when(e.g < e.G - 1)
    def _():
        dy_copy(e, B, m, True).start()


def ph_dy_edges(e, B):
    zero = jnp.zeros((MICRO, 3, COLS, C), BF16)

    @pl.when(e.g == 0)
    def _():
        B.hr[:, 0] = zero

    @pl.when(e.g == e.G - 1)
    def _():
        B.hr[:, 1] = zero


def dy_take(e, B, m):
    @pl.when(e.g < e.G - 1)
    def _():
        dy_copy(e, B, m, False).wait_recv()

    @pl.when(e.g > 0)
    def _():
        dy_copy(e, B, m, True).wait_recv()

    for j in range(J):
        for side in range(2):
            for k in range(3):
                row = k if side == 0 else 11 + k
                v = B.hr[m, side, k, :, LANES * j : LANES * (j + 1)].astype(F32)
                B.big[pl.ds(xrow(j, m) + 3 * SUB + row, COLS, stride=SUB), :] = v


def ph_dy_done(e, B):
    for m in range(MICRO):

        @pl.when(e.g > 0)
        def _(m=m):
            dy_copy(e, B, m, False).wait_send()

        @pl.when(e.g < e.G - 1)
        def _(m=m):
            dy_copy(e, B, m, True).wait_send()


def ph_conv_kernel(e, B, parts, steps):
    halves = COLS // TILE

    def taps(it, _):
        hooks(it, steps)
        j = it // 7
        a = it % 7

        def body(k, dk):
            m = parts.start + k // halves
            c0 = k % halves * TILE
            dk = list(dk)
            at = j * NPOS + m * POS + c0 * OWN
            xs = [B.xc[pl.ds(pl.multiple_of(at + OWN * c, OWN), OWN), :] for c in range(TILE)]
            for c in range(TILE + 6):
                d = B.big[pl.ds(xrow(j, m) + (c0 + c) * SUB + a, OWN), :]
                for b in range(7):
                    if 0 <= c - b < TILE:
                        dk[b] = dk[b] + d * xs[c - b]
            return tuple(dk)

        zero = jnp.zeros((OWN, LANES), F32)
        dk = lax.fori_loop(0, halves * len(parts), body, (zero,) * 7)
        for b in range(7):
            tap = (6 - a) * 7 + 6 - b
            B.sg[pl.ds(tap * J + j, 1), :] += jnp.sum(dk[b], 0, keepdims=True)
        return 0

    lax.fori_loop(0, 7 * J, taps, 0)


def tap_low(B, t):
    return B.wh[16 * (t // 8) : 16 * (t // 8) + 16, LANES * (t % 8) : LANES * (t % 8 + 1)]


def ph_taps_low(e, B):
    for t in range(49 * J):
        row = B.kb[t]
        B.wh[16 * (t // 8) : 16 * (t // 8) + 16, LANES * (t % 8) : LANES * (t % 8 + 1)] = jnp.concatenate(
            [row, row], axis=0
        ).astype(BF16)


def ph_conv_input(e, B, steps):
    halves = COLS // TILE
    half = TILE // 2

    def body(it, _):
        m = it // halves
        c0 = it % halves * TILE
        for j in range(J):
            hooks(it, {k // J: v for k, v in steps.items() if k % J == j})
            acc = [None] * half
            for a in range(7):
                cols = []
                for c in range(half + 6):
                    at = xrow(j, m) + (c0 + c) * SUB + a
                    pair = [B.big[pl.ds(at, OWN), :], B.big[pl.ds(at + half * SUB, OWN), :]]
                    cols.append(jnp.concatenate(pair, axis=0).astype(BF16))
                for some in (range(0, 4), range(4, 7)):
                    taps = {b: tap_low(B, ((6 - a) * 7 + 6 - b) * J + j) for b in some}
                    for c in range(half):
                        part = [cols[c + b] * taps[b] for b in some]
                        while len(part) > 1:
                            part = [part[k] + part[k + 1] for k in range(0, len(part) - 1, 2)] + part[len(part) // 2 * 2 :]
                        low = part[0].astype(F32)
                        acc[c] = low if acc[c] is None else acc[c] + low
            at = j * NPOS + m * POS + c0 * OWN
            for c in range(half):
                for k in range(2):
                    span = pl.ds(pl.multiple_of(at + OWN * (c + half * k), OWN), OWN)
                    B.dx[span, :] = B.z[span, :] + acc[c][OWN * k : OWN * (k + 1), :]
        return 0

    lax.fori_loop(0, MICRO * halves, body, 0)


def ph_small_fill(e, B):
    for k in range(HID // LANES):
        B.sg[SG_CUP + k : SG_CUP + k + 1, :] = jnp.sum(B.acup[:, LANES * k : LANES * (k + 1)], 0, keepdims=True)
    for v in range(7):
        for j in range(J):
            row = SG_VEC + v * J + j
            B.sg[row : row + 1, :] = jnp.sum(B.acc[v, :, LANES * j : LANES * (j + 1)], 0, keepdims=True)


def out_copy(e, B, m, k, d):
    j = lax.rem(e.i + d, GROUP)
    cols = pl.ds(TILE * k, TILE)
    return remote(
        e,
        B.xg.at[m, pl.ds(3 + 2 * j, 2), cols],
        B.fo.at[m, e.i, :, cols],
        B.s_out.at[m, k, d],
        B.r_out.at[m, k, d],
        r=e.g * GROUP + j,
    )


def own_out_copy(e, B, m, k):
    cols = pl.ds(TILE * k, TILE)
    return pltpu.make_async_copy(
        B.xg.at[m, pl.ds(3 + 2 * e.i, 2), cols], B.fo.at[m, e.i, :, cols], B.s_outown.at[m, k]
    )


def out_send(e, B, m, k):
    for row in range(OWN):
        for j in range(J):
            v = B.dx[pl.ds(j * NPOS + m * POS + k * TILE * OWN + row, TILE, stride=OWN), :]
            B.xg[m, 3 + row, TILE * k : TILE * (k + 1), LANES * j : LANES * (j + 1)] = v.astype(BF16)
    own_out_copy(e, B, m, k).start()
    for d in (2, 3, 1):
        out_copy(e, B, m, k, d).start()


def ph_out_wait(e, B):
    for m in range(MICRO):
        for k in range(COLS // TILE):
            own_out_copy(e, B, m, k).wait()
            for d in range(1, GROUP):
                out_copy(e, B, m, k, d).wait()


PARTS = 4
PIECE = (144, 144, 288, 288)
START = (ROW_DOWN, ROW_DOWN + 16 * 144, ROW_UP, ROW_UP)


def rs_first(e, B, f):
    c = e.i % 2
    return remote(e, B.gb.at[f, :, :, 1 - c], B.ra1.at[f], B.s_rs.at[f, 0], B.r_rs.at[f, 0], r=e.r + 1 - 2 * c)


def rs_second(e, B, f):
    to = e.g * GROUP + lax.rem(e.i + 2, GROUP)
    return remote(e, B.sa2.at[f], B.ra2.at[f], B.s_rs.at[f, 1], B.r_rs.at[f, 1], r=to)


def group_of(e, q):
    return q * (e.G // 4)


def rs_third(e, B, f, q):
    to = group_of(e, q)
    d = lax.rem(to - e.g + e.G, e.G)
    return remote(e, B.sc.at[f, q], B.rc.at[f, d], B.s_rc.at[f, q], B.r_rc.at[f, d], r=to * GROUP + e.i)


def rs_third_wait(e, B, f, d):
    return remote(e, B.sc.at[f, 0], B.rc.at[f, d], B.s_rc.at[f, 0], B.r_rc.at[f, d], r=lax.rem(e.r + GROUP, e.n))


def rs_fourth(e, B, f, d):
    return remote(e, B.rb.at[f, 0], B.rb.at[f, d], B.s_rb.at[f, d], B.r_rb.at[f, d], b=lax.rem(e.b + d, e.nb))


def ends_here(e, body):
    if e.G == 4:
        body()
    else:
        pl.when(e.g % (e.G // 4) == 0)(body)


def rs_step1(e, B, f):
    rs_first(e, B, f).start()


def rs_step2(e, B, f):
    x, c = e.i // 2, e.i % 2
    rs_first(e, B, f).wait_recv()
    for q in range(4):
        B.sa2[f, q] = (B.gb[f, q, 1 - x, c].astype(F32) + B.ra1[f, q, 1 - x].astype(F32)).astype(BF16)
    rs_second(e, B, f).start()
    for q in range(4):
        B.h1[f, q] = B.gb[f, q, x, c].astype(F32) + B.ra1[f, q, x].astype(F32)


def rs_step3(e, B, f):
    rs_second(e, B, f).wait_recv()
    for q in range(4):
        B.h1[f, q] = B.h1[f, q] + B.ra2[f, q].astype(F32)
        B.sc[f, q] = B.h1[f, q].astype(BF16)
    for q in range(4):

        @pl.when(e.g != group_of(e, q))
        def _(q=q):
            rs_third(e, B, f, q).start()


def rs_step4(e, B, f):
    def body():
        total = B.h1[f, e.g // (e.G // 4)]
        for d in range(1, e.G):
            rs_third_wait(e, B, f, d).wait_recv()
            total = total + B.rc[f, d].astype(F32)
        B.rb[f, 0] = total.astype(BF16)
        for d in range(1, e.nb):
            rs_fourth(e, B, f, d).start()

    ends_here(e, body)


def piece_owners(e, f):
    start = START[f] + PIECE[f] * (e.g // (e.G // 4) * 4 + e.i)
    return start // e.slab, (start + PIECE[f] - 1) // e.slab


def own_slot(B, f, slot):
    return B.ro.at[f, slot] if f < 2 else B.ro_up.at[f - 2, slot]


def own_copy(e, B, f, k, owner):
    slot = lax.rem(e.g // (e.G // 4) * 4 + e.i, 16 if f < 2 else 8)
    return remote(e, B.fp.at[f], own_slot(B, f, slot), B.s_ro.at[f, k], B.r_ro.at[f, slot], r=owner)


def own_wait(e, B, f, slot, home):
    remote(e, B.fp.at[f], own_slot(B, f, slot), B.s_ro.at[f, 0], B.r_ro.at[f, slot], r=home).wait_recv()


def rs_step5(e, B, f):
    def body():
        for d in range(1, e.nb):
            rs_fourth(e, B, f, d).wait_recv()
        total = None
        for b in range(e.nb):
            part = B.rb[f, lax.rem(e.b - b + e.nb, e.nb)].astype(F32)
            total = part if total is None else total + part
        B.fp[f] = total.astype(BF16)
        lo, hi = piece_owners(e, f)

        @pl.when(lo != e.r)
        def _():
            own_copy(e, B, f, 0, lo).start()

        @pl.when(jnp.logical_and(hi != lo, hi != e.r))
        def _():
            own_copy(e, B, f, 1, hi).start()

    ends_here(e, body)


def place(B, f, off, tiles):
    for k in range(3):
        for t in range(3):
            for h in range(2):
                unit = 2 * t + h
                tile = tiles[k, t, 8 * h : 8 * h + 8, :].astype(F32)
                if f >= 2:
                    at = pl.ds(MARGIN + off + 96 * k + 6 * (f - 2) + unit, 8, stride=12)
                else:
                    at = pl.ds(MARGIN + off + 48 * k + 24 * (unit // 3) + unit % 3, 8, stride=3)
                B.gf[at, :] = tile


def rs_place(e, B, f):
    for p in range(16):
        off = START[f] + PIECE[f] * p - e.slab * e.r
        home = group_of(e, p // 4) * GROUP + p % 4

        @pl.when(jnp.logical_and(off < e.slab, off + PIECE[f] > 0))
        def _(p=p, off=off, home=home):
            slot = p % (16 if f < 2 else 8)

            @pl.when(e.r != home)
            def _():
                own_wait(e, B, f, slot, home)
                place(B, f, off, B.ro[f, slot] if f < 2 else B.ro_up[f - 2, slot])

            @pl.when(e.r == home)
            def _():
                place(B, f, off, B.fp[f])


def ph_rs_done(e, B):
    for f in range(PARTS):
        rs_first(e, B, f).wait_send()
        rs_second(e, B, f).wait_send()
        for q in range(4):

            @pl.when(e.g != group_of(e, q))
            def _(f=f, q=q):
                rs_third(e, B, f, q).wait_send()

        def body(f=f):
            for d in range(1, e.nb):
                rs_fourth(e, B, f, d).wait_send()
            lo, hi = piece_owners(e, f)

            @pl.when(lo != e.r)
            def _():
                own_copy(e, B, f, 0, lo).wait_send()

            @pl.when(jnp.logical_and(hi != lo, hi != e.r))
            def _():
                own_copy(e, B, f, 1, hi).wait_send()

        ends_here(e, body)


MARGIN = 1792


QUARTER = 80
SEGMENTS = (
    (0, 0, QUARTER, ROW_K),
    (1, 0, 49 * J - QUARTER, ROW_K + QUARTER),
    (2, 0, 7 * J, ROW_VEC),
    (3, 0, HID // LANES, ROW_CUP),
)


def small_group(e, B, d):
    j = lax.rem(e.i + d, GROUP)
    at = pl.ds(pl.multiple_of(j * QUARTER, QUARTER), QUARTER)
    return remote(e, B.sg.at[at], B.sg_group.at[d - 1], B.s_sg.at[d], B.r_sg.at[d], r=e.g * GROUP + j)


def small_line(e, B, d):
    to = lax.rem(e.g + d, e.G)
    return remote(e, B.sg_line.at[0], B.sg_line.at[d], B.s_sgl.at[d], B.r_sgl.at[d], r=to * GROUP + e.i)


def small_batch(e, B, d):
    return remote(e, B.sgb.at[0], B.sgb.at[d], B.s_sgb.at[d], B.r_sgb.at[d], b=lax.rem(e.b + d, e.nb))


def small_back(e, B, q, owner):
    at = pl.ds(q * QUARTER, QUARTER)
    return remote(e, B.sga.at[at], B.sga.at[at], B.s_sgg.at[q], B.r_sgg.at[q], r=owner)


def small_moves(e):
    for q, row, count, flat in SEGMENTS:
        owner = flat // e.slab
        holder = owner // GROUP * GROUP + q
        if owner != holder:
            yield q, holder, owner


def small_step1(e, B):
    for d in (2, 3, 1):
        small_group(e, B, d).start()


def small_step2(e, B):
    total = B.sg[pl.ds(pl.multiple_of(e.i * QUARTER, QUARTER), QUARTER), :]
    for d in range(1, GROUP):
        small_group(e, B, d).wait_recv()
        total = total + B.sg_group[d - 1]
    B.sg_line[0] = total
    for d in range(1, e.G):
        small_line(e, B, d).start()


def small_step3(e, B):
    for d in range(1, e.G):
        small_line(e, B, d).wait_recv()
    total = None
    for level in range(e.G):
        part = B.sg_line[lax.rem(e.g - level + e.G, e.G)]
        total = part if total is None else total + part
    B.sgb[0] = total
    for d in range(1, e.nb):
        small_batch(e, B, d).start()


def small_step4(e, B):
    for d in range(1, e.nb):
        small_batch(e, B, d).wait_recv()
    total = None
    for b in range(e.nb):
        part = B.sgb[lax.rem(e.b - b + e.nb, e.nb)]
        total = part if total is None else total + part
    B.sga[pl.ds(pl.multiple_of(e.i * QUARTER, QUARTER), QUARTER), :] = total
    for q, holder, owner in small_moves(e):

        @pl.when(e.r == holder)
        def _(q=q, owner=owner):
            small_back(e, B, q, owner).start()


def ph_small_place(e, B):
    for q, holder, owner in small_moves(e):

        @pl.when(e.r == owner)
        def _(q=q, holder=holder):
            small_back(e, B, q, holder).wait_recv()

    for q, row, count, flat in SEGMENTS:
        off = MARGIN + flat % e.slab
        at = q * QUARTER + row

        @pl.when(e.r == flat // e.slab)
        def _(off=off, at=at, count=count):
            B.gf[off : off + count, :] = B.sga[at : at + count, :]


def ph_small_done(e, B):
    for d in range(1, GROUP):
        small_group(e, B, d).wait_send()
    for d in range(1, e.G):
        small_line(e, B, d).wait_send()
    for d in range(1, e.nb):
        small_batch(e, B, d).wait_send()
    for q, holder, owner in small_moves(e):

        @pl.when(e.r == holder)
        def _(q=q, owner=owner):
            small_back(e, B, q, owner).wait_send()


def ph_head_grads(e, B):
    parts = GROUP * e.nb
    rows = 16 * parts
    sums = None
    for p in range(parts):
        x = B.pall[p].astype(F32)
        sums = x if sums is None else sums + x
        dd = x[6:9, 0:DOUT]
        B.gp[16 * p : 16 * p + 16, 0:DOUT] = jnp.concatenate([dd, dd, jnp.zeros((10, DOUT), F32)], axis=0).astype(BF16)
        dl = x[9:12, 0:CLSP]
        B.gp[rows + 16 * p : rows + 16 * p + 16, 0:CLSP] = jnp.concatenate(
            [jnp.zeros((6, CLSP), F32), dl, jnp.zeros((7, CLSP), F32)], axis=0
        ).astype(BF16)
    B.pb[...] = sums
    for q in range(4):
        for p in range(parts):
            B.v2[16 * p : 16 * p + 16, :] = B.pall[p, :, C * q : C * (q + 1)].astype(F32)
        for j in range(J):
            t = J * q + j
            B.u[LANES * t : LANES * (t + 1), 0:rows] = B.v2[0:rows, LANES * j : LANES * (j + 1)].T.astype(BF16)
    per = DOUT // LANES
    base = MARGIN - e.slab * e.r

    kc = 288
    low = e.slab * e.r - ROW_DS

    @pl.when(jnp.logical_and(low < 4 * C * per, low + e.slab > 0))
    def _():
        k0 = jnp.clip(low // (16 * per) * 16, 0, 4 * C - kc)
        k0 = pl.multiple_of(k0, 16)
        w = jnp.dot(B.u[pl.ds(k0, kc), 0:rows], B.gp[0:rows, 0:DOUT], preferred_element_type=F32)
        for j in range(per):
            B.gf[pl.ds(base + ROW_DS + per * k0 + j, kc, stride=per), :] = w[:, LANES * j : LANES * (j + 1)]

    low2 = e.slab * e.r - ROW_HEAD

    @pl.when(jnp.logical_and(low2 < DOUT * CLS // LANES, low2 + e.slab > 0))
    def _():
        g0 = jnp.clip(low2 // 125, 0, DOUT // 16 - 16)
        k0 = pl.multiple_of(DOUT + 16 * g0, 16)
        for t in range(8):
            B.big[256 * t : 256 * (t + 1), :] = jnp.dot(
                B.u[pl.ds(k0, 256), 0:rows],
                B.gp[rows : 2 * rows, LANES * t : LANES * (t + 1)],
                preferred_element_type=F32,
            )
        lane = lax.broadcasted_iota(jnp.int32, (16, LANES), 1)
        held = None
        for kk in range(16):
            o = (-CLS * kk) % LANES
            tiles = [B.big[pl.ds(256 * t + kk, 16, stride=16), :] for t in range(8)]
            if o:
                tiles = [pltpu.roll(tile, LANES - o, 1) for tile in tiles]
            for s in range(CLS * kk // LANES, (CLS * kk + CLS - 1) // LANES + 1):
                t0 = (LANES * s - CLS * kk) // LANES
                if o == 0:
                    value = tiles[t0]
                elif t0 < 0:
                    value = tiles[0]
                elif t0 + 1 > 7:
                    value = tiles[t0]
                else:
                    value = jnp.where(lane < LANES - o, tiles[t0], tiles[t0 + 1])
                border = CLS * kk - LANES * s
                if border > 0:
                    value = jnp.where(lane < border, held, value)
                if LANES * (s + 1) > CLS * (kk + 1):
                    held = value
                else:
                    B.gf[pl.ds(base + ROW_HEAD + 125 * g0 + s, 16, stride=125), :] = value

    @pl.when(e.r == ROW_OUT // e.slab)
    def _():
        off = MARGIN + ROW_OUT % e.slab
        for j in range(per):
            at = slice(LANES * j, LANES * (j + 1))
            B.gf[off + j : off + j + 1, :] = B.pb[6:7, at] * e.positions + (
                B.pb[7:8, at] * e.positions + B.pb[8:9, at] * e.positions
            )
            gain = B.pb[12:13, at] + B.pb[13:14, at] + B.pb[14:15, at]
            B.gf[off + per + j : off + per + j + 1, :] = gain
            at = slice(DOUT + LANES * j, DOUT + LANES * (j + 1))
            shift = B.pb[12:13, at] + B.pb[13:14, at] + B.pb[14:15, at]
            B.gf[off + 2 * per + j : off + 2 * per + j + 1, :] = shift

    @pl.when(e.r == ROW_BH // e.slab)
    def _():
        off = MARGIN + ROW_BH % e.slab
        for j in range(CLSP // LANES):
            at = slice(LANES * j, LANES * (j + 1))
            B.gf[off + j : off + j + 1, :] = B.pb[9:10, at] + B.pb[10:11, at] + B.pb[11:12, at]
        rest = FLAT - ROW_BH - CLSP // LANES
        B.gf[off + CLSP // LANES : off + CLSP // LANES + rest, :] = jnp.zeros((rest, LANES), F32)


def norm_copy(e, B, d):
    return remote(e, B.nrm.at[0], B.nrm.at[d], B.s_nrm.at[d], B.r_nrm.at[d], r=lax.rem(e.r + d, e.n))


def squares(v):
    return jnp.sum((v * v).reshape(-1, 8, LANES), 0)


def ph_norm_local(e, B):
    size = 64
    whole = e.slab // size

    def body(k, acc):
        return acc + squares(B.gf[pl.ds(pl.multiple_of(MARGIN + size * k, 8), size), :])

    part = lax.fori_loop(0, whole, body, jnp.zeros((8, LANES), F32))
    v = B.gf[MARGIN + whole * size : MARGIN + e.slab, :]
    B.nrm[0] = part + jnp.broadcast_to(jnp.sum(v * v, 0, keepdims=True) * 0.125, (8, LANES))


def ph_norm(e, B):
    def pieces():
        B.nrm[0] += squares(B.fp[...].astype(F32))

    ends_here(e, pieces)

    @pl.when(e.g == 0)
    def _():
        B.nrm[0] += squares(B.sga[pl.ds(pl.multiple_of(e.i * QUARTER, QUARTER), QUARTER), :])

    for d in range(1, e.n):
        norm_copy(e, B, d).start()


def ph_norm_wait(e, B):
    for d in range(1, e.n):
        norm_copy(e, B, d).wait_recv()
    total = None
    for k in range(e.n):
        part = B.nrm[lax.rem(e.r - k + e.n, e.n)]
        total = part if total is None else total + part
    square = jnp.sum(jnp.sum(total, 0, keepdims=True), 1, keepdims=True)
    B.o_norm[...] = jnp.broadcast_to(jnp.sqrt(square), (8, LANES))
    loss = B.pb[15:16, :]
    loss = loss[:, 0:LANES] + loss[:, LANES : 2 * LANES] + loss[:, 2 * LANES : 3 * LANES]
    B.o_loss[...] = jnp.broadcast_to(loss, (8, LANES))
    for d in range(1, e.n):
        norm_copy(e, B, d).wait_send()


def buffers(e):
    n, G, nb, slab = e.n, e.G, e.nb, e.slab
    tiles = (3, 3, 16, LANES)
    parts = GROUP * nb
    V = pltpu.VMEM
    D = pltpu.SemaphoreType.DMA
    return dict(
        gw=V((n, 2, e.half, LANES), BF16),
        tab=V((TAB_ROWS, LANES), F32),
        big=V((10816, LANES), F32),
        dx=V((8 * DOUT, LANES), F32),
        wup=V((C, HID), BF16),
        wdn=V((HID, C), BF16),
        wds=V((4 * C, DOUT), BF16),
        wh=V((DOUT, CLSP), BF16),
        xg=V((MICRO, 14, COLS, C), BF16),
        xc=V((J * NPOS, LANES), F32),
        kb=V((49 * J, 8, LANES), F32),
        v1=V((NPOS, C), F32),
        rs1=V((NPOS, LANES), F32),
        v2=V((NPOS, C), F32),
        rs2=V((NPOS, LANES), F32),
        n=V((NPOS, C), BF16),
        u=V((NPOS, HID), BF16),
        gp=V((NPOS, HID), BF16),
        z=V((J * NPOS, LANES), F32),
        dz=V((NPOS, C), BF16),
        ps=V((MICRO, 2, OWN, C), F32),
        sl=V((16, C), F32),
        sr=V((G, 16, C), F32),
        dn2=V((32, C), F32),
        dnt=V((MICRO, 2, OWN, C), F32),
        pb=V((16, 4 * C), F32),
        pall=V((parts, 16, 4 * C), BF16),
        acc=V((7, 8, C), F32),
        acup=V((8, HID), F32),
        hs=V((MICRO, 2, 3, COLS, C), BF16),
        hr=V((MICRO, 2, 3, COLS, C), BF16),
        gb=V((PARTS, 4, 2, 2) + tiles, BF16),
        ra1=V((PARTS, 4, 2) + tiles, BF16),
        sa2=V((PARTS, 4) + tiles, BF16),
        ra2=V((PARTS, 4) + tiles, BF16),
        h1=V((PARTS, 4) + tiles, F32),
        sc=V((PARTS, 4) + tiles, BF16),
        rc=V((PARTS, G) + tiles, BF16),
        rb=V((PARTS, nb) + tiles, BF16),
        fp=V((PARTS,) + tiles, BF16),
        ro=V((2, 16) + tiles, BF16),
        ro_up=V((2, 8) + tiles, BF16),
        gf=V((MARGIN + slab + MARGIN, LANES), F32),
        sg=V((SG_ROWS, LANES), F32),
        sg_group=V((GROUP - 1, QUARTER, LANES), F32),
        sg_line=V((G, QUARTER, LANES), F32),
        sgb=V((nb, QUARTER, LANES), F32),
        sga=V((SG_ROWS, LANES), F32),
        nrm=V((n, 8, LANES), F32),
        s_own=D((1,)),
        s_feat=D((MICRO, GROUP)),
        r_feat=D((MICRO, GROUP)),
        s_halo=D((2, MICRO)),
        r_halo=D((2, MICRO)),
        s_tab=D((len(TABLES), G)),
        s_tabg=D((len(TABLES), GROUP)),
        r_tab=D((len(TABLES),)),
        s_line=D((2, G)),
        r_line=D((G, CHUNKS)),
        s_pair=D((G,)),
        r_pair=D((G, CHUNKS)),
        s_row=D((2, G)),
        r_row=D((2, G, CHUNKS)),
        s_core=D((4, G)),
        r_core=D((4, G, CHUNKS)),
        s_patch=D((G,)),
        r_patch=D((G,)),
        s_pb=D((nb,)),
        r_pb=D((nb,)),
        s_pg=D((GROUP,)),
        r_pg=D((GROUP,)),
        s_dy=D((2, MICRO)),
        r_dy=D((2, MICRO)),
        s_out=D((MICRO, 2, GROUP)),
        r_out=D((MICRO, 2, GROUP)),
        s_outown=D((MICRO, 2)),
        s_rs=D((PARTS, 2)),
        r_rs=D((PARTS, 2)),
        s_rc=D((PARTS, 4)),
        r_rc=D((PARTS, G)),
        s_rb=D((PARTS, nb)),
        r_rb=D((PARTS, nb)),
        s_ro=D((PARTS, 2)),
        r_ro=D((PARTS, 16)),
        s_sg=D((GROUP,)),
        r_sg=D((GROUP,)),
        s_sgl=D((G,)),
        r_sgl=D((G,)),
        s_sgg=D((GROUP,)),
        r_sgg=D((GROUP,)),
        s_sgb=D((nb,)),
        r_sgb=D((nb,)),
        s_nrm=D((n,)),
        r_nrm=D((n,)),
    )


def ph_clear(e, B):
    B.sg[...] = jnp.zeros_like(B.sg)
    B.gf[...] = jnp.zeros_like(B.gf)


def ph_result(e, B):
    B.o_grad[...] = B.gf[MARGIN : MARGIN + e.slab, :]


def schedule(e, B):
    def do(step, *args):
        return lambda: step(e, B, *args)

    def level_of(row):
        return row // e.slab // GROUP

    up = range(0, level_of(ROW_CUP - 1) + 1)
    down = range(up.stop, level_of(ROW_VEC - 1) + 1)
    rest = range(down.stop, e.G)
    ph_barrier_signal(e, B)
    ph_cast(e, B)
    ph_feat_zero(e, B)
    ph_clear(e, B)
    ph_barrier_wait(e, B)
    every = range(CHUNKS)
    one, two = range(0, CHUNKS // 2), range(CHUNKS // 2, CHUNKS)

    def hops(some):
        return range(max(max(level, e.G - 1 - level) for level in some) + 1)

    def steps(step, some, which, chunks):
        return [do(step, some, h, chunks) for h in which]

    ph_tables_start(e, B)
    feat_start(e, B, 0)
    line_send(e, B, range(e.G), every)
    tables_forward(e, B, (0, 2))
    feat_start(e, B, 1)
    line_step(e, B, up, 1, every)
    halo_start(e, B, 0)
    feat_start(e, B, 2)
    for h in hops(up)[2:3]:
        line_step(e, B, up, h, every)
    for h in hops(up)[:3]:
        pair_step(e, B, up, h, every)
    tables_wait(e, B, (0, 2))
    ph_taps(e, B)
    ph_conv_fwd(
        e,
        B,
        {
            0: [do(halo_wait, 0), do(transpose, 0)],
            1: [do(halo_start, 1)] + steps(line_step, rest, [1], one),
            2: steps(line_step, rest, [1], two) + steps(line_step, up, hops(up)[3:], every) + steps(pair_step, up, hops(up)[3:], every),
            4: [do(halo_start, 2)] + steps(line_step, down, [1], every) + steps(pair_step, down, hops(down)[:2], every),
            6: [do(halo_wait, 1), do(transpose, 1)],
            7: [do(tables_forward, (1, 3, 4))] + steps(row_step, up, hops(up), one),
            8: steps(line_step, rest, hops(rest)[2:3], one) + steps(pair_step, rest, hops(rest)[:2], every),
            9: steps(row_step, up, hops(up), two),
            10: steps(line_step, rest, hops(rest)[2:3], two),
            11: steps(pair_step, rest, hops(rest)[2:3], every),
            12: [do(halo_wait, 2), do(transpose, 2)]
            + steps(line_step, down, hops(down)[2:], every)
            + steps(pair_step, down, hops(down)[2:], every),
            13: steps(row_step, down, hops(down)[:2], every),
            14: steps(core_step, up, hops(up), one),
            15: steps(line_step, rest, hops(rest)[3:], every) + steps(pair_step, rest, hops(rest)[3:], every),
            16: steps(row_step, rest, [0], every),
            17: steps(core_step, up, hops(up), two),
        },
    )
    ph_norm_one(e, B)
    tables_wait(e, B, (1, 3, 4))
    row_step(e, B, rest, 1, every)
    gather_ready(e, B, up)
    ph_weights_up(e, B)
    ph_mlp_up(
        e,
        B,
        {
            0: steps(row_step, down, hops(down)[2:], every),
            1: steps(row_step, rest, hops(rest)[2:3], every),
            2: steps(core_step, down, hops(down)[:2], every),
            3: steps(row_step, rest, hops(rest)[3:], every) + steps(core_step, rest, [0], every),
            5: steps(core_step, down, hops(down)[2:], every),
        },
    )
    gather_ready(e, B, down)
    ph_weights_down(e, B)
    ph_mlp_down(
        e,
        B,
        {
            0: steps(core_step, rest, [1], every),
            2: steps(core_step, rest, hops(rest)[2:3], every),
            5: steps(core_step, rest, hops(rest)[3:], every),
        },
    )
    ph_patch_local(e, B)
    patch_start(e, B)
    gather_ready(e, B, rest)
    ph_weights_head(e, B)
    patch_wait(e, B)
    ph_head(e, B)
    ph_payload_batch(e, B)
    ph_dy_edges(e, B)
    ph_bwd_one(e, B)
    for f in (0, 1):
        wgrad_down(e, B, f)
        rs_step1(e, B, f)
    ph_bwd_two(
        e,
        B,
        {
            1: [do(ph_payload_group)],
            2: [do(dy_send, 0), do(rs_step2, 0)],
            3: [do(rs_step2, 1)],
            4: [do(dy_send, 1)],
        },
    )
    dy_send(e, B, 2)
    for f in (2, 3):
        wgrad_up(e, B, f)
        rs_step1(e, B, f)
    dy_take(e, B, 0)
    dy_take(e, B, 1)
    rs_step3(e, B, 0)
    ph_conv_kernel(
        e,
        B,
        range(0, MICRO - 1),
        {
            4: [do(rs_step3, 1)],
            6: [do(rs_step2, 2)],
            9: [do(rs_step2, 3)],
            20: [do(rs_step3, 2)],
        },
    )
    dy_take(e, B, MICRO - 1)
    ph_conv_kernel(
        e,
        B,
        range(MICRO - 1, MICRO),
        {
            7: [do(rs_step3, 3)],
            12: [do(rs_step4, 0)],
            17: [do(rs_step4, 1)],
        },
    )
    ph_small_fill(e, B)
    small_step1(e, B)
    ph_feat_done(e, B)
    ph_taps_low(e, B)
    ph_conv_input(
        e,
        B,
        {
            3: [do(out_send, 0, 0)],
            5: [do(rs_step4, 2)],
            6: [do(small_step2), do(out_send, 0, 1)],
            7: [do(rs_step5, 0), do(rs_step4, 3)],
            8: [do(rs_step5, 1)],
            9: [do(rs_step5, 2), do(out_send, 1, 0)],
            11: [do(rs_step5, 3)],
            12: [do(out_send, 1, 1)],
            13: [do(small_step3)],
            15: [do(out_send, 2, 0)],
        },
    )
    ph_payload_wait(e, B)
    ph_head_grads(e, B)
    ph_norm_local(e, B)
    small_step4(e, B)
    ph_norm(e, B)
    out_send(e, B, 2, 1)
    for f in range(PARTS):
        rs_place(e, B, f)
    ph_small_place(e, B)
    ph_result(e, B)
    ph_tables_done(e, B)
    ph_gather_done(e, B)
    ph_dy_done(e, B)
    ph_rs_done(e, B)
    ph_small_done(e, B)
    ph_norm_wait(e, B)
    ph_out_wait(e, B)


def step_kernel(e, names, *refs):
    B = Env()
    for name, ref in zip(names, refs):
        setattr(B, name, ref)
    here(e)
    schedule(e, B)


def train_step(e, features, mask, labels, params):
    bufs = buffers(e)
    names = ["mask", "labels", "features", "params", "o_grad", "o_norm", "o_loss", "fo"] + list(bufs)
    return pl.pallas_call(
        functools.partial(step_kernel, e, names),
        out_shape=(
            jax.ShapeDtypeStruct((e.slab, LANES), F32),
            jax.ShapeDtypeStruct((8, LANES), F32),
            jax.ShapeDtypeStruct((8, LANES), F32),
            jax.ShapeDtypeStruct((MICRO, GROUP, 2, COLS, C), BF16),
        ),
        in_specs=[
            pl.BlockSpec(memory_space=pltpu.SMEM),
            pl.BlockSpec(memory_space=pltpu.SMEM),
            pl.BlockSpec(memory_space=pl.ANY),
            pl.BlockSpec(memory_space=pltpu.VMEM),
        ],
        out_specs=(
            pl.BlockSpec(memory_space=pltpu.VMEM),
            pl.BlockSpec(memory_space=pltpu.VMEM),
            pl.BlockSpec(memory_space=pltpu.VMEM),
            pl.BlockSpec(memory_space=pl.ANY),
        ),
        scratch_shapes=list(bufs.values()),
        compiler_params=pltpu.CompilerParams(collective_id=0, has_side_effects=True, vmem_limit_bytes=64 * MB - 65536),
        name="train_step",
    )(mask, labels, features, params)


def update_kernel(e, norm, loss, grad, params, m1, m2, out, o_norm, o_loss, new_params, first, second, feats, *scratch):
    g, p, a, b, fin, fout, s_in, s_out, s_feat, s_fout = scratch
    parts = 4
    size = e.slab // parts // 8 * 8
    spans = [(k * size, size if k < parts - 1 else e.slab - k * size) for k in range(parts)]
    copy = pltpu.make_async_copy
    ins = []
    for k, (at, count) in enumerate(spans):
        for q, (src, dst) in enumerate(((grad, g), (params, p), (m1, a), (m2, b))):
            ins.append(copy(src.at[pl.ds(at, count)], dst.at[pl.ds(at, count)], s_in.at[k, q]))
            ins[-1].start()
    fins = [copy(out.at[k], fin.at[k], s_feat.at[k]) for k in range(MICRO)]
    for cp in fins:
        cp.start()
    o_norm[0, 0] = jnp.max(norm[...])
    o_loss[0, 0] = jnp.max(loss[...])
    scale = jnp.minimum(1.0, CLIP / (norm[0:1, 0:1] + 1e-06))
    outs = []
    for k, (at, count) in enumerate(spans):
        for q in range(4):
            ins[4 * k + q].wait()
        rows = slice(at, at + count)
        clipped = g[rows, :] * scale
        one = BETA_ONE * a[rows, :] + (1.0 - BETA_ONE) * clipped
        two = BETA_TWO * b[rows, :] + (1.0 - BETA_TWO) * clipped * clipped
        a[rows, :] = one
        b[rows, :] = two
        ratio = one / (1.0 - BETA_ONE**STEP) / (jnp.sqrt(two / (1.0 - BETA_TWO**STEP)) + EPS_ADAM)
        p[rows, :] = p[rows, :] - RATE * (ratio + DECAY * p[rows, :])
        for q, (src, dst) in enumerate(((p, new_params), (a, first), (b, second))):
            outs.append(copy(src.at[pl.ds(at, count)], dst.at[pl.ds(at, count)], s_out.at[k, q]))
            outs[-1].start()
        if k < MICRO:
            fins[k].wait()
            fout[k] = fin[k].astype(F32)
            outs.append(copy(fout.at[k], feats.at[k], s_fout.at[k]))
            outs[-1].start()
    for cp in outs:
        cp.wait()


def update(e, grad, norm, loss, params, m1, m2, out):
    flat = jax.ShapeDtypeStruct((e.slab, LANES), F32)
    scalar = jax.ShapeDtypeStruct((1, 1), F32)
    shape = (MICRO, GROUP, 2, COLS, C)
    near, far, one = (pl.BlockSpec(memory_space=k) for k in (pltpu.VMEM, pl.ANY, pltpu.SMEM))
    D = pltpu.SemaphoreType.DMA
    return pl.pallas_call(
        functools.partial(update_kernel, e),
        in_specs=[near, near, far, far, far, far, far],
        out_specs=(one, one, far, far, far, far),
        out_shape=(scalar, scalar, flat, flat, flat, jax.ShapeDtypeStruct(shape, F32)),
        scratch_shapes=[pltpu.VMEM((e.slab, LANES), F32)] * 4
        + [pltpu.VMEM(shape, BF16), pltpu.VMEM(shape, F32), D((4, 4)), D((4, 3)), D((MICRO,)), D((MICRO,))],
        compiler_params=pltpu.CompilerParams(vmem_limit_bytes=64 * MB - 65536),
        name="update",
    )(norm, loss, grad, params, m1, m2, out)


def local(e, features, drop_mask, labels, params, moment1, moment2):
    flat = [v.reshape(e.slab, LANES) for v in (params, moment1, moment2)]
    grad, norm, loss, out = train_step(e, features, drop_mask, labels, flat[0])
    norm, loss, new_params, first, second, feats = update(e, grad, norm, loss, *flat, out)
    size = e.slab * LANES
    return (
        new_params.reshape(size),
        first.reshape(size),
        second.reshape(size),
        loss.reshape(()),
        norm.reshape(()),
        feats,
    )


def solution(mesh):
    e = Env()
    e.n = mesh.shape["rows"]
    e.nb = mesh.shape["batch"]
    e.G = e.n // GROUP
    e.slab = FLAT // e.n
    e.half = (e.slab + 31) // 32 * 16
    e.positions = float(e.n * COLS // 2)
    e.inv_count = 1.0 / (MICRO * GROUP * e.nb)
    return jax.shard_map(
        functools.partial(local, e),
        mesh=mesh,
        in_specs=(
            P(None, "batch", "rows", None, None),
            P(None, "batch"),
            P(None, "batch"),
            P("rows"),
            P("rows"),
            P("rows"),
        ),
        out_specs=(P("rows"), P("rows"), P("rows"), P(), P(), P(None, "batch", "rows", None, None)),
        check_vma=False,
    )
```
